32 devices in a mesh: fsdp: 2 (over y), ctx: 16 (over z, x, core).
Axes of the slice: x: 2, y: 2, z: 4, core: 2. Of those that a mesh axis runs over, the one named last changes fastest.
Arguments:
- tokens: bfloat16 [16, 2048, 576], P('fsdp', 'ctx'), may hold values from -6 to 6
- gain_attn: bfloat16 [576], P('fsdp'), may hold values from 0.5 to 1.5
- w_query: bfloat16 [576, 576], P('fsdp'), may hold values from -0.25 to 0.25
- w_key: bfloat16 [576, 192], P('fsdp'), may hold values from -0.25 to 0.25
- w_value: bfloat16 [576, 192], P('fsdp'), may hold values from -0.25 to 0.25
- w_out: bfloat16 [576, 576], P('fsdp'), may hold values from -2 to 2
- gain_ffn: bfloat16 [576], P('fsdp'), may hold values from 0.5 to 1.5
- w_gate: bfloat16 [576, 1536], P('fsdp'), may hold values from -0.25 to 0.25
- w_up: bfloat16 [576, 1536], P('fsdp'), may hold values from -0.25 to 0.25
- w_down: bfloat16 [1536, 576], P('fsdp'), may hold values from -0.15625 to 0.15625
- cotangent: bfloat16 [16, 2048, 576], P('fsdp', 'ctx'), may hold values from -6 to 6
Outputs:
- mixed_out: bfloat16 [16, 2048, 576], P('fsdp', 'ctx')
- grad_tokens: bfloat16 [16, 2048, 576], P('fsdp', 'ctx')
- grad_gain_attn: float32 [576], P('fsdp')
- grad_query: float32 [576, 576], P('fsdp')
- grad_key: float32 [576, 192], P('fsdp')
- grad_value: float32 [576, 192], P('fsdp')
- grad_out: float32 [576, 576], P('fsdp')
- grad_gain_ffn: float32 [576], P('fsdp')
- grad_gate: float32 [576, 1536], P('fsdp')
- grad_up: float32 [576, 1536], P('fsdp')
- grad_down: float32 [1536, 576], P('fsdp')
The draws below stay inside these ranges and needn't reach their ends.
All inputs are finite; a program needn't handle non-finite values.
Results may differ from the reference program's by a relative error of at most 0.03.
Values may be sent and summed in bfloat16 or wider, within the bound.
No kernel may reach another device: no remote copies, remote signals or barrier semaphores. Data moves between devices by JAX's collectives and lax.ppermute only.
A program may use at most 256 MiB of HBM per device.

```python
import math
import jax
import jax.numpy as jnp
from jax import lax

D = 576
HEADS = 9
KV_HEADS = 3
HEAD_DIM = 64
FF = 1536
SEQS = 16
LENGTH = 2048


def steps_of(own_key, dims, pieces, smallest, top_value):
    level = 1.0
    for position, blocks in pieces:
        heights = jax.random.uniform(jax.random.fold_in(jax.random.fold_in(own_key, 6), position), (blocks,), jnp.float32, smallest / len(pieces), top_value / len(pieces))
        level = level * jnp.repeat(jnp.exp(heights), dims[position] // blocks).reshape((-1,) + (1,) * (len(dims) - 1 - position))
    return level


def normal_values(own_key, extent, scale, limit, pieces=(), held_as=jnp.bfloat16):
    factor_of = steps_of(own_key, extent, pieces, -0.22, 0.18) if pieces else 1.0
    values = jax.random.normal(own_key, extent, jnp.float32) * scale * factor_of
    return jnp.minimum(jnp.maximum(values, -limit), limit).astype(held_as)


def setup_inputs(seed: int = 0) -> dict:
    arg_keys = jax.random.split(jax.random.key(seed), 12)
    tokens = normal_values(arg_keys[0], (SEQS, LENGTH, D), 1.0, 6.0, ((0, 2), (1, 16)))
    gain_attn = jnp.clip(1.0 + 0.1 * jax.random.normal(arg_keys[1], (D,), jnp.float32), 0.5, 1.5).astype(jnp.bfloat16)
    w_query = normal_values(arg_keys[2], (D, D), D ** -0.5, 0.25, ((0, 2),))
    w_key = normal_values(arg_keys[3], (D, KV_HEADS * HEAD_DIM), D ** -0.5, 0.25, ((0, 2),))
    w_value = normal_values(arg_keys[4], (D, KV_HEADS * HEAD_DIM), D ** -0.5, 0.25, ((0, 2),))
    w_out = normal_values(arg_keys[5], (D, D), (max(D // 64, 1)) ** -0.5, 2.0, ((0, 2),))
    gain_ffn = jnp.clip(1.0 + 0.1 * jax.random.normal(arg_keys[6], (D,), jnp.float32), 0.5, 1.5).astype(jnp.bfloat16)
    w_gate = normal_values(arg_keys[7], (D, FF), D ** -0.5, 0.25, ((0, 2),))
    w_up = normal_values(arg_keys[8], (D, FF), D ** -0.5, 0.25, ((0, 2),))
    w_down = normal_values(arg_keys[9], (FF, D), FF ** -0.5, 0.15625, ((0, 2),))
    cotangent = normal_values(arg_keys[10], (SEQS, LENGTH, D), 1.0, 6.0, ((0, 2), (1, 16)))
    return dict(tokens=tokens, gain_attn=gain_attn, w_query=w_query, w_key=w_key, w_value=w_value, w_out=w_out, gain_ffn=gain_ffn, w_gate=w_gate, w_up=w_up, w_down=w_down, cotangent=cotangent)


EPSILON = 1e-05
THETA = 100000.0
NEGATIVE = -1e+30
HIGHEST = lax.Precision.HIGHEST

@jax.custom_vjp
def low(v):
    return lax.optimization_barrier(v.astype(jnp.bfloat16)).astype(jnp.float32)

@jax.custom_vjp
def low_back(v):
    return v

def low_keep(v):
    return (low(v), None)

def low_pass(kept, grad):
    return (grad,)

def back_keep(v):
    return (v, None)

def back_low(kept, grad):
    return (low(grad),)
low.defvjp(low_keep, low_pass)
low_back.defvjp(back_keep, back_low)

def rope_tables(positions, head_size):
    halves = head_size // 2
    frequency = THETA ** (-jnp.arange(halves, dtype=jnp.float32) * 2.0 / head_size)
    angles = positions.astype(jnp.float32)[:, None] * frequency[None, :]
    return (jnp.cos(angles), jnp.sin(angles))

def rotate(values, cosine, sine):
    halves = values.shape[-1] // 2
    leading = values[..., :halves]
    trailing = values[..., halves:]
    cos_rows = cosine[:, None, :]
    sin_rows = sine[:, None, :]
    return jnp.concatenate([leading * cos_rows - trailing * sin_rows, trailing * cos_rows + leading * sin_rows], axis=-1)

def rms_scale(values):
    return lax.rsqrt(lax.optimization_barrier(jnp.mean(values * values, axis=-1, keepdims=True)) + EPSILON)

def product(left, right):
    return jnp.dot(left, right, preferred_element_type=jnp.float32, precision=HIGHEST)

def attend_block(query_block, block_start, key_all, value_all):
    factor = HEAD_DIM ** (-0.5)
    span_rows = query_block.shape[0]
    scores = jnp.einsum('qkgd,nkd->kgqn', query_block, key_all, precision=HIGHEST) * factor
    scores = low_back(scores)
    query_pos = block_start + jnp.arange(span_rows, dtype=jnp.int32)
    key_pos = jnp.arange(key_all.shape[0], dtype=jnp.int32)
    causal = query_pos[:, None] >= key_pos[None, :]
    scores = jnp.where(causal, scores, NEGATIVE)
    top_row = lax.optimization_barrier(jnp.max(scores, axis=-1, keepdims=True))
    exponent = jnp.exp(scores - top_row)
    weights = low(exponent / lax.optimization_barrier(jnp.sum(exponent, axis=-1, keepdims=True)))
    return jnp.einsum('kgqn,nkd->qkgd', weights, value_all, precision=HIGHEST)

def sequence_forward(source, gain_attn, w_query, w_key, w_value, w_out, gain_ffn, w_gate, w_up, w_down):
    length_now = source.shape[0]
    group_size = HEADS // KV_HEADS
    cosine, sine = rope_tables(jnp.arange(length_now, dtype=jnp.int32), HEAD_DIM)
    hidden_one = low(source * rms_scale(source) * gain_attn)
    query_lin = low_back(product(hidden_one, w_query))
    key_lin = low_back(product(hidden_one, w_key))
    value_all = low(low_back(product(hidden_one, w_value))).reshape(length_now, KV_HEADS, HEAD_DIM)
    query_rot = low(rotate(query_lin.reshape(length_now, HEADS, HEAD_DIM), cosine, sine))
    query_rot = query_rot.reshape(length_now, KV_HEADS, group_size, HEAD_DIM)
    key_rot = low(rotate(key_lin.reshape(length_now, KV_HEADS, HEAD_DIM), cosine, sine))
    block_rows = math.gcd(512, length_now)
    block_count = length_now // block_rows
    query_blocks = query_rot.reshape(block_count, block_rows, KV_HEADS, group_size, HEAD_DIM)
    block_starts = jnp.arange(block_count, dtype=jnp.int32) * block_rows
    checked = jax.checkpoint(attend_block)

    def one_block(couple):
        return checked(couple[0], couple[1], key_rot, value_all)
    attended = lax.map(one_block, (query_blocks, block_starts))
    attn_mixed = low(low_back(attended.reshape(length_now, HEADS * HEAD_DIM)))
    residual = source + low_back(product(attn_mixed, w_out))
    hidden_two = low(residual * rms_scale(residual) * gain_ffn)
    gate_lin = low_back(product(hidden_two, w_gate))
    up_lin = low_back(product(hidden_two, w_up))
    activated = low(jax.nn.silu(gate_lin) * up_lin)
    return residual + product(activated, w_down)

def reference(tokens, gain_attn, w_query, w_key, w_value, w_out, gain_ffn, w_gate, w_up, w_down, cotangent):
    weights = tuple((weight.astype(jnp.float32) for weight in (gain_attn, w_query, w_key, w_value, w_out, gain_ffn, w_gate, w_up, w_down)))

    def one_sequence(totals, couple):
        seq_tokens, seq_cot = couple
        result, pullback = jax.vjp(sequence_forward, seq_tokens.astype(jnp.float32), *weights)
        grads_all = pullback(seq_cot.astype(jnp.float32))
        totals = tuple((summed + grad_one for summed, grad_one in zip(totals, grads_all[1:])))
        return (totals, (result.astype(jnp.bfloat16), grads_all[0].astype(jnp.bfloat16)))
    initial = tuple((jnp.zeros_like(weight) for weight in weights))
    totals, outputs = lax.scan(one_sequence, initial, (tokens, cotangent))
    return (outputs[0], outputs[1], totals[0], totals[1], totals[2], totals[3], totals[4], totals[5], totals[6], totals[7], totals[8])
```

```python
import jax, functools
import jax.numpy as jnp
from jax import lax
from jax.experimental import pallas as pl
from jax.experimental.pallas import tpu as pltpu
F32=jnp.float32; BF=jnp.bfloat16
NT=(((1,),(1,)),((),()))
NN=(((1,),(0,)),((),()))
def mm(a,b,dims=NN):
    return lax.dot_general(a,b,dims,preferred_element_type=F32)

def heads_of(ref, kv, group):
    return jnp.concatenate([ref[(kv*group+h)*64:(kv*group+h+1)*64,:] for h in range(group)],axis=1)

def fwd_kernel(bias_ref, q_ref, kv_ref, o_ref, lse_ref, k_scr, m_scr, acc_scr, *, kvs, group, slots, rows):
    i=pl.program_id(0)
    kw=kvs*64
    @pl.when(i==0)
    def _():
        for s in range(slots):
            for h in range(kvs):
                k_scr[h,s]=kv_ref[s,h*64:(h+1)*64,:].T
    qs=[heads_of(q_ref,h,group) for h in range(kvs)]
    width=group*128
    m_scr[...]=jnp.full(m_scr.shape,-1e30,F32)
    acc_scr[...]=jnp.zeros(acc_scr.shape,F32)
    ones=jnp.ones((8,slots*128),BF)
    def chunk(c, masked):
        off=pl.multiple_of(c*128,128)
        for h in range(kvs):
            k=jnp.concatenate([k_scr[h,s,pl.ds(off,128),:] for s in range(slots)],axis=0)
            v=jnp.concatenate([kv_ref[s,kw+h*64:kw+(h+1)*64,pl.ds(off,128)] for s in range(slots)],axis=1)
            v=jnp.concatenate([v,ones],axis=0)
            st=mm(k,qs[h])
            if masked:
                b=bias_ref[...].reshape(slots*128,128)
                st=st+jnp.concatenate([b]*group,axis=1)
            m_old=m_scr[h:h+1,:]
            m_new=jnp.maximum(m_old,jnp.max(st,axis=0,keepdims=True))
            p=jnp.exp2(st-m_new).astype(BF)
            acc_scr[h]=acc_scr[h]*jnp.exp2(m_old-m_new)+mm(v,p)
            m_scr[h:h+1,:]=m_new
    def body(c,_):
        chunk(c,False); return 0
    lax.fori_loop(0,i,body,0)
    chunk(i,True)
    for h in range(kvs):
        acc=acc_scr[h]
        tot=acc[64:65,:]
        o=acc[:64,:]*(1.0/tot)
        lse=m_scr[h:h+1,:]+jnp.log2(tot)
        for g in range(group):
            r=h*group+g
            o_ref[r*64:(r+1)*64,:]=o[:,g*128:(g+1)*128]
            lse_ref[r:r+1,:]=lse[:,g*128:(g+1)*128]

def attn_fwd(bias, qT, kvT, kvs=3, group=3):
    slots,_,rows=kvT.shape
    n=rows//128
    heads=kvs*group
    return pl.pallas_call(
        functools.partial(fwd_kernel,kvs=kvs,group=group,slots=slots,rows=rows),
        grid=(n,),
        in_specs=[pl.BlockSpec((slots,128,128),lambda i:(0,0,0)),
                  pl.BlockSpec((heads*64,128),lambda i:(0,i)),
                  pl.BlockSpec((slots,2*kvs*64,rows),lambda i:(0,0,0))],
        out_specs=[pl.BlockSpec((heads*64,128),lambda i:(0,i)),
                   pl.BlockSpec((16,128),lambda i:(0,i))],
        out_shape=[jax.ShapeDtypeStruct((heads*64,rows),F32),jax.ShapeDtypeStruct((16,rows),F32)],
        scratch_shapes=[pltpu.VMEM((kvs,slots,rows,64),BF),pltpu.VMEM((8,group*128),F32),
                        pltpu.VMEM((kvs,72,group*128),F32)],
        compiler_params=pltpu.CompilerParams(vmem_limit_bytes=56*2**20),
        cost_estimate=pl.CostEstimate(flops=int(6e9),bytes_accessed=int(8e6),transcendentals=int(1e7)),
    )(bias,qT,kvT)

def bwd_kernel(bias_ref, q_ref, kv_ref, do_ref, lse_ref, rd_ref, dq_ref, dkv_ref, kv_scr, acc_scr, *, kvs, group, slots, rows, n):
    i=pl.program_id(0)
    kw=kvs*64
    @pl.when(i==0)
    def _():
        for s in range(slots):
            for h in range(2*kvs):
                kv_scr[h,s]=kv_ref[s,h*64:(h+1)*64,:].T
        acc_scr[...]=jnp.zeros(acc_scr.shape,F32)
    dq_ref[...]=jnp.zeros(dq_ref.shape,F32)
    qs=[heads_of(q_ref,h,group) for h in range(kvs)]
    dos=[heads_of(do_ref,h,group) for h in range(kvs)]
    lses=[jnp.concatenate([lse_ref[h*group+g:h*group+g+1,:] for g in range(group)],axis=1) for h in range(kvs)]
    rds=[jnp.concatenate([rd_ref[h*group+g:h*group+g+1,:] for g in range(group)],axis=1) for h in range(kvs)]
    def chunk(c, masked):
        off=pl.multiple_of(c*128,128)
        for h in range(kvs):
            k=jnp.concatenate([kv_scr[h,s,pl.ds(off,128),:] for s in range(slots)],axis=0)
            v=jnp.concatenate([kv_scr[kvs+h,s,pl.ds(off,128),:] for s in range(slots)],axis=0)
            kT=jnp.concatenate([kv_ref[s,h*64:(h+1)*64,pl.ds(off,128)] for s in range(slots)],axis=1)
            st=mm(k,qs[h])
            if masked:
                b=bias_ref[...].reshape(slots*128,128)
                st=st+jnp.concatenate([b]*group,axis=1)
            p=jnp.exp2(st-lses[h])
            dp=mm(v,dos[h])
            ds=(p*(dp-rds[h])).astype(BF)
            dk=mm(qs[h],ds,NT)
            dv=mm(dos[h],p.astype(BF),NT)
            dq=mm(kT,ds)
            for s in range(slots):
                acc_scr[s,h*64:(h+1)*64,pl.ds(off,128)]+=dk[:,s*128:(s+1)*128]
                acc_scr[s,kw+h*64:kw+(h+1)*64,pl.ds(off,128)]+=dv[:,s*128:(s+1)*128]
            for g in range(group):
                r=h*group+g
                dq_ref[r*64:(r+1)*64,:]+=dq[:,g*128:(g+1)*128]
    def body(c,_):
        chunk(c,False); return 0
    lax.fori_loop(0,i,body,0)
    chunk(i,True)
    @pl.when(i==n-1)
    def _():
        dkv_ref[...]=acc_scr[...]

def attn_bwd(bias, qT, kvT, doT, lse, rd, kvs=3, group=3):
    slots,_,rows=kvT.shape
    n=rows//128
    heads=kvs*group
    return pl.pallas_call(
        functools.partial(bwd_kernel,kvs=kvs,group=group,slots=slots,rows=rows,n=n),
        grid=(n,),
        in_specs=[pl.BlockSpec((slots,128,128),lambda i:(0,0,0)),
                  pl.BlockSpec((heads*64,128),lambda i:(0,i)),
                  pl.BlockSpec((slots,2*kvs*64,rows),lambda i:(0,0,0)),
                  pl.BlockSpec((heads*64,128),lambda i:(0,i)),
                  pl.BlockSpec((16,128),lambda i:(0,i)),
                  pl.BlockSpec((16,128),lambda i:(0,i))],
        out_specs=[pl.BlockSpec((heads*64,128),lambda i:(0,i)),
                   pl.BlockSpec((slots,2*kvs*64,rows),lambda i:(0,0,0))],
        out_shape=[jax.ShapeDtypeStruct((heads*64,rows),F32),jax.ShapeDtypeStruct((slots,2*kvs*64,rows),F32)],
        scratch_shapes=[pltpu.VMEM((2*kvs,slots,rows,64),BF),pltpu.VMEM((slots,2*kvs*64,rows),F32)],
        compiler_params=pltpu.CompilerParams(vmem_limit_bytes=56*2**20),
        cost_estimate=pl.CostEstimate(flops=int(15e9),bytes_accessed=int(16e6),transcendentals=int(1e7)),
    )(bias,qT,kvT,doT,lse,rd)


from jax.sharding import PartitionSpec as P

HEADS = 9
KV_HEADS = 3
HEAD_DIM = 64
EPSILON = 1e-05
THETA = 100000.0
NEGATIVE = -1e30
LOG2E = 1.4426950408889634
LN2 = 0.6931471805599453


def swap(x, axis, bit):
    n = lax.axis_size(axis)
    return lax.ppermute(x, axis, [(i, i ^ (1 << bit)) for i in range(n)])


def bit_of(axis, bit):
    return (lax.axis_index(axis) >> bit) & 1


def in_order(flag, mine, other, axis):
    return jnp.where(
        flag == 0,
        jnp.concatenate([mine, other], axis=axis),
        jnp.concatenate([other, mine], axis=axis),
    )


def gather_rows(shard, split):
    if lax.axis_size("fsdp") != 2:
        return lax.all_gather(shard, "fsdp", axis=0, tiled=True)
    core = bit_of("ctx", 0)
    half = shard.shape[split] // 2
    mine = lax.dynamic_slice_in_dim(shard, core * half, half, split)
    got = swap(mine, "fsdp", 0)
    other = in_order(core, got, swap(got, "ctx", 0), split)
    return in_order(bit_of("fsdp", 0), shard, other, 0)


def half_sum(x, axis, bit, dim):
    me = bit_of(axis, bit)
    half = x.shape[dim] // 2
    keep = lax.dynamic_slice_in_dim(x, me * half, half, dim)
    send = lax.dynamic_slice_in_dim(x, (1 - me) * half, half, dim)
    got = swap(send, axis, bit)
    return (keep.astype(F32) + got.astype(F32)).astype(BF)


def half_join(x, axis, bit, dim):
    return in_order(bit_of(axis, bit), x, swap(x, axis, bit), dim)


def reduce_rows(x):
    x = x.astype(BF)
    count = lax.axis_size("ctx")
    if lax.axis_size("fsdp") != 2 or count != 16:
        mine = lax.psum_scatter(x, "fsdp", scatter_dimension=0, tiled=True)
        return lax.psum(mine, "ctx").astype(F32)
    wide = x.shape[1] % 512 == 0
    if wide:
        stages = [("ctx", 0, 1), ("fsdp", 0, 0), ("ctx", 1, 1), ("ctx", 2, 0), ("ctx", 3, 0)]
    else:
        rows = x.shape[0]
        x = x.reshape(2, rows // 2, x.shape[1])
        stages = [("ctx", 0, 1), ("fsdp", 0, 0), ("ctx", 1, 1), ("ctx", 2, 1), ("ctx", 3, 1)]
    for axis, bit, dim in stages:
        x = half_sum(x, axis, bit, dim)
    for axis, bit, dim in reversed(stages):
        if axis == "ctx":
            x = half_join(x, axis, bit, dim)
    if not wide:
        x = x.reshape(rows // 2, x.shape[2])
    return x.astype(F32)


def rms_scale(values):
    return lax.rsqrt(jnp.mean(values * values, axis=-1, keepdims=True) + EPSILON)


def rotate_t(values, cosine, sine):
    halves = values.shape[1] // 2
    a, b = values[:, :halves], values[:, halves:]
    return jnp.concatenate([a * cosine - b * sine, b * cosine + a * sine], axis=1)


def norm_backward(grad_hidden, normed, scale_rows, gain_rows):
    grad_gain = jnp.sum(grad_hidden * normed, axis=0)
    grad_normed = grad_hidden * gain_rows
    inner_mean = jnp.mean(grad_normed * normed, axis=-1, keepdims=True)
    return grad_gain, scale_rows * (grad_normed - normed * inner_mean)


def local(tokens, gain_attn, w_query, w_key, w_value, w_out, gain_ffn, w_gate, w_up, w_down, cotangent):
    seqs, length, width = tokens.shape
    count = lax.axis_size("ctx")
    team = count // seqs
    sub = length // team
    rows = count * sub
    kv_width = KV_HEADS * HEAD_DIM
    index = lax.axis_index("ctx")
    place = index % team

    def spread(x):
        x = x.reshape(count, sub, width)
        return lax.all_to_all(x, "ctx", 0, 0, tiled=True).reshape(rows, width)

    def home(x):
        x = lax.all_to_all(x.reshape(count, sub, width), "ctx", 0, 0, tiled=True)
        return x.reshape(seqs, length, width)

    source_low = spread(tokens)
    gains = jnp.zeros((8, w_gate.shape[1]), BF)
    own = gain_attn.shape[0]
    gains = gains.at[0, :own].set(gain_attn).at[1, :own].set(gain_ffn)
    first = jnp.concatenate([w_query, w_key, w_value, w_out], axis=1)
    first = jnp.concatenate([first, gains], axis=0)
    first = gather_rows(first, 1).reshape(-1, own + 8, first.shape[1])
    gain_first = first[:, own, :own].reshape(width).astype(F32)
    gain_second = first[:, own + 1, :own].reshape(width).astype(F32)
    first = first[:, :own].reshape(width, first.shape[2])
    gate_w, up_w, down_w = gather_rows(w_gate, 1), gather_rows(w_up, 1), gather_rows(w_down, 0)
    cot_rows = spread(cotangent)
    qkv_cols = width + 2 * kv_width
    qkv_w, out_w = first[:, :qkv_cols], first[:, qkv_cols:]

    row = jnp.arange(rows, dtype=jnp.int32)
    position = (row // sub) * length + place * sub + row % sub
    frequency = THETA ** (-jnp.arange(HEAD_DIM // 2, dtype=F32) * 2.0 / HEAD_DIM)
    angles = frequency[:, None] * position.astype(F32)[None, :]
    cosine, sine = jnp.cos(angles), jnp.sin(angles)

    source = source_low.astype(F32)
    scale_one = rms_scale(source)
    normed_one = source * scale_one
    hidden_one = (normed_one * gain_first).astype(BF)
    qkv = lax.dot_general(qkv_w, hidden_one, (((0,), (1,)), ((), ())), preferred_element_type=F32)
    query = rotate_t(qkv[:width].reshape(HEADS, HEAD_DIM, rows), cosine, sine)
    query = (query * (HEAD_DIM**-0.5 * LOG2E)).astype(BF).reshape(width, rows)
    key = rotate_t(qkv[width : width + kv_width].reshape(KV_HEADS, HEAD_DIM, rows), cosine, sine)
    kv_own = jnp.concatenate([key.reshape(kv_width, rows), qkv[width + kv_width :]], axis=0).astype(BF)
    groups = [[t * team + p for p in range(team)] for t in range(seqs)]
    if team == 2:
        kv_all = jnp.stack([kv_own, swap(kv_own, "ctx", 0)])
        slots = jnp.stack([place, 1 - place])
    else:
        kv_all = lax.all_gather(kv_own, "ctx", axis=0, axis_index_groups=groups)
        slots = jnp.arange(team)
    head_row = jnp.arange(128, dtype=jnp.int32)
    base = (head_row // sub) * length + head_row % sub
    key_pos = base[None, :] + slots[:, None] * sub
    query_pos = base + place * sub
    bias = jnp.where(key_pos[:, :, None] <= query_pos[None, None, :], 0.0, NEGATIVE).astype(F32)

    attended, log_total = attn_fwd(bias, query, kv_all)
    mixed = attended.astype(BF)
    residual = source + lax.dot_general(mixed, out_w, (((0,), (0,)), ((), ())), preferred_element_type=F32)
    scale_two = rms_scale(residual)
    normed_two = residual * scale_two
    hidden_two = (normed_two * gain_second).astype(BF)
    gate_lin = mm(hidden_two, gate_w)
    up_lin = mm(hidden_two, up_w)
    sigmoid_gate = jax.nn.sigmoid(gate_lin)
    silu_gate = gate_lin * sigmoid_gate
    activated = (silu_gate * up_lin).astype(BF)
    mixed_out = home((residual + mm(activated, down_w)).astype(BF))

    grad_act = mm(cot_rows, down_w, NT)
    grad_down = mm(activated.T, cot_rows)
    d_gate = (grad_act * up_lin * sigmoid_gate * (1.0 + gate_lin * (1.0 - sigmoid_gate))).astype(BF)
    d_up = (grad_act * silu_gate).astype(BF)
    grad_gate = mm(hidden_two.T, d_gate)
    grad_up = mm(hidden_two.T, d_up)
    d_hidden_two = mm(d_gate, gate_w, NT) + mm(d_up, up_w, NT)
    grad_gain_ffn, d_norm = norm_backward(d_hidden_two, normed_two, scale_two, gain_second)
    d_residual = cot_rows.astype(F32) + d_norm
    d_res_low = d_residual.astype(BF)
    grad_out = mm(mixed, d_res_low)
    d_attended = lax.dot_general(out_w, d_res_low, NT, preferred_element_type=F32).astype(BF)
    row_dot = jnp.sum((d_attended.astype(F32) * attended).reshape(HEADS, HEAD_DIM, rows), axis=1)
    row_dot = jnp.pad(row_dot, ((0, 16 - HEADS), (0, 0)))
    own_down, own_gate, own_up = reduce_rows(grad_down), reduce_rows(grad_gate), reduce_rows(grad_up)

    d_query, d_kv = attn_bwd(bias, query, kv_all, d_attended, log_total, row_dot)
    d_query = d_query * (HEAD_DIM**-0.5)
    if team == 2:
        d_kv = d_kv[0] + swap(d_kv[1].astype(BF), "ctx", 0).astype(F32)
    else:
        d_kv = lax.psum_scatter(
            d_kv.astype(BF), "ctx", scatter_dimension=0, axis_index_groups=groups
        ).astype(F32)
    d_key = d_kv[:kv_width] * LN2
    d_query = rotate_t(d_query.reshape(HEADS, HEAD_DIM, rows), cosine, -sine).reshape(width, rows)
    d_key = rotate_t(d_key.reshape(KV_HEADS, HEAD_DIM, rows), cosine, -sine).reshape(kv_width, rows)
    d_qkv = jnp.concatenate([d_query, d_key, d_kv[kv_width:]], axis=0).astype(BF)
    grad_qkv = lax.dot_general(hidden_one, d_qkv, (((0,), (1,)), ((), ())), preferred_element_type=F32)
    d_hidden_one = lax.dot_general(d_qkv, qkv_w, (((0,), (1,)), ((), ())), preferred_element_type=F32)
    grad_gain_attn, d_norm = norm_backward(d_hidden_one, normed_one, scale_one, gain_first)
    grad_tokens = home((d_residual + d_norm).astype(BF))
    own_first = reduce_rows(jnp.concatenate([grad_qkv, grad_out], axis=1))
    gain_grads = jnp.stack([grad_gain_attn, grad_gain_ffn], axis=1).astype(BF)
    gain_grads = lax.psum(gain_grads, ("fsdp", "ctx"))
    gain_grads = lax.dynamic_slice_in_dim(gain_grads, lax.axis_index("fsdp") * own, own, 0).astype(F32)
    return (
        mixed_out,
        grad_tokens,
        gain_grads[:, 0],
        own_first[:, :width],
        own_first[:, width : width + kv_width],
        own_first[:, width + kv_width : qkv_cols],
        own_first[:, qkv_cols:],
        gain_grads[:, 1],
        own_gate,
        own_up,
        own_down,
    )


def solution(mesh):
    rows, flat, seq = P("fsdp", None), P("fsdp"), P("fsdp", "ctx", None)
    return jax.shard_map(
        local,
        mesh=mesh,
        in_specs=(seq, flat, rows, rows, rows, rows, flat, rows, rows, rows, seq),
        out_specs=(seq, seq, flat, rows, rows, rows, rows, flat, rows, rows, rows),
        check_vma=False,
    )
```

```python
import functools

import jax
import jax.numpy as jnp
from jax import lax
from jax.experimental import pallas as pl
from jax.experimental.pallas import tpu as pltpu
from jax.sharding import PartitionSpec as P

HEADS = 9
KV_HEADS = 3
HEAD_DIM = 64
EPSILON = 1e-05
THETA = 100000.0
NEGATIVE = -1e30
LOG2E = 1.4426950408889634
LN2 = 0.6931471805599453
F32=jnp.float32; BF=jnp.bfloat16
NT=(((1,),(1,)),((),()))
NN=(((1,),(0,)),((),()))
def mm(a,b,dims=NN):
    return lax.dot_general(a,b,dims,preferred_element_type=F32)

def heads_of(ref, kv, group):
    return jnp.concatenate([ref[(kv*group+h)*64:(kv*group+h+1)*64,:] for h in range(group)],axis=1)

def fwd_kernel(bias_ref, q_ref, kv_ref, o_ref, lse_ref, k_scr, m_scr, acc_scr, *, kvs, group, slots, rows, qb):
    i=pl.program_id(0)
    kw=kvs*64
    @pl.when(i==0)
    def _():
        for s in range(slots):
            for h in range(kvs):
                k_scr[h,s]=kv_ref[s,h*64:(h+1)*64,:].T
    qs=[heads_of(q_ref,h,group) for h in range(kvs)]
    width=group*qb
    m_scr[...]=jnp.full(m_scr.shape,-1e30,F32)
    acc_scr[...]=jnp.zeros(acc_scr.shape,F32)
    ones=jnp.ones((8,slots*qb),BF)
    def chunk(c, masked):
        off=pl.multiple_of(c*qb,qb)
        for h in range(kvs):
            k=jnp.concatenate([k_scr[h,s,pl.ds(off,qb),:] for s in range(slots)],axis=0)
            v=jnp.concatenate([kv_ref[s,kw+h*64:kw+(h+1)*64,pl.ds(off,qb)] for s in range(slots)],axis=1)
            v=jnp.concatenate([v,ones],axis=0)
            st=mm(k,qs[h])
            if masked:
                b=bias_ref[...].reshape(slots*qb,qb)
                st=st+jnp.concatenate([b]*group,axis=1)
            m_old=m_scr[h:h+1,:]
            m_new=jnp.maximum(m_old,jnp.max(st,axis=0,keepdims=True))
            p=jnp.exp2(st-m_new).astype(BF)
            acc_scr[h]=acc_scr[h]*jnp.exp2(m_old-m_new)+mm(v,p)
            m_scr[h:h+1,:]=m_new
    def body(c,_):
        chunk(c,False); return 0
    lax.fori_loop(0,i,body,0)
    chunk(i,True)
    for h in range(kvs):
        acc=acc_scr[h]
        tot=acc[64:65,:]
        o=acc[:64,:]*(1.0/tot)
        lse=m_scr[h:h+1,:]+jnp.log2(tot)
        for g in range(group):
            r=h*group+g
            o_ref[r*64:(r+1)*64,:]=o[:,g*qb:(g+1)*qb]
            lse_ref[r:r+1,:]=lse[:,g*qb:(g+1)*qb]

def attn_fwd(bias, qT, kvT, kvs=3, group=3, qb=256):
    slots,_,rows=kvT.shape
    n=rows//qb
    heads=kvs*group
    return pl.pallas_call(
        functools.partial(fwd_kernel,kvs=kvs,group=group,slots=slots,rows=rows,qb=qb),
        grid=(n,),
        in_specs=[pl.BlockSpec((slots,qb,qb),lambda i:(0,0,0)),
                  pl.BlockSpec((heads*64,qb),lambda i:(0,i)),
                  pl.BlockSpec((slots,2*kvs*64,rows),lambda i:(0,0,0))],
        out_specs=[pl.BlockSpec((heads*64,qb),lambda i:(0,i)),
                   pl.BlockSpec((16,qb),lambda i:(0,i))],
        out_shape=[jax.ShapeDtypeStruct((heads*64,rows),F32),jax.ShapeDtypeStruct((16,rows),F32)],
        scratch_shapes=[pltpu.VMEM((kvs,slots,rows,64),BF),pltpu.VMEM((8,group*qb),F32),
                        pltpu.VMEM((kvs,72,group*qb),F32)],
        compiler_params=pltpu.CompilerParams(vmem_limit_bytes=56*2**20),
        cost_estimate=pl.CostEstimate(flops=int(25e9),bytes_accessed=int(8e6),transcendentals=int(1e7)),
    )(bias,qT,kvT)

def bwd_kernel(*refs, kvs, group, slots, qb, lo, first, last):
    bias_ref, q_ref, kv_ref, do_ref, lse_ref, rd_ref = refs[:6]
    refs = refs[6:]
    if not first:
        before_ref, refs = refs[0], refs[1:]
    if last:
        dq_ref, dkv_ref, low_ref, kv_scr = refs
    else:
        dq_ref, dkv_ref, kv_scr = refs
    step = pl.program_id(0)
    kw = kvs * 64

    @pl.when(step == 0)
    def _():
        for s in range(slots):
            for h in range(2 * kvs):
                kv_scr[h, s] = kv_ref[s, h * 64 : (h + 1) * 64, :].T
        dkv_ref[...] = jnp.zeros(dkv_ref.shape, F32) if first else before_ref[...]

    dq_ref[...] = jnp.zeros(dq_ref.shape, F32)
    qs = [heads_of(q_ref, h, group) for h in range(kvs)]
    dos = [heads_of(do_ref, h, group) for h in range(kvs)]

    def along(ref, h):
        return jnp.concatenate([ref[h * group + g : h * group + g + 1, :] for g in range(group)], axis=1)

    lses = [along(lse_ref, h) for h in range(kvs)]
    rds = [along(rd_ref, h) for h in range(kvs)]

    def chunk(c, masked):
        off = pl.multiple_of(c * qb, qb)
        for h in range(kvs):
            k = jnp.concatenate([kv_scr[h, s, pl.ds(off, qb), :] for s in range(slots)], axis=0)
            v = jnp.concatenate([kv_scr[kvs + h, s, pl.ds(off, qb), :] for s in range(slots)], axis=0)
            k_t = jnp.concatenate([kv_ref[s, h * 64 : (h + 1) * 64, pl.ds(off, qb)] for s in range(slots)], axis=1)
            st = mm(k, qs[h])
            if masked:
                st = st + jnp.concatenate([bias_ref[...].reshape(slots * qb, qb)] * group, axis=1)
            p = jnp.exp2(st - lses[h])
            dp = mm(v, dos[h])
            ds = (p * (dp - rds[h])).astype(BF)
            dk = mm(qs[h], ds, NT)
            dv = mm(dos[h], p.astype(BF), NT)
            dq = mm(k_t, ds)
            for s in range(slots):
                dkv_ref[s, h * 64 : (h + 1) * 64, pl.ds(off, qb)] += dk[:, s * qb : (s + 1) * qb]
                dkv_ref[s, kw + h * 64 : kw + (h + 1) * 64, pl.ds(off, qb)] += dv[:, s * qb : (s + 1) * qb]
            for g in range(group):
                r = h * group + g
                dq_ref[r * 64 : (r + 1) * 64, :] += dq[:, g * qb : (g + 1) * qb]

    def body(c, carry):
        chunk(c, False)
        return carry

    lax.fori_loop(0, step + lo, body, 0)
    chunk(step + lo, True)
    if last:

        @pl.when(step == pl.num_programs(0) - 1)
        def _():
            low_ref[...] = dkv_ref[...].astype(BF)


def attn_bwd(bias, q_t, kv_t, do_t, lse, rd, lo, hi, before=None, last=False, kvs=3, group=3, qb=256):
    slots, _, rows = kv_t.shape
    width = kvs * group * 64
    whole = pl.BlockSpec((slots, 2 * kvs * 64, rows), lambda i: (0, 0, 0))
    tall = pl.BlockSpec((width, qb), lambda i: (0, i + lo))
    stat = pl.BlockSpec((16, qb), lambda i: (0, i + lo))
    out_specs = [pl.BlockSpec((width, qb), lambda i: (0, i)), whole]
    out_shape = [
        jax.ShapeDtypeStruct((width, (hi - lo) * qb), F32),
        jax.ShapeDtypeStruct((slots, 2 * kvs * 64, rows), F32),
    ]
    if last:
        out_specs.append(whole)
        out_shape.append(jax.ShapeDtypeStruct((slots, 2 * kvs * 64, rows), BF))
    args = (bias, q_t, kv_t, do_t, lse, rd) + (() if before is None else (before,))
    units = sum(range(lo + 1, hi + 1))
    return pl.pallas_call(
        functools.partial(
            bwd_kernel, kvs=kvs, group=group, slots=slots, qb=qb, lo=lo, first=before is None, last=last
        ),
        grid=(hi - lo,),
        in_specs=[pl.BlockSpec((slots, qb, qb), lambda i: (0, 0, 0)), tall, whole, tall, stat, stat]
        + ([] if before is None else [whole]),
        out_specs=out_specs,
        out_shape=out_shape,
        scratch_shapes=[pltpu.VMEM((2 * kvs, slots, rows, 64), BF)],
        compiler_params=pltpu.CompilerParams(vmem_limit_bytes=60 * 2**20),
        cost_estimate=pl.CostEstimate(flops=int(4e9) * units, bytes_accessed=int(16e6), transcendentals=0),
    )(*args)


TN = (((0,), (0,)), ((), ()))
TT = (((0,), (1,)), ((), ()))
BLOCK = 256
PIECES = 8
LIMIT = 60 * 2**20


def rotated(values, cosine, sine):
    a, b = values[:32], values[32:]
    return jnp.concatenate([a * cosine - b * sine, b * cosine + a * sine], axis=0)


def flat_rows(ref):
    count, sub, width = ref.shape
    return ref[...].reshape(count * sub, width)


def rms(values):
    return lax.rsqrt(jnp.mean(values * values, axis=-1, keepdims=True) + EPSILON)


def qkv_kernel(x_ref, w_ref, gain_ref, cos_ref, sin_ref, q_ref, kv_ref, wt_scr):
    @pl.when(pl.program_id(0) == 0)
    def _():
        wt_scr[...] = w_ref[:, : wt_scr.shape[0]].T

    source = flat_rows(x_ref).astype(F32)
    hidden = (source * rms(source) * gain_ref[0:1, :]).astype(BF)
    out = mm(wt_scr[...], hidden, NT)
    cosine, sine = cos_ref[...], sin_ref[...]
    for h in range(HEADS):
        part = rotated(out[h * 64 : (h + 1) * 64], cosine, sine)
        q_ref[h * 64 : (h + 1) * 64, :] = (part * (HEAD_DIM**-0.5 * LOG2E)).astype(BF)
    top = HEADS * 64
    for h in range(KV_HEADS):
        part = rotated(out[top + h * 64 : top + (h + 1) * 64], cosine, sine)
        kv_ref[h * 64 : (h + 1) * 64, :] = part.astype(BF)
    kv_ref[KV_HEADS * 64 :, :] = out[top + KV_HEADS * 64 :].astype(BF)


def project_qkv(x, first, gains, cosine, sine):
    count, sub, width = x.shape
    rows = count * sub
    per = BLOCK // sub
    kv2 = 2 * KV_HEADS * HEAD_DIM
    return pl.pallas_call(
        qkv_kernel,
        grid=(rows // BLOCK,),
        in_specs=[
            pl.BlockSpec((per, sub, width), lambda i: (i, 0, 0)),
            pl.BlockSpec(first.shape, lambda i: (0, 0)),
            pl.BlockSpec(gains.shape, lambda i: (0, 0)),
            pl.BlockSpec((32, BLOCK), lambda i: (0, i)),
            pl.BlockSpec((32, BLOCK), lambda i: (0, i)),
        ],
        out_specs=[pl.BlockSpec((width, BLOCK), lambda i: (0, i)), pl.BlockSpec((kv2, BLOCK), lambda i: (0, i))],
        out_shape=[jax.ShapeDtypeStruct((width, rows), BF), jax.ShapeDtypeStruct((kv2, rows), BF)],
        scratch_shapes=[pltpu.VMEM((width + kv2, width), BF)],
        compiler_params=pltpu.CompilerParams(vmem_limit_bytes=LIMIT),
        cost_estimate=pl.CostEstimate(flops=int(6e9), bytes_accessed=int(5e6), transcendentals=0),
    )(x, first, gains, cosine, sine)


def ffn_kernel(
    place_ref, o_ref, x_ref, cot_ref, first_ref, gate_ref, up_ref, down_ref, gain_ref,
    mixed_ref, dres_ref, datt_ref, rd_ref, keep_gu, send_gu, keep_do, send_do, gg_ref,
    acc_gu, acc_down, acc_out, out_scr,
):
    step = pl.program_id(0)
    width = x_ref.shape[2]

    @pl.when(step == 0)
    def _():
        acc_gu[...] = jnp.zeros(acc_gu.shape, F32)
        acc_down[...] = jnp.zeros(acc_down.shape, F32)
        acc_out[...] = jnp.zeros(acc_out.shape, F32)
        gg_ref[...] = jnp.zeros(gg_ref.shape, F32)

    cols = first_ref.shape[1]
    out_w = first_ref[:, cols - width :]
    attended = o_ref[...]
    mixed = attended.astype(BF)
    residual = flat_rows(x_ref).astype(F32) + mm(mixed, out_w, TN)
    scale = rms(residual)
    normed = residual * scale
    gain = gain_ref[1:2, :]
    hidden = (normed * gain).astype(BF)
    gate = mm(hidden, gate_ref[...])
    up = mm(hidden, up_ref[...])
    sig = 0.5 * jnp.tanh(0.5 * gate) + 0.5
    silu = gate * sig
    activated = (silu * up).astype(BF)
    mixed_out = (residual + mm(activated, down_ref[...])).astype(BF)
    mixed_ref[...] = mixed_out.reshape(mixed_ref.shape)
    cot = flat_rows(cot_ref)
    d_act = mm(cot, down_ref[...], NT)
    acc_down[...] += mm(activated, cot, TN)
    d_gate = (d_act * up * sig * (1.0 + gate * (1.0 - sig))).astype(BF)
    d_up = (d_act * silu).astype(BF)
    acc_gu[0] += mm(hidden, d_gate, TN)
    acc_gu[1] += mm(hidden, d_up, TN)
    d_hidden = mm(d_gate, gate_ref[...], NT) + mm(d_up, up_ref[...], NT)
    dn = d_hidden * normed
    gg_ref[...] += jnp.sum(dn.reshape(-1, 8, width), axis=0)
    inner = jnp.mean(dn * gain, axis=-1, keepdims=True)
    d_res = cot.astype(F32) + scale * (d_hidden * gain - normed * inner)
    dres_ref[...] = d_res
    d_low = d_res.astype(BF)
    acc_out[: acc_out.shape[0] - 16] += mm(mixed, d_low)
    d_att = mm(out_w, d_low, NT).astype(BF)
    datt_ref[...] = d_att
    prod = d_att.astype(F32) * attended
    for h in range(HEADS):
        rd_ref[h : h + 1, :] = jnp.sum(prod[h * 64 : (h + 1) * 64], axis=0, keepdims=True)
    rd_ref[HEADS:, :] = jnp.zeros((16 - HEADS, rd_ref.shape[1]), F32)

    @pl.when(step == pl.num_programs(0) - 1)
    def _():
        core = place_ref[0]
        half = width // 2
        ff = acc_gu.shape[2]
        for y in range(2):
            for p in range(PIECES):
                rs = slice(y * half + (p // 4) * (half // 2), y * half + (p // 4 + 1) * (half // 2))
                cs = slice((p % 4) * (ff // 4), (p % 4 + 1) * (ff // 4))
                keep_gu[y, p] = acc_gu[core, rs, cs].astype(BF)
                send_gu[y, p] = acc_gu[1 - core, rs, cs].astype(BF)
        down_rows, out_rows = ff // 32, width // 32
        for m in range(32):
            out_scr[m] = acc_out[m * out_rows : m * out_rows + 24, :].astype(F32)
        for y in range(2):
            for p in range(PIECES):
                for ref, c in ((keep_do, core), (send_do, 1 - core)):
                    start = pl.multiple_of(y * (ff // 2) + (PIECES * c + p) * down_rows, 16)
                    ref[y, p, :down_rows] = acc_down[pl.ds(start, down_rows), :].astype(BF)
                    ref[y, p, down_rows:] = out_scr[y * 16 + PIECES * c + p].astype(BF)


def feed_forward(place, attended, x, cot, first, gate_w, up_w, down_w, gains):
    count, sub, width = x.shape
    rows, ff = count * sub, gate_w.shape[1]
    per = BLOCK // sub
    gu = (2, PIECES, width // 4, ff // 4)
    do = (2, PIECES, ff // 32 + 24, width)

    def whole(shape):
        return pl.BlockSpec(shape, lambda i: (0,) * len(shape))

    seq = pl.BlockSpec((per, sub, width), lambda i: (i, 0, 0))
    tall = pl.BlockSpec((width, BLOCK), lambda i: (0, i))
    return pl.pallas_call(
        ffn_kernel,
        grid=(rows // BLOCK,),
        in_specs=[
            pl.BlockSpec(memory_space=pltpu.SMEM), tall, seq, seq,
            whole(first.shape), whole(gate_w.shape), whole(up_w.shape), whole(down_w.shape), whole(gains.shape),
        ],
        out_specs=[
            seq, pl.BlockSpec((BLOCK, width), lambda i: (i, 0)), tall, pl.BlockSpec((16, BLOCK), lambda i: (0, i)),
            whole(gu), whole(gu), whole(do), whole(do), whole((8, width)),
        ],
        out_shape=[
            jax.ShapeDtypeStruct(x.shape, BF),
            jax.ShapeDtypeStruct((rows, width), F32),
            jax.ShapeDtypeStruct((width, rows), BF),
            jax.ShapeDtypeStruct((16, rows), F32),
            jax.ShapeDtypeStruct(gu, BF), jax.ShapeDtypeStruct(gu, BF),
            jax.ShapeDtypeStruct(do, BF), jax.ShapeDtypeStruct(do, BF),
            jax.ShapeDtypeStruct((8, width), F32),
        ],
        scratch_shapes=[
            pltpu.VMEM((2, width, ff), F32), pltpu.VMEM((ff, width), F32), pltpu.VMEM((width + 16, width), F32),
            pltpu.VMEM((32, 24, width), F32),
        ],
        compiler_params=pltpu.CompilerParams(vmem_limit_bytes=LIMIT),
        cost_estimate=pl.CostEstimate(flops=int(32e9), bytes_accessed=int(20e6), transcendentals=0),
    )(place, attended, x, cot, first, gate_w, up_w, down_w, gains)


def back_kernel(*refs, spans):
    place_ref, refs = refs[0], refs[1:]
    dq_refs, refs = refs[: len(spans)], refs[len(spans) :]
    own_ref, got_ref, x_ref, dres_ref, first_ref, gain_ref, cos_ref, sin_ref, gg_ref, dx_ref = refs[:10]
    keep_ref, send_ref, acc, dt_scr, ga_scr, w_scr = refs[10:]
    step = pl.program_id(0)
    width = x_ref.shape[2]
    kv = KV_HEADS * 64
    total = width + 2 * kv

    @pl.when(step == 0)
    def _():
        acc[...] = jnp.zeros(acc.shape, F32)
        ga_scr[...] = jnp.zeros(ga_scr.shape, F32)
        w_scr[...] = first_ref[:, :total].T

    cosine, sine = cos_ref[...], -sin_ref[...]
    for (lo, hi), dq_ref in zip(spans, dq_refs):

        @pl.when((step >= lo) & (step < hi))
        def _():
            for h in range(HEADS):
                part = dq_ref[h * 64 : (h + 1) * 64, :] * (HEAD_DIM**-0.5)
                dt_scr[h * 64 : (h + 1) * 64, :] = rotated(part, cosine, sine).astype(BF)

    d_kv = own_ref[0] + got_ref[...].astype(F32)
    for h in range(KV_HEADS):
        part = d_kv[h * 64 : (h + 1) * 64] * LN2
        dt_scr[width + h * 64 : width + (h + 1) * 64, :] = rotated(part, cosine, sine).astype(BF)
    dt_scr[width + kv :, :] = d_kv[kv:].astype(BF)
    d_t = dt_scr[...]
    source = flat_rows(x_ref).astype(F32)
    scale = rms(source)
    normed = source * scale
    gain = gain_ref[0:1, :]
    hidden = (normed * gain).astype(BF)
    acc[:total] += mm(d_t, hidden)
    d_hidden = mm(d_t, w_scr[...], TN)
    dn = d_hidden * normed
    ga_scr[...] += jnp.sum(dn.reshape(-1, 8, width), axis=0)
    inner = jnp.mean(dn * gain, axis=-1, keepdims=True)
    grad = dres_ref[...] + scale * (d_hidden * gain - normed * inner)
    dx_ref[...] = grad.astype(BF).reshape(dx_ref.shape)

    @pl.when(step == pl.num_programs(0) - 1)
    def _():
        core = place_ref[0]
        acc[total : total + 1, :] = jnp.sum(ga_scr[...], axis=0, keepdims=True)
        acc[total + 1 : total + 2, :] = jnp.sum(gg_ref[...], axis=0, keepdims=True)
        half, deep = width // 2, width // 4
        for ct in range(4):
            for ref, c in ((keep_ref, core), (send_ref, 1 - core)):
                start = pl.multiple_of(c * 512 + ct * 128, 128)
                block = acc[pl.ds(start, 128), :].T.astype(BF)
                for y in range(2):
                    for rh in range(2):
                        low = y * half + rh * deep
                        ref[y, rh * 4 + ct] = block[low : low + deep]


def back_qkv(place, spans, d_query, d_kv, got, x, d_res, first, gains, cosine, sine, gg):
    count, sub, width = x.shape
    rows = count * sub
    per = BLOCK // sub
    kv2 = 2 * KV_HEADS * HEAD_DIM
    piece = (2, PIECES, width // 4, 128)

    def whole(shape):
        return pl.BlockSpec(shape, lambda i: (0,) * len(shape))

    seq = pl.BlockSpec((per, sub, width), lambda i: (i, 0, 0))
    return pl.pallas_call(
        functools.partial(back_kernel, spans=spans),
        grid=(rows // BLOCK,),
        in_specs=[
            pl.BlockSpec(memory_space=pltpu.SMEM),
            *(
                pl.BlockSpec((width, BLOCK), lambda i, lo=lo, hi=hi: (0, jnp.clip(i - lo, 0, hi - lo - 1)))
                for lo, hi in spans
            ),
            pl.BlockSpec((1, kv2, BLOCK), lambda i: (0, 0, i)),
            pl.BlockSpec((kv2, BLOCK), lambda i: (0, i)),
            seq, pl.BlockSpec((BLOCK, width), lambda i: (i, 0)),
            whole(first.shape), whole(gains.shape),
            pl.BlockSpec((32, BLOCK), lambda i: (0, i)), pl.BlockSpec((32, BLOCK), lambda i: (0, i)),
            whole(gg.shape),
        ],
        out_specs=[seq, whole(piece), whole(piece)],
        out_shape=[jax.ShapeDtypeStruct(x.shape, BF), jax.ShapeDtypeStruct(piece, BF), jax.ShapeDtypeStruct(piece, BF)],
        scratch_shapes=[
            pltpu.VMEM((1024, width), F32), pltpu.VMEM((width + kv2, BLOCK), BF), pltpu.VMEM((8, width), F32),
            pltpu.VMEM((width + kv2, width), BF),
        ],
        compiler_params=pltpu.CompilerParams(vmem_limit_bytes=LIMIT),
        cost_estimate=pl.CostEstimate(flops=int(10e9), bytes_accessed=int(10e6), transcendentals=0),
    )(place, *d_query, d_kv, got, x, d_res, first, gains, cosine, sine, gg)


def swap(x, axis, bit):
    n = lax.axis_size(axis)
    return lax.ppermute(x, axis, [(i, i ^ (1 << bit)) for i in range(n)])


def bit_of(axis, bit):
    return (lax.axis_index(axis) >> bit) & 1


def pin(*arrays):
    return lax.optimization_barrier(arrays)


def pick(x, at):
    return lax.dynamic_index_in_dim(x, at, 0, keepdims=False)


def in_order(flag, mine, other, axis):
    return jnp.where(
        flag == 0,
        jnp.concatenate([mine, other], axis=axis),
        jnp.concatenate([other, mine], axis=axis),
    )


def plus(a, b):
    return (a.astype(F32) + b.astype(F32)).astype(BF)


def two_level():
    return lax.axis_size("fsdp") == 2 and lax.axis_size("ctx") == 16


def z_groups():
    return [[4 * z + r for z in range(4)] for r in range(4)]


def z_sum(x):
    x = lax.all_to_all(x, "ctx", 0, 0, tiled=True, axis_index_groups=z_groups())
    return jnp.sum(x.astype(F32), axis=0).astype(BF)


def z_join(piece):
    whole = jnp.broadcast_to(piece[None], (4,) + piece.shape)
    return lax.all_to_all(whole, "ctx", 0, 0, tiled=True, axis_index_groups=z_groups())


def join(x, bit):
    return swap(x, "ctx", bit)


def natural_gu(pieces):
    _, a, b = pieces.shape
    return pieces.reshape(2, 4, a, b).transpose(0, 2, 1, 3).reshape(2 * a, 4 * b).astype(F32)


def other_sum(x):
    x = lax.psum_scatter(x.astype(BF), "fsdp", scatter_dimension=0, tiled=True)
    return lax.psum(x, "ctx").astype(F32)


def local(tokens, gain_attn, w_query, w_key, w_value, w_out, gain_ffn, w_gate, w_up, w_down, cotangent):
    seqs, length, width = tokens.shape
    count = lax.axis_size("ctx")
    team = count // seqs
    sub = length // team
    rows = count * sub
    ff = w_gate.shape[1]
    kv_width = KV_HEADS * HEAD_DIM
    qkv_cols = width + 2 * kv_width
    place = lax.axis_index("ctx") % team
    own = gain_attn.shape[0]
    fast = two_level()

    def move(x):
        return lax.all_to_all(x.reshape(count, sub, width), "ctx", 0, 0, tiled=True)

    x = move(tokens)
    gain_rows = jnp.zeros((8, ff), BF).at[0, :own].set(gain_attn).at[1, :own].set(gain_ffn)
    first = jnp.concatenate([jnp.concatenate([w_query, w_key, w_value, w_out], axis=1), gain_rows], axis=0)
    if fast:
        core, rank = bit_of("ctx", 0), bit_of("fsdp", 0)

        def halved(shard, axis):
            half = shard.shape[axis] // 2
            return lax.dynamic_slice_in_dim(shard, core * half, half, axis)

        def other_shard(got, axis):
            return in_order(core, got, swap(got, "ctx", 0), axis)

        got = swap(halved(first, 1), "fsdp", 0)
        other = other_shard(got, 1)
        gains = in_order(rank, first[own : own + 2, :own], other[own : own + 2, :own], 1).astype(F32)
        first = in_order(rank, first[:own], other[:own], 0)
        gate_half, up_half, down_half, got = pin(halved(w_gate, 1), halved(w_up, 1), halved(w_down, 0), got)
        gate_w = in_order(rank, w_gate, other_shard(swap(gate_half, "fsdp", 0), 1), 0)
        up_w = in_order(rank, w_up, other_shard(swap(up_half, "fsdp", 0), 1), 0)
        down_w = in_order(rank, w_down, other_shard(swap(down_half, "fsdp", 0), 0), 0)
    else:
        first = lax.all_gather(first, "fsdp", axis=0)
        gains = first[:, own : own + 2, :own].transpose(1, 0, 2).reshape(2, width).astype(F32)
        first = first[:, :own].reshape(width, first.shape[2])
        gate_w, up_w, down_w = (lax.all_gather(w, "fsdp", axis=0, tiled=True) for w in (w_gate, w_up, w_down))
    gains = jnp.pad(gains, ((0, 6), (0, 0)))

    row = jnp.arange(rows, dtype=jnp.int32)
    position = (row // sub) * length + place * sub + row % sub
    frequency = THETA ** (-jnp.arange(HEAD_DIM // 2, dtype=F32) * 2.0 / HEAD_DIM)
    angles = frequency[:, None] * position.astype(F32)[None, :]
    cosine, sine = jnp.cos(angles), jnp.sin(angles)
    groups = [[t * team + p for p in range(team)] for t in range(seqs)]
    slots = jnp.stack([place, 1 - place]) if team == 2 else jnp.arange(team)
    block_row = jnp.arange(BLOCK, dtype=jnp.int32)
    base = (block_row // sub) * length + block_row % sub
    key_pos = base[None, :] + slots[:, None] * sub
    query_pos = base + place * sub
    bias = jnp.where(key_pos[:, :, None] <= query_pos[None, None, :], 0.0, NEGATIVE).astype(F32)
    flags = jnp.stack([core, rank]) if fast else jnp.zeros((2,), jnp.int32)

    x, cot_send = pin(x, cotangent)
    cot = move(cot_send)
    query, kv_own = project_qkv(x, first, gains, cosine, sine)
    if team == 2:
        kv_all = jnp.stack([kv_own, swap(kv_own, "ctx", 0)])
    else:
        kv_all = lax.all_gather(kv_own, "ctx", axis=0, axis_index_groups=groups)
    attended, log_total = attn_fwd(bias, query, kv_all)
    attended, cot = pin(attended, cot)
    mixed, d_res, d_att, row_dot, keep_gu, send_gu, keep_do, send_do, gain_sum = feed_forward(
        flags, attended, x, cot, first, gate_w, up_w, down_w, gains
    )
    mixed_out = move(mixed)

    n = rows // BLOCK
    spans = ((0, n // 2), (n - 1, n), (n // 2, n - 1))
    part = functools.partial(attn_bwd, bias, query, kv_all, d_att, log_total, row_dot)
    if fast:
        got_gu, got_do = swap(send_gu, "ctx", 0), swap(send_do, "ctx", 0)
        dq_a, before = part(*spans[0])
        got_gu, got_do, before = pin(got_gu, got_do, before)
        x_bit = bit_of("ctx", 1)
        gu, do = plus(keep_gu, got_gu), plus(keep_do, got_do)
        gu = gu.reshape((2, 2, 4) + gu.shape[2:]).swapaxes(0, 1)
        keep_gu, send_gu = pick(gu, x_bit), pick(gu, 1 - x_bit)
        keep_do, send_do = pick(do, rank), pick(do, 1 - rank)
        send_gu, send_do, before = pin(send_gu, send_do, before)
        got_gu, got_do = swap(send_gu, "ctx", 1), swap(send_do, "fsdp", 0)
        dq_b, before = part(*spans[1], before=before)
        got_gu, got_do, mixed_out, before = pin(got_gu, got_do, mixed_out, before)
        gu, do = plus(keep_gu, got_gu), plus(keep_do, got_do)
        do = do.reshape((2, 4) + do.shape[1:])
        keep_gu, send_gu = pick(gu, rank), pick(gu, 1 - rank)
        keep_do, send_do = pick(do, x_bit), pick(do, 1 - x_bit)
        send_gu, send_do, before = pin(send_gu, send_do, before)
        got_gu, got_do = swap(send_gu, "fsdp", 0), swap(send_do, "ctx", 1)
        dq_c, d_kv, d_kv_low = part(*spans[2], before=before, last=True)
        got_gu, got_do, d_kv_low, dq_c = pin(got_gu, got_do, d_kv_low, dq_c)
        gu, do = plus(keep_gu, got_gu), plus(keep_do, got_do)
    else:
        dq_a, before = part(*spans[0])
        dq_b, before = part(*spans[1], before=before)
        dq_c, d_kv, d_kv_low = part(*spans[2], before=before, last=True)
    if team == 2:
        own_kv, got_kv = d_kv[:1], swap(d_kv_low[1], "ctx", 0)
    else:
        own_kv = lax.psum_scatter(d_kv_low, "ctx", scatter_dimension=0, axis_index_groups=groups)
        own_kv, got_kv = own_kv.astype(F32)[None], jnp.zeros((2 * kv_width, rows), BF)
    d_x, keep_t, send_t = back_qkv(
        flags, spans, (dq_a, dq_b, dq_c), own_kv, got_kv, x, d_res, first, gains, cosine, sine, gain_sum
    )
    grad_tokens = move(d_x)
    if fast:
        gu, do = z_sum(gu), z_sum(do)
        t = plus(keep_t, swap(send_t, "ctx", 0))
        t = plus(pick(t, rank), swap(pick(t, 1 - rank), "fsdp", 0))
        t = t.reshape((2, 4) + t.shape[1:])
        t = plus(pick(t, x_bit), swap(pick(t, 1 - x_bit), "ctx", 1))
        t = z_sum(t)

        def widen(piece):
            four = z_join(piece)
            eight = in_order(x_bit, four, join(four, 1), 0)
            return eight, join(eight, 0)

        gu, gu_other = widen(gu)
        do, do_other = widen(do)
        t, t_other = widen(t)
        own_gate = natural_gu(jnp.where(core == 0, gu, gu_other))
        own_up = natural_gu(jnp.where(core == 0, gu_other, gu))
        do = in_order(core, do, do_other, 0)
        deep = ff // 32
        own_down = do[:, :deep].reshape(ff // 2, width).astype(F32)
        own_out = do[:, deep : deep + width // 32].reshape(width // 2, width).astype(F32)
        t0, t1 = jnp.where(core == 0, t, t_other), jnp.where(core == 0, t_other, t)
        own_t = jnp.concatenate([natural_gu(t0), natural_gu(t1)], axis=1)
    else:
        pair = jnp.stack([keep_gu, send_gu])
        gate, up = (jnp.concatenate([natural_gu(pair[c, y]) for y in range(2)], axis=0) for c in range(2))
        do = jnp.stack([keep_do, send_do], axis=1).reshape((32,) + keep_do.shape[2:])
        deep = ff // 32
        own_gate, own_up = other_sum(gate), other_sum(up)
        own_down = other_sum(do[:, :deep].reshape(ff, width))
        own_out = other_sum(do[:, deep : deep + width // 32].reshape(width, width))
        pair = jnp.stack([keep_t, send_t])
        t = [jnp.concatenate([natural_gu(pair[c, y]) for c in range(2)], axis=1) for y in range(2)]
        own_t = other_sum(jnp.concatenate(t, axis=0))
    return (
        mixed_out.reshape(tokens.shape),
        grad_tokens.reshape(tokens.shape),
        own_t[:, qkv_cols],
        own_t[:, :width],
        own_t[:, width : width + kv_width],
        own_t[:, width + kv_width : qkv_cols],
        own_out,
        own_t[:, qkv_cols + 1],
        own_gate,
        own_up,
        own_down,
    )


def solution(mesh):
    rows, flat, seq = P("fsdp", None), P("fsdp"), P("fsdp", "ctx", None)
    return jax.shard_map(
        local,
        mesh=mesh,
        in_specs=(seq, flat, rows, rows, rows, rows, flat, rows, rows, rows, seq),
        out_specs=(seq, seq, flat, rows, rows, rows, rows, flat, rows, rows, rows),
        check_vma=False,
    )
```

```python
import functools

import jax
import jax.numpy as jnp
from jax import lax
from jax.experimental import pallas as pl
from jax.experimental.pallas import tpu as pltpu
from jax.sharding import PartitionSpec as P

HEADS = 9
KV_HEADS = 3
HEAD_DIM = 64
EPSILON = 1e-05
THETA = 100000.0
NEGATIVE = -1e30
LOG2E = 1.4426950408889634
LN2 = 0.6931471805599453
F32=jnp.float32; BF=jnp.bfloat16
NT=(((1,),(1,)),((),()))
NN=(((1,),(0,)),((),()))
def mm(a,b,dims=NN):
    return lax.dot_general(a,b,dims,preferred_element_type=F32)

def heads_of(ref, kv, group):
    return jnp.concatenate([ref[(kv*group+h)*64:(kv*group+h+1)*64,:] for h in range(group)],axis=1)

def fwd_kernel(bias_ref, q_ref, *refs, kvs, group, slots, rows, qb):
    kv_ref, (o_ref, lse_ref, k_scr, m_scr, acc_scr)=refs[:slots], refs[slots:]
    i=pl.program_id(0)
    kw=kvs*64
    @pl.when(i==0)
    def _():
        for s in range(slots):
            for h in range(kvs):
                k_scr[h,s]=kv_ref[s][h*64:(h+1)*64,:].T
    qs=[heads_of(q_ref,h,group) for h in range(kvs)]
    width=group*qb
    m_scr[...]=jnp.full(m_scr.shape,-1e30,F32)
    acc_scr[...]=jnp.zeros(acc_scr.shape,F32)
    ones=jnp.ones((8,slots*qb),BF)
    def chunk(c, masked):
        off=pl.multiple_of(c*qb,qb)
        for h in range(kvs):
            k=jnp.concatenate([k_scr[h,s,pl.ds(off,qb),:] for s in range(slots)],axis=0)
            v=jnp.concatenate([kv_ref[s][kw+h*64:kw+(h+1)*64,pl.ds(off,qb)] for s in range(slots)],axis=1)
            v=jnp.concatenate([v,ones],axis=0)
            st=mm(k,qs[h])
            if masked:
                b=bias_ref[...].reshape(slots*qb,qb)
                st=st+jnp.concatenate([b]*group,axis=1)
            m_old=m_scr[h:h+1,:]
            m_new=jnp.maximum(m_old,jnp.max(st,axis=0,keepdims=True))
            p=jnp.exp2(st-m_new).astype(BF)
            acc_scr[h]=acc_scr[h]*jnp.exp2(m_old-m_new)+mm(v,p)
            m_scr[h:h+1,:]=m_new
    def body(c,_):
        chunk(c,False); return 0
    lax.fori_loop(0,i,body,0)
    chunk(i,True)
    for h in range(kvs):
        acc=acc_scr[h]
        tot=acc[64:65,:]
        o=acc[:64,:]*(1.0/tot)
        lse=m_scr[h:h+1,:]+jnp.log2(tot)
        for g in range(group):
            r=h*group+g
            o_ref[r*64:(r+1)*64,:]=o[:,g*qb:(g+1)*qb]
            lse_ref[r:r+1,:]=lse[:,g*qb:(g+1)*qb]

def attn_fwd(bias, qT, kvT, kvs=3, group=3, qb=256):
    slots,rows=len(kvT),kvT[0].shape[1]
    n=rows//qb
    heads=kvs*group
    return pl.pallas_call(
        functools.partial(fwd_kernel,kvs=kvs,group=group,slots=slots,rows=rows,qb=qb),
        grid=(n,),
        in_specs=[pl.BlockSpec((slots,qb,qb),lambda i:(0,0,0)),
                  pl.BlockSpec((heads*64,qb),lambda i:(0,i)),
                  *[pl.BlockSpec((2*kvs*64,rows),lambda i:(0,0))]*slots],
        out_specs=[pl.BlockSpec((heads*64,qb),lambda i:(0,i)),
                   pl.BlockSpec((16,qb),lambda i:(0,i))],
        out_shape=[jax.ShapeDtypeStruct((heads*64,rows),F32),jax.ShapeDtypeStruct((16,rows),F32)],
        scratch_shapes=[pltpu.VMEM((kvs,slots,rows,64),BF),pltpu.VMEM((8,group*qb),F32),
                        pltpu.VMEM((kvs,72,group*qb),F32)],
        compiler_params=pltpu.CompilerParams(vmem_limit_bytes=56*2**20),
        cost_estimate=pl.CostEstimate(flops=int(25e9),bytes_accessed=int(8e6),transcendentals=int(1e7)),
    )(bias,qT,*kvT)

def bwd_kernel(*refs, kvs, group, slots, qb, lo, first, last):
    bias_ref, q_ref, do_ref, lse_ref, rd_ref = refs[:5]
    kv_ref, refs = refs[5 : 5 + slots], refs[5 + slots :]
    if not first:
        before_ref, refs = refs[0], refs[1:]
    if last:
        dq_ref, dkv_ref, low_ref, kv_scr = refs
    else:
        dq_ref, dkv_ref, kv_scr = refs
    step = pl.program_id(0)
    kw = kvs * 64

    @pl.when(step == 0)
    def _():
        for s in range(slots):
            for h in range(2 * kvs):
                kv_scr[h, s] = kv_ref[s][h * 64 : (h + 1) * 64, :].T
        dkv_ref[...] = jnp.zeros(dkv_ref.shape, F32) if first else before_ref[...]

    dq_ref[...] = jnp.zeros(dq_ref.shape, F32)
    qs = [heads_of(q_ref, h, group) for h in range(kvs)]
    dos = [heads_of(do_ref, h, group) for h in range(kvs)]

    def along(ref, h):
        return jnp.concatenate([ref[h * group + g : h * group + g + 1, :] for g in range(group)], axis=1)

    lses = [along(lse_ref, h) for h in range(kvs)]
    rds = [along(rd_ref, h) for h in range(kvs)]

    def chunk(c, masked):
        off = pl.multiple_of(c * qb, qb)
        for h in range(kvs):
            k = jnp.concatenate([kv_scr[h, s, pl.ds(off, qb), :] for s in range(slots)], axis=0)
            v = jnp.concatenate([kv_scr[kvs + h, s, pl.ds(off, qb), :] for s in range(slots)], axis=0)
            k_t = jnp.concatenate([kv_ref[s][h * 64 : (h + 1) * 64, pl.ds(off, qb)] for s in range(slots)], axis=1)
            st = mm(k, qs[h])
            if masked:
                st = st + jnp.concatenate([bias_ref[...].reshape(slots * qb, qb)] * group, axis=1)
            p = jnp.exp2(st - lses[h])
            dp = mm(v, dos[h])
            ds = (p * (dp - rds[h])).astype(BF)
            dk = mm(qs[h], ds, NT)
            dv = mm(dos[h], p.astype(BF), NT)
            dq = mm(k_t, ds)
            for s in range(slots):
                dkv_ref[s, h * 64 : (h + 1) * 64, pl.ds(off, qb)] += dk[:, s * qb : (s + 1) * qb]
                dkv_ref[s, kw + h * 64 : kw + (h + 1) * 64, pl.ds(off, qb)] += dv[:, s * qb : (s + 1) * qb]
            for g in range(group):
                r = h * group + g
                dq_ref[r * 64 : (r + 1) * 64, :] += dq[:, g * qb : (g + 1) * qb]

    def body(c, carry):
        chunk(c, False)
        return carry

    lax.fori_loop(0, step + lo, body, 0)
    chunk(step + lo, True)
    if last:

        @pl.when(step == pl.num_programs(0) - 1)
        def _():
            low_ref[...] = dkv_ref[...].astype(BF)


def attn_bwd(bias, q_t, kv_t, do_t, lse, rd, lo, hi, before=None, last=False, kvs=3, group=3, qb=256):
    slots, rows = len(kv_t), kv_t[0].shape[1]
    width = kvs * group * 64
    whole = pl.BlockSpec((slots, 2 * kvs * 64, rows), lambda i: (0, 0, 0))
    tall = pl.BlockSpec((width, qb), lambda i: (0, i + lo))
    stat = pl.BlockSpec((16, qb), lambda i: (0, i + lo))
    out_specs = [pl.BlockSpec((width, qb), lambda i: (0, i)), whole]
    out_shape = [
        jax.ShapeDtypeStruct((width, (hi - lo) * qb), F32),
        jax.ShapeDtypeStruct((slots, 2 * kvs * 64, rows), F32),
    ]
    if last:
        out_specs.append(whole)
        out_shape.append(jax.ShapeDtypeStruct((slots, 2 * kvs * 64, rows), BF))
    args = (bias, q_t, do_t, lse, rd, *kv_t) + (() if before is None else (before,))
    units = sum(range(lo + 1, hi + 1))
    return pl.pallas_call(
        functools.partial(
            bwd_kernel, kvs=kvs, group=group, slots=slots, qb=qb, lo=lo, first=before is None, last=last
        ),
        grid=(hi - lo,),
        in_specs=[pl.BlockSpec((slots, qb, qb), lambda i: (0, 0, 0)), tall, tall, stat, stat]
        + [pl.BlockSpec((2 * kvs * 64, rows), lambda i: (0, 0))] * slots
        + ([] if before is None else [whole]),
        out_specs=out_specs,
        out_shape=out_shape,
        scratch_shapes=[pltpu.VMEM((2 * kvs, slots, rows, 64), BF)],
        compiler_params=pltpu.CompilerParams(vmem_limit_bytes=60 * 2**20),
        cost_estimate=pl.CostEstimate(flops=int(4e9) * units, bytes_accessed=int(16e6), transcendentals=0),
    )(*args)


TN = (((0,), (0,)), ((), ()))
TT = (((0,), (1,)), ((), ()))
BLOCK = 256
PIECES = 8
LIMIT = 60 * 2**20


def rotated(values, cosine, sine):
    a, b = values[:32], values[32:]
    return jnp.concatenate([a * cosine - b * sine, b * cosine + a * sine], axis=0)


def flat_rows(ref):
    count, sub, width = ref.shape
    return ref[...].reshape(count * sub, width)


def rms(values):
    return lax.rsqrt(jnp.mean(values * values, axis=-1, keepdims=True) + EPSILON)


def qkv_kernel(x_ref, w_ref, gain_ref, cos_ref, sin_ref, q_ref, kv_ref, wt_scr):
    @pl.when(pl.program_id(0) == 0)
    def _():
        wt_scr[...] = w_ref[:, : wt_scr.shape[0]].T

    source = flat_rows(x_ref).astype(F32)
    hidden = (source * rms(source) * gain_ref[0:1, :]).astype(BF)
    out = mm(wt_scr[...], hidden, NT)
    cosine, sine = cos_ref[...], sin_ref[...]
    for h in range(HEADS):
        part = rotated(out[h * 64 : (h + 1) * 64], cosine, sine)
        q_ref[h * 64 : (h + 1) * 64, :] = (part * (HEAD_DIM**-0.5 * LOG2E)).astype(BF)
    top = HEADS * 64
    for h in range(KV_HEADS):
        part = rotated(out[top + h * 64 : top + (h + 1) * 64], cosine, sine)
        kv_ref[h * 64 : (h + 1) * 64, :] = part.astype(BF)
    kv_ref[KV_HEADS * 64 :, :] = out[top + KV_HEADS * 64 :].astype(BF)


def project_qkv(x, first, gains, cosine, sine):
    count, sub, width = x.shape
    rows = count * sub
    per = BLOCK // sub
    kv2 = 2 * KV_HEADS * HEAD_DIM
    return pl.pallas_call(
        qkv_kernel,
        grid=(rows // BLOCK,),
        in_specs=[
            pl.BlockSpec((per, sub, width), lambda i: (i, 0, 0)),
            pl.BlockSpec(first.shape, lambda i: (0, 0)),
            pl.BlockSpec(gains.shape, lambda i: (0, 0)),
            pl.BlockSpec((32, BLOCK), lambda i: (0, i)),
            pl.BlockSpec((32, BLOCK), lambda i: (0, i)),
        ],
        out_specs=[pl.BlockSpec((width, BLOCK), lambda i: (0, i)), pl.BlockSpec((kv2, BLOCK), lambda i: (0, i))],
        out_shape=[jax.ShapeDtypeStruct((width, rows), BF), jax.ShapeDtypeStruct((kv2, rows), BF)],
        scratch_shapes=[pltpu.VMEM((width + kv2, width), BF)],
        compiler_params=pltpu.CompilerParams(vmem_limit_bytes=LIMIT),
        cost_estimate=pl.CostEstimate(flops=int(6e9), bytes_accessed=int(5e6), transcendentals=0),
    )(x, first, gains, cosine, sine)


def ffn_kernel(
    place_ref, o_ref, x_ref, cot_ref, first_ref, gate_ref, up_ref, down_ref, gain_ref,
    mixed_ref, dres_ref, datt_ref, rd_ref, keep_gu, send_gu, keep_do, send_do, gg_ref,
    acc_gu, acc_down, acc_out,
):
    step = pl.program_id(0)
    width = x_ref.shape[2]

    @pl.when(step == 0)
    def _():
        acc_gu[...] = jnp.zeros(acc_gu.shape, F32)
        acc_down[...] = jnp.zeros(acc_down.shape, F32)
        acc_out[...] = jnp.zeros(acc_out.shape, F32)
        gg_ref[...] = jnp.zeros(gg_ref.shape, F32)

    cols = first_ref.shape[1]
    out_w = first_ref[:, cols - width :]
    attended = o_ref[...]
    mixed = attended.astype(BF)
    residual = flat_rows(x_ref).astype(F32) + mm(mixed, out_w, TN)
    scale = rms(residual)
    normed = residual * scale
    gain = gain_ref[1:2, :]
    hidden = (normed * gain).astype(BF)
    gate = mm(hidden, gate_ref[...])
    up = mm(hidden, up_ref[...])
    sig = 0.5 * jnp.tanh(0.5 * gate) + 0.5
    silu = gate * sig
    activated = (silu * up).astype(BF)
    mixed_out = (residual + mm(activated, down_ref[...])).astype(BF)
    mixed_ref[...] = mixed_out.reshape(mixed_ref.shape)
    cot = flat_rows(cot_ref)
    d_act = mm(cot, down_ref[...], NT)
    acc_down[...] += mm(activated, cot, TN)
    d_gate = (d_act * up * sig * (1.0 + gate * (1.0 - sig))).astype(BF)
    d_up = (d_act * silu).astype(BF)
    acc_gu[0] += mm(hidden, d_gate, TN)
    acc_gu[1] += mm(hidden, d_up, TN)
    d_hidden = mm(d_gate, gate_ref[...], NT) + mm(d_up, up_ref[...], NT)
    dn = d_hidden * normed
    gg_ref[...] += jnp.sum(dn.reshape(-1, 8, width), axis=0)
    inner = jnp.mean(dn * gain, axis=-1, keepdims=True)
    d_res = cot.astype(F32) + scale * (d_hidden * gain - normed * inner)
    dres_ref[...] = d_res
    d_low = d_res.astype(BF)
    acc_out[...] += mm(mixed, d_low)
    d_att = mm(out_w, d_low, NT).astype(BF)
    datt_ref[...] = d_att
    prod = d_att.astype(F32) * attended
    for h in range(HEADS):
        rd_ref[h : h + 1, :] = jnp.sum(prod[h * 64 : (h + 1) * 64], axis=0, keepdims=True)
    rd_ref[HEADS:, :] = jnp.zeros((16 - HEADS, rd_ref.shape[1]), F32)

    @pl.when(step == pl.num_programs(0) - 1)
    def _():
        core = place_ref[0]
        half = width // 2
        ff = acc_gu.shape[2]
        for y in range(2):
            for p in range(PIECES):
                rs = slice(y * half + (p // 4) * (half // 2), y * half + (p // 4 + 1) * (half // 2))
                cs = slice((p % 4) * (ff // 4), (p % 4 + 1) * (ff // 4))
                keep_gu[y, p] = acc_gu[core, rs, cs].astype(BF)
                send_gu[y, p] = acc_gu[1 - core, rs, cs].astype(BF)
        down_rows, out_rows = ff // 32, width // 24
        for y in range(2):
            for p in range(PIECES):
                for ref, c in ((keep_do, core), (send_do, 1 - core)):
                    start = pl.multiple_of(y * (ff // 2) + (PIECES * c + p) * down_rows, 16)
                    ref[y, p, :down_rows] = acc_down[pl.ds(start, down_rows), :].astype(BF)
                    start = y * half + jnp.minimum(PIECES * c + p, half // out_rows - 1) * out_rows
                    ref[y, p, down_rows:] = acc_out[pl.ds(pl.multiple_of(start, 8), out_rows), :].astype(BF)


def feed_forward(place, attended, x, cot, first, gate_w, up_w, down_w, gains):
    count, sub, width = x.shape
    rows, ff = count * sub, gate_w.shape[1]
    per = BLOCK // sub
    gu = (2, PIECES, width // 4, ff // 4)
    do = (2, PIECES, ff // 32 + width // 24, width)

    def whole(shape):
        return pl.BlockSpec(shape, lambda i: (0,) * len(shape))

    seq = pl.BlockSpec((per, sub, width), lambda i: (i, 0, 0))
    tall = pl.BlockSpec((width, BLOCK), lambda i: (0, i))
    return pl.pallas_call(
        ffn_kernel,
        grid=(rows // BLOCK,),
        in_specs=[
            pl.BlockSpec(memory_space=pltpu.SMEM), tall, seq, seq,
            whole(first.shape), whole(gate_w.shape), whole(up_w.shape), whole(down_w.shape), whole(gains.shape),
        ],
        out_specs=[
            seq, pl.BlockSpec((BLOCK, width), lambda i: (i, 0)), tall, pl.BlockSpec((16, BLOCK), lambda i: (0, i)),
            whole(gu), whole(gu), whole(do), whole(do), whole((8, width)),
        ],
        out_shape=[
            jax.ShapeDtypeStruct(x.shape, BF),
            jax.ShapeDtypeStruct((rows, width), F32),
            jax.ShapeDtypeStruct((width, rows), BF),
            jax.ShapeDtypeStruct((16, rows), F32),
            jax.ShapeDtypeStruct(gu, BF), jax.ShapeDtypeStruct(gu, BF),
            jax.ShapeDtypeStruct(do, BF), jax.ShapeDtypeStruct(do, BF),
            jax.ShapeDtypeStruct((8, width), F32),
        ],
        scratch_shapes=[
            pltpu.VMEM((2, width, ff), F32), pltpu.VMEM((ff, width), F32), pltpu.VMEM((width, width), F32),
        ],
        compiler_params=pltpu.CompilerParams(vmem_limit_bytes=LIMIT),
        cost_estimate=pl.CostEstimate(flops=int(32e9), bytes_accessed=int(20e6), transcendentals=0),
    )(place, attended, x, cot, first, gate_w, up_w, down_w, gains)


def back_kernel(*refs, spans):
    place_ref, refs = refs[0], refs[1:]
    dq_refs, refs = refs[: len(spans)], refs[len(spans) :]
    own_ref, got_ref, x_ref, dres_ref, first_ref, gain_ref, cos_ref, sin_ref, gg_ref, dx_ref = refs[:10]
    keep_ref, send_ref, acc, dt_scr, ga_scr, w_scr = refs[10:]
    step = pl.program_id(0)
    width = x_ref.shape[2]
    kv = KV_HEADS * 64
    total = width + 2 * kv

    @pl.when(step == 0)
    def _():
        acc[...] = jnp.zeros(acc.shape, F32)
        ga_scr[...] = jnp.zeros(ga_scr.shape, F32)
        w_scr[...] = first_ref[:, :total].T

    cosine, sine = cos_ref[...], -sin_ref[...]
    for (lo, hi), dq_ref in zip(spans, dq_refs):

        @pl.when((step >= lo) & (step < hi))
        def _():
            for h in range(HEADS):
                part = dq_ref[h * 64 : (h + 1) * 64, :] * (HEAD_DIM**-0.5)
                dt_scr[h * 64 : (h + 1) * 64, :] = rotated(part, cosine, sine).astype(BF)

    d_kv = own_ref[0] + got_ref[...].astype(F32)
    for h in range(KV_HEADS):
        part = d_kv[h * 64 : (h + 1) * 64] * LN2
        dt_scr[width + h * 64 : width + (h + 1) * 64, :] = rotated(part, cosine, sine).astype(BF)
    dt_scr[width + kv :, :] = d_kv[kv:].astype(BF)
    d_t = dt_scr[...]
    source = flat_rows(x_ref).astype(F32)
    scale = rms(source)
    normed = source * scale
    gain = gain_ref[0:1, :]
    hidden = (normed * gain).astype(BF)
    acc[:total] += mm(d_t, hidden)
    d_hidden = mm(d_t, w_scr[...], TN)
    dn = d_hidden * normed
    ga_scr[...] += jnp.sum(dn.reshape(-1, 8, width), axis=0)
    inner = jnp.mean(dn * gain, axis=-1, keepdims=True)
    grad = dres_ref[...] + scale * (d_hidden * gain - normed * inner)
    dx_ref[...] = grad.astype(BF).reshape(dx_ref.shape)

    @pl.when(step == pl.num_programs(0) - 1)
    def _():
        core = place_ref[0]
        acc[total : total + 1, :] = jnp.sum(ga_scr[...], axis=0, keepdims=True)
        acc[total + 1 : total + 2, :] = jnp.sum(gg_ref[...], axis=0, keepdims=True)
        half, deep = width // 2, width // 4
        for ct in range(4):
            for ref, c in ((keep_ref, core), (send_ref, 1 - core)):
                start = pl.multiple_of(c * 512 + ct * 128, 128)
                block = acc[pl.ds(start, 128), :].T.astype(BF)
                for y in range(2):
                    for rh in range(2):
                        low = y * half + rh * deep
                        ref[y, rh * 4 + ct] = block[low : low + deep]


def back_qkv(place, spans, d_query, d_kv, got, x, d_res, first, gains, cosine, sine, gg):
    count, sub, width = x.shape
    rows = count * sub
    per = BLOCK // sub
    kv2 = 2 * KV_HEADS * HEAD_DIM
    piece = (2, PIECES, width // 4, 128)

    def whole(shape):
        return pl.BlockSpec(shape, lambda i: (0,) * len(shape))

    seq = pl.BlockSpec((per, sub, width), lambda i: (i, 0, 0))
    return pl.pallas_call(
        functools.partial(back_kernel, spans=spans),
        grid=(rows // BLOCK,),
        in_specs=[
            pl.BlockSpec(memory_space=pltpu.SMEM),
            *(
                pl.BlockSpec((width, BLOCK), lambda i, lo=lo, hi=hi: (0, jnp.clip(i - lo, 0, hi - lo - 1)))
                for lo, hi in spans
            ),
            pl.BlockSpec((1, kv2, BLOCK), lambda i: (0, 0, i)),
            pl.BlockSpec((kv2, BLOCK), lambda i: (0, i)),
            seq, pl.BlockSpec((BLOCK, width), lambda i: (i, 0)),
            whole(first.shape), whole(gains.shape),
            pl.BlockSpec((32, BLOCK), lambda i: (0, i)), pl.BlockSpec((32, BLOCK), lambda i: (0, i)),
            whole(gg.shape),
        ],
        out_specs=[seq, whole(piece), whole(piece)],
        out_shape=[jax.ShapeDtypeStruct(x.shape, BF), jax.ShapeDtypeStruct(piece, BF), jax.ShapeDtypeStruct(piece, BF)],
        scratch_shapes=[
            pltpu.VMEM((1024, width), F32), pltpu.VMEM((width + kv2, BLOCK), BF), pltpu.VMEM((8, width), F32),
            pltpu.VMEM((width + kv2, width), BF),
        ],
        compiler_params=pltpu.CompilerParams(vmem_limit_bytes=LIMIT),
        cost_estimate=pl.CostEstimate(flops=int(10e9), bytes_accessed=int(10e6), transcendentals=0),
    )(place, *d_query, d_kv, got, x, d_res, first, gains, cosine, sine, gg)


def final_kernel(
    at_ref, gu4, gu_x, gu_c, do4, do_x, do_c, gate_ref, up_ref, down_ref, out_ref
):
    core, xb, z = at_ref[0], at_ref[1], at_ref[2]
    deep, wide = gu4.shape[1:]
    for f in range(2):
        for e in range(2):
            for d in range(4):
                gu = (gu4[d] if e == 0 else gu_x[d]) if f == 0 else gu_c[e * 4 + d]
                do = (do4[d] if e == 0 else do_x[d]) if f == 0 else do_c[e * 4 + d]
                rs = pl.ds(pl.multiple_of((xb ^ e) * deep, 16), deep)
                cs = pl.ds(pl.multiple_of((z ^ d) * wide, 128), wide)
                for c, ref in ((0, gate_ref), (1, up_ref)):

                    @pl.when((core ^ f) == c)
                    def _():
                        ref[rs, cs] = gu.astype(F32)

                m = (core ^ f) * 8 + (xb ^ e) * 4 + (z ^ d)
                rows = down_ref.shape[0] // 16
                down_ref[pl.ds(pl.multiple_of(m * rows, 8), rows), :] = do[:rows].astype(F32)
                few = do.shape[0] - rows

                @pl.when(m < out_ref.shape[0] // few)
                def _():
                    out_ref[pl.ds(pl.multiple_of(m * few, 8), few), :] = do[rows:].astype(F32)


def final_ffn(at, gu4, gu_x, gu_c, do4, do_x, do_c, half, ff, width):
    f32 = lambda *s: jax.ShapeDtypeStruct(s, F32)
    return pl.pallas_call(
        final_kernel,
        in_specs=[pl.BlockSpec(memory_space=pltpu.SMEM)] + [pl.BlockSpec(memory_space=pltpu.VMEM)] * 6,
        out_specs=[pl.BlockSpec(memory_space=pltpu.VMEM)] * 4,
        out_shape=[f32(half, ff), f32(half, ff), f32(ff // 2, width), f32(half, width)],
        compiler_params=pltpu.CompilerParams(vmem_limit_bytes=LIMIT),
        cost_estimate=pl.CostEstimate(flops=int(5e9), bytes_accessed=int(10e6), transcendentals=0),
    )(at, gu4, gu_x, gu_c, do4, do_x, do_c)


def final_t_kernel(at_ref, t4, t_x, t_c, q_ref, k_ref, v_ref, g_ref, whole):
    core, xb, z = at_ref[0], at_ref[1], at_ref[2]
    deep, wide = t4.shape[1:]
    for f in range(2):
        for e in range(2):
            for d in range(4):
                t = (t4[d] if e == 0 else t_x[d]) if f == 0 else t_c[e * 4 + d]
                rs = pl.ds(pl.multiple_of((xb ^ e) * deep, 16), deep)
                cs = pl.ds(pl.multiple_of((core ^ f) * 512 + (z ^ d) * wide, 128), wide)
                whole[rs, cs] = t.astype(F32)
    a = q_ref.shape[1]
    b = a + k_ref.shape[1]
    c = b + v_ref.shape[1]
    q_ref[...] = whole[:, :a]
    k_ref[...] = whole[:, a:b]
    v_ref[...] = whole[:, b:c]
    g_ref[...] = whole[:, c:].T[:8]


def final_t(at, t4, t_x, t_c, half, width, kv_width):
    f32 = lambda *s: jax.ShapeDtypeStruct(s, F32)
    return pl.pallas_call(
        final_t_kernel,
        in_specs=[pl.BlockSpec(memory_space=pltpu.SMEM)] + [pl.BlockSpec(memory_space=pltpu.VMEM)] * 3,
        out_specs=[pl.BlockSpec(memory_space=pltpu.VMEM)] * 4,
        out_shape=[f32(half, width), f32(half, kv_width), f32(half, kv_width), f32(8, half)],
        scratch_shapes=[pltpu.VMEM((half, 1024), F32)],
        compiler_params=pltpu.CompilerParams(vmem_limit_bytes=LIMIT),
        cost_estimate=pl.CostEstimate(flops=int(1e9), bytes_accessed=int(2e6), transcendentals=0),
    )(at, t4, t_x, t_c)


def swap(x, axis, bit):
    n = lax.axis_size(axis)
    return lax.ppermute(x, axis, [(i, i ^ (1 << bit)) for i in range(n)])


def bit_of(axis, bit):
    return (lax.axis_index(axis) >> bit) & 1


def pin(*arrays):
    return lax.optimization_barrier(arrays)


def pick(x, at):
    return lax.dynamic_index_in_dim(x, at, 0, keepdims=False)


def in_order(flag, mine, other, axis):
    return jnp.where(
        flag == 0,
        jnp.concatenate([mine, other], axis=axis),
        jnp.concatenate([other, mine], axis=axis),
    )


def plus(a, b):
    return (a.astype(F32) + b.astype(F32)).astype(BF)


def two_level():
    return lax.axis_size("fsdp") == 2 and lax.axis_size("ctx") == 16


def z_swap(x, by):
    return lax.ppermute(x, "ctx", [(i, i ^ (4 * by)) for i in range(16)])


def z_sum(x):
    z = lax.axis_index("ctx") >> 2
    total = pick(x, z).astype(F32)
    for by in range(1, 4):
        total = total + z_swap(pick(x, z ^ by), by).astype(F32)
    return total.astype(BF)


def z_join(piece):
    return jnp.stack([piece] + [z_swap(piece, by) for by in range(1, 4)])


def natural_gu(pieces):
    _, a, b = pieces.shape
    return pieces.reshape(2, 4, a, b).transpose(0, 2, 1, 3).reshape(2 * a, 4 * b).astype(F32)


def other_sum(x):
    x = lax.psum_scatter(x.astype(BF), "fsdp", scatter_dimension=0, tiled=True)
    return lax.psum(x, "ctx").astype(F32)


def local(tokens, gain_attn, w_query, w_key, w_value, w_out, gain_ffn, w_gate, w_up, w_down, cotangent):
    seqs, length, width = tokens.shape
    count = lax.axis_size("ctx")
    team = count // seqs
    sub = length // team
    rows = count * sub
    ff = w_gate.shape[1]
    kv_width = KV_HEADS * HEAD_DIM
    qkv_cols = width + 2 * kv_width
    place = lax.axis_index("ctx") % team
    own = gain_attn.shape[0]
    fast = two_level()

    def move(x):
        return lax.all_to_all(x.reshape(count, sub, width), "ctx", 0, 0, tiled=True)

    x = move(tokens)
    gain_rows = jnp.zeros((8, ff), BF).at[0, :own].set(gain_attn).at[1, :own].set(gain_ffn)
    first = jnp.concatenate([jnp.concatenate([w_query, w_key, w_value, w_out], axis=1), gain_rows], axis=0)
    if fast:
        core, rank = bit_of("ctx", 0), bit_of("fsdp", 0)

        def halved(shard, axis):
            half = shard.shape[axis] // 2
            return lax.dynamic_slice_in_dim(shard, core * half, half, axis)

        def other_shard(got, axis):
            return in_order(core, got, swap(got, "ctx", 0), axis)

        got = swap(halved(first, 1), "fsdp", 0)
        other = other_shard(got, 1)
        gains = in_order(rank, first[own : own + 2, :own], other[own : own + 2, :own], 1).astype(F32)
        first = in_order(rank, first[:own], other[:own], 0)
        gate_half, up_half, down_half, got = pin(halved(w_gate, 1), halved(w_up, 1), halved(w_down, 0), got)
        gate_got, up_got, down_got = (swap(h, "fsdp", 0) for h in (gate_half, up_half, down_half))
    else:
        first = lax.all_gather(first, "fsdp", axis=0)
        gains = first[:, own : own + 2, :own].transpose(1, 0, 2).reshape(2, width).astype(F32)
        first = first[:, :own].reshape(width, first.shape[2])
        gate_w, up_w, down_w = (lax.all_gather(w, "fsdp", axis=0, tiled=True) for w in (w_gate, w_up, w_down))
    gains = jnp.pad(gains, ((0, 6), (0, 0)))

    row = jnp.arange(rows, dtype=jnp.int32)
    position = (row // sub) * length + place * sub + row % sub
    frequency = THETA ** (-jnp.arange(HEAD_DIM // 2, dtype=F32) * 2.0 / HEAD_DIM)
    angles = frequency[:, None] * position.astype(F32)[None, :]
    cosine, sine = jnp.cos(angles), jnp.sin(angles)
    groups = [[t * team + p for p in range(team)] for t in range(seqs)]
    slots = jnp.stack([place, 1 - place]) if team == 2 else jnp.arange(team)
    block_row = jnp.arange(BLOCK, dtype=jnp.int32)
    base = (block_row // sub) * length + block_row % sub
    key_pos = base[None, :] + slots[:, None] * sub
    query_pos = base + place * sub
    bias = jnp.where(key_pos[:, :, None] <= query_pos[None, None, :], 0.0, NEGATIVE).astype(F32)
    flags = jnp.stack([core, rank]) if fast else jnp.zeros((2,), jnp.int32)

    x, cot_send = pin(x, cotangent)
    cot = move(cot_send)
    query, kv_own = project_qkv(x, first, gains, cosine, sine)
    if fast:
        kv_own, gate_got, up_got, down_got = pin(kv_own, gate_got, up_got, down_got)
        gate_w = in_order(rank, w_gate, other_shard(gate_got, 1), 0)
        up_w = in_order(rank, w_up, other_shard(up_got, 1), 0)
        down_w = in_order(rank, w_down, other_shard(down_got, 0), 0)
    if team == 2:
        kv_all = (kv_own, swap(kv_own, "ctx", 0))
    else:
        kv_all = lax.all_gather(kv_own, "ctx", axis=0, axis_index_groups=groups)
        kv_all = tuple(kv_all[s] for s in range(team))
    attended, log_total = attn_fwd(bias, query, kv_all)
    attended, cot = pin(attended, cot)
    mixed, d_res, d_att, row_dot, keep_gu, send_gu, keep_do, send_do, gain_sum = feed_forward(
        flags, attended, x, cot, first, gate_w, up_w, down_w, gains
    )
    mixed_out = move(mixed)

    n = rows // BLOCK
    spans = ((0, n - 1), (n - 1, n))
    part = functools.partial(attn_bwd, bias, query, kv_all, d_att, log_total, row_dot)
    if fast:
        x_bit = bit_of("ctx", 1)
        got_gu, got_do = swap(send_gu, "ctx", 0), swap(send_do, "ctx", 0)
        gu, do = plus(keep_gu, got_gu), plus(keep_do, got_do)
        gu = gu.reshape((2, 2, 4) + gu.shape[2:]).swapaxes(0, 1)
        keep_gu, send_gu = pick(gu, x_bit), pick(gu, 1 - x_bit)
        keep_do, send_do = pick(do, rank), pick(do, 1 - rank)
        send_gu, send_do, row_dot = pin(send_gu, send_do, row_dot)
        part = functools.partial(attn_bwd, bias, query, kv_all, d_att, log_total, row_dot)
        got_gu, got_do = swap(send_gu, "ctx", 1), swap(send_do, "fsdp", 0)
        dq_a, before = part(*spans[0])
        got_gu, got_do, mixed_out, before = pin(got_gu, got_do, mixed_out, before)
        gu, do = plus(keep_gu, got_gu), plus(keep_do, got_do)
        do = do.reshape((2, 4) + do.shape[1:])
        keep_gu, send_gu = pick(gu, rank), pick(gu, 1 - rank)
        keep_do, send_do = pick(do, x_bit), pick(do, 1 - x_bit)
        send_gu, send_do, before = pin(send_gu, send_do, before)
        got_gu, got_do = swap(send_gu, "fsdp", 0), swap(send_do, "ctx", 1)
        dq_b, d_kv, d_kv_low = part(*spans[1], before=before, last=True)
        got_gu, got_do, d_kv_low, dq_b = pin(got_gu, got_do, d_kv_low, dq_b)
        gu, do = plus(keep_gu, got_gu), plus(keep_do, got_do)
    else:
        dq_a, before = part(*spans[0])
        dq_b, d_kv, d_kv_low = part(*spans[1], before=before, last=True)
    if team == 2:
        own_kv, got_kv = d_kv[:1], swap(d_kv_low[1], "ctx", 0)
    else:
        own_kv = lax.psum_scatter(d_kv_low, "ctx", scatter_dimension=0, axis_index_groups=groups)
        own_kv, got_kv = own_kv.astype(F32)[None], jnp.zeros((2 * kv_width, rows), BF)
    d_x, keep_t, send_t = back_qkv(
        flags, spans, (dq_a, dq_b), own_kv, got_kv, x, d_res, first, gains, cosine, sine, gain_sum
    )
    grad_tokens = move(d_x)
    if fast:
        gu, do = z_sum(gu), z_sum(do)
        t = plus(keep_t, swap(send_t, "ctx", 0))
        t = plus(pick(t, rank), swap(pick(t, 1 - rank), "fsdp", 0))
        t = t.reshape((2, 4) + t.shape[1:])
        t = plus(pick(t, x_bit), swap(pick(t, 1 - x_bit), "ctx", 1))
        t = z_sum(t)

        def widen(piece):
            four = z_join(piece)
            across = swap(four, "ctx", 1)
            return four, across, swap(jnp.concatenate([four, across], axis=0), "ctx", 0)

        at = jnp.stack([core, x_bit, lax.axis_index("ctx") >> 2])
        own_gate, own_up, own_down, own_out = final_ffn(at, *widen(gu), *widen(do), width // 2, ff, width)
        own_query, own_key, own_value, own_gains = final_t(at, *widen(t), width // 2, width, kv_width)
    else:
        pair = jnp.stack([keep_gu, send_gu])
        gate, up = (jnp.concatenate([natural_gu(pair[c, y]) for y in range(2)], axis=0) for c in range(2))
        do = jnp.stack([keep_do, send_do], axis=1).reshape((32,) + keep_do.shape[2:])
        deep = ff // 32
        own_gate, own_up = other_sum(gate), other_sum(up)
        own_down = other_sum(do[:, :deep].reshape(ff, width))
        out = do[:, deep:].reshape((2, -1, width))[:, : width // 2]
        own_out = other_sum(out.reshape(width, width))
        pair = jnp.stack([keep_t, send_t])
        t = [jnp.concatenate([natural_gu(pair[c, y]) for c in range(2)], axis=1) for y in range(2)]
        own_t = other_sum(jnp.concatenate(t, axis=0))
        own_query, own_key = own_t[:, :width], own_t[:, width : width + kv_width]
        own_value, own_gains = own_t[:, width + kv_width : qkv_cols], own_t[:, qkv_cols:].T
    return (
        mixed_out.reshape(tokens.shape),
        grad_tokens.reshape(tokens.shape),
        own_gains[0],
        own_query,
        own_key,
        own_value,
        own_out,
        own_gains[1],
        own_gate,
        own_up,
        own_down,
    )


def solution(mesh):
    rows, flat, seq = P("fsdp", None), P("fsdp"), P("fsdp", "ctx", None)
    return jax.shard_map(
        local,
        mesh=mesh,
        in_specs=(seq, flat, rows, rows, rows, rows, flat, rows, rows, rows, seq),
        out_specs=(seq, seq, flat, rows, rows, rows, rows, flat, rows, rows, rows),
        check_vma=False,
    )
```

```python
import functools

import jax
import jax.numpy as jnp
from jax import lax
from jax.experimental import pallas as pl
from jax.experimental.pallas import tpu as pltpu
from jax.sharding import PartitionSpec as P

HEADS = 9
KV_HEADS = 3
HEAD_DIM = 64
EPSILON = 1e-05
THETA = 100000.0
NEGATIVE = -1e30
LOG2E = 1.4426950408889634
LN2 = 0.6931471805599453
F32=jnp.float32; BF=jnp.bfloat16
NT=(((1,),(1,)),((),()))
NN=(((1,),(0,)),((),()))
def mm(a,b,dims=NN):
    return lax.dot_general(a,b,dims,preferred_element_type=F32)

def heads_of(ref, kv, group):
    return jnp.concatenate([ref[(kv*group+h)*64:(kv*group+h+1)*64,:] for h in range(group)],axis=1)

def fwd_kernel(bias_ref, q_ref, *refs, kvs, group, slots, rows, qb):
    kv_ref, (o_ref, lse_ref, k_scr, m_scr, acc_scr)=refs[:slots], refs[slots:]
    i=pl.program_id(0)
    kw=kvs*64
    @pl.when(i==0)
    def _():
        for s in range(slots):
            for h in range(kvs):
                k_scr[h,s]=kv_ref[s][h*64:(h+1)*64,:].T
    qs=[heads_of(q_ref,h,group) for h in range(kvs)]
    width=group*qb
    m_scr[...]=jnp.full(m_scr.shape,-1e30,F32)
    acc_scr[...]=jnp.zeros(acc_scr.shape,F32)
    ones=jnp.ones((8,slots*qb),BF)
    def chunk(c, masked):
        off=pl.multiple_of(c*qb,qb)
        for h in range(kvs):
            k=jnp.concatenate([k_scr[h,s,pl.ds(off,qb),:] for s in range(slots)],axis=0)
            v=jnp.concatenate([kv_ref[s][kw+h*64:kw+(h+1)*64,pl.ds(off,qb)] for s in range(slots)],axis=1)
            v=jnp.concatenate([v,ones],axis=0)
            st=mm(k,qs[h])
            if masked:
                b=bias_ref[...].reshape(slots*qb,qb)
                st=st+jnp.concatenate([b]*group,axis=1)
            m_old=m_scr[h:h+1,:]
            m_new=jnp.maximum(m_old,jnp.max(st,axis=0,keepdims=True))
            p=jnp.exp2(st-m_new).astype(BF)
            acc_scr[h]=acc_scr[h]*jnp.exp2(m_old-m_new)+mm(v,p)
            m_scr[h:h+1,:]=m_new
    def body(c,_):
        chunk(c,False); return 0
    lax.fori_loop(0,i,body,0)
    chunk(i,True)
    for h in range(kvs):
        acc=acc_scr[h]
        tot=acc[64:65,:]
        o=acc[:64,:]*(1.0/tot)
        lse=m_scr[h:h+1,:]+jnp.log2(tot)
        for g in range(group):
            r=h*group+g
            o_ref[r*64:(r+1)*64,:]=o[:,g*qb:(g+1)*qb]
            lse_ref[r:r+1,:]=lse[:,g*qb:(g+1)*qb]

def attn_fwd(bias, qT, kvT, kvs=3, group=3, qb=256):
    slots,rows=len(kvT),kvT[0].shape[1]
    n=rows//qb
    heads=kvs*group
    return pl.pallas_call(
        functools.partial(fwd_kernel,kvs=kvs,group=group,slots=slots,rows=rows,qb=qb),
        grid=(n,),
        in_specs=[pl.BlockSpec((slots,qb,qb),lambda i:(0,0,0)),
                  pl.BlockSpec((heads*64,qb),lambda i:(0,i)),
                  *[pl.BlockSpec((2*kvs*64,rows),lambda i:(0,0))]*slots],
        out_specs=[pl.BlockSpec((heads*64,qb),lambda i:(0,i)),
                   pl.BlockSpec((16,qb),lambda i:(0,i))],
        out_shape=[jax.ShapeDtypeStruct((heads*64,rows),F32),jax.ShapeDtypeStruct((16,rows),F32)],
        scratch_shapes=[pltpu.VMEM((kvs,slots,rows,64),BF),pltpu.VMEM((8,group*qb),F32),
                        pltpu.VMEM((kvs,72,group*qb),F32)],
        compiler_params=pltpu.CompilerParams(vmem_limit_bytes=56*2**20),
        cost_estimate=pl.CostEstimate(flops=int(25e9),bytes_accessed=int(8e6),transcendentals=int(1e7)),
    )(bias,qT,*kvT)

def bwd_kernel(*refs, kvs, group, slots, qb, lo, first, last):
    bias_ref, q_ref, do_ref, lse_ref, rd_ref = refs[:5]
    kv_ref, refs = refs[5 : 5 + slots], refs[5 + slots :]
    if not first:
        before_ref, refs = refs[0], refs[1:]
    if last:
        dq_ref, dkv_ref, low_ref, kv_scr = refs
    else:
        dq_ref, dkv_ref, kv_scr = refs
    step = pl.program_id(0)
    kw = kvs * 64

    @pl.when(step == 0)
    def _():
        for s in range(slots):
            for h in range(2 * kvs):
                kv_scr[h, s] = kv_ref[s][h * 64 : (h + 1) * 64, :].T
        dkv_ref[...] = jnp.zeros(dkv_ref.shape, F32) if first else before_ref[...]

    dq_ref[...] = jnp.zeros(dq_ref.shape, F32)
    qs = [heads_of(q_ref, h, group) for h in range(kvs)]
    dos = [heads_of(do_ref, h, group) for h in range(kvs)]

    def along(ref, h):
        return jnp.concatenate([ref[h * group + g : h * group + g + 1, :] for g in range(group)], axis=1)

    lses = [along(lse_ref, h) for h in range(kvs)]
    rds = [along(rd_ref, h) for h in range(kvs)]

    def chunk(c, masked):
        off = pl.multiple_of(c * qb, qb)
        for h in range(kvs):
            k = jnp.concatenate([kv_scr[h, s, pl.ds(off, qb), :] for s in range(slots)], axis=0)
            v = jnp.concatenate([kv_scr[kvs + h, s, pl.ds(off, qb), :] for s in range(slots)], axis=0)
            k_t = jnp.concatenate([kv_ref[s][h * 64 : (h + 1) * 64, pl.ds(off, qb)] for s in range(slots)], axis=1)
            st = mm(k, qs[h])
            if masked:
                st = st + jnp.concatenate([bias_ref[...].reshape(slots * qb, qb)] * group, axis=1)
            p = jnp.exp2(st - lses[h])
            dp = mm(v, dos[h])
            ds = (p * (dp - rds[h])).astype(BF)
            dk = mm(qs[h], ds, NT)
            dv = mm(dos[h], p.astype(BF), NT)
            dq = mm(k_t, ds)
            for s in range(slots):
                dkv_ref[s, h * 64 : (h + 1) * 64, pl.ds(off, qb)] += dk[:, s * qb : (s + 1) * qb]
                dkv_ref[s, kw + h * 64 : kw + (h + 1) * 64, pl.ds(off, qb)] += dv[:, s * qb : (s + 1) * qb]
            for g in range(group):
                r = h * group + g
                dq_ref[r * 64 : (r + 1) * 64, :] += dq[:, g * qb : (g + 1) * qb]

    def body(c, carry):
        chunk(c, False)
        return carry

    lax.fori_loop(0, step + lo, body, 0)
    chunk(step + lo, True)
    if last:

        @pl.when(step == pl.num_programs(0) - 1)
        def _():
            low_ref[...] = dkv_ref[...].astype(BF)


def attn_bwd(bias, q_t, kv_t, do_t, lse, rd, lo, hi, before=None, last=False, kvs=3, group=3, qb=256):
    slots, rows = len(kv_t), kv_t[0].shape[1]
    width = kvs * group * 64
    whole = pl.BlockSpec((slots, 2 * kvs * 64, rows), lambda i: (0, 0, 0))
    tall = pl.BlockSpec((width, qb), lambda i: (0, i + lo))
    stat = pl.BlockSpec((16, qb), lambda i: (0, i + lo))
    out_specs = [pl.BlockSpec((width, qb), lambda i: (0, i)), whole]
    out_shape = [
        jax.ShapeDtypeStruct((width, (hi - lo) * qb), F32),
        jax.ShapeDtypeStruct((slots, 2 * kvs * 64, rows), F32),
    ]
    if last:
        out_specs.append(whole)
        out_shape.append(jax.ShapeDtypeStruct((slots, 2 * kvs * 64, rows), BF))
    args = (bias, q_t, do_t, lse, rd, *kv_t) + (() if before is None else (before,))
    units = sum(range(lo + 1, hi + 1))
    return pl.pallas_call(
        functools.partial(
            bwd_kernel, kvs=kvs, group=group, slots=slots, qb=qb, lo=lo, first=before is None, last=last
        ),
        grid=(hi - lo,),
        in_specs=[pl.BlockSpec((slots, qb, qb), lambda i: (0, 0, 0)), tall, tall, stat, stat]
        + [pl.BlockSpec((2 * kvs * 64, rows), lambda i: (0, 0))] * slots
        + ([] if before is None else [whole]),
        out_specs=out_specs,
        out_shape=out_shape,
        scratch_shapes=[pltpu.VMEM((2 * kvs, slots, rows, 64), BF)],
        compiler_params=pltpu.CompilerParams(vmem_limit_bytes=60 * 2**20),
        cost_estimate=pl.CostEstimate(flops=int(4e9) * units, bytes_accessed=int(16e6), transcendentals=0),
    )(*args)


TN = (((0,), (0,)), ((), ()))
TT = (((0,), (1,)), ((), ()))
BLOCK = 256
PIECES = 8
LIMIT = 60 * 2**20


def rotated(values, cosine, sine):
    a, b = values[:32], values[32:]
    return jnp.concatenate([a * cosine - b * sine, b * cosine + a * sine], axis=0)


def flat_rows(ref):
    count, sub, width = ref.shape
    return ref[...].reshape(count * sub, width)


def rms(values):
    return lax.rsqrt(jnp.mean(values * values, axis=-1, keepdims=True) + EPSILON)


def qkv_kernel(x_ref, w_ref, gain_ref, cos_ref, sin_ref, q_ref, kv_ref, wt_scr):
    @pl.when(pl.program_id(0) == 0)
    def _():
        wt_scr[...] = w_ref[:, : wt_scr.shape[0]].T

    source = flat_rows(x_ref).astype(F32)
    hidden = (source * rms(source) * gain_ref[0:1, :]).astype(BF)
    out = mm(wt_scr[...], hidden, NT)
    cosine, sine = cos_ref[...], sin_ref[...]
    for h in range(HEADS):
        part = rotated(out[h * 64 : (h + 1) * 64], cosine, sine)
        q_ref[h * 64 : (h + 1) * 64, :] = (part * (HEAD_DIM**-0.5 * LOG2E)).astype(BF)
    top = HEADS * 64
    for h in range(KV_HEADS):
        part = rotated(out[top + h * 64 : top + (h + 1) * 64], cosine, sine)
        kv_ref[h * 64 : (h + 1) * 64, :] = part.astype(BF)
    kv_ref[KV_HEADS * 64 :, :] = out[top + KV_HEADS * 64 :].astype(BF)


def project_qkv(x, first, gains, cosine, sine):
    count, sub, width = x.shape
    rows = count * sub
    per = BLOCK // sub
    kv2 = 2 * KV_HEADS * HEAD_DIM
    return pl.pallas_call(
        qkv_kernel,
        grid=(rows // BLOCK,),
        in_specs=[
            pl.BlockSpec((per, sub, width), lambda i: (i, 0, 0)),
            pl.BlockSpec(first.shape, lambda i: (0, 0)),
            pl.BlockSpec(gains.shape, lambda i: (0, 0)),
            pl.BlockSpec((32, BLOCK), lambda i: (0, i)),
            pl.BlockSpec((32, BLOCK), lambda i: (0, i)),
        ],
        out_specs=[pl.BlockSpec((width, BLOCK), lambda i: (0, i)), pl.BlockSpec((kv2, BLOCK), lambda i: (0, i))],
        out_shape=[jax.ShapeDtypeStruct((width, rows), BF), jax.ShapeDtypeStruct((kv2, rows), BF)],
        scratch_shapes=[pltpu.VMEM((width + kv2, width), BF)],
        compiler_params=pltpu.CompilerParams(vmem_limit_bytes=LIMIT),
        cost_estimate=pl.CostEstimate(flops=int(6e9), bytes_accessed=int(5e6), transcendentals=0),
    )(x, first, gains, cosine, sine)


def ffn_kernel(
    place_ref, o_ref, x_ref, cot_ref, first_ref, gain_ref,
    gate_own, gate_got, gate_swap, up_own, up_got, up_swap, down_own, down_got, down_swap,
    mixed_ref, dres_ref, datt_ref, rd_ref, keep_gu, send_gu, keep_do, send_do, gg_ref,
    acc_gu, acc_down, acc_out, gate_ref, up_ref, down_ref,
):
    step = pl.program_id(0)
    width = x_ref.shape[2]

    @pl.when(step == 0)
    def _():
        acc_gu[...] = jnp.zeros(acc_gu.shape, F32)
        acc_down[...] = jnp.zeros(acc_down.shape, F32)
        acc_out[...] = jnp.zeros(acc_out.shape, F32)
        gg_ref[...] = jnp.zeros(gg_ref.shape, F32)
        for rank in range(2):

            @pl.when(place_ref[1] == rank)
            def _():
                for ref, own in ((gate_ref, gate_own), (up_ref, up_own), (down_ref, down_own)):
                    n = own.shape[0]
                    ref[rank * n : (rank + 1) * n] = own[...]
                for core in range(2):

                    @pl.when(place_ref[0] == core)
                    def _():
                        for ref, parts in ((gate_ref, (gate_got, gate_swap)), (up_ref, (up_got, up_swap))):
                            n, m = parts[0].shape
                            for k, part in ((core, parts[0]), (1 - core, parts[1])):
                                ref[(1 - rank) * n : (2 - rank) * n, k * m : (k + 1) * m] = part[...]
                        n = down_got.shape[0]
                        for k, part in ((core, down_got), (1 - core, down_swap)):
                            low = (2 * (1 - rank) + k) * n
                            down_ref[low : low + n] = part[...]

    cols = first_ref.shape[1]
    out_w = first_ref[:, cols - width :]
    attended = o_ref[...]
    mixed = attended.astype(BF)
    residual = flat_rows(x_ref).astype(F32) + mm(mixed, out_w, TN)
    scale = rms(residual)
    normed = residual * scale
    gain = gain_ref[1:2, :]
    hidden = (normed * gain).astype(BF)
    gate = mm(hidden, gate_ref[...])
    up = mm(hidden, up_ref[...])
    sig = 0.5 * jnp.tanh(0.5 * gate) + 0.5
    silu = gate * sig
    activated = (silu * up).astype(BF)
    mixed_out = (residual + mm(activated, down_ref[...])).astype(BF)
    mixed_ref[...] = mixed_out.reshape(mixed_ref.shape)
    cot = flat_rows(cot_ref)
    d_act = mm(cot, down_ref[...], NT)
    acc_down[...] += mm(activated, cot, TN)
    d_gate = (d_act * up * sig * (1.0 + gate * (1.0 - sig))).astype(BF)
    d_up = (d_act * silu).astype(BF)
    acc_gu[0] += mm(hidden, d_gate, TN)
    acc_gu[1] += mm(hidden, d_up, TN)
    d_hidden = mm(d_gate, gate_ref[...], NT) + mm(d_up, up_ref[...], NT)
    dn = d_hidden * normed
    gg_ref[...] += jnp.sum(dn.reshape(-1, 8, width), axis=0)
    inner = jnp.mean(dn * gain, axis=-1, keepdims=True)
    d_res = cot.astype(F32) + scale * (d_hidden * gain - normed * inner)
    dres_ref[...] = d_res
    d_low = d_res.astype(BF)
    acc_out[...] += mm(mixed, d_low)
    d_att = mm(out_w, d_low, NT).astype(BF)
    datt_ref[...] = d_att
    prod = d_att.astype(F32) * attended
    for h in range(HEADS):
        rd_ref[h : h + 1, :] = jnp.sum(prod[h * 64 : (h + 1) * 64], axis=0, keepdims=True)
    rd_ref[HEADS:, :] = jnp.zeros((16 - HEADS, rd_ref.shape[1]), F32)

    @pl.when(step == pl.num_programs(0) - 1)
    def _():
        core = place_ref[0]
        half = width // 2
        ff = acc_gu.shape[2]
        for y in range(2):
            for p in range(PIECES):
                rs = slice(y * half + (p // 4) * (half // 2), y * half + (p // 4 + 1) * (half // 2))
                cs = slice((p % 4) * (ff // 4), (p % 4 + 1) * (ff // 4))
                keep_gu[y, p] = acc_gu[core, rs, cs].astype(BF)
                send_gu[y, p] = acc_gu[1 - core, rs, cs].astype(BF)
        down_rows, out_rows = ff // 32, width // 24
        for y in range(2):
            for p in range(PIECES):
                for ref, c in ((keep_do, core), (send_do, 1 - core)):
                    start = pl.multiple_of(y * (ff // 2) + (PIECES * c + p) * down_rows, 16)
                    ref[y, p, :down_rows] = acc_down[pl.ds(start, down_rows), :].astype(BF)
                    start = y * half + jnp.minimum(PIECES * c + p, half // out_rows - 1) * out_rows
                    ref[y, p, down_rows:] = acc_out[pl.ds(pl.multiple_of(start, 8), out_rows), :].astype(BF)


def feed_forward(place, attended, x, cot, first, gains, weights):
    count, sub, width = x.shape
    rows, ff = count * sub, weights[0].shape[1]
    per = BLOCK // sub
    gu = (2, PIECES, width // 4, ff // 4)
    do = (2, PIECES, ff // 32 + width // 24, width)

    def whole(shape):
        return pl.BlockSpec(shape, lambda i: (0,) * len(shape))

    seq = pl.BlockSpec((per, sub, width), lambda i: (i, 0, 0))
    tall = pl.BlockSpec((width, BLOCK), lambda i: (0, i))
    return pl.pallas_call(
        ffn_kernel,
        grid=(rows // BLOCK,),
        in_specs=[
            pl.BlockSpec(memory_space=pltpu.SMEM), tall, seq, seq,
            whole(first.shape), whole(gains.shape), *(whole(w.shape) for w in weights),
        ],
        out_specs=[
            seq, pl.BlockSpec((BLOCK, width), lambda i: (i, 0)), tall, pl.BlockSpec((16, BLOCK), lambda i: (0, i)),
            whole(gu), whole(gu), whole(do), whole(do), whole((8, width)),
        ],
        out_shape=[
            jax.ShapeDtypeStruct(x.shape, BF),
            jax.ShapeDtypeStruct((rows, width), F32),
            jax.ShapeDtypeStruct((width, rows), BF),
            jax.ShapeDtypeStruct((16, rows), F32),
            jax.ShapeDtypeStruct(gu, BF), jax.ShapeDtypeStruct(gu, BF),
            jax.ShapeDtypeStruct(do, BF), jax.ShapeDtypeStruct(do, BF),
            jax.ShapeDtypeStruct((8, width), F32),
        ],
        scratch_shapes=[
            pltpu.VMEM((2, width, ff), F32), pltpu.VMEM((ff, width), F32), pltpu.VMEM((width, width), F32),
            pltpu.VMEM((width, ff), BF), pltpu.VMEM((width, ff), BF), pltpu.VMEM((ff, width), BF),
        ],
        compiler_params=pltpu.CompilerParams(vmem_limit_bytes=LIMIT),
        cost_estimate=pl.CostEstimate(flops=int(32e9), bytes_accessed=int(20e6), transcendentals=0),
    )(place, attended, x, cot, first, gains, *weights)


def back_kernel(*refs, spans):
    place_ref, refs = refs[0], refs[1:]
    dq_refs, refs = refs[: len(spans)], refs[len(spans) :]
    own_ref, got_ref, x_ref, dres_ref, first_ref, gain_ref, cos_ref, sin_ref, gg_ref, dx_ref = refs[:10]
    keep_ref, send_ref, acc, dt_scr, ga_scr, w_scr = refs[10:]
    step = pl.program_id(0)
    width = x_ref.shape[2]
    kv = KV_HEADS * 64
    total = width + 2 * kv

    @pl.when(step == 0)
    def _():
        acc[...] = jnp.zeros(acc.shape, F32)
        ga_scr[...] = jnp.zeros(ga_scr.shape, F32)
        w_scr[...] = first_ref[:, :total].T

    cosine, sine = cos_ref[...], -sin_ref[...]
    for (lo, hi), dq_ref in zip(spans, dq_refs):

        @pl.when((step >= lo) & (step < hi))
        def _():
            for h in range(HEADS):
                part = dq_ref[h * 64 : (h + 1) * 64, :] * (HEAD_DIM**-0.5)
                dt_scr[h * 64 : (h + 1) * 64, :] = rotated(part, cosine, sine).astype(BF)

    d_kv = own_ref[0] + got_ref[...].astype(F32)
    for h in range(KV_HEADS):
        part = d_kv[h * 64 : (h + 1) * 64] * LN2
        dt_scr[width + h * 64 : width + (h + 1) * 64, :] = rotated(part, cosine, sine).astype(BF)
    dt_scr[width + kv :, :] = d_kv[kv:].astype(BF)
    d_t = dt_scr[...]
    source = flat_rows(x_ref).astype(F32)
    scale = rms(source)
    normed = source * scale
    gain = gain_ref[0:1, :]
    hidden = (normed * gain).astype(BF)
    acc[:total] += mm(d_t, hidden)
    d_hidden = mm(d_t, w_scr[...], TN)
    dn = d_hidden * normed
    ga_scr[...] += jnp.sum(dn.reshape(-1, 8, width), axis=0)
    inner = jnp.mean(dn * gain, axis=-1, keepdims=True)
    grad = dres_ref[...] + scale * (d_hidden * gain - normed * inner)
    dx_ref[...] = grad.astype(BF).reshape(dx_ref.shape)

    @pl.when(step == pl.num_programs(0) - 1)
    def _():
        core = place_ref[0]
        acc[total : total + 1, :] = jnp.sum(ga_scr[...], axis=0, keepdims=True)
        acc[total + 1 : total + 2, :] = jnp.sum(gg_ref[...], axis=0, keepdims=True)
        half, deep = width // 2, width // 4
        for ct in range(4):
            for ref, c in ((keep_ref, core), (send_ref, 1 - core)):
                start = pl.multiple_of(c * 512 + ct * 128, 128)
                block = acc[pl.ds(start, 128), :].T.astype(BF)
                for y in range(2):
                    for rh in range(2):
                        low = y * half + rh * deep
                        ref[y, rh * 4 + ct] = block[low : low + deep]


def back_qkv(place, spans, d_query, d_kv, got, x, d_res, first, gains, cosine, sine, gg):
    count, sub, width = x.shape
    rows = count * sub
    per = BLOCK // sub
    kv2 = 2 * KV_HEADS * HEAD_DIM
    piece = (2, PIECES, width // 4, 128)

    def whole(shape):
        return pl.BlockSpec(shape, lambda i: (0,) * len(shape))

    seq = pl.BlockSpec((per, sub, width), lambda i: (i, 0, 0))
    return pl.pallas_call(
        functools.partial(back_kernel, spans=spans),
        grid=(rows // BLOCK,),
        in_specs=[
            pl.BlockSpec(memory_space=pltpu.SMEM),
            *(
                pl.BlockSpec((width, BLOCK), lambda i, lo=lo, hi=hi: (0, jnp.clip(i - lo, 0, hi - lo - 1)))
                for lo, hi in spans
            ),
            pl.BlockSpec((1, kv2, BLOCK), lambda i: (0, 0, i)),
            pl.BlockSpec((kv2, BLOCK), lambda i: (0, i)),
            seq, pl.BlockSpec((BLOCK, width), lambda i: (i, 0)),
            whole(first.shape), whole(gains.shape),
            pl.BlockSpec((32, BLOCK), lambda i: (0, i)), pl.BlockSpec((32, BLOCK), lambda i: (0, i)),
            whole(gg.shape),
        ],
        out_specs=[seq, whole(piece), whole(piece)],
        out_shape=[jax.ShapeDtypeStruct(x.shape, BF), jax.ShapeDtypeStruct(piece, BF), jax.ShapeDtypeStruct(piece, BF)],
        scratch_shapes=[
            pltpu.VMEM((1024, width), F32), pltpu.VMEM((width + kv2, BLOCK), BF), pltpu.VMEM((8, width), F32),
            pltpu.VMEM((width + kv2, width), BF),
        ],
        compiler_params=pltpu.CompilerParams(vmem_limit_bytes=LIMIT),
        cost_estimate=pl.CostEstimate(flops=int(10e9), bytes_accessed=int(10e6), transcendentals=0),
    )(place, *d_query, d_kv, got, x, d_res, first, gains, cosine, sine, gg)


def final_kernel(
    at_ref, gu4, gu_x, gu_c, do4, do_x, do_c, gate_ref, up_ref, down_ref, out_ref
):
    core, xb, z = at_ref[0], at_ref[1], at_ref[2]
    deep, wide = gu4.shape[1:]
    for f in range(2):
        for e in range(2):
            for d in range(4):
                gu = (gu4[d] if e == 0 else gu_x[d]) if f == 0 else gu_c[e * 4 + d]
                do = (do4[d] if e == 0 else do_x[d]) if f == 0 else do_c[e * 4 + d]
                rs = pl.ds(pl.multiple_of((xb ^ e) * deep, 16), deep)
                cs = pl.ds(pl.multiple_of((z ^ d) * wide, 128), wide)
                for c, ref in ((0, gate_ref), (1, up_ref)):

                    @pl.when((core ^ f) == c)
                    def _():
                        ref[rs, cs] = gu.astype(F32)

                m = (core ^ f) * 8 + (xb ^ e) * 4 + (z ^ d)
                rows = down_ref.shape[0] // 16
                down_ref[pl.ds(pl.multiple_of(m * rows, 8), rows), :] = do[:rows].astype(F32)
                few = do.shape[0] - rows

                @pl.when(m < out_ref.shape[0] // few)
                def _():
                    out_ref[pl.ds(pl.multiple_of(m * few, 8), few), :] = do[rows:].astype(F32)


def final_ffn(at, gu4, gu_x, gu_c, do4, do_x, do_c, half, ff, width):
    f32 = lambda *s: jax.ShapeDtypeStruct(s, F32)
    return pl.pallas_call(
        final_kernel,
        in_specs=[pl.BlockSpec(memory_space=pltpu.SMEM)] + [pl.BlockSpec(memory_space=pltpu.VMEM)] * 6,
        out_specs=[pl.BlockSpec(memory_space=pltpu.VMEM)] * 4,
        out_shape=[f32(half, ff), f32(half, ff), f32(ff // 2, width), f32(half, width)],
        compiler_params=pltpu.CompilerParams(vmem_limit_bytes=LIMIT),
        cost_estimate=pl.CostEstimate(flops=int(5e9), bytes_accessed=int(10e6), transcendentals=0),
    )(at, gu4, gu_x, gu_c, do4, do_x, do_c)


def final_t_kernel(at_ref, t4, t_x, t_c, q_ref, k_ref, v_ref, g_ref, whole):
    core, xb, z = at_ref[0], at_ref[1], at_ref[2]
    deep, wide = t4.shape[1:]
    for f in range(2):
        for e in range(2):
            for d in range(4):
                t = (t4[d] if e == 0 else t_x[d]) if f == 0 else t_c[e * 4 + d]
                rs = pl.ds(pl.multiple_of((xb ^ e) * deep, 16), deep)
                cs = pl.ds(pl.multiple_of((core ^ f) * 512 + (z ^ d) * wide, 128), wide)
                whole[rs, cs] = t.astype(F32)
    a = q_ref.shape[1]
    b = a + k_ref.shape[1]
    c = b + v_ref.shape[1]
    q_ref[...] = whole[:, :a]
    k_ref[...] = whole[:, a:b]
    v_ref[...] = whole[:, b:c]
    g_ref[...] = whole[:, c:].T[:8]


def final_t(at, t4, t_x, t_c, half, width, kv_width):
    f32 = lambda *s: jax.ShapeDtypeStruct(s, F32)
    return pl.pallas_call(
        final_t_kernel,
        in_specs=[pl.BlockSpec(memory_space=pltpu.SMEM)] + [pl.BlockSpec(memory_space=pltpu.VMEM)] * 3,
        out_specs=[pl.BlockSpec(memory_space=pltpu.VMEM)] * 4,
        out_shape=[f32(half, width), f32(half, kv_width), f32(half, kv_width), f32(8, half)],
        scratch_shapes=[pltpu.VMEM((half, 1024), F32)],
        compiler_params=pltpu.CompilerParams(vmem_limit_bytes=LIMIT),
        cost_estimate=pl.CostEstimate(flops=int(1e9), bytes_accessed=int(2e6), transcendentals=0),
    )(at, t4, t_x, t_c)


def swap(x, axis, bit):
    n = lax.axis_size(axis)
    return lax.ppermute(x, axis, [(i, i ^ (1 << bit)) for i in range(n)])


def bit_of(axis, bit):
    return (lax.axis_index(axis) >> bit) & 1


def pin(*arrays):
    return lax.optimization_barrier(arrays)


def pick(x, at):
    return lax.dynamic_index_in_dim(x, at, 0, keepdims=False)


def in_order(flag, mine, other, axis):
    return jnp.where(
        flag == 0,
        jnp.concatenate([mine, other], axis=axis),
        jnp.concatenate([other, mine], axis=axis),
    )


def plus(a, b):
    return (a.astype(F32) + b.astype(F32)).astype(BF)


def two_level():
    return lax.axis_size("fsdp") == 2 and lax.axis_size("ctx") == 16


def z_swap(x, by):
    return lax.ppermute(x, "ctx", [(i, i ^ (4 * by)) for i in range(16)])


def z_send(x):
    z = lax.axis_index("ctx") >> 2
    return pick(x, z), [pick(x, z ^ by) for by in range(1, 4)]


def z_pass(pieces):
    return [z_swap(p, by) for by, p in zip(range(1, 4), pieces)]


def z_total(mine, got):
    return sum((g.astype(F32) for g in got), mine.astype(F32)).astype(BF)


def z_join(piece):
    return jnp.stack([piece] + [z_swap(piece, by) for by in range(1, 4)])


def natural_gu(pieces):
    _, a, b = pieces.shape
    return pieces.reshape(2, 4, a, b).transpose(0, 2, 1, 3).reshape(2 * a, 4 * b).astype(F32)


def other_sum(x):
    x = lax.psum_scatter(x.astype(BF), "fsdp", scatter_dimension=0, tiled=True)
    return lax.psum(x, "ctx").astype(F32)


def local(tokens, gain_attn, w_query, w_key, w_value, w_out, gain_ffn, w_gate, w_up, w_down, cotangent):
    seqs, length, width = tokens.shape
    count = lax.axis_size("ctx")
    team = count // seqs
    sub = length // team
    rows = count * sub
    ff = w_gate.shape[1]
    kv_width = KV_HEADS * HEAD_DIM
    qkv_cols = width + 2 * kv_width
    place = lax.axis_index("ctx") % team
    own = gain_attn.shape[0]
    fast = two_level()

    def move(x):
        return lax.all_to_all(x.reshape(count, sub, width), "ctx", 0, 0, tiled=True)

    x = move(tokens)
    gain_rows = jnp.zeros((8, ff), BF).at[0, :own].set(gain_attn).at[1, :own].set(gain_ffn)
    first = jnp.concatenate([jnp.concatenate([w_query, w_key, w_value, w_out], axis=1), gain_rows], axis=0)
    if fast:
        core, rank = bit_of("ctx", 0), bit_of("fsdp", 0)

        def halved(shard, axis):
            half = shard.shape[axis] // 2
            return lax.dynamic_slice_in_dim(shard, core * half, half, axis)

        def other_shard(got, axis):
            return in_order(core, got, swap(got, "ctx", 0), axis)

        got = swap(halved(first, 1), "fsdp", 0)
        other = other_shard(got, 1)
        gains = in_order(rank, first[own : own + 2, :own], other[own : own + 2, :own], 1).astype(F32)
        first = in_order(rank, first[:own], other[:own], 0)
        gate_half, up_half, down_half, got = pin(halved(w_gate, 1), halved(w_up, 1), halved(w_down, 0), got)
        gate_got, up_got, down_got = (swap(h, "fsdp", 0) for h in (gate_half, up_half, down_half))
    else:
        first = lax.all_gather(first, "fsdp", axis=0)
        gains = first[:, own : own + 2, :own].transpose(1, 0, 2).reshape(2, width).astype(F32)
        first = first[:, :own].reshape(width, first.shape[2])
        gate_w, up_w, down_w = (lax.all_gather(w, "fsdp", axis=0, tiled=True) for w in (w_gate, w_up, w_down))
    gains = jnp.pad(gains, ((0, 6), (0, 0)))

    row = jnp.arange(rows, dtype=jnp.int32)
    position = (row // sub) * length + place * sub + row % sub
    frequency = THETA ** (-jnp.arange(HEAD_DIM // 2, dtype=F32) * 2.0 / HEAD_DIM)
    angles = frequency[:, None] * position.astype(F32)[None, :]
    cosine, sine = jnp.cos(angles), jnp.sin(angles)
    groups = [[t * team + p for p in range(team)] for t in range(seqs)]
    slots = jnp.stack([place, 1 - place]) if team == 2 else jnp.arange(team)
    block_row = jnp.arange(BLOCK, dtype=jnp.int32)
    base = (block_row // sub) * length + block_row % sub
    key_pos = base[None, :] + slots[:, None] * sub
    query_pos = base + place * sub
    bias = jnp.where(key_pos[:, :, None] <= query_pos[None, None, :], 0.0, NEGATIVE).astype(F32)
    flags = jnp.stack([core, rank]) if fast else jnp.zeros((2,), jnp.int32)

    x, cot_send = pin(x, cotangent)
    cot = move(cot_send)
    query, kv_own = project_qkv(x, first, gains, cosine, sine)
    if fast:
        kv_own, gate_got = pin(kv_own, gate_got)
    if team == 2:
        kv_all = (kv_own, swap(kv_own, "ctx", 0))
    else:
        kv_all = lax.all_gather(kv_own, "ctx", axis=0, axis_index_groups=groups)
        kv_all = tuple(kv_all[s] for s in range(team))
    attended, log_total = attn_fwd(bias, query, kv_all)
    if fast:
        attended, cot, *gots = pin(attended, cot, gate_got, up_got, down_got)
        gots = [(got, swap(got, "ctx", 0)) for got in gots]
        weights = [a for own_w, two in zip((w_gate, w_up, w_down), gots) for a in (own_w, *two)]
    else:
        attended, cot = pin(attended, cot)
        low, side = width // 2, ff // 2
        weights = [a for w in (gate_w, up_w) for a in (w[:low], w[low:, :side], w[low:, side:])]
        weights += [down_w[:side], down_w[side : side + side // 2], down_w[side + side // 2 :]]
    mixed, d_res, d_att, row_dot, keep_gu, send_gu, keep_do, send_do, gain_sum = feed_forward(
        flags, attended, x, cot, first, gains, weights
    )
    mixed_out = move(mixed)

    n = rows // BLOCK
    spans = ((0, n - 1), (n - 1, n))
    part = functools.partial(attn_bwd, bias, query, kv_all, d_att, log_total, row_dot)
    if fast:
        x_bit = bit_of("ctx", 1)
        got_gu, got_do = swap(send_gu, "ctx", 0), swap(send_do, "ctx", 0)
        gu, do = plus(keep_gu, got_gu), plus(keep_do, got_do)
        gu = gu.reshape((2, 2, 4) + gu.shape[2:]).swapaxes(0, 1)
        keep_gu, send_gu = pick(gu, x_bit), pick(gu, 1 - x_bit)
        keep_do, send_do = pick(do, rank), pick(do, 1 - rank)
        send_gu, send_do, row_dot = pin(send_gu, send_do, row_dot)
        part = functools.partial(attn_bwd, bias, query, kv_all, d_att, log_total, row_dot)
        got_gu, got_do = swap(send_gu, "ctx", 1), swap(send_do, "fsdp", 0)
        dq_a, before = part(*spans[0])
        got_gu, got_do, mixed_out, before = pin(got_gu, got_do, mixed_out, before)
        gu, do = plus(keep_gu, got_gu), plus(keep_do, got_do)
        do = do.reshape((2, 4) + do.shape[1:])
        keep_gu, send_gu = pick(gu, rank), pick(gu, 1 - rank)
        keep_do, send_do = pick(do, x_bit), pick(do, 1 - x_bit)
        send_gu, send_do, before = pin(send_gu, send_do, before)
        got_gu, got_do = swap(send_gu, "fsdp", 0), swap(send_do, "ctx", 1)
        dq_b, d_kv, d_kv_low = part(*spans[1], before=before, last=True)
        got_gu, got_do, d_kv_low, dq_b = pin(got_gu, got_do, d_kv_low, dq_b)
        gu, do = plus(keep_gu, got_gu), plus(keep_do, got_do)
    else:
        dq_a, before = part(*spans[0])
        dq_b, d_kv, d_kv_low = part(*spans[1], before=before, last=True)
    if team == 2:
        own_kv, got_kv = d_kv[:1], swap(d_kv_low[1], "ctx", 0)
    else:
        own_kv = lax.psum_scatter(d_kv_low, "ctx", scatter_dimension=0, axis_index_groups=groups)
        own_kv, got_kv = own_kv.astype(F32)[None], jnp.zeros((2 * kv_width, rows), BF)
    if fast:
        z_gu, z_do = z_send(gu), z_send(do)
        send_pin = pin(own_kv, got_kv, *z_gu[1], *z_do[1])
        own_kv, got_kv = send_pin[:2]
        z_gu, z_do = (z_gu[0], send_pin[2:5]), (z_do[0], send_pin[5:])
        z_got = [z_pass(z_gu[1]), z_pass(z_do[1])]
    d_x, keep_t, send_t = back_qkv(
        flags, spans, (dq_a, dq_b), own_kv, got_kv, x, d_res, first, gains, cosine, sine, gain_sum
    )
    if fast:
        d_x, *got = pin(d_x, *z_got[0], *z_got[1])
        gu, do = z_total(z_gu[0], got[:3]), z_total(z_do[0], got[3:])
    grad_tokens = move(d_x)
    if fast:
        t = plus(keep_t, swap(send_t, "ctx", 0))
        t = plus(pick(t, rank), swap(pick(t, 1 - rank), "fsdp", 0))
        t = t.reshape((2, 4) + t.shape[1:])
        t = plus(pick(t, x_bit), swap(pick(t, 1 - x_bit), "ctx", 1))
        keep_t, send_t = z_send(t)
        t = z_total(keep_t, z_pass(send_t))

        def widen(piece):
            four = z_join(piece)
            across = swap(four, "ctx", 1)
            return four, across, swap(jnp.concatenate([four, across], axis=0), "ctx", 0)

        at = jnp.stack([core, x_bit, lax.axis_index("ctx") >> 2])
        own_gate, own_up, own_down, own_out = final_ffn(at, *widen(gu), *widen(do), width // 2, ff, width)
        own_query, own_key, own_value, own_gains = final_t(at, *widen(t), width // 2, width, kv_width)
    else:
        pair = jnp.stack([keep_gu, send_gu])
        gate, up = (jnp.concatenate([natural_gu(pair[c, y]) for y in range(2)], axis=0) for c in range(2))
        do = jnp.stack([keep_do, send_do], axis=1).reshape((32,) + keep_do.shape[2:])
        deep = ff // 32
        own_gate, own_up = other_sum(gate), other_sum(up)
        own_down = other_sum(do[:, :deep].reshape(ff, width))
        out = do[:, deep:].reshape((2, -1, width))[:, : width // 2]
        own_out = other_sum(out.reshape(width, width))
        pair = jnp.stack([keep_t, send_t])
        t = [jnp.concatenate([natural_gu(pair[c, y]) for c in range(2)], axis=1) for y in range(2)]
        own_t = other_sum(jnp.concatenate(t, axis=0))
        own_query, own_key = own_t[:, :width], own_t[:, width : width + kv_width]
        own_value, own_gains = own_t[:, width + kv_width : qkv_cols], own_t[:, qkv_cols:].T
    return (
        mixed_out.reshape(tokens.shape),
        grad_tokens.reshape(tokens.shape),
        own_gains[0],
        own_query,
        own_key,
        own_value,
        own_out,
        own_gains[1],
        own_gate,
        own_up,
        own_down,
    )


def solution(mesh):
    rows, flat, seq = P("fsdp", None), P("fsdp"), P("fsdp", "ctx", None)
    return jax.shard_map(
        local,
        mesh=mesh,
        in_specs=(seq, flat, rows, rows, rows, rows, flat, rows, rows, rows, seq),
        out_specs=(seq, seq, flat, rows, rows, rows, rows, flat, rows, rows, rows),
        check_vma=False,
    )
```

```python
import functools

import jax
import jax.numpy as jnp
from jax import lax
from jax.experimental import pallas as pl
from jax.experimental.pallas import tpu as pltpu
from jax.sharding import PartitionSpec as P

HEADS = 9
KV_HEADS = 3
HEAD_DIM = 64
EPSILON = 1e-05
THETA = 100000.0
NEGATIVE = -1e30
LOG2E = 1.4426950408889634
LN2 = 0.6931471805599453
F32=jnp.float32; BF=jnp.bfloat16
NT=(((1,),(1,)),((),()))
NN=(((1,),(0,)),((),()))
def mm(a,b,dims=NN):
    return lax.dot_general(a,b,dims,preferred_element_type=F32)

def heads_of(ref, kv, group):
    return jnp.concatenate([ref[(kv*group+h)*64:(kv*group+h+1)*64,:] for h in range(group)],axis=1)

def fwd_kernel(bias_ref, q_ref, *refs, kvs, group, slots, rows, qb):
    kv_ref, (o_ref, lse_ref, k_scr, m_scr, acc_scr)=refs[:slots], refs[slots:]
    i=pl.program_id(0)
    kw=kvs*64
    @pl.when(i==0)
    def _():
        for s in range(slots):
            for h in range(kvs):
                k_scr[h,s]=kv_ref[s][h*64:(h+1)*64,:].T
    qs=[heads_of(q_ref,h,group) for h in range(kvs)]
    width=group*qb
    m_scr[...]=jnp.full(m_scr.shape,-1e30,F32)
    acc_scr[...]=jnp.zeros(acc_scr.shape,F32)
    ones=jnp.ones((8,slots*qb),BF)
    def chunk(c, masked):
        off=pl.multiple_of(c*qb,qb)
        for h in range(kvs):
            k=jnp.concatenate([k_scr[h,s,pl.ds(off,qb),:] for s in range(slots)],axis=0)
            v=jnp.concatenate([kv_ref[s][kw+h*64:kw+(h+1)*64,pl.ds(off,qb)] for s in range(slots)],axis=1)
            v=jnp.concatenate([v,ones],axis=0)
            st=mm(k,qs[h])
            if masked:
                b=bias_ref[...].reshape(slots*qb,qb)
                st=st+jnp.concatenate([b]*group,axis=1)
            m_old=m_scr[h:h+1,:]
            m_new=jnp.maximum(m_old,jnp.max(st,axis=0,keepdims=True))
            p=jnp.exp2(st-m_new).astype(BF)
            acc_scr[h]=acc_scr[h]*jnp.exp2(m_old-m_new)+mm(v,p)
            m_scr[h:h+1,:]=m_new
    def body(c,_):
        chunk(c,False); return 0
    lax.fori_loop(0,i,body,0)
    chunk(i,True)
    for h in range(kvs):
        acc=acc_scr[h]
        tot=acc[64:65,:]
        o=acc[:64,:]*(1.0/tot)
        lse=m_scr[h:h+1,:]+jnp.log2(tot)
        for g in range(group):
            r=h*group+g
            o_ref[r*64:(r+1)*64,:]=o[:,g*qb:(g+1)*qb]
            lse_ref[r:r+1,:]=lse[:,g*qb:(g+1)*qb]

def attn_fwd(bias, qT, kvT, kvs=3, group=3, qb=256):
    slots,rows=len(kvT),kvT[0].shape[1]
    n=rows//qb
    heads=kvs*group
    return pl.pallas_call(
        functools.partial(fwd_kernel,kvs=kvs,group=group,slots=slots,rows=rows,qb=qb),
        grid=(n,),
        in_specs=[pl.BlockSpec((slots,qb,qb),lambda i:(0,0,0)),
                  pl.BlockSpec((heads*64,qb),lambda i:(0,i)),
                  *[pl.BlockSpec((2*kvs*64,rows),lambda i:(0,0))]*slots],
        out_specs=[pl.BlockSpec((heads*64,qb),lambda i:(0,i)),
                   pl.BlockSpec((16,qb),lambda i:(0,i))],
        out_shape=[jax.ShapeDtypeStruct((heads*64,rows),F32),jax.ShapeDtypeStruct((16,rows),F32)],
        scratch_shapes=[pltpu.VMEM((kvs,slots,rows,64),BF),pltpu.VMEM((8,group*qb),F32),
                        pltpu.VMEM((kvs,72,group*qb),F32)],
        compiler_params=pltpu.CompilerParams(vmem_limit_bytes=56*2**20),
        cost_estimate=pl.CostEstimate(flops=int(25e9),bytes_accessed=int(8e6),transcendentals=int(1e7)),
    )(bias,qT,*kvT)

def bwd_kernel(*refs, kvs, group, slots, qb, lo, first, last):
    bias_ref, q_ref, do_ref, lse_ref, rd_ref = refs[:5]
    kv_ref, refs = refs[5 : 5 + slots], refs[5 + slots :]
    if not first:
        before_ref, refs = refs[0], refs[1:]
    if last:
        dq_ref, dkv_ref, low_ref, kv_scr = refs
    else:
        dq_ref, dkv_ref, kv_scr = refs
    step = pl.program_id(0)
    kw = kvs * 64

    @pl.when(step == 0)
    def _():
        for s in range(slots):
            for h in range(2 * kvs):
                kv_scr[h, s] = kv_ref[s][h * 64 : (h + 1) * 64, :].T
        dkv_ref[...] = jnp.zeros(dkv_ref.shape, F32) if first else before_ref[...]

    dq_ref[...] = jnp.zeros(dq_ref.shape, F32)
    qs = [heads_of(q_ref, h, group) for h in range(kvs)]
    dos = [heads_of(do_ref, h, group) for h in range(kvs)]

    def along(ref, h):
        return jnp.concatenate([ref[h * group + g : h * group + g + 1, :] for g in range(group)], axis=1)

    lses = [along(lse_ref, h) for h in range(kvs)]
    rds = [along(rd_ref, h) for h in range(kvs)]

    def chunk(c, masked):
        off = pl.multiple_of(c * qb, qb)
        for h in range(kvs):
            k = jnp.concatenate([kv_scr[h, s, pl.ds(off, qb), :] for s in range(slots)], axis=0)
            v = jnp.concatenate([kv_scr[kvs + h, s, pl.ds(off, qb), :] for s in range(slots)], axis=0)
            k_t = jnp.concatenate([kv_ref[s][h * 64 : (h + 1) * 64, pl.ds(off, qb)] for s in range(slots)], axis=1)
            st = mm(k, qs[h])
            if masked:
                st = st + jnp.concatenate([bias_ref[...].reshape(slots * qb, qb)] * group, axis=1)
            p = jnp.exp2(st - lses[h])
            dp = mm(v, dos[h])
            ds = (p * (dp - rds[h])).astype(BF)
            dk = mm(qs[h], ds, NT)
            dv = mm(dos[h], p.astype(BF), NT)
            dq = mm(k_t, ds)
            for s in range(slots):
                dkv_ref[s, h * 64 : (h + 1) * 64, pl.ds(off, qb)] += dk[:, s * qb : (s + 1) * qb]
                dkv_ref[s, kw + h * 64 : kw + (h + 1) * 64, pl.ds(off, qb)] += dv[:, s * qb : (s + 1) * qb]
            for g in range(group):
                r = h * group + g
                dq_ref[r * 64 : (r + 1) * 64, :] += dq[:, g * qb : (g + 1) * qb]

    def body(c, carry):
        chunk(c, False)
        return carry

    lax.fori_loop(0, step + lo, body, 0)
    chunk(step + lo, True)
    if last:

        @pl.when(step == pl.num_programs(0) - 1)
        def _():
            low_ref[...] = dkv_ref[...].astype(BF)


def attn_bwd(bias, q_t, kv_t, do_t, lse, rd, lo, hi, before=None, last=False, kvs=3, group=3, qb=256):
    slots, rows = len(kv_t), kv_t[0].shape[1]
    width = kvs * group * 64
    whole = pl.BlockSpec((slots, 2 * kvs * 64, rows), lambda i: (0, 0, 0))
    tall = pl.BlockSpec((width, qb), lambda i: (0, i + lo))
    stat = pl.BlockSpec((16, qb), lambda i: (0, i + lo))
    out_specs = [pl.BlockSpec((width, qb), lambda i: (0, i)), whole]
    out_shape = [
        jax.ShapeDtypeStruct((width, (hi - lo) * qb), F32),
        jax.ShapeDtypeStruct((slots, 2 * kvs * 64, rows), F32),
    ]
    if last:
        out_specs.append(whole)
        out_shape.append(jax.ShapeDtypeStruct((slots, 2 * kvs * 64, rows), BF))
    args = (bias, q_t, do_t, lse, rd, *kv_t) + (() if before is None else (before,))
    units = sum(range(lo + 1, hi + 1))
    return pl.pallas_call(
        functools.partial(
            bwd_kernel, kvs=kvs, group=group, slots=slots, qb=qb, lo=lo, first=before is None, last=last
        ),
        grid=(hi - lo,),
        in_specs=[pl.BlockSpec((slots, qb, qb), lambda i: (0, 0, 0)), tall, tall, stat, stat]
        + [pl.BlockSpec((2 * kvs * 64, rows), lambda i: (0, 0))] * slots
        + ([] if before is None else [whole]),
        out_specs=out_specs,
        out_shape=out_shape,
        scratch_shapes=[pltpu.VMEM((2 * kvs, slots, rows, 64), BF)],
        compiler_params=pltpu.CompilerParams(vmem_limit_bytes=60 * 2**20),
        cost_estimate=pl.CostEstimate(flops=int(4e9) * units, bytes_accessed=int(16e6), transcendentals=0),
    )(*args)


TN = (((0,), (0,)), ((), ()))
TT = (((0,), (1,)), ((), ()))
BLOCK = 256
PIECES = 8
LIMIT = 60 * 2**20


def rotated(values, cosine, sine):
    a, b = values[:32], values[32:]
    return jnp.concatenate([a * cosine - b * sine, b * cosine + a * sine], axis=0)


def flat_rows(ref):
    count, sub, width = ref.shape
    return ref[...].reshape(count * sub, width)


def rms(values):
    return lax.rsqrt(jnp.mean(values * values, axis=-1, keepdims=True) + EPSILON)


def qkv_kernel(x_ref, w_ref, gain_ref, cos_ref, sin_ref, q_ref, kv_ref, wt_scr):
    @pl.when(pl.program_id(0) == 0)
    def _():
        wt_scr[...] = w_ref[:, : wt_scr.shape[0]].T

    source = flat_rows(x_ref).astype(F32)
    hidden = (source * rms(source) * gain_ref[0:1, :]).astype(BF)
    out = mm(wt_scr[...], hidden, NT)
    cosine, sine = cos_ref[...], sin_ref[...]
    for h in range(HEADS):
        part = rotated(out[h * 64 : (h + 1) * 64], cosine, sine)
        q_ref[h * 64 : (h + 1) * 64, :] = (part * (HEAD_DIM**-0.5 * LOG2E)).astype(BF)
    top = HEADS * 64
    for h in range(KV_HEADS):
        part = rotated(out[top + h * 64 : top + (h + 1) * 64], cosine, sine)
        kv_ref[h * 64 : (h + 1) * 64, :] = part.astype(BF)
    kv_ref[KV_HEADS * 64 :, :] = out[top + KV_HEADS * 64 :].astype(BF)


def project_qkv(x, first, gains, cosine, sine):
    count, sub, width = x.shape
    rows = count * sub
    per = BLOCK // sub
    kv2 = 2 * KV_HEADS * HEAD_DIM
    return pl.pallas_call(
        qkv_kernel,
        grid=(rows // BLOCK,),
        in_specs=[
            pl.BlockSpec((per, sub, width), lambda i: (i, 0, 0)),
            pl.BlockSpec(first.shape, lambda i: (0, 0)),
            pl.BlockSpec(gains.shape, lambda i: (0, 0)),
            pl.BlockSpec((32, BLOCK), lambda i: (0, i)),
            pl.BlockSpec((32, BLOCK), lambda i: (0, i)),
        ],
        out_specs=[pl.BlockSpec((width, BLOCK), lambda i: (0, i)), pl.BlockSpec((kv2, BLOCK), lambda i: (0, i))],
        out_shape=[jax.ShapeDtypeStruct((width, rows), BF), jax.ShapeDtypeStruct((kv2, rows), BF)],
        scratch_shapes=[pltpu.VMEM((width + kv2, width), BF)],
        compiler_params=pltpu.CompilerParams(vmem_limit_bytes=LIMIT),
        cost_estimate=pl.CostEstimate(flops=int(6e9), bytes_accessed=int(5e6), transcendentals=0),
    )(x, first, gains, cosine, sine)


def ffn_kernel(
    place_ref, o_ref, x_ref, cot_ref, first_ref, gain_ref,
    gate_own, gate_got, gate_swap, up_own, up_got, up_swap, down_own, down_got, down_swap,
    mixed_ref, dres_ref, datt_ref, rd_ref, keep_gu, send_gu, keep_do, send_do, gg_ref,
    acc_gu, acc_down, acc_out, gate_ref, up_ref, down_ref,
):
    step = pl.program_id(0)
    width = x_ref.shape[2]

    @pl.when(step == 0)
    def _():
        acc_gu[...] = jnp.zeros(acc_gu.shape, F32)
        acc_down[...] = jnp.zeros(acc_down.shape, F32)
        acc_out[...] = jnp.zeros(acc_out.shape, F32)
        gg_ref[...] = jnp.zeros(gg_ref.shape, F32)
        for rank in range(2):

            @pl.when(place_ref[1] == rank)
            def _():
                for ref, own in ((gate_ref, gate_own), (up_ref, up_own), (down_ref, down_own)):
                    n = own.shape[0]
                    ref[rank * n : (rank + 1) * n] = own[...]
                for core in range(2):

                    @pl.when(place_ref[0] == core)
                    def _():
                        for ref, parts in ((gate_ref, (gate_got, gate_swap)), (up_ref, (up_got, up_swap))):
                            n, m = parts[0].shape
                            for k, part in ((core, parts[0]), (1 - core, parts[1])):
                                ref[(1 - rank) * n : (2 - rank) * n, k * m : (k + 1) * m] = part[...]
                        n = down_got.shape[0]
                        for k, part in ((core, down_got), (1 - core, down_swap)):
                            low = (2 * (1 - rank) + k) * n
                            down_ref[low : low + n] = part[...]

    cols = first_ref.shape[1]
    out_w = first_ref[:, cols - width :]
    attended = o_ref[...]
    mixed = attended.astype(BF)
    residual = flat_rows(x_ref).astype(F32) + mm(mixed, out_w, TN)
    scale = rms(residual)
    normed = residual * scale
    gain = gain_ref[1:2, :]
    hidden = (normed * gain).astype(BF)
    gate = mm(hidden, gate_ref[...])
    up = mm(hidden, up_ref[...])
    sig = 0.5 * jnp.tanh(0.5 * gate) + 0.5
    silu = gate * sig
    activated = (silu * up).astype(BF)
    mixed_out = (residual + mm(activated, down_ref[...])).astype(BF)
    mixed_ref[...] = mixed_out.reshape(mixed_ref.shape)
    cot = flat_rows(cot_ref)
    d_act = mm(cot, down_ref[...], NT)
    acc_down[...] += mm(activated, cot, TN)
    d_gate = (d_act * up * sig * (1.0 + gate * (1.0 - sig))).astype(BF)
    d_up = (d_act * silu).astype(BF)
    acc_gu[0] += mm(hidden, d_gate, TN)
    acc_gu[1] += mm(hidden, d_up, TN)
    d_hidden = mm(d_gate, gate_ref[...], NT) + mm(d_up, up_ref[...], NT)
    dn = d_hidden * normed
    gg_ref[...] += jnp.sum(dn.reshape(-1, 8, width), axis=0)
    inner = jnp.mean(dn * gain, axis=-1, keepdims=True)
    d_res = cot.astype(F32) + scale * (d_hidden * gain - normed * inner)
    dres_ref[...] = d_res
    d_low = d_res.astype(BF)
    acc_out[...] += mm(mixed, d_low)
    d_att = mm(out_w, d_low, NT).astype(BF)
    datt_ref[...] = d_att
    prod = d_att.astype(F32) * attended
    for h in range(HEADS):
        rd_ref[h : h + 1, :] = jnp.sum(prod[h * 64 : (h + 1) * 64], axis=0, keepdims=True)
    rd_ref[HEADS:, :] = jnp.zeros((16 - HEADS, rd_ref.shape[1]), F32)

    @pl.when(step == pl.num_programs(0) - 1)
    def _():
        core = place_ref[0]
        half = width // 2
        ff = acc_gu.shape[2]
        for y in range(2):
            for p in range(PIECES):
                rs = slice(y * half + (p // 4) * (half // 2), y * half + (p // 4 + 1) * (half // 2))
                cs = slice((p % 4) * (ff // 4), (p % 4 + 1) * (ff // 4))
                keep_gu[y, p] = acc_gu[core, rs, cs].astype(BF)
                send_gu[y, p] = acc_gu[1 - core, rs, cs].astype(BF)
        down_rows, out_rows = ff // 32, width // 24
        for y in range(2):
            for p in range(PIECES):
                for ref, c in ((keep_do, core), (send_do, 1 - core)):
                    start = pl.multiple_of(y * (ff // 2) + (PIECES * c + p) * down_rows, 16)
                    ref[y, p, :down_rows] = acc_down[pl.ds(start, down_rows), :].astype(BF)
                    start = y * half + jnp.minimum(PIECES * c + p, half // out_rows - 1) * out_rows
                    ref[y, p, down_rows:] = acc_out[pl.ds(pl.multiple_of(start, 8), out_rows), :].astype(BF)


def feed_forward(place, attended, x, cot, first, gains, weights):
    count, sub, width = x.shape
    rows, ff = count * sub, weights[0].shape[1]
    per = BLOCK // sub
    gu = (2, PIECES, width // 4, ff // 4)
    do = (2, PIECES, ff // 32 + width // 24, width)

    def whole(shape):
        return pl.BlockSpec(shape, lambda i: (0,) * len(shape))

    seq = pl.BlockSpec((per, sub, width), lambda i: (i, 0, 0))
    tall = pl.BlockSpec((width, BLOCK), lambda i: (0, i))
    return pl.pallas_call(
        ffn_kernel,
        grid=(rows // BLOCK,),
        in_specs=[
            pl.BlockSpec(memory_space=pltpu.SMEM), tall, seq, seq,
            whole(first.shape), whole(gains.shape), *(whole(w.shape) for w in weights),
        ],
        out_specs=[
            seq, pl.BlockSpec((BLOCK, width), lambda i: (i, 0)), tall, pl.BlockSpec((16, BLOCK), lambda i: (0, i)),
            whole(gu), whole(gu), whole(do), whole(do), whole((8, width)),
        ],
        out_shape=[
            jax.ShapeDtypeStruct(x.shape, BF),
            jax.ShapeDtypeStruct((rows, width), F32),
            jax.ShapeDtypeStruct((width, rows), BF),
            jax.ShapeDtypeStruct((16, rows), F32),
            jax.ShapeDtypeStruct(gu, BF), jax.ShapeDtypeStruct(gu, BF),
            jax.ShapeDtypeStruct(do, BF), jax.ShapeDtypeStruct(do, BF),
            jax.ShapeDtypeStruct((8, width), F32),
        ],
        scratch_shapes=[
            pltpu.VMEM((2, width, ff), F32), pltpu.VMEM((ff, width), F32), pltpu.VMEM((width, width), F32),
            pltpu.VMEM((width, ff), BF), pltpu.VMEM((width, ff), BF), pltpu.VMEM((ff, width), BF),
        ],
        compiler_params=pltpu.CompilerParams(vmem_limit_bytes=LIMIT),
        cost_estimate=pl.CostEstimate(flops=int(32e9), bytes_accessed=int(20e6), transcendentals=0),
    )(place, attended, x, cot, first, gains, *weights)


def back_kernel(*refs, spans):
    place_ref, refs = refs[0], refs[1:]
    dq_refs, refs = refs[: len(spans)], refs[len(spans) :]
    own_ref, got_ref, x_ref, dres_ref, first_ref, gain_ref, cos_ref, sin_ref, gg_ref, dx_ref = refs[:10]
    keep_ref, send_ref, acc, dt_scr, ga_scr, w_scr = refs[10:]
    step = pl.program_id(0)
    width = x_ref.shape[2]
    kv = KV_HEADS * 64
    total = width + 2 * kv

    @pl.when(step == 0)
    def _():
        acc[...] = jnp.zeros(acc.shape, F32)
        ga_scr[...] = jnp.zeros(ga_scr.shape, F32)
        w_scr[...] = first_ref[:, :total].T

    cosine, sine = cos_ref[...], -sin_ref[...]
    for (lo, hi), dq_ref in zip(spans, dq_refs):

        @pl.when((step >= lo) & (step < hi))
        def _():
            for h in range(HEADS):
                part = dq_ref[h * 64 : (h + 1) * 64, :] * (HEAD_DIM**-0.5)
                dt_scr[h * 64 : (h + 1) * 64, :] = rotated(part, cosine, sine).astype(BF)

    d_kv = own_ref[0] + got_ref[...].astype(F32)
    for h in range(KV_HEADS):
        part = d_kv[h * 64 : (h + 1) * 64] * LN2
        dt_scr[width + h * 64 : width + (h + 1) * 64, :] = rotated(part, cosine, sine).astype(BF)
    dt_scr[width + kv :, :] = d_kv[kv:].astype(BF)
    d_t = dt_scr[...]
    source = flat_rows(x_ref).astype(F32)
    scale = rms(source)
    normed = source * scale
    gain = gain_ref[0:1, :]
    hidden = (normed * gain).astype(BF)
    acc[:total] += mm(d_t, hidden)
    d_hidden = mm(d_t, w_scr[...], TN)
    dn = d_hidden * normed
    ga_scr[...] += jnp.sum(dn.reshape(-1, 8, width), axis=0)
    inner = jnp.mean(dn * gain, axis=-1, keepdims=True)
    grad = dres_ref[...] + scale * (d_hidden * gain - normed * inner)
    dx_ref[...] = grad.astype(BF).reshape(dx_ref.shape)

    @pl.when(step == pl.num_programs(0) - 1)
    def _():
        core = place_ref[0]
        acc[total : total + 1, :] = jnp.sum(ga_scr[...], axis=0, keepdims=True)
        acc[total + 1 : total + 2, :] = jnp.sum(gg_ref[...], axis=0, keepdims=True)
        half, deep = width // 2, width // 4
        for ct in range(4):
            for ref, c in ((keep_ref, core), (send_ref, 1 - core)):
                start = pl.multiple_of(c * 512 + ct * 128, 128)
                block = acc[pl.ds(start, 128), :].T.astype(BF)
                for y in range(2):
                    for rh in range(2):
                        low = y * half + rh * deep
                        ref[y, rh * 4 + ct] = block[low : low + deep]


def back_qkv(place, spans, d_query, d_kv, got, x, d_res, first, gains, cosine, sine, gg):
    count, sub, width = x.shape
    rows = count * sub
    per = BLOCK // sub
    kv2 = 2 * KV_HEADS * HEAD_DIM
    piece = (2, PIECES, width // 4, 128)

    def whole(shape):
        return pl.BlockSpec(shape, lambda i: (0,) * len(shape))

    seq = pl.BlockSpec((per, sub, width), lambda i: (i, 0, 0))
    return pl.pallas_call(
        functools.partial(back_kernel, spans=spans),
        grid=(rows // BLOCK,),
        in_specs=[
            pl.BlockSpec(memory_space=pltpu.SMEM),
            *(
                pl.BlockSpec((width, BLOCK), lambda i, lo=lo, hi=hi: (0, jnp.clip(i - lo, 0, hi - lo - 1)))
                for lo, hi in spans
            ),
            pl.BlockSpec((1, kv2, BLOCK), lambda i: (0, 0, i)),
            pl.BlockSpec((kv2, BLOCK), lambda i: (0, i)),
            seq, pl.BlockSpec((BLOCK, width), lambda i: (i, 0)),
            whole(first.shape), whole(gains.shape),
            pl.BlockSpec((32, BLOCK), lambda i: (0, i)), pl.BlockSpec((32, BLOCK), lambda i: (0, i)),
            whole(gg.shape),
        ],
        out_specs=[seq, whole(piece), whole(piece)],
        out_shape=[jax.ShapeDtypeStruct(x.shape, BF), jax.ShapeDtypeStruct(piece, BF), jax.ShapeDtypeStruct(piece, BF)],
        scratch_shapes=[
            pltpu.VMEM((1024, width), F32), pltpu.VMEM((width + kv2, BLOCK), BF), pltpu.VMEM((8, width), F32),
            pltpu.VMEM((width + kv2, width), BF),
        ],
        compiler_params=pltpu.CompilerParams(vmem_limit_bytes=LIMIT),
        cost_estimate=pl.CostEstimate(flops=int(10e9), bytes_accessed=int(10e6), transcendentals=0),
    )(place, *d_query, d_kv, got, x, d_res, first, gains, cosine, sine, gg)


def final_kernel(
    at_ref, gu4, gu_x, gu_c, do4, do_x, do_c, gate_ref, up_ref, down_ref, out_ref
):
    core, xb, z = at_ref[0], at_ref[1], at_ref[2]
    deep, wide = gu4.shape[1:]
    for f in range(2):
        for e in range(2):
            for d in range(4):
                gu = (gu4[d] if e == 0 else gu_x[d]) if f == 0 else gu_c[e * 4 + d]
                do = (do4[d] if e == 0 else do_x[d]) if f == 0 else do_c[e * 4 + d]
                rs = pl.ds(pl.multiple_of((xb ^ e) * deep, 16), deep)
                cs = pl.ds(pl.multiple_of((z ^ d) * wide, 128), wide)
                for c, ref in ((0, gate_ref), (1, up_ref)):

                    @pl.when((core ^ f) == c)
                    def _():
                        ref[rs, cs] = gu.astype(F32)

                m = (core ^ f) * 8 + (xb ^ e) * 4 + (z ^ d)
                rows = down_ref.shape[0] // 16
                down_ref[pl.ds(pl.multiple_of(m * rows, 8), rows), :] = do[:rows].astype(F32)
                few = do.shape[0] - rows

                @pl.when(m < out_ref.shape[0] // few)
                def _():
                    out_ref[pl.ds(pl.multiple_of(m * few, 8), few), :] = do[rows:].astype(F32)


def final_ffn(at, gu4, gu_x, gu_c, do4, do_x, do_c, half, ff, width):
    f32 = lambda *s: jax.ShapeDtypeStruct(s, F32)
    return pl.pallas_call(
        final_kernel,
        in_specs=[pl.BlockSpec(memory_space=pltpu.SMEM)] + [pl.BlockSpec(memory_space=pltpu.VMEM)] * 6,
        out_specs=[pl.BlockSpec(memory_space=pltpu.VMEM)] * 4,
        out_shape=[f32(half, ff), f32(half, ff), f32(ff // 2, width), f32(half, width)],
        compiler_params=pltpu.CompilerParams(vmem_limit_bytes=LIMIT),
        cost_estimate=pl.CostEstimate(flops=int(5e9), bytes_accessed=int(10e6), transcendentals=0),
    )(at, gu4, gu_x, gu_c, do4, do_x, do_c)


def final_t_kernel(at_ref, t4, t_x, t_c, q_ref, k_ref, v_ref, g_ref, whole):
    core, xb, z = at_ref[0], at_ref[1], at_ref[2]
    deep, wide = t4.shape[1:]
    for f in range(2):
        for e in range(2):
            for d in range(4):
                t = (t4[d] if e == 0 else t_x[d]) if f == 0 else t_c[e * 4 + d]
                rs = pl.ds(pl.multiple_of((xb ^ e) * deep, 16), deep)
                cs = pl.ds(pl.multiple_of((core ^ f) * 512 + (z ^ d) * wide, 128), wide)
                whole[rs, cs] = t.astype(F32)
    a = q_ref.shape[1]
    b = a + k_ref.shape[1]
    c = b + v_ref.shape[1]
    q_ref[...] = whole[:, :a]
    k_ref[...] = whole[:, a:b]
    v_ref[...] = whole[:, b:c]
    g_ref[...] = whole[:, c:].T[:8]


def final_t(at, t4, t_x, t_c, half, width, kv_width):
    f32 = lambda *s: jax.ShapeDtypeStruct(s, F32)
    return pl.pallas_call(
        final_t_kernel,
        in_specs=[pl.BlockSpec(memory_space=pltpu.SMEM)] + [pl.BlockSpec(memory_space=pltpu.VMEM)] * 3,
        out_specs=[pl.BlockSpec(memory_space=pltpu.VMEM)] * 4,
        out_shape=[f32(half, width), f32(half, kv_width), f32(half, kv_width), f32(8, half)],
        scratch_shapes=[pltpu.VMEM((half, 1024), F32)],
        compiler_params=pltpu.CompilerParams(vmem_limit_bytes=LIMIT),
        cost_estimate=pl.CostEstimate(flops=int(1e9), bytes_accessed=int(2e6), transcendentals=0),
    )(at, t4, t_x, t_c)


def swap(x, axis, bit):
    n = lax.axis_size(axis)
    return lax.ppermute(x, axis, [(i, i ^ (1 << bit)) for i in range(n)])


def bit_of(axis, bit):
    return (lax.axis_index(axis) >> bit) & 1


def pin(*arrays):
    return lax.optimization_barrier(arrays)


def pick(x, at):
    return lax.dynamic_index_in_dim(x, at, 0, keepdims=False)


def in_order(flag, mine, other, axis):
    return jnp.where(
        flag == 0,
        jnp.concatenate([mine, other], axis=axis),
        jnp.concatenate([other, mine], axis=axis),
    )


def plus(a, b):
    return (a.astype(F32) + b.astype(F32)).astype(BF)


def two_level():
    return lax.axis_size("fsdp") == 2 and lax.axis_size("ctx") == 16


def z_swap(x, by):
    return lax.ppermute(x, "ctx", [(i, i ^ (4 * by)) for i in range(16)])


def z_send(x):
    z = lax.axis_index("ctx") >> 2
    return pick(x, z), [pick(x, z ^ by) for by in range(1, 4)]


def z_pass(pieces):
    return [z_swap(p, by) for by, p in zip(range(1, 4), pieces)]


def z_total(mine, got):
    return sum((g.astype(F32) for g in got), mine.astype(F32)).astype(BF)


def z_join(piece):
    return [piece] + [z_swap(piece, by) for by in range(1, 4)]


def natural_gu(pieces):
    _, a, b = pieces.shape
    return pieces.reshape(2, 4, a, b).transpose(0, 2, 1, 3).reshape(2 * a, 4 * b).astype(F32)


def other_sum(x):
    x = lax.psum_scatter(x.astype(BF), "fsdp", scatter_dimension=0, tiled=True)
    return lax.psum(x, "ctx").astype(F32)


def local(tokens, gain_attn, w_query, w_key, w_value, w_out, gain_ffn, w_gate, w_up, w_down, cotangent):
    seqs, length, width = tokens.shape
    count = lax.axis_size("ctx")
    team = count // seqs
    sub = length // team
    rows = count * sub
    ff = w_gate.shape[1]
    kv_width = KV_HEADS * HEAD_DIM
    qkv_cols = width + 2 * kv_width
    place = lax.axis_index("ctx") % team
    own = gain_attn.shape[0]
    fast = two_level()

    def move(x):
        return lax.all_to_all(x.reshape(count, sub, width), "ctx", 0, 0, tiled=True)

    x = move(tokens)
    gain_rows = jnp.zeros((8, ff), BF).at[0, :own].set(gain_attn).at[1, :own].set(gain_ffn)
    first = jnp.concatenate([jnp.concatenate([w_query, w_key, w_value, w_out], axis=1), gain_rows], axis=0)
    if fast:
        core, rank = bit_of("ctx", 0), bit_of("fsdp", 0)

        def halved(shard, axis):
            half = shard.shape[axis] // 2
            return lax.dynamic_slice_in_dim(shard, core * half, half, axis)

        def other_shard(got, axis):
            return in_order(core, got, swap(got, "ctx", 0), axis)

        got = swap(halved(first, 1), "fsdp", 0)
        other = other_shard(got, 1)
        gains = in_order(rank, first[own : own + 2, :own], other[own : own + 2, :own], 1).astype(F32)
        first = in_order(rank, first[:own], other[:own], 0)
        gate_half, up_half, down_half, got = pin(halved(w_gate, 1), halved(w_up, 1), halved(w_down, 0), got)
        gate_got, up_got, down_got = (swap(h, "fsdp", 0) for h in (gate_half, up_half, down_half))
    else:
        first = lax.all_gather(first, "fsdp", axis=0)
        gains = first[:, own : own + 2, :own].transpose(1, 0, 2).reshape(2, width).astype(F32)
        first = first[:, :own].reshape(width, first.shape[2])
        gate_w, up_w, down_w = (lax.all_gather(w, "fsdp", axis=0, tiled=True) for w in (w_gate, w_up, w_down))
    gains = jnp.pad(gains, ((0, 6), (0, 0)))

    row = jnp.arange(rows, dtype=jnp.int32)
    position = (row // sub) * length + place * sub + row % sub
    frequency = THETA ** (-jnp.arange(HEAD_DIM // 2, dtype=F32) * 2.0 / HEAD_DIM)
    angles = frequency[:, None] * position.astype(F32)[None, :]
    cosine, sine = jnp.cos(angles), jnp.sin(angles)
    groups = [[t * team + p for p in range(team)] for t in range(seqs)]
    slots = jnp.stack([place, 1 - place]) if team == 2 else jnp.arange(team)
    block_row = jnp.arange(BLOCK, dtype=jnp.int32)
    base = (block_row // sub) * length + block_row % sub
    key_pos = base[None, :] + slots[:, None] * sub
    query_pos = base + place * sub
    bias = jnp.where(key_pos[:, :, None] <= query_pos[None, None, :], 0.0, NEGATIVE).astype(F32)
    flags = jnp.stack([core, rank]) if fast else jnp.zeros((2,), jnp.int32)

    x, cot_send = pin(x, cotangent)
    cot = move(cot_send)
    query, kv_own = project_qkv(x, first, gains, cosine, sine)
    if fast:
        kv_own, gate_got = pin(kv_own, gate_got)
    if team == 2:
        kv_all = (kv_own, swap(kv_own, "ctx", 0))
    else:
        kv_all = lax.all_gather(kv_own, "ctx", axis=0, axis_index_groups=groups)
        kv_all = tuple(kv_all[s] for s in range(team))
    attended, log_total = attn_fwd(bias, query, kv_all)
    if fast:
        attended, cot, *gots = pin(attended, cot, gate_got, up_got, down_got)
        gots = [(got, swap(got, "ctx", 0)) for got in gots]
        weights = [a for own_w, two in zip((w_gate, w_up, w_down), gots) for a in (own_w, *two)]
    else:
        attended, cot = pin(attended, cot)
        low, side = width // 2, ff // 2
        weights = [a for w in (gate_w, up_w) for a in (w[:low], w[low:, :side], w[low:, side:])]
        weights += [down_w[:side], down_w[side : side + side // 2], down_w[side + side // 2 :]]
    mixed, d_res, d_att, row_dot, keep_gu, send_gu, keep_do, send_do, gain_sum = feed_forward(
        flags, attended, x, cot, first, gains, weights
    )
    mixed_out = move(mixed)

    n = rows // BLOCK
    spans = ((0, n - 1), (n - 1, n))
    part = functools.partial(attn_bwd, bias, query, kv_all, d_att, log_total, row_dot)
    if fast:
        x_bit = bit_of("ctx", 1)
        got_gu, got_do = swap(send_gu, "ctx", 0), swap(send_do, "ctx", 0)
        gu, do = plus(keep_gu, got_gu), plus(keep_do, got_do)
        gu = gu.reshape((2, 2, 4) + gu.shape[2:]).swapaxes(0, 1)
        keep_gu, send_gu = pick(gu, x_bit), pick(gu, 1 - x_bit)
        keep_do, send_do = pick(do, rank), pick(do, 1 - rank)
        send_gu, send_do, row_dot = pin(send_gu, send_do, row_dot)
        part = functools.partial(attn_bwd, bias, query, kv_all, d_att, log_total, row_dot)
        got_gu, got_do = swap(send_gu, "ctx", 1), swap(send_do, "fsdp", 0)
        dq_a, before = part(*spans[0])
        got_gu, got_do, mixed_out, before = pin(got_gu, got_do, mixed_out, before)
        gu, do = plus(keep_gu, got_gu), plus(keep_do, got_do)
        do = do.reshape((2, 4) + do.shape[1:])
        keep_gu, send_gu = pick(gu, rank), pick(gu, 1 - rank)
        keep_do, send_do = pick(do, x_bit), pick(do, 1 - x_bit)
        send_gu, send_do, before = pin(send_gu, send_do, before)
        got_gu, got_do = swap(send_gu, "fsdp", 0), swap(send_do, "ctx", 1)
        dq_b, d_kv, d_kv_low = part(*spans[1], before=before, last=True)
        got_gu, got_do, d_kv_low, dq_b = pin(got_gu, got_do, d_kv_low, dq_b)
        gu, do = plus(keep_gu, got_gu), plus(keep_do, got_do)
    else:
        dq_a, before = part(*spans[0])
        dq_b, d_kv, d_kv_low = part(*spans[1], before=before, last=True)
    if team == 2:
        own_kv, got_kv = d_kv[:1], swap(d_kv_low[1], "ctx", 0)
    else:
        own_kv = lax.psum_scatter(d_kv_low, "ctx", scatter_dimension=0, axis_index_groups=groups)
        own_kv, got_kv = own_kv.astype(F32)[None], jnp.zeros((2 * kv_width, rows), BF)
    if fast:
        z_gu, z_do = z_send(gu), z_send(do)
        send_pin = pin(own_kv, got_kv, *z_gu[1], *z_do[1])
        own_kv, got_kv = send_pin[:2]
        z_gu, z_do = (z_gu[0], send_pin[2:5]), (z_do[0], send_pin[5:])
        z_got = [z_pass(z_gu[1]), z_pass(z_do[1])]
    d_x, keep_t, send_t = back_qkv(
        flags, spans, (dq_a, dq_b), own_kv, got_kv, x, d_res, first, gains, cosine, sine, gain_sum
    )
    if fast:
        d_x, *got = pin(d_x, *z_got[0], *z_got[1])
        gu, do = z_total(z_gu[0], got[:3]), z_total(z_do[0], got[3:])
    grad_tokens = move(d_x)
    if fast:
        gu_four, do_four = z_join(gu), z_join(do)
        t = plus(keep_t, swap(send_t, "ctx", 0))
        t = plus(pick(t, rank), swap(pick(t, 1 - rank), "fsdp", 0))
        t = t.reshape((2, 4) + t.shape[1:])
        t = plus(pick(t, x_bit), swap(pick(t, 1 - x_bit), "ctx", 1))
        keep_t, send_t = z_send(t)
        t_got = z_pass(send_t)
        *t_got, d0, d1, d2 = pin(*t_got, *do_four[1:])
        t_four = z_join(z_total(keep_t, t_got))
        do_four = jnp.stack([do_four[0], d0, d1, d2])
        do_x = swap(do_four, "ctx", 1)
        t0, t1, t2, g0, g1, g2 = pin(*t_four[1:], *gu_four[1:])
        gu_four = jnp.stack([gu_four[0], g0, g1, g2])
        gu_x = swap(gu_four, "ctx", 1)
        t_four = jnp.stack([t_four[0], t0, t1, t2])
        t_x = swap(t_four, "ctx", 1)
        t_x, do_x = pin(t_x, do_x)
        do_c = swap(jnp.concatenate([do_four, do_x], axis=0), "ctx", 0)
        t_c = swap(jnp.concatenate([t_four, t_x], axis=0), "ctx", 0)
        gu_x, t_c = pin(gu_x, t_c)
        gu_c = swap(jnp.concatenate([gu_four, gu_x], axis=0), "ctx", 0)
        at = jnp.stack([core, x_bit, lax.axis_index("ctx") >> 2])
        own_query, own_key, own_value, own_gains = final_t(at, t_four, t_x, t_c, width // 2, width, kv_width)
        own_gate, own_up, own_down, own_out = final_ffn(
            at, gu_four, gu_x, gu_c, do_four, do_x, do_c, width // 2, ff, width
        )
    else:
        pair = jnp.stack([keep_gu, send_gu])
        gate, up = (jnp.concatenate([natural_gu(pair[c, y]) for y in range(2)], axis=0) for c in range(2))
        do = jnp.stack([keep_do, send_do], axis=1).reshape((32,) + keep_do.shape[2:])
        deep = ff // 32
        own_gate, own_up = other_sum(gate), other_sum(up)
        own_down = other_sum(do[:, :deep].reshape(ff, width))
        out = do[:, deep:].reshape((2, -1, width))[:, : width // 2]
        own_out = other_sum(out.reshape(width, width))
        pair = jnp.stack([keep_t, send_t])
        t = [jnp.concatenate([natural_gu(pair[c, y]) for c in range(2)], axis=1) for y in range(2)]
        own_t = other_sum(jnp.concatenate(t, axis=0))
        own_query, own_key = own_t[:, :width], own_t[:, width : width + kv_width]
        own_value, own_gains = own_t[:, width + kv_width : qkv_cols], own_t[:, qkv_cols:].T
    return (
        mixed_out.reshape(tokens.shape),
        grad_tokens.reshape(tokens.shape),
        own_gains[0],
        own_query,
        own_key,
        own_value,
        own_out,
        own_gains[1],
        own_gate,
        own_up,
        own_down,
    )


def solution(mesh):
    rows, flat, seq = P("fsdp", None), P("fsdp"), P("fsdp", "ctx", None)
    return jax.shard_map(
        local,
        mesh=mesh,
        in_specs=(seq, flat, rows, rows, rows, rows, flat, rows, rows, rows, seq),
        out_specs=(seq, seq, flat, rows, rows, rows, rows, flat, rows, rows, rows),
        check_vma=False,
    )
```

```python
import functools

import jax
import jax.numpy as jnp
from jax import lax
from jax.experimental import pallas as pl
from jax.experimental.pallas import tpu as pltpu
from jax.sharding import PartitionSpec as P

HEADS = 9
KV_HEADS = 3
HEAD_DIM = 64
EPSILON = 1e-05
THETA = 100000.0
NEGATIVE = -1e30
LOG2E = 1.4426950408889634
LN2 = 0.6931471805599453
F32=jnp.float32; BF=jnp.bfloat16
NT=(((1,),(1,)),((),()))
NN=(((1,),(0,)),((),()))
def mm(a,b,dims=NN):
    return lax.dot_general(a,b,dims,preferred_element_type=F32)

def heads_of(ref, kv, group):
    return jnp.concatenate([ref[(kv*group+h)*64:(kv*group+h+1)*64,:] for h in range(group)],axis=1)

def fwd_kernel(bias_ref, q_ref, *refs, kvs, group, slots, rows, qb):
    kv_ref, (o_ref, lse_ref, k_scr, m_scr, acc_scr)=refs[:slots], refs[slots:]
    i=pl.program_id(0)
    kw=kvs*64
    @pl.when(i==0)
    def _():
        for s in range(slots):
            for h in range(kvs):
                k_scr[h,s]=kv_ref[s][h*64:(h+1)*64,:].T
    qs=[heads_of(q_ref,h,group) for h in range(kvs)]
    width=group*qb
    m_scr[...]=jnp.full(m_scr.shape,-1e30,F32)
    acc_scr[...]=jnp.zeros(acc_scr.shape,F32)
    ones=jnp.ones((8,slots*qb),BF)
    def chunk(c, masked):
        off=pl.multiple_of(c*qb,qb)
        for h in range(kvs):
            k=jnp.concatenate([k_scr[h,s,pl.ds(off,qb),:] for s in range(slots)],axis=0)
            v=jnp.concatenate([kv_ref[s][kw+h*64:kw+(h+1)*64,pl.ds(off,qb)] for s in range(slots)],axis=1)
            v=jnp.concatenate([v,ones],axis=0)
            st=mm(k,qs[h])
            if masked:
                b=bias_ref[...].reshape(slots*qb,qb)
                st=st+jnp.concatenate([b]*group,axis=1)
            m_old=m_scr[h:h+1,:]
            m_new=jnp.maximum(m_old,jnp.max(st,axis=0,keepdims=True))
            p=jnp.exp2(st-m_new).astype(BF)
            acc_scr[h]=acc_scr[h]*jnp.exp2(m_old-m_new)+mm(v,p)
            m_scr[h:h+1,:]=m_new
    def body(c,_):
        chunk(c,False); return 0
    lax.fori_loop(0,i,body,0)
    chunk(i,True)
    for h in range(kvs):
        acc=acc_scr[h]
        tot=acc[64:65,:]
        o=acc[:64,:]*(1.0/tot)
        lse=m_scr[h:h+1,:]+jnp.log2(tot)
        for g in range(group):
            r=h*group+g
            o_ref[r*64:(r+1)*64,:]=o[:,g*qb:(g+1)*qb]
            lse_ref[r:r+1,:]=lse[:,g*qb:(g+1)*qb]

def attn_fwd(bias, qT, kvT, kvs=3, group=3, qb=256):
    slots,rows=len(kvT),kvT[0].shape[1]
    n=rows//qb
    heads=kvs*group
    return pl.pallas_call(
        functools.partial(fwd_kernel,kvs=kvs,group=group,slots=slots,rows=rows,qb=qb),
        grid=(n,),
        in_specs=[pl.BlockSpec((slots,qb,qb),lambda i:(0,0,0)),
                  pl.BlockSpec((heads*64,qb),lambda i:(0,i)),
                  *[pl.BlockSpec((2*kvs*64,rows),lambda i:(0,0))]*slots],
        out_specs=[pl.BlockSpec((heads*64,qb),lambda i:(0,i)),
                   pl.BlockSpec((16,qb),lambda i:(0,i))],
        out_shape=[jax.ShapeDtypeStruct((heads*64,rows),F32),jax.ShapeDtypeStruct((16,rows),F32)],
        scratch_shapes=[pltpu.VMEM((kvs,slots,rows,64),BF),pltpu.VMEM((8,group*qb),F32),
                        pltpu.VMEM((kvs,72,group*qb),F32)],
        compiler_params=pltpu.CompilerParams(vmem_limit_bytes=56*2**20),
        cost_estimate=pl.CostEstimate(flops=int(25e9),bytes_accessed=int(8e6),transcendentals=int(1e7)),
    )(bias,qT,*kvT)

def bwd_kernel(*refs, kvs, group, slots, qb, lo, first, last):
    bias_ref, q_ref, do_ref, lse_ref, rd_ref = refs[:5]
    kv_ref, refs = refs[5 : 5 + slots], refs[5 + slots :]
    if not first:
        before_ref, refs = refs[0], refs[1:]
    if last:
        dq_ref, dkv_ref, low_ref, kv_scr = refs
    else:
        dq_ref, dkv_ref, kv_scr = refs
    step = pl.program_id(0)
    kw = kvs * 64

    @pl.when(step == 0)
    def _():
        for s in range(slots):
            for h in range(2 * kvs):
                kv_scr[h, s] = kv_ref[s][h * 64 : (h + 1) * 64, :].T
        dkv_ref[...] = jnp.zeros(dkv_ref.shape, F32) if first else before_ref[...]

    dq_ref[...] = jnp.zeros(dq_ref.shape, F32)
    qs = [heads_of(q_ref, h, group) for h in range(kvs)]
    dos = [heads_of(do_ref, h, group) for h in range(kvs)]

    def along(ref, h):
        return jnp.concatenate([ref[h * group + g : h * group + g + 1, :] for g in range(group)], axis=1)

    lses = [along(lse_ref, h) for h in range(kvs)]
    rds = [along(rd_ref, h) for h in range(kvs)]

    def chunk(c, masked):
        off = pl.multiple_of(c * qb, qb)
        for h in range(kvs):
            k = jnp.concatenate([kv_scr[h, s, pl.ds(off, qb), :] for s in range(slots)], axis=0)
            v = jnp.concatenate([kv_scr[kvs + h, s, pl.ds(off, qb), :] for s in range(slots)], axis=0)
            k_t = jnp.concatenate([kv_ref[s][h * 64 : (h + 1) * 64, pl.ds(off, qb)] for s in range(slots)], axis=1)
            st = mm(k, qs[h])
            if masked:
                st = st + jnp.concatenate([bias_ref[...].reshape(slots * qb, qb)] * group, axis=1)
            p = jnp.exp2(st - lses[h])
            dp = mm(v, dos[h])
            ds = (p * (dp - rds[h])).astype(BF)
            dk = mm(qs[h], ds, NT)
            dv = mm(dos[h], p.astype(BF), NT)
            dq = mm(k_t, ds)
            for s in range(slots):
                dkv_ref[s, h * 64 : (h + 1) * 64, pl.ds(off, qb)] += dk[:, s * qb : (s + 1) * qb]
                dkv_ref[s, kw + h * 64 : kw + (h + 1) * 64, pl.ds(off, qb)] += dv[:, s * qb : (s + 1) * qb]
            for g in range(group):
                r = h * group + g
                dq_ref[r * 64 : (r + 1) * 64, :] += dq[:, g * qb : (g + 1) * qb]

    def body(c, carry):
        chunk(c, False)
        return carry

    lax.fori_loop(0, step + lo, body, 0)
    chunk(step + lo, True)
    if last:

        @pl.when(step == pl.num_programs(0) - 1)
        def _():
            low_ref[...] = dkv_ref[slots - low_ref.shape[0] :].astype(BF)


def attn_bwd(bias, q_t, kv_t, do_t, lse, rd, lo, hi, before=None, last=False, kvs=3, group=3, qb=256):
    slots, rows = len(kv_t), kv_t[0].shape[1]
    width = kvs * group * 64
    whole = pl.BlockSpec((slots, 2 * kvs * 64, rows), lambda i: (0, 0, 0))
    tall = pl.BlockSpec((width, qb), lambda i: (0, i + lo))
    stat = pl.BlockSpec((16, qb), lambda i: (0, i + lo))
    out_specs = [pl.BlockSpec((width, qb), lambda i: (0, i)), whole]
    out_shape = [
        jax.ShapeDtypeStruct((width, (hi - lo) * qb), F32),
        jax.ShapeDtypeStruct((slots, 2 * kvs * 64, rows), F32),
    ]
    if last:
        sent = (1 if slots == 2 else slots, 2 * kvs * 64, rows)
        out_specs.append(pl.BlockSpec(sent, lambda i: (0, 0, 0)))
        out_shape.append(jax.ShapeDtypeStruct(sent, BF))
    args = (bias, q_t, do_t, lse, rd, *kv_t) + (() if before is None else (before,))
    units = sum(range(lo + 1, hi + 1))
    return pl.pallas_call(
        functools.partial(
            bwd_kernel, kvs=kvs, group=group, slots=slots, qb=qb, lo=lo, first=before is None, last=last
        ),
        grid=(hi - lo,),
        in_specs=[pl.BlockSpec((slots, qb, qb), lambda i: (0, 0, 0)), tall, tall, stat, stat]
        + [pl.BlockSpec((2 * kvs * 64, rows), lambda i: (0, 0))] * slots
        + ([] if before is None else [whole]),
        out_specs=out_specs,
        out_shape=out_shape,
        scratch_shapes=[pltpu.VMEM((2 * kvs, slots, rows, 64), BF)],
        compiler_params=pltpu.CompilerParams(vmem_limit_bytes=60 * 2**20),
        cost_estimate=pl.CostEstimate(flops=int(4e9) * units, bytes_accessed=int(16e6), transcendentals=0),
    )(*args)


TN = (((0,), (0,)), ((), ()))
TT = (((0,), (1,)), ((), ()))
BLOCK = 256
PIECES = 8
LIMIT = 60 * 2**20


def rotated(values, cosine, sine):
    a, b = values[:32], values[32:]
    return jnp.concatenate([a * cosine - b * sine, b * cosine + a * sine], axis=0)


def flat_rows(ref):
    count, sub, width = ref.shape
    return ref[...].reshape(count * sub, width)


def rms(values):
    return lax.rsqrt(jnp.mean(values * values, axis=-1, keepdims=True) + EPSILON)


def qkv_kernel(x_ref, w_ref, gain_ref, cos_ref, sin_ref, q_ref, kv_ref, wt_scr):
    @pl.when(pl.program_id(0) == 0)
    def _():
        wt_scr[...] = w_ref[:, : wt_scr.shape[0]].T

    source = flat_rows(x_ref).astype(F32)
    hidden = (source * rms(source) * gain_ref[0:1, :]).astype(BF)
    out = mm(wt_scr[...], hidden, NT)
    cosine, sine = cos_ref[...], sin_ref[...]
    for h in range(HEADS):
        part = rotated(out[h * 64 : (h + 1) * 64], cosine, sine)
        q_ref[h * 64 : (h + 1) * 64, :] = (part * (HEAD_DIM**-0.5 * LOG2E)).astype(BF)
    top = HEADS * 64
    for h in range(KV_HEADS):
        part = rotated(out[top + h * 64 : top + (h + 1) * 64], cosine, sine)
        kv_ref[h * 64 : (h + 1) * 64, :] = part.astype(BF)
    kv_ref[KV_HEADS * 64 :, :] = out[top + KV_HEADS * 64 :].astype(BF)


def project_qkv(x, first, gains, cosine, sine):
    count, sub, width = x.shape
    rows = count * sub
    per = BLOCK // sub
    kv2 = 2 * KV_HEADS * HEAD_DIM
    return pl.pallas_call(
        qkv_kernel,
        grid=(rows // BLOCK,),
        in_specs=[
            pl.BlockSpec((per, sub, width), lambda i: (i, 0, 0)),
            pl.BlockSpec(first.shape, lambda i: (0, 0)),
            pl.BlockSpec(gains.shape, lambda i: (0, 0)),
            pl.BlockSpec((32, BLOCK), lambda i: (0, i)),
            pl.BlockSpec((32, BLOCK), lambda i: (0, i)),
        ],
        out_specs=[pl.BlockSpec((width, BLOCK), lambda i: (0, i)), pl.BlockSpec((kv2, BLOCK), lambda i: (0, i))],
        out_shape=[jax.ShapeDtypeStruct((width, rows), BF), jax.ShapeDtypeStruct((kv2, rows), BF)],
        scratch_shapes=[pltpu.VMEM((width + kv2, width), BF)],
        compiler_params=pltpu.CompilerParams(vmem_limit_bytes=LIMIT),
        cost_estimate=pl.CostEstimate(flops=int(6e9), bytes_accessed=int(5e6), transcendentals=0),
    )(x, first, gains, cosine, sine)


def ffn_kernel(
    place_ref, o_ref, x_ref, cot_ref, first_ref, gain_ref,
    gate_own, gate_got, gate_swap, up_own, up_got, up_swap, down_own, down_got, down_swap,
    mixed_ref, dres_ref, datt_ref, rd_ref, keep_gu, send_gu, keep_do, send_do, gg_ref,
    acc_gu, acc_down, acc_out, gate_ref, up_ref, down_ref,
):
    step = pl.program_id(0)
    width = x_ref.shape[2]

    @pl.when(step == 0)
    def _():
        acc_gu[...] = jnp.zeros(acc_gu.shape, F32)
        acc_down[...] = jnp.zeros(acc_down.shape, F32)
        acc_out[...] = jnp.zeros(acc_out.shape, F32)
        gg_ref[...] = jnp.zeros(gg_ref.shape, F32)
        for rank in range(2):

            @pl.when(place_ref[1] == rank)
            def _():
                for ref, own in ((gate_ref, gate_own), (up_ref, up_own), (down_ref, down_own)):
                    n = own.shape[0]
                    ref[rank * n : (rank + 1) * n] = own[...]
                for core in range(2):

                    @pl.when(place_ref[0] == core)
                    def _():
                        for ref, parts in ((gate_ref, (gate_got, gate_swap)), (up_ref, (up_got, up_swap))):
                            n, m = parts[0].shape
                            for k, part in ((core, parts[0]), (1 - core, parts[1])):
                                ref[(1 - rank) * n : (2 - rank) * n, k * m : (k + 1) * m] = part[...]
                        n = down_got.shape[0]
                        for k, part in ((core, down_got), (1 - core, down_swap)):
                            low = (2 * (1 - rank) + k) * n
                            down_ref[low : low + n] = part[...]

    cols = first_ref.shape[1]
    out_w = first_ref[:, cols - width :]
    attended = o_ref[...]
    mixed = attended.astype(BF)
    residual = flat_rows(x_ref).astype(F32) + mm(mixed, out_w, TN)
    scale = rms(residual)
    normed = residual * scale
    gain = gain_ref[1:2, :]
    hidden = (normed * gain).astype(BF)
    gate = mm(hidden, gate_ref[...])
    up = mm(hidden, up_ref[...])
    sig = 0.5 * jnp.tanh(0.5 * gate) + 0.5
    silu = gate * sig
    activated = (silu * up).astype(BF)
    mixed_out = (residual + mm(activated, down_ref[...])).astype(BF)
    mixed_ref[...] = mixed_out.reshape(mixed_ref.shape)
    cot = flat_rows(cot_ref)
    d_act = mm(cot, down_ref[...], NT)
    acc_down[...] += mm(activated, cot, TN)
    d_gate = (d_act * up * sig * (1.0 + gate * (1.0 - sig))).astype(BF)
    d_up = (d_act * silu).astype(BF)
    acc_gu[0] += mm(hidden, d_gate, TN)
    acc_gu[1] += mm(hidden, d_up, TN)
    d_hidden = mm(d_gate, gate_ref[...], NT) + mm(d_up, up_ref[...], NT)
    dn = d_hidden * normed
    gg_ref[...] += jnp.sum(dn.reshape(-1, 8, width), axis=0)
    inner = jnp.mean(dn * gain, axis=-1, keepdims=True)
    d_res = cot.astype(F32) + scale * (d_hidden * gain - normed * inner)
    dres_ref[...] = d_res
    d_low = d_res.astype(BF)
    acc_out[...] += mm(mixed, d_low)
    d_att = mm(out_w, d_low, NT).astype(BF)
    datt_ref[...] = d_att
    prod = d_att.astype(F32) * attended
    for h in range(HEADS):
        rd_ref[h : h + 1, :] = jnp.sum(prod[h * 64 : (h + 1) * 64], axis=0, keepdims=True)
    rd_ref[HEADS:, :] = jnp.zeros((16 - HEADS, rd_ref.shape[1]), F32)

    @pl.when(step == pl.num_programs(0) - 1)
    def _():
        core = place_ref[0]
        half = width // 2
        ff = acc_gu.shape[2]
        for y in range(2):
            for p in range(PIECES):
                rs = slice(y * half + (p // 4) * (half // 2), y * half + (p // 4 + 1) * (half // 2))
                cs = slice((p % 4) * (ff // 4), (p % 4 + 1) * (ff // 4))
                keep_gu[y, p] = acc_gu[core, rs, cs].astype(BF)
                send_gu[y, p] = acc_gu[1 - core, rs, cs].astype(BF)
        down_rows, out_rows = ff // 32, width // 24
        for y in range(2):
            for p in range(PIECES):
                for ref, c in ((keep_do, core), (send_do, 1 - core)):
                    start = pl.multiple_of(y * (ff // 2) + (PIECES * c + p) * down_rows, 16)
                    ref[y, p, :down_rows] = acc_down[pl.ds(start, down_rows), :].astype(BF)
                    start = y * half + jnp.minimum(PIECES * c + p, half // out_rows - 1) * out_rows
                    ref[y, p, down_rows:] = acc_out[pl.ds(pl.multiple_of(start, 8), out_rows), :].astype(BF)


def feed_forward(place, attended, x, cot, first, gains, weights):
    count, sub, width = x.shape
    rows, ff = count * sub, weights[0].shape[1]
    per = BLOCK // sub
    gu = (2, PIECES, width // 4, ff // 4)
    do = (2, PIECES, ff // 32 + width // 24, width)

    def whole(shape):
        return pl.BlockSpec(shape, lambda i: (0,) * len(shape))

    seq = pl.BlockSpec((per, sub, width), lambda i: (i, 0, 0))
    tall = pl.BlockSpec((width, BLOCK), lambda i: (0, i))
    return pl.pallas_call(
        ffn_kernel,
        grid=(rows // BLOCK,),
        in_specs=[
            pl.BlockSpec(memory_space=pltpu.SMEM), tall, seq, seq,
            whole(first.shape), whole(gains.shape), *(whole(w.shape) for w in weights),
        ],
        out_specs=[
            seq, pl.BlockSpec((BLOCK, width), lambda i: (i, 0)), tall, pl.BlockSpec((16, BLOCK), lambda i: (0, i)),
            whole(gu), whole(gu), whole(do), whole(do), whole((8, width)),
        ],
        out_shape=[
            jax.ShapeDtypeStruct(x.shape, BF),
            jax.ShapeDtypeStruct((rows, width), F32),
            jax.ShapeDtypeStruct((width, rows), BF),
            jax.ShapeDtypeStruct((16, rows), F32),
            jax.ShapeDtypeStruct(gu, BF), jax.ShapeDtypeStruct(gu, BF),
            jax.ShapeDtypeStruct(do, BF), jax.ShapeDtypeStruct(do, BF),
            jax.ShapeDtypeStruct((8, width), F32),
        ],
        scratch_shapes=[
            pltpu.VMEM((2, width, ff), F32), pltpu.VMEM((ff, width), F32), pltpu.VMEM((width, width), F32),
            pltpu.VMEM((width, ff), BF), pltpu.VMEM((width, ff), BF), pltpu.VMEM((ff, width), BF),
        ],
        compiler_params=pltpu.CompilerParams(vmem_limit_bytes=LIMIT),
        cost_estimate=pl.CostEstimate(flops=int(32e9), bytes_accessed=int(20e6), transcendentals=0),
    )(place, attended, x, cot, first, gains, *weights)


def back_kernel(*refs, spans):
    place_ref, refs = refs[0], refs[1:]
    dq_refs, refs = refs[: len(spans)], refs[len(spans) :]
    own_ref, got_ref, x_ref, dres_ref, first_ref, gain_ref, cos_ref, sin_ref, gg_ref, dx_ref = refs[:10]
    keep_ref, send_ref, acc, dt_scr, ga_scr, w_scr = refs[10:]
    step = pl.program_id(0)
    width = x_ref.shape[2]
    kv = KV_HEADS * 64
    total = width + 2 * kv

    @pl.when(step == 0)
    def _():
        acc[...] = jnp.zeros(acc.shape, F32)
        ga_scr[...] = jnp.zeros(ga_scr.shape, F32)
        w_scr[...] = first_ref[:, :total].T

    cosine, sine = cos_ref[...], -sin_ref[...]
    for (lo, hi), dq_ref in zip(spans, dq_refs):

        @pl.when((step >= lo) & (step < hi))
        def _():
            for h in range(HEADS):
                part = dq_ref[h * 64 : (h + 1) * 64, :] * (HEAD_DIM**-0.5)
                dt_scr[h * 64 : (h + 1) * 64, :] = rotated(part, cosine, sine).astype(BF)

    d_kv = own_ref[0] + got_ref[...].astype(F32)
    for h in range(KV_HEADS):
        part = d_kv[h * 64 : (h + 1) * 64] * LN2
        dt_scr[width + h * 64 : width + (h + 1) * 64, :] = rotated(part, cosine, sine).astype(BF)
    dt_scr[width + kv :, :] = d_kv[kv:].astype(BF)
    d_t = dt_scr[...]
    source = flat_rows(x_ref).astype(F32)
    scale = rms(source)
    normed = source * scale
    gain = gain_ref[0:1, :]
    hidden = (normed * gain).astype(BF)
    acc[:total] += mm(d_t, hidden)
    d_hidden = mm(d_t, w_scr[...], TN)
    dn = d_hidden * normed
    ga_scr[...] += jnp.sum(dn.reshape(-1, 8, width), axis=0)
    inner = jnp.mean(dn * gain, axis=-1, keepdims=True)
    grad = dres_ref[...] + scale * (d_hidden * gain - normed * inner)
    dx_ref[...] = grad.astype(BF).reshape(dx_ref.shape)

    @pl.when(step == pl.num_programs(0) - 1)
    def _():
        core = place_ref[0]
        acc[total : total + 1, :] = jnp.sum(ga_scr[...], axis=0, keepdims=True)
        acc[total + 1 : total + 2, :] = jnp.sum(gg_ref[...], axis=0, keepdims=True)
        half, deep = width // 2, width // 4
        for ct in range(4):
            for ref, c in ((keep_ref, core), (send_ref, 1 - core)):
                start = pl.multiple_of(c * 512 + ct * 128, 128)
                block = acc[pl.ds(start, 128), :].T.astype(BF)
                for y in range(2):
                    for rh in range(2):
                        low = y * half + rh * deep
                        ref[y, rh * 4 + ct] = block[low : low + deep]


def back_qkv(place, spans, d_query, d_kv, got, x, d_res, first, gains, cosine, sine, gg):
    count, sub, width = x.shape
    rows = count * sub
    per = BLOCK // sub
    kv2 = 2 * KV_HEADS * HEAD_DIM
    piece = (2, PIECES, width // 4, 128)

    def whole(shape):
        return pl.BlockSpec(shape, lambda i: (0,) * len(shape))

    seq = pl.BlockSpec((per, sub, width), lambda i: (i, 0, 0))
    return pl.pallas_call(
        functools.partial(back_kernel, spans=spans),
        grid=(rows // BLOCK,),
        in_specs=[
            pl.BlockSpec(memory_space=pltpu.SMEM),
            *(
                pl.BlockSpec((width, BLOCK), lambda i, lo=lo, hi=hi: (0, jnp.clip(i - lo, 0, hi - lo - 1)))
                for lo, hi in spans
            ),
            pl.BlockSpec((1, kv2, BLOCK), lambda i: (0, 0, i)),
            pl.BlockSpec((kv2, BLOCK), lambda i: (0, i)),
            seq, pl.BlockSpec((BLOCK, width), lambda i: (i, 0)),
            whole(first.shape), whole(gains.shape),
            pl.BlockSpec((32, BLOCK), lambda i: (0, i)), pl.BlockSpec((32, BLOCK), lambda i: (0, i)),
            whole(gg.shape),
        ],
        out_specs=[seq, whole(piece), whole(piece)],
        out_shape=[jax.ShapeDtypeStruct(x.shape, BF), jax.ShapeDtypeStruct(piece, BF), jax.ShapeDtypeStruct(piece, BF)],
        scratch_shapes=[
            pltpu.VMEM((1024, width), F32), pltpu.VMEM((width + kv2, BLOCK), BF), pltpu.VMEM((8, width), F32),
            pltpu.VMEM((width + kv2, width), BF),
        ],
        compiler_params=pltpu.CompilerParams(vmem_limit_bytes=LIMIT),
        cost_estimate=pl.CostEstimate(flops=int(10e9), bytes_accessed=int(10e6), transcendentals=0),
    )(place, *d_query, d_kv, got, x, d_res, first, gains, cosine, sine, gg)


def final_kernel(
    at_ref, gu4, gu_x, gu_c, do4, do_x, do_c, gate_ref, up_ref, down_ref, out_ref
):
    core, xb, z = at_ref[0], at_ref[1], at_ref[2]
    deep, wide = gu4.shape[1:]
    for f in range(2):
        for e in range(2):
            for d in range(4):
                gu = (gu4[d] if e == 0 else gu_x[d]) if f == 0 else gu_c[e * 4 + d]
                do = (do4[d] if e == 0 else do_x[d]) if f == 0 else do_c[e * 4 + d]
                rs = pl.ds(pl.multiple_of((xb ^ e) * deep, 16), deep)
                cs = pl.ds(pl.multiple_of((z ^ d) * wide, 128), wide)
                for c, ref in ((0, gate_ref), (1, up_ref)):

                    @pl.when((core ^ f) == c)
                    def _():
                        ref[rs, cs] = gu.astype(F32)

                m = (core ^ f) * 8 + (xb ^ e) * 4 + (z ^ d)
                rows = down_ref.shape[0] // 16
                down_ref[pl.ds(pl.multiple_of(m * rows, 8), rows), :] = do[:rows].astype(F32)
                few = do.shape[0] - rows

                @pl.when(m < out_ref.shape[0] // few)
                def _():
                    out_ref[pl.ds(pl.multiple_of(m * few, 8), few), :] = do[rows:].astype(F32)


def final_ffn(at, gu4, gu_x, gu_c, do4, do_x, do_c, half, ff, width):
    f32 = lambda *s: jax.ShapeDtypeStruct(s, F32)
    return pl.pallas_call(
        final_kernel,
        in_specs=[pl.BlockSpec(memory_space=pltpu.SMEM)] + [pl.BlockSpec(memory_space=pltpu.VMEM)] * 6,
        out_specs=[pl.BlockSpec(memory_space=pltpu.VMEM)] * 4,
        out_shape=[f32(half, ff), f32(half, ff), f32(ff // 2, width), f32(half, width)],
        compiler_params=pltpu.CompilerParams(vmem_limit_bytes=LIMIT),
        cost_estimate=pl.CostEstimate(flops=int(5e9), bytes_accessed=int(10e6), transcendentals=0),
    )(at, gu4, gu_x, gu_c, do4, do_x, do_c)


def final_t_kernel(at_ref, t4, t_x, t_c, q_ref, k_ref, v_ref, g_ref, whole):
    core, xb, z = at_ref[0], at_ref[1], at_ref[2]
    deep, wide = t4.shape[1:]
    for f in range(2):
        for e in range(2):
            for d in range(4):
                t = (t4[d] if e == 0 else t_x[d]) if f == 0 else t_c[e * 4 + d]
                rs = pl.ds(pl.multiple_of((xb ^ e) * deep, 16), deep)
                cs = pl.ds(pl.multiple_of((core ^ f) * 512 + (z ^ d) * wide, 128), wide)
                whole[rs, cs] = t.astype(F32)
    a = q_ref.shape[1]
    b = a + k_ref.shape[1]
    c = b + v_ref.shape[1]
    q_ref[...] = whole[:, :a]
    k_ref[...] = whole[:, a:b]
    v_ref[...] = whole[:, b:c]
    g_ref[...] = whole[:, c:].T[:8]


def final_t(at, t4, t_x, t_c, half, width, kv_width):
    f32 = lambda *s: jax.ShapeDtypeStruct(s, F32)
    return pl.pallas_call(
        final_t_kernel,
        in_specs=[pl.BlockSpec(memory_space=pltpu.SMEM)] + [pl.BlockSpec(memory_space=pltpu.VMEM)] * 3,
        out_specs=[pl.BlockSpec(memory_space=pltpu.VMEM)] * 4,
        out_shape=[f32(half, width), f32(half, kv_width), f32(half, kv_width), f32(8, half)],
        scratch_shapes=[pltpu.VMEM((half, 1024), F32)],
        compiler_params=pltpu.CompilerParams(vmem_limit_bytes=LIMIT),
        cost_estimate=pl.CostEstimate(flops=int(1e9), bytes_accessed=int(2e6), transcendentals=0),
    )(at, t4, t_x, t_c)


def swap(x, axis, bit):
    n = lax.axis_size(axis)
    return lax.ppermute(x, axis, [(i, i ^ (1 << bit)) for i in range(n)])


def bit_of(axis, bit):
    return (lax.axis_index(axis) >> bit) & 1


def pin(*arrays):
    return lax.optimization_barrier(arrays)


def pick(x, at):
    return lax.dynamic_index_in_dim(x, at, 0, keepdims=False)


def in_order(flag, mine, other, axis):
    return jnp.where(
        flag == 0,
        jnp.concatenate([mine, other], axis=axis),
        jnp.concatenate([other, mine], axis=axis),
    )


def plus(a, b):
    return (a.astype(F32) + b.astype(F32)).astype(BF)


def two_level():
    return lax.axis_size("fsdp") == 2 and lax.axis_size("ctx") == 16


def z_swap(x, by):
    return lax.ppermute(x, "ctx", [(i, i ^ (4 * by)) for i in range(16)])


def z_send(x):
    z = lax.axis_index("ctx") >> 2
    return pick(x, z), [pick(x, z ^ by) for by in range(1, 4)]


def z_pass(pieces):
    return [z_swap(p, by) for by, p in zip(range(1, 4), pieces)]


def z_total(mine, got):
    return sum((g.astype(F32) for g in got), mine.astype(F32)).astype(BF)


def z_join(piece):
    return [piece] + [z_swap(piece, by) for by in range(1, 4)]


def natural_gu(pieces):
    _, a, b = pieces.shape
    return pieces.reshape(2, 4, a, b).transpose(0, 2, 1, 3).reshape(2 * a, 4 * b).astype(F32)


def other_sum(x):
    x = lax.psum_scatter(x.astype(BF), "fsdp", scatter_dimension=0, tiled=True)
    return lax.psum(x, "ctx").astype(F32)


def local(tokens, gain_attn, w_query, w_key, w_value, w_out, gain_ffn, w_gate, w_up, w_down, cotangent):
    seqs, length, width = tokens.shape
    count = lax.axis_size("ctx")
    team = count // seqs
    sub = length // team
    rows = count * sub
    ff = w_gate.shape[1]
    kv_width = KV_HEADS * HEAD_DIM
    qkv_cols = width + 2 * kv_width
    place = lax.axis_index("ctx") % team
    own = gain_attn.shape[0]
    fast = two_level()

    def move(x):
        return lax.all_to_all(x.reshape(count, sub, width), "ctx", 0, 0, tiled=True)

    x = move(tokens)
    gain_rows = jnp.zeros((8, ff), BF).at[0, :own].set(gain_attn).at[1, :own].set(gain_ffn)
    first = jnp.concatenate([jnp.concatenate([w_query, w_key, w_value, w_out], axis=1), gain_rows], axis=0)
    if fast:
        core, rank = bit_of("ctx", 0), bit_of("fsdp", 0)

        def halved(shard, axis):
            half = shard.shape[axis] // 2
            return lax.dynamic_slice_in_dim(shard, core * half, half, axis)

        def other_shard(got, axis):
            return in_order(core, got, swap(got, "ctx", 0), axis)

        got = swap(halved(first, 1), "fsdp", 0)
        other = other_shard(got, 1)
        gains = in_order(rank, first[own : own + 2, :own], other[own : own + 2, :own], 1).astype(F32)
        first = in_order(rank, first[:own], other[:own], 0)
        gate_half, up_half, down_half, got = pin(halved(w_gate, 1), halved(w_up, 1), halved(w_down, 0), got)
        gate_got, up_got, down_got = (swap(h, "fsdp", 0) for h in (gate_half, up_half, down_half))
    else:
        first = lax.all_gather(first, "fsdp", axis=0)
        gains = first[:, own : own + 2, :own].transpose(1, 0, 2).reshape(2, width).astype(F32)
        first = first[:, :own].reshape(width, first.shape[2])
        gate_w, up_w, down_w = (lax.all_gather(w, "fsdp", axis=0, tiled=True) for w in (w_gate, w_up, w_down))
    gains = jnp.pad(gains, ((0, 6), (0, 0)))

    row = jnp.arange(rows, dtype=jnp.int32)
    position = (row // sub) * length + place * sub + row % sub
    frequency = THETA ** (-jnp.arange(HEAD_DIM // 2, dtype=F32) * 2.0 / HEAD_DIM)
    angles = frequency[:, None] * position.astype(F32)[None, :]
    cosine, sine = jnp.cos(angles), jnp.sin(angles)
    groups = [[t * team + p for p in range(team)] for t in range(seqs)]
    slots = jnp.stack([place, 1 - place]) if team == 2 else jnp.arange(team)
    block_row = jnp.arange(BLOCK, dtype=jnp.int32)
    base = (block_row // sub) * length + block_row % sub
    key_pos = base[None, :] + slots[:, None] * sub
    query_pos = base + place * sub
    bias = jnp.where(key_pos[:, :, None] <= query_pos[None, None, :], 0.0, NEGATIVE).astype(F32)
    flags = jnp.stack([core, rank]) if fast else jnp.zeros((2,), jnp.int32)

    x, cot_send = pin(x, cotangent)
    cot = move(cot_send)
    query, kv_own = project_qkv(x, first, gains, cosine, sine)
    if fast:
        kv_own, gate_got = pin(kv_own, gate_got)
    if team == 2:
        kv_all = (kv_own, swap(kv_own, "ctx", 0))
    else:
        kv_all = lax.all_gather(kv_own, "ctx", axis=0, axis_index_groups=groups)
        kv_all = tuple(kv_all[s] for s in range(team))
    attended, log_total = attn_fwd(bias, query, kv_all)
    if fast:
        attended, cot, *gots = pin(attended, cot, gate_got, up_got, down_got)
        gots = [(got, swap(got, "ctx", 0)) for got in gots]
        weights = [a for own_w, two in zip((w_gate, w_up, w_down), gots) for a in (own_w, *two)]
    else:
        attended, cot = pin(attended, cot)
        low, side = width // 2, ff // 2
        weights = [a for w in (gate_w, up_w) for a in (w[:low], w[low:, :side], w[low:, side:])]
        weights += [down_w[:side], down_w[side : side + side // 2], down_w[side + side // 2 :]]
    mixed, d_res, d_att, row_dot, keep_gu, send_gu, keep_do, send_do, gain_sum = feed_forward(
        flags, attended, x, cot, first, gains, weights
    )
    mixed_out = move(mixed)

    n = rows // BLOCK
    spans = ((0, n - 1), (n - 1, n))
    part = functools.partial(attn_bwd, bias, query, kv_all, d_att, log_total, row_dot)
    if fast:
        x_bit = bit_of("ctx", 1)
        got_gu, got_do = swap(send_gu, "ctx", 0), swap(send_do, "ctx", 0)
        gu, do = plus(keep_gu, got_gu), plus(keep_do, got_do)
        gu = gu.reshape((2, 2, 4) + gu.shape[2:]).swapaxes(0, 1)
        keep_gu, send_gu = pick(gu, x_bit), pick(gu, 1 - x_bit)
        keep_do, send_do = pick(do, rank), pick(do, 1 - rank)
        send_gu, send_do, row_dot = pin(send_gu, send_do, row_dot)
        part = functools.partial(attn_bwd, bias, query, kv_all, d_att, log_total, row_dot)
        got_gu, got_do = swap(send_gu, "ctx", 1), swap(send_do, "fsdp", 0)
        dq_a, before = part(*spans[0])
        got_gu, got_do, mixed_out, before = pin(got_gu, got_do, mixed_out, before)
        gu, do = plus(keep_gu, got_gu), plus(keep_do, got_do)
        do = do.reshape((2, 4) + do.shape[1:])
        keep_gu, send_gu = pick(gu, rank), pick(gu, 1 - rank)
        keep_do, send_do = pick(do, x_bit), pick(do, 1 - x_bit)
        send_gu, send_do, before = pin(send_gu, send_do, before)
        got_gu, got_do = swap(send_gu, "fsdp", 0), swap(send_do, "ctx", 1)
        dq_b, d_kv, d_kv_low = part(*spans[1], before=before, last=True)
        got_gu, got_do, d_kv_low, dq_b = pin(got_gu, got_do, d_kv_low, dq_b)
        gu, do = plus(keep_gu, got_gu), plus(keep_do, got_do)
    else:
        dq_a, before = part(*spans[0])
        dq_b, d_kv, d_kv_low = part(*spans[1], before=before, last=True)
    if team == 2:
        own_kv, got_kv = d_kv, swap(d_kv_low.reshape(2 * kv_width, rows), "ctx", 0)
    else:
        own_kv = lax.psum_scatter(d_kv_low, "ctx", scatter_dimension=0, axis_index_groups=groups)
        own_kv, got_kv = own_kv.astype(F32)[None], jnp.zeros((2 * kv_width, rows), BF)
    if fast:
        z_gu, z_do = z_send(gu), z_send(do)
        send_pin = pin(own_kv, got_kv, *z_gu[1], *z_do[1])
        own_kv, got_kv = send_pin[:2]
        z_gu, z_do = (z_gu[0], send_pin[2:5]), (z_do[0], send_pin[5:])
        z_got = [z_pass(z_gu[1]), z_pass(z_do[1])]
    d_x, keep_t, send_t = back_qkv(
        flags, spans, (dq_a, dq_b), own_kv, got_kv, x, d_res, first, gains, cosine, sine, gain_sum
    )
    if fast:
        d_x, keep_t, send_t, *got = pin(d_x, keep_t, send_t, *z_got[0], *z_got[1])
        gu, do = z_total(z_gu[0], got[:3]), z_total(z_do[0], got[3:])
    grad_tokens = move(d_x)
    if fast:
        gu_four, do_four = z_join(gu), z_join(do)
        t = plus(keep_t, swap(send_t, "ctx", 0))
        t = plus(pick(t, rank), swap(pick(t, 1 - rank), "fsdp", 0))
        t = t.reshape((2, 4) + t.shape[1:])
        t = plus(pick(t, x_bit), swap(pick(t, 1 - x_bit), "ctx", 1))
        keep_t, send_t = z_send(t)
        t_got = z_pass(send_t)
        *t_got, grad_tokens, d0, d1, d2 = pin(*t_got, grad_tokens, *do_four[1:])
        t_four = z_join(z_total(keep_t, t_got))
        do_four = jnp.stack([do_four[0], d0, d1, d2])
        do_x = swap(do_four, "ctx", 1)
        t0, t1, t2, g0, g1, g2 = pin(*t_four[1:], *gu_four[1:])
        gu_four = jnp.stack([gu_four[0], g0, g1, g2])
        gu_x = swap(gu_four, "ctx", 1)
        t_four = jnp.stack([t_four[0], t0, t1, t2])
        t_x = swap(t_four, "ctx", 1)
        t_x, do_x = pin(t_x, do_x)
        do_c = swap(jnp.concatenate([do_four, do_x], axis=0), "ctx", 0)
        t_c = swap(jnp.concatenate([t_four, t_x], axis=0), "ctx", 0)
        gu_x, t_c = pin(gu_x, t_c)
        gu_c = swap(jnp.concatenate([gu_four, gu_x], axis=0), "ctx", 0)
        at = jnp.stack([core, x_bit, lax.axis_index("ctx") >> 2])
        own_query, own_key, own_value, own_gains = final_t(at, t_four, t_x, t_c, width // 2, width, kv_width)
        own_gate, own_up, own_down, own_out = final_ffn(
            at, gu_four, gu_x, gu_c, do_four, do_x, do_c, width // 2, ff, width
        )
    else:
        pair = jnp.stack([keep_gu, send_gu])
        gate, up = (jnp.concatenate([natural_gu(pair[c, y]) for y in range(2)], axis=0) for c in range(2))
        do = jnp.stack([keep_do, send_do], axis=1).reshape((32,) + keep_do.shape[2:])
        deep = ff // 32
        own_gate, own_up = other_sum(gate), other_sum(up)
        own_down = other_sum(do[:, :deep].reshape(ff, width))
        out = do[:, deep:].reshape((2, -1, width))[:, : width // 2]
        own_out = other_sum(out.reshape(width, width))
        pair = jnp.stack([keep_t, send_t])
        t = [jnp.concatenate([natural_gu(pair[c, y]) for c in range(2)], axis=1) for y in range(2)]
        own_t = other_sum(jnp.concatenate(t, axis=0))
        own_query, own_key = own_t[:, :width], own_t[:, width : width + kv_width]
        own_value, own_gains = own_t[:, width + kv_width : qkv_cols], own_t[:, qkv_cols:].T
    return (
        mixed_out.reshape(tokens.shape),
        grad_tokens.reshape(tokens.shape),
        own_gains[0],
        own_query,
        own_key,
        own_value,
        own_out,
        own_gains[1],
        own_gate,
        own_up,
        own_down,
    )


def solution(mesh):
    rows, flat, seq = P("fsdp", None), P("fsdp"), P("fsdp", "ctx", None)
    return jax.shard_map(
        local,
        mesh=mesh,
        in_specs=(seq, flat, rows, rows, rows, rows, flat, rows, rows, rows, seq),
        out_specs=(seq, seq, flat, rows, rows, rows, rows, flat, rows, rows, rows),
        check_vma=False,
    )
```

```python
import functools

import jax
import jax.numpy as jnp
from jax import lax
from jax.experimental import pallas as pl
from jax.experimental.pallas import tpu as pltpu
from jax.sharding import PartitionSpec as P

HEADS = 9
KV_HEADS = 3
HEAD_DIM = 64
EPSILON = 1e-05
THETA = 100000.0
NEGATIVE = -1e30
LOG2E = 1.4426950408889634
LN2 = 0.6931471805599453
F32=jnp.float32; BF=jnp.bfloat16
NT=(((1,),(1,)),((),()))
NN=(((1,),(0,)),((),()))
def mm(a,b,dims=NN):
    return lax.dot_general(a,b,dims,preferred_element_type=F32)

def heads_of(ref, kv, group):
    return jnp.concatenate([ref[(kv*group+h)*64:(kv*group+h+1)*64,:] for h in range(group)],axis=1)

def fwd_kernel(bias_ref, q_ref, *refs, kvs, group, slots, rows, qb):
    kv_ref, (o_ref, lse_ref, k_scr, m_scr, acc_scr)=refs[:slots], refs[slots:]
    i=pl.program_id(0)
    kw=kvs*64
    @pl.when(i==0)
    def _():
        for s in range(slots):
            for h in range(kvs):
                k_scr[h,s]=kv_ref[s][h*64:(h+1)*64,:].T
    qs=[heads_of(q_ref,h,group) for h in range(kvs)]
    width=group*qb
    m_scr[...]=jnp.full(m_scr.shape,-1e30,F32)
    acc_scr[...]=jnp.zeros(acc_scr.shape,F32)
    ones=jnp.ones((8,slots*qb),BF)
    def chunk(c, masked):
        off=pl.multiple_of(c*qb,qb)
        for h in range(kvs):
            k=jnp.concatenate([k_scr[h,s,pl.ds(off,qb),:] for s in range(slots)],axis=0)
            v=jnp.concatenate([kv_ref[s][kw+h*64:kw+(h+1)*64,pl.ds(off,qb)] for s in range(slots)],axis=1)
            v=jnp.concatenate([v,ones],axis=0)
            st=mm(k,qs[h])
            if masked:
                b=bias_ref[...].reshape(slots*qb,qb)
                st=st+jnp.concatenate([b]*group,axis=1)
            m_old=m_scr[h:h+1,:]
            m_new=jnp.maximum(m_old,jnp.max(st,axis=0,keepdims=True))
            p=jnp.exp2(st-m_new).astype(BF)
            acc_scr[h]=acc_scr[h]*jnp.exp2(m_old-m_new)+mm(v,p)
            m_scr[h:h+1,:]=m_new
    def body(c,_):
        chunk(c,False); return 0
    lax.fori_loop(0,i,body,0)
    chunk(i,True)
    for h in range(kvs):
        acc=acc_scr[h]
        tot=acc[64:65,:]
        o=acc[:64,:]*(1.0/tot)
        lse=m_scr[h:h+1,:]+jnp.log2(tot)
        for g in range(group):
            r=h*group+g
            o_ref[r*64:(r+1)*64,:]=o[:,g*qb:(g+1)*qb]
            lse_ref[r:r+1,:]=lse[:,g*qb:(g+1)*qb]

def attn_fwd(bias, qT, kvT, kvs=3, group=3, qb=256):
    slots,rows=len(kvT),kvT[0].shape[1]
    n=rows//qb
    heads=kvs*group
    return pl.pallas_call(
        functools.partial(fwd_kernel,kvs=kvs,group=group,slots=slots,rows=rows,qb=qb),
        grid=(n,),
        in_specs=[pl.BlockSpec((slots,qb,qb),lambda i:(0,0,0)),
                  pl.BlockSpec((heads*64,qb),lambda i:(0,i)),
                  *[pl.BlockSpec((2*kvs*64,rows),lambda i:(0,0))]*slots],
        out_specs=[pl.BlockSpec((heads*64,qb),lambda i:(0,i)),
                   pl.BlockSpec((16,qb),lambda i:(0,i))],
        out_shape=[jax.ShapeDtypeStruct((heads*64,rows),F32),jax.ShapeDtypeStruct((16,rows),F32)],
        scratch_shapes=[pltpu.VMEM((kvs,slots,rows,64),BF),pltpu.VMEM((8,group*qb),F32),
                        pltpu.VMEM((kvs,72,group*qb),F32)],
        compiler_params=pltpu.CompilerParams(vmem_limit_bytes=56*2**20),
        cost_estimate=pl.CostEstimate(flops=int(25e9),bytes_accessed=int(8e6),transcendentals=int(1e7)),
    )(bias,qT,*kvT)

def bwd_kernel(*refs, kvs, group, slots, qb, lo, first, last):
    bias_ref, q_ref, do_ref, lse_ref, rd_ref = refs[:5]
    kv_ref, refs = refs[5 : 5 + slots], refs[5 + slots :]
    if not first:
        before_ref, refs = refs[0], refs[1:]
    if last:
        dq_ref, dkv_ref, low_ref, kv_scr = refs
    else:
        dq_ref, dkv_ref, kv_scr = refs
    step = pl.program_id(0)
    kw = kvs * 64

    @pl.when(step == 0)
    def _():
        for s in range(slots):
            for h in range(2 * kvs):
                kv_scr[h, s] = kv_ref[s][h * 64 : (h + 1) * 64, :].T
        dkv_ref[...] = jnp.zeros(dkv_ref.shape, F32) if first else before_ref[...]

    dq_ref[...] = jnp.zeros(dq_ref.shape, F32)
    qs = [heads_of(q_ref, h, group) for h in range(kvs)]
    dos = [heads_of(do_ref, h, group) for h in range(kvs)]

    def along(ref, h):
        return jnp.concatenate([ref[h * group + g : h * group + g + 1, :] for g in range(group)], axis=1)

    lses = [along(lse_ref, h) for h in range(kvs)]
    rds = [along(rd_ref, h) for h in range(kvs)]

    def chunk(c, masked):
        off = pl.multiple_of(c * qb, qb)
        for h in range(kvs):
            k = jnp.concatenate([kv_scr[h, s, pl.ds(off, qb), :] for s in range(slots)], axis=0)
            v = jnp.concatenate([kv_scr[kvs + h, s, pl.ds(off, qb), :] for s in range(slots)], axis=0)
            k_t = jnp.concatenate([kv_ref[s][h * 64 : (h + 1) * 64, pl.ds(off, qb)] for s in range(slots)], axis=1)
            st = mm(k, qs[h])
            if masked:
                st = st + jnp.concatenate([bias_ref[...].reshape(slots * qb, qb)] * group, axis=1)
            p = jnp.exp2(st - lses[h])
            dp = mm(v, dos[h])
            ds = (p * (dp - rds[h])).astype(BF)
            dk = mm(qs[h], ds, NT)
            dv = mm(dos[h], p.astype(BF), NT)
            dq = mm(k_t, ds)
            for s in range(slots):
                dkv_ref[s, h * 64 : (h + 1) * 64, pl.ds(off, qb)] += dk[:, s * qb : (s + 1) * qb]
                dkv_ref[s, kw + h * 64 : kw + (h + 1) * 64, pl.ds(off, qb)] += dv[:, s * qb : (s + 1) * qb]
            for g in range(group):
                r = h * group + g
                dq_ref[r * 64 : (r + 1) * 64, :] += dq[:, g * qb : (g + 1) * qb]

    def body(c, carry):
        chunk(c, False)
        return carry

    lax.fori_loop(0, step + lo, body, 0)
    chunk(step + lo, True)
    if last:

        @pl.when(step == pl.num_programs(0) - 1)
        def _():
            low_ref[...] = dkv_ref[slots - low_ref.shape[0] :].astype(BF)


def attn_bwd(bias, q_t, kv_t, do_t, lse, rd, lo, hi, before=None, last=False, kvs=3, group=3, qb=256):
    slots, rows = len(kv_t), kv_t[0].shape[1]
    width = kvs * group * 64
    whole = pl.BlockSpec((slots, 2 * kvs * 64, rows), lambda i: (0, 0, 0))
    tall = pl.BlockSpec((width, qb), lambda i: (0, i + lo))
    stat = pl.BlockSpec((16, qb), lambda i: (0, i + lo))
    out_specs = [pl.BlockSpec((width, qb), lambda i: (0, i)), whole]
    out_shape = [
        jax.ShapeDtypeStruct((width, (hi - lo) * qb), F32),
        jax.ShapeDtypeStruct((slots, 2 * kvs * 64, rows), F32),
    ]
    if last:
        sent = (1 if slots == 2 else slots, 2 * kvs * 64, rows)
        out_specs.append(pl.BlockSpec(sent, lambda i: (0, 0, 0)))
        out_shape.append(jax.ShapeDtypeStruct(sent, BF))
    args = (bias, q_t, do_t, lse, rd, *kv_t) + (() if before is None else (before,))
    units = sum(range(lo + 1, hi + 1))
    return pl.pallas_call(
        functools.partial(
            bwd_kernel, kvs=kvs, group=group, slots=slots, qb=qb, lo=lo, first=before is None, last=last
        ),
        grid=(hi - lo,),
        in_specs=[pl.BlockSpec((slots, qb, qb), lambda i: (0, 0, 0)), tall, tall, stat, stat]
        + [pl.BlockSpec((2 * kvs * 64, rows), lambda i: (0, 0))] * slots
        + ([] if before is None else [whole]),
        out_specs=out_specs,
        out_shape=out_shape,
        scratch_shapes=[pltpu.VMEM((2 * kvs, slots, rows, 64), BF)],
        compiler_params=pltpu.CompilerParams(vmem_limit_bytes=60 * 2**20),
        cost_estimate=pl.CostEstimate(flops=int(4e9) * units, bytes_accessed=int(16e6), transcendentals=0),
    )(*args)


TN = (((0,), (0,)), ((), ()))
TT = (((0,), (1,)), ((), ()))
BLOCK = 256
PIECES = 8
LIMIT = 60 * 2**20


def rotated(values, cosine, sine):
    a, b = values[:32], values[32:]
    return jnp.concatenate([a * cosine - b * sine, b * cosine + a * sine], axis=0)


def flat_rows(ref):
    count, sub, width = ref.shape
    return ref[...].reshape(count * sub, width)


def rms(values):
    return lax.rsqrt(jnp.mean(values * values, axis=-1, keepdims=True) + EPSILON)


def qkv_kernel(x_ref, w_ref, gain_ref, cos_ref, sin_ref, q_ref, kv_ref, wt_scr):
    @pl.when(pl.program_id(0) == 0)
    def _():
        wt_scr[...] = w_ref[:, : wt_scr.shape[0]].T

    source = flat_rows(x_ref).astype(F32)
    hidden = (source * rms(source) * gain_ref[0:1, :]).astype(BF)
    out = mm(wt_scr[...], hidden, NT)
    cosine, sine = cos_ref[...], sin_ref[...]
    for h in range(HEADS):
        part = rotated(out[h * 64 : (h + 1) * 64], cosine, sine)
        q_ref[h * 64 : (h + 1) * 64, :] = (part * (HEAD_DIM**-0.5 * LOG2E)).astype(BF)
    top = HEADS * 64
    for h in range(KV_HEADS):
        part = rotated(out[top + h * 64 : top + (h + 1) * 64], cosine, sine)
        kv_ref[h * 64 : (h + 1) * 64, :] = part.astype(BF)
    kv_ref[KV_HEADS * 64 :, :] = out[top + KV_HEADS * 64 :].astype(BF)


def project_qkv(x, first, gains, cosine, sine):
    count, sub, width = x.shape
    rows = count * sub
    per = BLOCK // sub
    kv2 = 2 * KV_HEADS * HEAD_DIM
    return pl.pallas_call(
        qkv_kernel,
        grid=(rows // BLOCK,),
        in_specs=[
            pl.BlockSpec((per, sub, width), lambda i: (i, 0, 0)),
            pl.BlockSpec(first.shape, lambda i: (0, 0)),
            pl.BlockSpec(gains.shape, lambda i: (0, 0)),
            pl.BlockSpec((32, BLOCK), lambda i: (0, i)),
            pl.BlockSpec((32, BLOCK), lambda i: (0, i)),
        ],
        out_specs=[pl.BlockSpec((width, BLOCK), lambda i: (0, i)), pl.BlockSpec((kv2, BLOCK), lambda i: (0, i))],
        out_shape=[jax.ShapeDtypeStruct((width, rows), BF), jax.ShapeDtypeStruct((kv2, rows), BF)],
        scratch_shapes=[pltpu.VMEM((width + kv2, width), BF)],
        compiler_params=pltpu.CompilerParams(vmem_limit_bytes=LIMIT),
        cost_estimate=pl.CostEstimate(flops=int(6e9), bytes_accessed=int(5e6), transcendentals=0),
    )(x, first, gains, cosine, sine)


def ffn_kernel(
    place_ref, o_ref, x_ref, cot_ref, first_ref, gain_ref,
    gate_own, gate_got, gate_swap, up_own, up_got, up_swap, down_own, down_got, down_swap,
    mixed_ref, dres_ref, datt_ref, rd_ref, keep_gu, send_gu, keep_do, send_do, gg_ref,
    acc_gu, acc_down, acc_out, gate_ref, up_ref, down_ref,
):
    step = pl.program_id(0)
    width = x_ref.shape[2]

    @pl.when(step == 0)
    def _():
        acc_gu[...] = jnp.zeros(acc_gu.shape, F32)
        acc_down[...] = jnp.zeros(acc_down.shape, F32)
        acc_out[...] = jnp.zeros(acc_out.shape, F32)
        gg_ref[...] = jnp.zeros(gg_ref.shape, F32)
        for rank in range(2):

            @pl.when(place_ref[1] == rank)
            def _():
                for ref, own in ((gate_ref, gate_own), (up_ref, up_own), (down_ref, down_own)):
                    n = own.shape[0]
                    ref[rank * n : (rank + 1) * n] = own[...]
                for core in range(2):

                    @pl.when(place_ref[0] == core)
                    def _():
                        for ref, parts in ((gate_ref, (gate_got, gate_swap)), (up_ref, (up_got, up_swap))):
                            n, m = parts[0].shape
                            for k, part in ((core, parts[0]), (1 - core, parts[1])):
                                ref[(1 - rank) * n : (2 - rank) * n, k * m : (k + 1) * m] = part[...]
                        n = down_got.shape[0]
                        for k, part in ((core, down_got), (1 - core, down_swap)):
                            low = (2 * (1 - rank) + k) * n
                            down_ref[low : low + n] = part[...]

    cols = first_ref.shape[1]
    out_w = first_ref[:, cols - width :]
    attended = o_ref[...]
    mixed = attended.astype(BF)
    residual = flat_rows(x_ref).astype(F32) + mm(mixed, out_w, TN)
    scale = rms(residual)
    normed = residual * scale
    gain = gain_ref[1:2, :]
    hidden = (normed * gain).astype(BF)
    gate = mm(hidden, gate_ref[...])
    up = mm(hidden, up_ref[...])
    sig = 0.5 * jnp.tanh(0.5 * gate) + 0.5
    silu = gate * sig
    activated = (silu * up).astype(BF)
    mixed_out = (residual + mm(activated, down_ref[...])).astype(BF)
    mixed_ref[...] = mixed_out.reshape(mixed_ref.shape)
    cot = flat_rows(cot_ref)
    d_act = mm(cot, down_ref[...], NT)
    acc_down[...] += mm(activated, cot, TN)
    d_gate = (d_act * up * sig * (1.0 + gate * (1.0 - sig))).astype(BF)
    d_up = (d_act * silu).astype(BF)
    acc_gu[0] += mm(hidden, d_gate, TN)
    acc_gu[1] += mm(hidden, d_up, TN)
    d_hidden = mm(d_gate, gate_ref[...], NT) + mm(d_up, up_ref[...], NT)
    dn = d_hidden * normed
    gg_ref[...] += jnp.sum(dn.reshape(-1, 8, width), axis=0)
    inner = jnp.mean(dn * gain, axis=-1, keepdims=True)
    d_res = cot.astype(F32) + scale * (d_hidden * gain - normed * inner)
    dres_ref[...] = d_res
    d_low = d_res.astype(BF)
    acc_out[...] += mm(mixed, d_low)
    d_att = mm(out_w, d_low, NT).astype(BF)
    datt_ref[...] = d_att
    prod = d_att.astype(F32) * attended
    for h in range(HEADS):
        rd_ref[h : h + 1, :] = jnp.sum(prod[h * 64 : (h + 1) * 64], axis=0, keepdims=True)
    rd_ref[HEADS:, :] = jnp.zeros((16 - HEADS, rd_ref.shape[1]), F32)

    @pl.when(step == pl.num_programs(0) - 1)
    def _():
        core = place_ref[0]
        half = width // 2
        ff = acc_gu.shape[2]
        for y in range(2):
            for p in range(PIECES):
                rs = slice(y * half + (p // 4) * (half // 2), y * half + (p // 4 + 1) * (half // 2))
                cs = slice((p % 4) * (ff // 4), (p % 4 + 1) * (ff // 4))
                keep_gu[y, p] = acc_gu[core, rs, cs].astype(BF)
                send_gu[y, p] = acc_gu[1 - core, rs, cs].astype(BF)
        down_rows, out_rows = ff // 32, width // 24
        for y in range(2):
            for p in range(PIECES):
                for ref, c in ((keep_do, core), (send_do, 1 - core)):
                    start = pl.multiple_of(y * (ff // 2) + (PIECES * c + p) * down_rows, 16)
                    ref[y, p, :down_rows] = acc_down[pl.ds(start, down_rows), :].astype(BF)
                    start = y * half + jnp.minimum(PIECES * c + p, half // out_rows - 1) * out_rows
                    ref[y, p, down_rows:] = acc_out[pl.ds(pl.multiple_of(start, 8), out_rows), :].astype(BF)


def feed_forward(place, attended, x, cot, first, gains, weights):
    count, sub, width = x.shape
    rows, ff = count * sub, weights[0].shape[1]
    per = BLOCK // sub
    gu = (2, PIECES, width // 4, ff // 4)
    do = (2, PIECES, ff // 32 + width // 24, width)

    def whole(shape):
        return pl.BlockSpec(shape, lambda i: (0,) * len(shape))

    seq = pl.BlockSpec((per, sub, width), lambda i: (i, 0, 0))
    tall = pl.BlockSpec((width, BLOCK), lambda i: (0, i))
    return pl.pallas_call(
        ffn_kernel,
        grid=(rows // BLOCK,),
        in_specs=[
            pl.BlockSpec(memory_space=pltpu.SMEM), tall, seq, seq,
            whole(first.shape), whole(gains.shape), *(whole(w.shape) for w in weights),
        ],
        out_specs=[
            seq, pl.BlockSpec((BLOCK, width), lambda i: (i, 0)), tall, pl.BlockSpec((16, BLOCK), lambda i: (0, i)),
            whole(gu), whole(gu), whole(do), whole(do), whole((8, width)),
        ],
        out_shape=[
            jax.ShapeDtypeStruct(x.shape, BF),
            jax.ShapeDtypeStruct((rows, width), F32),
            jax.ShapeDtypeStruct((width, rows), BF),
            jax.ShapeDtypeStruct((16, rows), F32),
            jax.ShapeDtypeStruct(gu, BF), jax.ShapeDtypeStruct(gu, BF),
            jax.ShapeDtypeStruct(do, BF), jax.ShapeDtypeStruct(do, BF),
            jax.ShapeDtypeStruct((8, width), F32),
        ],
        scratch_shapes=[
            pltpu.VMEM((2, width, ff), F32), pltpu.VMEM((ff, width), F32), pltpu.VMEM((width, width), F32),
            pltpu.VMEM((width, ff), BF), pltpu.VMEM((width, ff), BF), pltpu.VMEM((ff, width), BF),
        ],
        compiler_params=pltpu.CompilerParams(vmem_limit_bytes=LIMIT),
        cost_estimate=pl.CostEstimate(flops=int(32e9), bytes_accessed=int(20e6), transcendentals=0),
    )(place, attended, x, cot, first, gains, *weights)


def back_kernel(*refs, spans):
    place_ref, refs = refs[0], refs[1:]
    dq_refs, refs = refs[: len(spans)], refs[len(spans) :]
    own_ref, got_ref, x_ref, dres_ref, first_ref, gain_ref, cos_ref, sin_ref, gg_ref, dx_ref = refs[:10]
    keep_ref, send_ref, acc, dt_scr, ga_scr, w_scr = refs[10:]
    step = pl.program_id(0)
    width = x_ref.shape[2]
    kv = KV_HEADS * 64
    total = width + 2 * kv

    @pl.when(step == 0)
    def _():
        acc[...] = jnp.zeros(acc.shape, F32)
        ga_scr[...] = jnp.zeros(ga_scr.shape, F32)
        w_scr[...] = first_ref[:, :total].T

    cosine, sine = cos_ref[...], -sin_ref[...]
    for (lo, hi), dq_ref in zip(spans, dq_refs):

        @pl.when((step >= lo) & (step < hi))
        def _():
            for h in range(HEADS):
                part = dq_ref[h * 64 : (h + 1) * 64, :] * (HEAD_DIM**-0.5)
                dt_scr[h * 64 : (h + 1) * 64, :] = rotated(part, cosine, sine).astype(BF)

    d_kv = own_ref[0] + got_ref[...].astype(F32)
    for h in range(KV_HEADS):
        part = d_kv[h * 64 : (h + 1) * 64] * LN2
        dt_scr[width + h * 64 : width + (h + 1) * 64, :] = rotated(part, cosine, sine).astype(BF)
    dt_scr[width + kv :, :] = d_kv[kv:].astype(BF)
    d_t = dt_scr[...]
    source = flat_rows(x_ref).astype(F32)
    scale = rms(source)
    normed = source * scale
    gain = gain_ref[0:1, :]
    hidden = (normed * gain).astype(BF)
    acc[:total] += mm(d_t, hidden)
    d_hidden = mm(d_t, w_scr[...], TN)
    dn = d_hidden * normed
    ga_scr[...] += jnp.sum(dn.reshape(-1, 8, width), axis=0)
    inner = jnp.mean(dn * gain, axis=-1, keepdims=True)
    grad = dres_ref[...] + scale * (d_hidden * gain - normed * inner)
    dx_ref[...] = grad.astype(BF).reshape(dx_ref.shape)

    @pl.when(step == pl.num_programs(0) - 1)
    def _():
        core = place_ref[0]
        acc[total : total + 1, :] = jnp.sum(ga_scr[...], axis=0, keepdims=True)
        acc[total + 1 : total + 2, :] = jnp.sum(gg_ref[...], axis=0, keepdims=True)
        half, deep = width // 2, width // 4
        for ct in range(4):
            for ref, c in ((keep_ref, core), (send_ref, 1 - core)):
                start = pl.multiple_of(c * 512 + ct * 128, 128)
                block = acc[pl.ds(start, 128), :].T.astype(BF)
                for y in range(2):
                    for rh in range(2):
                        low = y * half + rh * deep
                        ref[y, rh * 4 + ct] = block[low : low + deep]


def back_qkv(place, spans, d_query, d_kv, got, x, d_res, first, gains, cosine, sine, gg):
    count, sub, width = x.shape
    rows = count * sub
    per = BLOCK // sub
    kv2 = 2 * KV_HEADS * HEAD_DIM
    piece = (2, PIECES, width // 4, 128)

    def whole(shape):
        return pl.BlockSpec(shape, lambda i: (0,) * len(shape))

    seq = pl.BlockSpec((per, sub, width), lambda i: (i, 0, 0))
    return pl.pallas_call(
        functools.partial(back_kernel, spans=spans),
        grid=(rows // BLOCK,),
        in_specs=[
            pl.BlockSpec(memory_space=pltpu.SMEM),
            *(
                pl.BlockSpec((width, BLOCK), lambda i, lo=lo, hi=hi: (0, jnp.clip(i - lo, 0, hi - lo - 1)))
                for lo, hi in spans
            ),
            pl.BlockSpec((1, kv2, BLOCK), lambda i: (0, 0, i)),
            pl.BlockSpec((kv2, BLOCK), lambda i: (0, i)),
            seq, pl.BlockSpec((BLOCK, width), lambda i: (i, 0)),
            whole(first.shape), whole(gains.shape),
            pl.BlockSpec((32, BLOCK), lambda i: (0, i)), pl.BlockSpec((32, BLOCK), lambda i: (0, i)),
            whole(gg.shape),
        ],
        out_specs=[seq, whole(piece), whole(piece)],
        out_shape=[jax.ShapeDtypeStruct(x.shape, BF), jax.ShapeDtypeStruct(piece, BF), jax.ShapeDtypeStruct(piece, BF)],
        scratch_shapes=[
            pltpu.VMEM((1024, width), F32), pltpu.VMEM((width + kv2, BLOCK), BF), pltpu.VMEM((8, width), F32),
            pltpu.VMEM((width + kv2, width), BF),
        ],
        compiler_params=pltpu.CompilerParams(vmem_limit_bytes=LIMIT),
        cost_estimate=pl.CostEstimate(flops=int(10e9), bytes_accessed=int(10e6), transcendentals=0),
    )(place, *d_query, d_kv, got, x, d_res, first, gains, cosine, sine, gg)


def final_kernel(
    at_ref, gu4, gu_x, gu_c, do4, do_x, do_c, gate_ref, up_ref, down_ref, out_ref
):
    core, xb, z = at_ref[0], at_ref[1], at_ref[2]
    deep, wide = gu4.shape[1:]
    for f in range(2):
        for e in range(2):
            for d in range(4):
                gu = (gu4[d] if e == 0 else gu_x[d]) if f == 0 else gu_c[e * 4 + d]
                do = (do4[d] if e == 0 else do_x[d]) if f == 0 else do_c[e * 4 + d]
                rs = pl.ds(pl.multiple_of((xb ^ e) * deep, 16), deep)
                cs = pl.ds(pl.multiple_of((z ^ d) * wide, 128), wide)
                for c, ref in ((0, gate_ref), (1, up_ref)):

                    @pl.when((core ^ f) == c)
                    def _():
                        ref[rs, cs] = gu.astype(F32)

                m = (core ^ f) * 8 + (xb ^ e) * 4 + (z ^ d)
                rows = down_ref.shape[0] // 16
                down_ref[pl.ds(pl.multiple_of(m * rows, 8), rows), :] = do[:rows].astype(F32)
                few = do.shape[0] - rows

                @pl.when(m < out_ref.shape[0] // few)
                def _():
                    out_ref[pl.ds(pl.multiple_of(m * few, 8), few), :] = do[rows:].astype(F32)


def final_ffn(at, gu4, gu_x, gu_c, do4, do_x, do_c, half, ff, width):
    f32 = lambda *s: jax.ShapeDtypeStruct(s, F32)
    return pl.pallas_call(
        final_kernel,
        in_specs=[pl.BlockSpec(memory_space=pltpu.SMEM)] + [pl.BlockSpec(memory_space=pltpu.VMEM)] * 6,
        out_specs=[pl.BlockSpec(memory_space=pltpu.VMEM)] * 4,
        out_shape=[f32(half, ff), f32(half, ff), f32(ff // 2, width), f32(half, width)],
        compiler_params=pltpu.CompilerParams(vmem_limit_bytes=LIMIT),
        cost_estimate=pl.CostEstimate(flops=int(5e9), bytes_accessed=int(10e6), transcendentals=0),
    )(at, gu4, gu_x, gu_c, do4, do_x, do_c)


def final_t_kernel(at_ref, t4, t_x, t_c, q_ref, k_ref, v_ref, g_ref, whole):
    core, xb, z = at_ref[0], at_ref[1], at_ref[2]
    deep, wide = t4.shape[1:]
    for f in range(2):
        for e in range(2):
            for d in range(4):
                t = (t4[d] if e == 0 else t_x[d]) if f == 0 else t_c[e * 4 + d]
                rs = pl.ds(pl.multiple_of((xb ^ e) * deep, 16), deep)
                cs = pl.ds(pl.multiple_of((core ^ f) * 512 + (z ^ d) * wide, 128), wide)
                whole[rs, cs] = t.astype(F32)
    a = q_ref.shape[1]
    b = a + k_ref.shape[1]
    c = b + v_ref.shape[1]
    q_ref[...] = whole[:, :a]
    k_ref[...] = whole[:, a:b]
    v_ref[...] = whole[:, b:c]
    g_ref[...] = whole[:, c:].T[:8]


def final_t(at, t4, t_x, t_c, half, width, kv_width):
    f32 = lambda *s: jax.ShapeDtypeStruct(s, F32)
    return pl.pallas_call(
        final_t_kernel,
        in_specs=[pl.BlockSpec(memory_space=pltpu.SMEM)] + [pl.BlockSpec(memory_space=pltpu.VMEM)] * 3,
        out_specs=[pl.BlockSpec(memory_space=pltpu.VMEM)] * 4,
        out_shape=[f32(half, width), f32(half, kv_width), f32(half, kv_width), f32(8, half)],
        scratch_shapes=[pltpu.VMEM((half, 1024), F32)],
        compiler_params=pltpu.CompilerParams(vmem_limit_bytes=LIMIT),
        cost_estimate=pl.CostEstimate(flops=int(1e9), bytes_accessed=int(2e6), transcendentals=0),
    )(at, t4, t_x, t_c)


def swap(x, axis, bit):
    n = lax.axis_size(axis)
    return lax.ppermute(x, axis, [(i, i ^ (1 << bit)) for i in range(n)])


def bit_of(axis, bit):
    return (lax.axis_index(axis) >> bit) & 1


def pin(*arrays):
    return lax.optimization_barrier(arrays)


def pick(x, at):
    return lax.dynamic_index_in_dim(x, at, 0, keepdims=False)


def in_order(flag, mine, other, axis):
    return jnp.where(
        flag == 0,
        jnp.concatenate([mine, other], axis=axis),
        jnp.concatenate([other, mine], axis=axis),
    )


def plus(a, b):
    return (a.astype(F32) + b.astype(F32)).astype(BF)


def two_level():
    return lax.axis_size("fsdp") == 2 and lax.axis_size("ctx") == 16


def z_swap(x, by):
    return lax.ppermute(x, "ctx", [(i, i ^ (4 * by)) for i in range(16)])


def z_send(x):
    z = lax.axis_index("ctx") >> 2
    return pick(x, z), [pick(x, z ^ by) for by in range(1, 4)]


def z_pass(pieces):
    return [z_swap(p, by) for by, p in zip(range(1, 4), pieces)]


def z_total(mine, got):
    return sum((g.astype(F32) for g in got), mine.astype(F32)).astype(BF)


def z_join(piece):
    return [piece] + [z_swap(piece, by) for by in range(1, 4)]


def natural_gu(pieces):
    _, a, b = pieces.shape
    return pieces.reshape(2, 4, a, b).transpose(0, 2, 1, 3).reshape(2 * a, 4 * b).astype(F32)


def other_sum(x):
    x = lax.psum_scatter(x.astype(BF), "fsdp", scatter_dimension=0, tiled=True)
    return lax.psum(x, "ctx").astype(F32)


def local(tokens, gain_attn, w_query, w_key, w_value, w_out, gain_ffn, w_gate, w_up, w_down, cotangent):
    seqs, length, width = tokens.shape
    count = lax.axis_size("ctx")
    team = count // seqs
    sub = length // team
    rows = count * sub
    ff = w_gate.shape[1]
    kv_width = KV_HEADS * HEAD_DIM
    qkv_cols = width + 2 * kv_width
    place = lax.axis_index("ctx") % team
    own = gain_attn.shape[0]
    fast = two_level()

    def move(x):
        return lax.all_to_all(x.reshape(count, sub, width), "ctx", 0, 0, tiled=True)

    x = move(tokens)
    gain_rows = jnp.zeros((8, ff), BF).at[0, :own].set(gain_attn).at[1, :own].set(gain_ffn)
    first = jnp.concatenate([jnp.concatenate([w_query, w_key, w_value, w_out], axis=1), gain_rows], axis=0)
    if fast:
        core, rank = bit_of("ctx", 0), bit_of("fsdp", 0)

        def halved(shard, axis):
            half = shard.shape[axis] // 2
            return lax.dynamic_slice_in_dim(shard, core * half, half, axis)

        def other_shard(got, axis):
            return in_order(core, got, swap(got, "ctx", 0), axis)

        got = swap(halved(first, 1), "fsdp", 0)
        other = other_shard(got, 1)
        gains = in_order(rank, first[own : own + 2, :own], other[own : own + 2, :own], 1).astype(F32)
        first = in_order(rank, first[:own], other[:own], 0)
        gate_half, up_half, down_half, got = pin(halved(w_gate, 1), halved(w_up, 1), halved(w_down, 0), got)
        gate_got, up_got, down_got = (swap(h, "fsdp", 0) for h in (gate_half, up_half, down_half))
    else:
        first = lax.all_gather(first, "fsdp", axis=0)
        gains = first[:, own : own + 2, :own].transpose(1, 0, 2).reshape(2, width).astype(F32)
        first = first[:, :own].reshape(width, first.shape[2])
        gate_w, up_w, down_w = (lax.all_gather(w, "fsdp", axis=0, tiled=True) for w in (w_gate, w_up, w_down))
    gains = jnp.pad(gains, ((0, 6), (0, 0)))

    row = jnp.arange(rows, dtype=jnp.int32)
    position = (row // sub) * length + place * sub + row % sub
    frequency = THETA ** (-jnp.arange(HEAD_DIM // 2, dtype=F32) * 2.0 / HEAD_DIM)
    angles = frequency[:, None] * position.astype(F32)[None, :]
    cosine, sine = jnp.cos(angles), jnp.sin(angles)
    groups = [[t * team + p for p in range(team)] for t in range(seqs)]
    slots = jnp.stack([place, 1 - place]) if team == 2 else jnp.arange(team)
    block_row = jnp.arange(BLOCK, dtype=jnp.int32)
    base = (block_row // sub) * length + block_row % sub
    key_pos = base[None, :] + slots[:, None] * sub
    query_pos = base + place * sub
    bias = jnp.where(key_pos[:, :, None] <= query_pos[None, None, :], 0.0, NEGATIVE).astype(F32)
    flags = jnp.stack([core, rank]) if fast else jnp.zeros((2,), jnp.int32)

    x, cot_send = pin(x, cotangent)
    cot = move(cot_send)
    query, kv_own = project_qkv(x, first, gains, cosine, sine)
    if fast:
        kv_own, gate_got = pin(kv_own, gate_got)
    if team == 2:
        kv_all = (kv_own, swap(kv_own, "ctx", 0))
    else:
        kv_all = lax.all_gather(kv_own, "ctx", axis=0, axis_index_groups=groups)
        kv_all = tuple(kv_all[s] for s in range(team))
    attended, log_total = attn_fwd(bias, query, kv_all)
    if fast:
        attended, cot, *gots = pin(attended, cot, gate_got, up_got, down_got)
        gots = [(got, swap(got, "ctx", 0)) for got in gots]
        weights = [a for own_w, two in zip((w_gate, w_up, w_down), gots) for a in (own_w, *two)]
    else:
        attended, cot = pin(attended, cot)
        low, side = width // 2, ff // 2
        weights = [a for w in (gate_w, up_w) for a in (w[:low], w[low:, :side], w[low:, side:])]
        weights += [down_w[:side], down_w[side : side + side // 2], down_w[side + side // 2 :]]
    mixed, d_res, d_att, row_dot, keep_gu, send_gu, keep_do, send_do, gain_sum = feed_forward(
        flags, attended, x, cot, first, gains, weights
    )
    mixed_out = move(mixed)

    n = rows // BLOCK
    spans = ((0, n - 1), (n - 1, n))
    part = functools.partial(attn_bwd, bias, query, kv_all, d_att, log_total, row_dot)
    if fast:
        x_bit = bit_of("ctx", 1)
        got_gu, got_do = swap(send_gu, "ctx", 0), swap(send_do, "ctx", 0)
        gu, do = plus(keep_gu, got_gu), plus(keep_do, got_do)
        gu = gu.reshape((2, 2, 4) + gu.shape[2:]).swapaxes(0, 1)
        keep_gu, send_gu = pick(gu, x_bit), pick(gu, 1 - x_bit)
        keep_do, send_do = pick(do, rank), pick(do, 1 - rank)
        send_gu, send_do, row_dot = pin(send_gu, send_do, row_dot)
        part = functools.partial(attn_bwd, bias, query, kv_all, d_att, log_total, row_dot)
        got_gu, got_do = swap(send_gu, "ctx", 1), swap(send_do, "fsdp", 0)
        dq_a, before = part(*spans[0])
        got_gu, got_do, mixed_out, before = pin(got_gu, got_do, mixed_out, before)
        gu, do = plus(keep_gu, got_gu), plus(keep_do, got_do)
        do = do.reshape((2, 4) + do.shape[1:])
        keep_gu, send_gu = pick(gu, rank), pick(gu, 1 - rank)
        keep_do, send_do = pick(do, x_bit), pick(do, 1 - x_bit)
        send_gu, send_do, before = pin(send_gu, send_do, before)
        got_gu, got_do = swap(send_gu, "fsdp", 0), swap(send_do, "ctx", 1)
        dq_b, d_kv, d_kv_low = part(*spans[1], before=before, last=True)
        got_gu, got_do, d_kv_low, dq_b = pin(got_gu, got_do, d_kv_low, dq_b)
        gu, do = plus(keep_gu, got_gu), plus(keep_do, got_do)
    else:
        dq_a, before = part(*spans[0])
        dq_b, d_kv, d_kv_low = part(*spans[1], before=before, last=True)
    if team == 2:
        own_kv, got_kv = d_kv, swap(d_kv_low.reshape(2 * kv_width, rows), "ctx", 0)
    else:
        own_kv = lax.psum_scatter(d_kv_low, "ctx", scatter_dimension=0, axis_index_groups=groups)
        own_kv, got_kv = own_kv.astype(F32)[None], jnp.zeros((2 * kv_width, rows), BF)
    if fast:
        z_gu, z_do = z_send(gu), z_send(do)
        send_pin = pin(own_kv, got_kv, *z_gu[1], *z_do[1])
        own_kv, got_kv = send_pin[:2]
        z_gu, z_do = (z_gu[0], send_pin[2:5]), (z_do[0], send_pin[5:])
        z_got = [z_pass(z_gu[1]), z_pass(z_do[1])]
    d_x, keep_t, send_t = back_qkv(
        flags, spans, (dq_a, dq_b), own_kv, got_kv, x, d_res, first, gains, cosine, sine, gain_sum
    )
    if fast:
        d_x, keep_t, send_t, *got = pin(d_x, keep_t, send_t, *z_got[0], *z_got[1])
        gu, do = z_total(z_gu[0], got[:3]), z_total(z_do[0], got[3:])
    grad_tokens = move(d_x)
    if fast:
        gu_four, do_four = z_join(gu), z_join(do)
        t = plus(keep_t, swap(send_t, "ctx", 0))
        t = plus(pick(t, rank), swap(pick(t, 1 - rank), "fsdp", 0))
        t = t.reshape((2, 4) + t.shape[1:])
        t = plus(pick(t, x_bit), swap(pick(t, 1 - x_bit), "ctx", 1))
        keep_t, send_t = z_send(t)
        t_got = z_pass(send_t)
        *t_got, grad_tokens, d0, d1, d2, g0, g1, g2 = pin(*t_got, grad_tokens, *do_four[1:], *gu_four[1:])
        t_four = z_join(z_total(keep_t, t_got))
        do_four = jnp.stack([do_four[0], d0, d1, d2])
        gu_four = jnp.stack([gu_four[0], g0, g1, g2])
        do_x, gu_x = swap(do_four, "ctx", 1), swap(gu_four, "ctx", 1)
        t_four = jnp.stack(t_four)
        t_x = swap(t_four, "ctx", 1)
        t_x, do_x, gu_x = pin(t_x, do_x, gu_x)
        gu_c = swap(jnp.concatenate([gu_four, gu_x], axis=0), "ctx", 0)
        do_c = swap(jnp.concatenate([do_four, do_x], axis=0), "ctx", 0)
        t_c = swap(jnp.concatenate([t_four, t_x], axis=0), "ctx", 0)
        at = jnp.stack([core, x_bit, lax.axis_index("ctx") >> 2])
        own_query, own_key, own_value, own_gains = final_t(at, t_four, t_x, t_c, width // 2, width, kv_width)
        own_gate, own_up, own_down, own_out = final_ffn(
            at, gu_four, gu_x, gu_c, do_four, do_x, do_c, width // 2, ff, width
        )
    else:
        pair = jnp.stack([keep_gu, send_gu])
        gate, up = (jnp.concatenate([natural_gu(pair[c, y]) for y in range(2)], axis=0) for c in range(2))
        do = jnp.stack([keep_do, send_do], axis=1).reshape((32,) + keep_do.shape[2:])
        deep = ff // 32
        own_gate, own_up = other_sum(gate), other_sum(up)
        own_down = other_sum(do[:, :deep].reshape(ff, width))
        out = do[:, deep:].reshape((2, -1, width))[:, : width // 2]
        own_out = other_sum(out.reshape(width, width))
        pair = jnp.stack([keep_t, send_t])
        t = [jnp.concatenate([natural_gu(pair[c, y]) for c in range(2)], axis=1) for y in range(2)]
        own_t = other_sum(jnp.concatenate(t, axis=0))
        own_query, own_key = own_t[:, :width], own_t[:, width : width + kv_width]
        own_value, own_gains = own_t[:, width + kv_width : qkv_cols], own_t[:, qkv_cols:].T
    return (
        mixed_out.reshape(tokens.shape),
        grad_tokens.reshape(tokens.shape),
        own_gains[0],
        own_query,
        own_key,
        own_value,
        own_out,
        own_gains[1],
        own_gate,
        own_up,
        own_down,
    )


def solution(mesh):
    rows, flat, seq = P("fsdp", None), P("fsdp"), P("fsdp", "ctx", None)
    return jax.shard_map(
        local,
        mesh=mesh,
        in_specs=(seq, flat, rows, rows, rows, rows, flat, rows, rows, rows, seq),
        out_specs=(seq, seq, flat, rows, rows, rows, rows, flat, rows, rows, rows),
        check_vma=False,
    )
```

```python
import functools

import jax
import jax.numpy as jnp
from jax import lax
from jax.experimental import pallas as pl
from jax.experimental.pallas import tpu as pltpu
from jax.sharding import PartitionSpec as P

HEADS = 9
KV_HEADS = 3
HEAD_DIM = 64
EPSILON = 1e-05
THETA = 100000.0
NEGATIVE = -1e30
LOG2E = 1.4426950408889634
LN2 = 0.6931471805599453
F32=jnp.float32; BF=jnp.bfloat16
NT=(((1,),(1,)),((),()))
NN=(((1,),(0,)),((),()))
def mm(a,b,dims=NN):
    return lax.dot_general(a,b,dims,preferred_element_type=F32)

def heads_of(ref, kv, group):
    return jnp.concatenate([ref[(kv*group+h)*64:(kv*group+h+1)*64,:] for h in range(group)],axis=1)

def fwd_kernel(bias_ref, q_ref, *refs, kvs, group, slots, rows, qb):
    kv_ref, (o_ref, lse_ref, k_scr, m_scr, acc_scr)=refs[:slots], refs[slots:]
    i=pl.program_id(0)
    kw=kvs*64
    @pl.when(i==0)
    def _():
        for s in range(slots):
            for h in range(kvs):
                k_scr[h,s]=kv_ref[s][h*64:(h+1)*64,:].T
    qs=[heads_of(q_ref,h,group) for h in range(kvs)]
    width=group*qb
    m_scr[...]=jnp.full(m_scr.shape,-1e30,F32)
    acc_scr[...]=jnp.zeros(acc_scr.shape,F32)
    ones=jnp.ones((8,slots*qb),BF)
    def chunk(c, masked):
        off=pl.multiple_of(c*qb,qb)
        for h in range(kvs):
            k=jnp.concatenate([k_scr[h,s,pl.ds(off,qb),:] for s in range(slots)],axis=0)
            v=jnp.concatenate([kv_ref[s][kw+h*64:kw+(h+1)*64,pl.ds(off,qb)] for s in range(slots)],axis=1)
            v=jnp.concatenate([v,ones],axis=0)
            st=mm(k,qs[h])
            if masked:
                b=bias_ref[...].reshape(slots*qb,qb)
                st=st+jnp.concatenate([b]*group,axis=1)
            m_old=m_scr[h:h+1,:]
            m_new=jnp.maximum(m_old,jnp.max(st,axis=0,keepdims=True))
            p=jnp.exp2(st-m_new).astype(BF)
            acc_scr[h]=acc_scr[h]*jnp.exp2(m_old-m_new)+mm(v,p)
            m_scr[h:h+1,:]=m_new
    def body(c,_):
        chunk(c,False); return 0
    lax.fori_loop(0,i,body,0)
    chunk(i,True)
    for h in range(kvs):
        acc=acc_scr[h]
        tot=acc[64:65,:]
        o=acc[:64,:]*(1.0/tot)
        lse=m_scr[h:h+1,:]+jnp.log2(tot)
        for g in range(group):
            r=h*group+g
            o_ref[r*64:(r+1)*64,:]=o[:,g*qb:(g+1)*qb]
            lse_ref[r:r+1,:]=lse[:,g*qb:(g+1)*qb]

def attn_fwd(bias, qT, kvT, kvs=3, group=3, qb=256):
    slots,rows=len(kvT),kvT[0].shape[1]
    n=rows//qb
    heads=kvs*group
    return pl.pallas_call(
        functools.partial(fwd_kernel,kvs=kvs,group=group,slots=slots,rows=rows,qb=qb),
        grid=(n,),
        in_specs=[pl.BlockSpec((slots,qb,qb),lambda i:(0,0,0)),
                  pl.BlockSpec((heads*64,qb),lambda i:(0,i)),
                  *[pl.BlockSpec((2*kvs*64,rows),lambda i:(0,0))]*slots],
        out_specs=[pl.BlockSpec((heads*64,qb),lambda i:(0,i)),
                   pl.BlockSpec((16,qb),lambda i:(0,i))],
        out_shape=[jax.ShapeDtypeStruct((heads*64,rows),F32),jax.ShapeDtypeStruct((16,rows),F32)],
        scratch_shapes=[pltpu.VMEM((kvs,slots,rows,64),BF),pltpu.VMEM((8,group*qb),F32),
                        pltpu.VMEM((kvs,72,group*qb),F32)],
        compiler_params=pltpu.CompilerParams(vmem_limit_bytes=56*2**20),
        cost_estimate=pl.CostEstimate(flops=int(25e9),bytes_accessed=int(8e6),transcendentals=int(1e7)),
    )(bias,qT,*kvT)

def bwd_kernel(*refs, kvs, group, slots, qb, lo, first, last):
    bias_ref, q_ref, do_ref, lse_ref, rd_ref = refs[:5]
    kv_ref, refs = refs[5 : 5 + slots], refs[5 + slots :]
    if not first:
        before_ref, refs = refs[0], refs[1:]
    if last:
        dq_ref, dkv_ref, low_ref, kv_scr = refs
    else:
        dq_ref, dkv_ref, kv_scr = refs
    step = pl.program_id(0)
    kw = kvs * 64

    @pl.when(step == 0)
    def _():
        for s in range(slots):
            for h in range(2 * kvs):
                kv_scr[h, s] = kv_ref[s][h * 64 : (h + 1) * 64, :].T
        dkv_ref[...] = jnp.zeros(dkv_ref.shape, F32) if first else before_ref[...]

    dq_ref[...] = jnp.zeros(dq_ref.shape, F32)
    qs = [heads_of(q_ref, h, group) for h in range(kvs)]
    dos = [heads_of(do_ref, h, group) for h in range(kvs)]

    def along(ref, h):
        return jnp.concatenate([ref[h * group + g : h * group + g + 1, :] for g in range(group)], axis=1)

    lses = [along(lse_ref, h) for h in range(kvs)]
    rds = [along(rd_ref, h) for h in range(kvs)]

    def chunk(c, masked):
        off = pl.multiple_of(c * qb, qb)
        for h in range(kvs):
            k = jnp.concatenate([kv_scr[h, s, pl.ds(off, qb), :] for s in range(slots)], axis=0)
            v = jnp.concatenate([kv_scr[kvs + h, s, pl.ds(off, qb), :] for s in range(slots)], axis=0)
            k_t = jnp.concatenate([kv_ref[s][h * 64 : (h + 1) * 64, pl.ds(off, qb)] for s in range(slots)], axis=1)
            st = mm(k, qs[h])
            if masked:
                st = st + jnp.concatenate([bias_ref[...].reshape(slots * qb, qb)] * group, axis=1)
            p = jnp.exp2(st - lses[h])
            dp = mm(v, dos[h])
            ds = (p * (dp - rds[h])).astype(BF)
            dk = mm(qs[h], ds, NT)
            dv = mm(dos[h], p.astype(BF), NT)
            dq = mm(k_t, ds)
            for s in range(slots):
                dkv_ref[s, h * 64 : (h + 1) * 64, pl.ds(off, qb)] += dk[:, s * qb : (s + 1) * qb]
                dkv_ref[s, kw + h * 64 : kw + (h + 1) * 64, pl.ds(off, qb)] += dv[:, s * qb : (s + 1) * qb]
            for g in range(group):
                r = h * group + g
                dq_ref[r * 64 : (r + 1) * 64, :] += dq[:, g * qb : (g + 1) * qb]

    def body(c, carry):
        chunk(c, False)
        return carry

    lax.fori_loop(0, step + lo, body, 0)
    chunk(step + lo, True)
    if last:

        @pl.when(step == pl.num_programs(0) - 1)
        def _():
            low_ref[...] = dkv_ref[slots - low_ref.shape[0] :].astype(BF)


def attn_bwd(bias, q_t, kv_t, do_t, lse, rd, lo, hi, before=None, last=False, kvs=3, group=3, qb=256):
    slots, rows = len(kv_t), kv_t[0].shape[1]
    width = kvs * group * 64
    whole = pl.BlockSpec((slots, 2 * kvs * 64, rows), lambda i: (0, 0, 0))
    tall = pl.BlockSpec((width, qb), lambda i: (0, i + lo))
    stat = pl.BlockSpec((16, qb), lambda i: (0, i + lo))
    out_specs = [pl.BlockSpec((width, qb), lambda i: (0, i)), whole]
    out_shape = [
        jax.ShapeDtypeStruct((width, (hi - lo) * qb), F32),
        jax.ShapeDtypeStruct((slots, 2 * kvs * 64, rows), F32),
    ]
    if last:
        sent = (1 if slots == 2 else slots, 2 * kvs * 64, rows)
        out_specs.append(pl.BlockSpec(sent, lambda i: (0, 0, 0)))
        out_shape.append(jax.ShapeDtypeStruct(sent, BF))
    args = (bias, q_t, do_t, lse, rd, *kv_t) + (() if before is None else (before,))
    units = sum(range(lo + 1, hi + 1))
    return pl.pallas_call(
        functools.partial(
            bwd_kernel, kvs=kvs, group=group, slots=slots, qb=qb, lo=lo, first=before is None, last=last
        ),
        grid=(hi - lo,),
        in_specs=[pl.BlockSpec((slots, qb, qb), lambda i: (0, 0, 0)), tall, tall, stat, stat]
        + [pl.BlockSpec((2 * kvs * 64, rows), lambda i: (0, 0))] * slots
        + ([] if before is None else [whole]),
        out_specs=out_specs,
        out_shape=out_shape,
        scratch_shapes=[pltpu.VMEM((2 * kvs, slots, rows, 64), BF)],
        compiler_params=pltpu.CompilerParams(vmem_limit_bytes=60 * 2**20),
        cost_estimate=pl.CostEstimate(flops=int(4e9) * units, bytes_accessed=int(16e6), transcendentals=0),
    )(*args)


TN = (((0,), (0,)), ((), ()))
TT = (((0,), (1,)), ((), ()))
BLOCK = 256
FF_BLOCK = 512
PIECES = 8
LIMIT = 60 * 2**20


def rotated(values, cosine, sine):
    a, b = values[:32], values[32:]
    return jnp.concatenate([a * cosine - b * sine, b * cosine + a * sine], axis=0)


def flat_rows(ref):
    count, sub, width = ref.shape
    return ref[...].reshape(count * sub, width)


def rms(values):
    return lax.rsqrt(jnp.mean(values * values, axis=-1, keepdims=True) + EPSILON)


def qkv_kernel(x_ref, w_ref, gain_ref, cos_ref, sin_ref, q_ref, kv_ref, wt_scr):
    @pl.when(pl.program_id(0) == 0)
    def _():
        wt_scr[...] = w_ref[:, : wt_scr.shape[0]].T

    source = flat_rows(x_ref).astype(F32)
    hidden = (source * rms(source) * gain_ref[0:1, :]).astype(BF)
    out = mm(wt_scr[...], hidden, NT)
    cosine, sine = cos_ref[...], sin_ref[...]
    for h in range(HEADS):
        part = rotated(out[h * 64 : (h + 1) * 64], cosine, sine)
        q_ref[h * 64 : (h + 1) * 64, :] = (part * (HEAD_DIM**-0.5 * LOG2E)).astype(BF)
    top = HEADS * 64
    for h in range(KV_HEADS):
        part = rotated(out[top + h * 64 : top + (h + 1) * 64], cosine, sine)
        kv_ref[h * 64 : (h + 1) * 64, :] = part.astype(BF)
    kv_ref[KV_HEADS * 64 :, :] = out[top + KV_HEADS * 64 :].astype(BF)


def project_qkv(x, first, gains, cosine, sine):
    count, sub, width = x.shape
    rows = count * sub
    per = BLOCK // sub
    kv2 = 2 * KV_HEADS * HEAD_DIM
    return pl.pallas_call(
        qkv_kernel,
        grid=(rows // BLOCK,),
        in_specs=[
            pl.BlockSpec((per, sub, width), lambda i: (i, 0, 0)),
            pl.BlockSpec(first.shape, lambda i: (0, 0)),
            pl.BlockSpec(gains.shape, lambda i: (0, 0)),
            pl.BlockSpec((32, BLOCK), lambda i: (0, i)),
            pl.BlockSpec((32, BLOCK), lambda i: (0, i)),
        ],
        out_specs=[pl.BlockSpec((width, BLOCK), lambda i: (0, i)), pl.BlockSpec((kv2, BLOCK), lambda i: (0, i))],
        out_shape=[jax.ShapeDtypeStruct((width, rows), BF), jax.ShapeDtypeStruct((kv2, rows), BF)],
        scratch_shapes=[pltpu.VMEM((width + kv2, width), BF)],
        compiler_params=pltpu.CompilerParams(vmem_limit_bytes=LIMIT),
        cost_estimate=pl.CostEstimate(flops=int(6e9), bytes_accessed=int(5e6), transcendentals=0),
    )(x, first, gains, cosine, sine)


def ffn_kernel(
    place_ref, o_ref, x_ref, cot_ref, first_ref, gain_ref,
    gate_own, gate_got, gate_swap, up_own, up_got, up_swap, down_own, down_got, down_swap,
    mixed_ref, dres_ref, datt_ref, rd_ref, keep_gu, send_gu, keep_do, send_do, gg_ref,
    acc_gu, acc_down, acc_out, gate_ref, up_ref, down_ref,
):
    step = pl.program_id(0)
    width = x_ref.shape[2]

    @pl.when(step == 0)
    def _():
        acc_gu[...] = jnp.zeros(acc_gu.shape, F32)
        acc_down[...] = jnp.zeros(acc_down.shape, F32)
        acc_out[...] = jnp.zeros(acc_out.shape, F32)
        gg_ref[...] = jnp.zeros(gg_ref.shape, F32)
        for rank in range(2):

            @pl.when(place_ref[1] == rank)
            def _():
                for ref, own in ((gate_ref, gate_own), (up_ref, up_own), (down_ref, down_own)):
                    n = own.shape[0]
                    ref[rank * n : (rank + 1) * n] = own[...]
                for core in range(2):

                    @pl.when(place_ref[0] == core)
                    def _():
                        for ref, parts in ((gate_ref, (gate_got, gate_swap)), (up_ref, (up_got, up_swap))):
                            n, m = parts[0].shape
                            for k, part in ((core, parts[0]), (1 - core, parts[1])):
                                ref[(1 - rank) * n : (2 - rank) * n, k * m : (k + 1) * m] = part[...]
                        n = down_got.shape[0]
                        for k, part in ((core, down_got), (1 - core, down_swap)):
                            low = (2 * (1 - rank) + k) * n
                            down_ref[low : low + n] = part[...]

    cols = first_ref.shape[1]
    out_w = first_ref[:, cols - width :]
    attended = o_ref[...]
    mixed = attended.astype(BF)
    residual = flat_rows(x_ref).astype(F32) + mm(mixed, out_w, TN)
    scale = rms(residual)
    normed = residual * scale
    gain = gain_ref[1:2, :]
    hidden = (normed * gain).astype(BF)
    gate = mm(hidden, gate_ref[...])
    up = mm(hidden, up_ref[...])
    sig = 0.5 * jnp.tanh(0.5 * gate) + 0.5
    silu = gate * sig
    activated = (silu * up).astype(BF)
    mixed_out = (residual + mm(activated, down_ref[...])).astype(BF)
    mixed_ref[...] = mixed_out.reshape(mixed_ref.shape)
    cot = flat_rows(cot_ref)
    d_act = mm(cot, down_ref[...], NT)
    acc_down[...] += mm(activated, cot, TN)
    d_gate = (d_act * up * sig * (1.0 + gate * (1.0 - sig))).astype(BF)
    d_up = (d_act * silu).astype(BF)
    acc_gu[0] += mm(hidden, d_gate, TN)
    acc_gu[1] += mm(hidden, d_up, TN)
    d_hidden = mm(d_gate, gate_ref[...], NT) + mm(d_up, up_ref[...], NT)
    dn = d_hidden * normed
    gg_ref[...] += jnp.sum(dn.reshape(-1, 8, width), axis=0)
    inner = jnp.mean(dn * gain, axis=-1, keepdims=True)
    d_res = cot.astype(F32) + scale * (d_hidden * gain - normed * inner)
    dres_ref[...] = d_res
    d_low = d_res.astype(BF)
    acc_out[...] += mm(mixed, d_low)
    d_att = mm(out_w, d_low, NT).astype(BF)
    datt_ref[...] = d_att
    prod = d_att.astype(F32) * attended
    for h in range(HEADS):
        rd_ref[h : h + 1, :] = jnp.sum(prod[h * 64 : (h + 1) * 64], axis=0, keepdims=True)
    rd_ref[HEADS:, :] = jnp.zeros((16 - HEADS, rd_ref.shape[1]), F32)

    @pl.when(step == pl.num_programs(0) - 1)
    def _():
        core = place_ref[0]
        half = width // 2
        ff = acc_gu.shape[2]
        for y in range(2):
            for p in range(PIECES):
                rs = slice(y * half + (p // 4) * (half // 2), y * half + (p // 4 + 1) * (half // 2))
                cs = slice((p % 4) * (ff // 4), (p % 4 + 1) * (ff // 4))
                keep_gu[y, p] = acc_gu[core, rs, cs].astype(BF)
                send_gu[y, p] = acc_gu[1 - core, rs, cs].astype(BF)
        down_rows, out_rows = ff // 32, width // 24
        for y in range(2):
            for p in range(PIECES):
                for ref, c in ((keep_do, core), (send_do, 1 - core)):
                    start = pl.multiple_of(y * (ff // 2) + (PIECES * c + p) * down_rows, 16)
                    ref[y, p, :down_rows] = acc_down[pl.ds(start, down_rows), :].astype(BF)
                    start = y * half + jnp.minimum(PIECES * c + p, half // out_rows - 1) * out_rows
                    ref[y, p, down_rows:] = acc_out[pl.ds(pl.multiple_of(start, 8), out_rows), :].astype(BF)


def feed_forward(place, attended, x, cot, first, gains, weights):
    count, sub, width = x.shape
    rows, ff = count * sub, weights[0].shape[1]
    per = FF_BLOCK // sub
    gu = (2, PIECES, width // 4, ff // 4)
    do = (2, PIECES, ff // 32 + width // 24, width)

    def whole(shape):
        return pl.BlockSpec(shape, lambda i: (0,) * len(shape), pipeline_mode=pl.Buffered(1))

    seq = pl.BlockSpec((per, sub, width), lambda i: (i, 0, 0))
    tall = pl.BlockSpec((width, FF_BLOCK), lambda i: (0, i))
    return pl.pallas_call(
        ffn_kernel,
        grid=(rows // FF_BLOCK,),
        in_specs=[
            pl.BlockSpec(memory_space=pltpu.SMEM), tall, seq, seq,
            whole(first.shape), whole(gains.shape), *(whole(w.shape) for w in weights),
        ],
        out_specs=[
            seq, pl.BlockSpec((FF_BLOCK, width), lambda i: (i, 0)), tall, pl.BlockSpec((16, FF_BLOCK), lambda i: (0, i)),
            whole(gu), whole(gu), whole(do), whole(do), whole((8, width)),
        ],
        out_shape=[
            jax.ShapeDtypeStruct(x.shape, BF),
            jax.ShapeDtypeStruct((rows, width), F32),
            jax.ShapeDtypeStruct((width, rows), BF),
            jax.ShapeDtypeStruct((16, rows), F32),
            jax.ShapeDtypeStruct(gu, BF), jax.ShapeDtypeStruct(gu, BF),
            jax.ShapeDtypeStruct(do, BF), jax.ShapeDtypeStruct(do, BF),
            jax.ShapeDtypeStruct((8, width), F32),
        ],
        scratch_shapes=[
            pltpu.VMEM((2, width, ff), F32), pltpu.VMEM((ff, width), F32), pltpu.VMEM((width, width), F32),
            pltpu.VMEM((width, ff), BF), pltpu.VMEM((width, ff), BF), pltpu.VMEM((ff, width), BF),
        ],
        compiler_params=pltpu.CompilerParams(vmem_limit_bytes=LIMIT),
        cost_estimate=pl.CostEstimate(flops=int(32e9), bytes_accessed=int(20e6), transcendentals=0),
    )(place, attended, x, cot, first, gains, *weights)


def back_kernel(*refs, spans):
    place_ref, refs = refs[0], refs[1:]
    dq_refs, refs = refs[: len(spans)], refs[len(spans) :]
    own_ref, got_ref, x_ref, dres_ref, first_ref, gain_ref, cos_ref, sin_ref, gg_ref, dx_ref = refs[:10]
    keep_ref, send_ref, acc, dt_scr, ga_scr, w_scr = refs[10:]
    step = pl.program_id(0)
    width = x_ref.shape[2]
    kv = KV_HEADS * 64
    total = width + 2 * kv

    @pl.when(step == 0)
    def _():
        acc[...] = jnp.zeros(acc.shape, F32)
        ga_scr[...] = jnp.zeros(ga_scr.shape, F32)
        w_scr[...] = first_ref[:, :total].T

    cosine, sine = cos_ref[...], -sin_ref[...]
    for (lo, hi), dq_ref in zip(spans, dq_refs):

        @pl.when((step >= lo) & (step < hi))
        def _():
            for h in range(HEADS):
                part = dq_ref[h * 64 : (h + 1) * 64, :] * (HEAD_DIM**-0.5)
                dt_scr[h * 64 : (h + 1) * 64, :] = rotated(part, cosine, sine).astype(BF)

    d_kv = own_ref[0] + got_ref[...].astype(F32)
    for h in range(KV_HEADS):
        part = d_kv[h * 64 : (h + 1) * 64] * LN2
        dt_scr[width + h * 64 : width + (h + 1) * 64, :] = rotated(part, cosine, sine).astype(BF)
    dt_scr[width + kv :, :] = d_kv[kv:].astype(BF)
    d_t = dt_scr[...]
    source = flat_rows(x_ref).astype(F32)
    scale = rms(source)
    normed = source * scale
    gain = gain_ref[0:1, :]
    hidden = (normed * gain).astype(BF)
    acc[:total] += mm(d_t, hidden)
    d_hidden = mm(d_t, w_scr[...], TN)
    dn = d_hidden * normed
    ga_scr[...] += jnp.sum(dn.reshape(-1, 8, width), axis=0)
    inner = jnp.mean(dn * gain, axis=-1, keepdims=True)
    grad = dres_ref[...] + scale * (d_hidden * gain - normed * inner)
    dx_ref[...] = grad.astype(BF).reshape(dx_ref.shape)

    @pl.when(step == pl.num_programs(0) - 1)
    def _():
        core = place_ref[0]
        acc[total : total + 1, :] = jnp.sum(ga_scr[...], axis=0, keepdims=True)
        acc[total + 1 : total + 2, :] = jnp.sum(gg_ref[...], axis=0, keepdims=True)
        half, deep = width // 2, width // 4
        for ct in range(4):
            for ref, c in ((keep_ref, core), (send_ref, 1 - core)):
                start = pl.multiple_of(c * 512 + ct * 128, 128)
                block = acc[pl.ds(start, 128), :].T.astype(BF)
                for y in range(2):
                    for rh in range(2):
                        low = y * half + rh * deep
                        ref[y, rh * 4 + ct] = block[low : low + deep]


def back_qkv(place, spans, d_query, d_kv, got, x, d_res, first, gains, cosine, sine, gg):
    count, sub, width = x.shape
    rows = count * sub
    per = BLOCK // sub
    kv2 = 2 * KV_HEADS * HEAD_DIM
    piece = (2, PIECES, width // 4, 128)

    def whole(shape):
        return pl.BlockSpec(shape, lambda i: (0,) * len(shape))

    seq = pl.BlockSpec((per, sub, width), lambda i: (i, 0, 0))
    return pl.pallas_call(
        functools.partial(back_kernel, spans=spans),
        grid=(rows // BLOCK,),
        in_specs=[
            pl.BlockSpec(memory_space=pltpu.SMEM),
            *(
                pl.BlockSpec((width, BLOCK), lambda i, lo=lo, hi=hi: (0, jnp.clip(i - lo, 0, hi - lo - 1)))
                for lo, hi in spans
            ),
            pl.BlockSpec((1, kv2, BLOCK), lambda i: (0, 0, i)),
            pl.BlockSpec((kv2, BLOCK), lambda i: (0, i)),
            seq, pl.BlockSpec((BLOCK, width), lambda i: (i, 0)),
            whole(first.shape), whole(gains.shape),
            pl.BlockSpec((32, BLOCK), lambda i: (0, i)), pl.BlockSpec((32, BLOCK), lambda i: (0, i)),
            whole(gg.shape),
        ],
        out_specs=[seq, whole(piece), whole(piece)],
        out_shape=[jax.ShapeDtypeStruct(x.shape, BF), jax.ShapeDtypeStruct(piece, BF), jax.ShapeDtypeStruct(piece, BF)],
        scratch_shapes=[
            pltpu.VMEM((1024, width), F32), pltpu.VMEM((width + kv2, BLOCK), BF), pltpu.VMEM((8, width), F32),
            pltpu.VMEM((width + kv2, width), BF),
        ],
        compiler_params=pltpu.CompilerParams(vmem_limit_bytes=LIMIT),
        cost_estimate=pl.CostEstimate(flops=int(10e9), bytes_accessed=int(10e6), transcendentals=0),
    )(place, *d_query, d_kv, got, x, d_res, first, gains, cosine, sine, gg)


def final_kernel(
    at_ref, gu4, gu_x, gu_c, do4, do_x, do_c, gate_ref, up_ref, down_ref, out_ref
):
    core, xb, z = at_ref[0], at_ref[1], at_ref[2]
    deep, wide = gu4.shape[1:]
    for f in range(2):
        for e in range(2):
            for j, d in enumerate((0, 2, 1, 3)):
                gu = (gu4[j] if e == 0 else gu_x[j]) if f == 0 else gu_c[e * 4 + j]
                do = (do4[j] if e == 0 else do_x[j]) if f == 0 else do_c[e * 4 + j]
                rs = pl.ds(pl.multiple_of((xb ^ e) * deep, 16), deep)
                cs = pl.ds(pl.multiple_of((z ^ d) * wide, 128), wide)
                for c, ref in ((0, gate_ref), (1, up_ref)):

                    @pl.when((core ^ f) == c)
                    def _():
                        ref[rs, cs] = gu.astype(F32)

                m = (core ^ f) * 8 + (xb ^ e) * 4 + (z ^ d)
                rows = down_ref.shape[0] // 16
                down_ref[pl.ds(pl.multiple_of(m * rows, 8), rows), :] = do[:rows].astype(F32)
                few = do.shape[0] - rows

                @pl.when(m < out_ref.shape[0] // few)
                def _():
                    out_ref[pl.ds(pl.multiple_of(m * few, 8), few), :] = do[rows:].astype(F32)


def final_ffn(at, gu4, gu_x, gu_c, do4, do_x, do_c, half, ff, width):
    f32 = lambda *s: jax.ShapeDtypeStruct(s, F32)
    return pl.pallas_call(
        final_kernel,
        in_specs=[pl.BlockSpec(memory_space=pltpu.SMEM)] + [pl.BlockSpec(memory_space=pltpu.VMEM)] * 6,
        out_specs=[pl.BlockSpec(memory_space=pltpu.VMEM)] * 4,
        out_shape=[f32(half, ff), f32(half, ff), f32(ff // 2, width), f32(half, width)],
        compiler_params=pltpu.CompilerParams(vmem_limit_bytes=LIMIT),
        cost_estimate=pl.CostEstimate(flops=int(5e9), bytes_accessed=int(10e6), transcendentals=0),
    )(at, gu4, gu_x, gu_c, do4, do_x, do_c)


def final_t_kernel(at_ref, t4, t_x, t_c, q_ref, k_ref, v_ref, g_ref, whole):
    core, xb, z = at_ref[0], at_ref[1], at_ref[2]
    deep, wide = t4.shape[1:]
    for f in range(2):
        for e in range(2):
            for j, d in enumerate((0, 2, 1, 3)):
                t = (t4[j] if e == 0 else t_x[j]) if f == 0 else t_c[e * 4 + j]
                rs = pl.ds(pl.multiple_of((xb ^ e) * deep, 16), deep)
                cs = pl.ds(pl.multiple_of((core ^ f) * 512 + (z ^ d) * wide, 128), wide)
                whole[rs, cs] = t.astype(F32)
    a = q_ref.shape[1]
    b = a + k_ref.shape[1]
    c = b + v_ref.shape[1]
    q_ref[...] = whole[:, :a]
    k_ref[...] = whole[:, a:b]
    v_ref[...] = whole[:, b:c]
    g_ref[...] = whole[:, c:].T[:8]


def final_t(at, t4, t_x, t_c, half, width, kv_width):
    f32 = lambda *s: jax.ShapeDtypeStruct(s, F32)
    return pl.pallas_call(
        final_t_kernel,
        in_specs=[pl.BlockSpec(memory_space=pltpu.SMEM)] + [pl.BlockSpec(memory_space=pltpu.VMEM)] * 3,
        out_specs=[pl.BlockSpec(memory_space=pltpu.VMEM)] * 4,
        out_shape=[f32(half, width), f32(half, kv_width), f32(half, kv_width), f32(8, half)],
        scratch_shapes=[pltpu.VMEM((half, 1024), F32)],
        compiler_params=pltpu.CompilerParams(vmem_limit_bytes=LIMIT),
        cost_estimate=pl.CostEstimate(flops=int(1e9), bytes_accessed=int(2e6), transcendentals=0),
    )(at, t4, t_x, t_c)


def swap(x, axis, bit):
    n = lax.axis_size(axis)
    return lax.ppermute(x, axis, [(i, i ^ (1 << bit)) for i in range(n)])


def bit_of(axis, bit):
    return (lax.axis_index(axis) >> bit) & 1


def pin(*arrays):
    return lax.optimization_barrier(arrays)


def pick(x, at):
    return lax.dynamic_index_in_dim(x, at, 0, keepdims=False)


def in_order(flag, mine, other, axis):
    return jnp.where(
        flag == 0,
        jnp.concatenate([mine, other], axis=axis),
        jnp.concatenate([other, mine], axis=axis),
    )


def plus(a, b):
    return (a.astype(F32) + b.astype(F32)).astype(BF)


def two_level():
    return lax.axis_size("fsdp") == 2 and lax.axis_size("ctx") == 16


def z_low_send(x):
    low = bit_of("ctx", 2)
    x = x.reshape((2, 2) + x.shape[1:]).swapaxes(0, 1)
    return pick(x, low), pick(x, 1 - low)


def high_send(x):
    high = bit_of("ctx", 3)
    return pick(x, high), pick(x, 1 - high)


def double(x, bit):
    return jnp.concatenate([x, swap(x, "ctx", bit)], axis=0)


def natural_gu(pieces):
    _, a, b = pieces.shape
    return pieces.reshape(2, 4, a, b).transpose(0, 2, 1, 3).reshape(2 * a, 4 * b).astype(F32)


def other_sum(x):
    x = lax.psum_scatter(x.astype(BF), "fsdp", scatter_dimension=0, tiled=True)
    return lax.psum(x, "ctx").astype(F32)


def local(tokens, gain_attn, w_query, w_key, w_value, w_out, gain_ffn, w_gate, w_up, w_down, cotangent):
    seqs, length, width = tokens.shape
    count = lax.axis_size("ctx")
    team = count // seqs
    sub = length // team
    rows = count * sub
    ff = w_gate.shape[1]
    kv_width = KV_HEADS * HEAD_DIM
    qkv_cols = width + 2 * kv_width
    place = lax.axis_index("ctx") % team
    own = gain_attn.shape[0]
    fast = two_level()

    def move(x):
        return lax.all_to_all(x.reshape(count, sub, width), "ctx", 0, 0, tiled=True)

    x = move(tokens)
    gain_rows = jnp.zeros((8, ff), BF).at[0, :own].set(gain_attn).at[1, :own].set(gain_ffn)
    first = jnp.concatenate([jnp.concatenate([w_query, w_key, w_value, w_out], axis=1), gain_rows], axis=0)
    if fast:
        core, rank = bit_of("ctx", 0), bit_of("fsdp", 0)

        def halved(shard, axis):
            half = shard.shape[axis] // 2
            return lax.dynamic_slice_in_dim(shard, core * half, half, axis)

        def other_shard(got, axis):
            return in_order(core, got, swap(got, "ctx", 0), axis)

        got = swap(halved(first, 1), "fsdp", 0)
        other = other_shard(got, 1)
        gains = in_order(rank, first[own : own + 2, :own], other[own : own + 2, :own], 1).astype(F32)
        first = in_order(rank, first[:own], other[:own], 0)
        gate_half, up_half, down_half, got = pin(halved(w_gate, 1), halved(w_up, 1), halved(w_down, 0), got)
        gate_got, up_got, down_got = (swap(h, "fsdp", 0) for h in (gate_half, up_half, down_half))
    else:
        first = lax.all_gather(first, "fsdp", axis=0)
        gains = first[:, own : own + 2, :own].transpose(1, 0, 2).reshape(2, width).astype(F32)
        first = first[:, :own].reshape(width, first.shape[2])
        gate_w, up_w, down_w = (lax.all_gather(w, "fsdp", axis=0, tiled=True) for w in (w_gate, w_up, w_down))
    gains = jnp.pad(gains, ((0, 6), (0, 0)))

    row = jnp.arange(rows, dtype=jnp.int32)
    position = (row // sub) * length + place * sub + row % sub
    frequency = THETA ** (-jnp.arange(HEAD_DIM // 2, dtype=F32) * 2.0 / HEAD_DIM)
    angles = frequency[:, None] * position.astype(F32)[None, :]
    cosine, sine = jnp.cos(angles), jnp.sin(angles)
    groups = [[t * team + p for p in range(team)] for t in range(seqs)]
    slots = jnp.stack([place, 1 - place]) if team == 2 else jnp.arange(team)
    block_row = jnp.arange(BLOCK, dtype=jnp.int32)
    base = (block_row // sub) * length + block_row % sub
    key_pos = base[None, :] + slots[:, None] * sub
    query_pos = base + place * sub
    bias = jnp.where(key_pos[:, :, None] <= query_pos[None, None, :], 0.0, NEGATIVE).astype(F32)
    flags = jnp.stack([core, rank]) if fast else jnp.zeros((2,), jnp.int32)

    x, cot_send = pin(x, cotangent)
    cot = move(cot_send)
    query, kv_own = project_qkv(x, first, gains, cosine, sine)
    if fast:
        kv_own, gate_got = pin(kv_own, gate_got)
    if team == 2:
        kv_all = (kv_own, swap(kv_own, "ctx", 0))
    else:
        kv_all = lax.all_gather(kv_own, "ctx", axis=0, axis_index_groups=groups)
        kv_all = tuple(kv_all[s] for s in range(team))
    attended, log_total = attn_fwd(bias, query, kv_all)
    if fast:
        attended, cot, *gots = pin(attended, cot, gate_got, up_got, down_got)
        gots = [(got, swap(got, "ctx", 0)) for got in gots]
        weights = [a for own_w, two in zip((w_gate, w_up, w_down), gots) for a in (own_w, *two)]
    else:
        attended, cot = pin(attended, cot)
        low, side = width // 2, ff // 2
        weights = [a for w in (gate_w, up_w) for a in (w[:low], w[low:, :side], w[low:, side:])]
        weights += [down_w[:side], down_w[side : side + side // 2], down_w[side + side // 2 :]]
    mixed, d_res, d_att, row_dot, keep_gu, send_gu, keep_do, send_do, gain_sum = feed_forward(
        flags, attended, x, cot, first, gains, weights
    )
    mixed_out = move(mixed)

    n = rows // BLOCK
    spans = ((0, n - 1), (n - 1, n))
    part = functools.partial(attn_bwd, bias, query, kv_all, d_att, log_total, row_dot)
    if fast:
        x_bit = bit_of("ctx", 1)
        got_gu, got_do = swap(send_gu, "ctx", 0), swap(send_do, "ctx", 0)
        gu, do = plus(keep_gu, got_gu), plus(keep_do, got_do)
        gu = gu.reshape((2, 2, 4) + gu.shape[2:]).swapaxes(0, 1)
        keep_gu, send_gu = pick(gu, x_bit), pick(gu, 1 - x_bit)
        keep_do, send_do = pick(do, rank), pick(do, 1 - rank)
        send_gu, send_do, row_dot = pin(send_gu, send_do, row_dot)
        part = functools.partial(attn_bwd, bias, query, kv_all, d_att, log_total, row_dot)
        got_gu, got_do = swap(send_gu, "ctx", 1), swap(send_do, "fsdp", 0)
        dq_a, before = part(*spans[0])
        got_gu, got_do, mixed_out, before = pin(got_gu, got_do, mixed_out, before)
        gu, do = plus(keep_gu, got_gu), plus(keep_do, got_do)
        do = do.reshape((2, 4) + do.shape[1:])
        keep_gu, send_gu = pick(gu, rank), pick(gu, 1 - rank)
        keep_do, send_do = pick(do, x_bit), pick(do, 1 - x_bit)
        send_gu, send_do, before = pin(send_gu, send_do, before)
        got_gu, got_do = swap(send_gu, "fsdp", 0), swap(send_do, "ctx", 1)
        dq_b, d_kv, d_kv_low = part(*spans[1], before=before, last=True)
        got_gu, got_do, d_kv_low, dq_b = pin(got_gu, got_do, d_kv_low, dq_b)
        gu, do = plus(keep_gu, got_gu), plus(keep_do, got_do)
    else:
        dq_a, before = part(*spans[0])
        dq_b, d_kv, d_kv_low = part(*spans[1], before=before, last=True)
    if team == 2:
        own_kv, got_kv = d_kv, swap(d_kv_low.reshape(2 * kv_width, rows), "ctx", 0)
    else:
        own_kv = lax.psum_scatter(d_kv_low, "ctx", scatter_dimension=0, axis_index_groups=groups)
        own_kv, got_kv = own_kv.astype(F32)[None], jnp.zeros((2 * kv_width, rows), BF)
    if fast:
        keep_gu, send_gu = z_low_send(gu)
        keep_do, send_do = z_low_send(do)
        own_kv, got_kv, send_gu, send_do = pin(own_kv, got_kv, send_gu, send_do)
        got_gu, got_do = swap(send_gu, "ctx", 2), swap(send_do, "ctx", 2)
    d_x, keep_t, send_t = back_qkv(
        flags, spans, (dq_a, dq_b), own_kv, got_kv, x, d_res, first, gains, cosine, sine, gain_sum
    )
    if fast:
        d_x, keep_t, send_t, got_gu, got_do = pin(d_x, keep_t, send_t, got_gu, got_do)
        gu, do = plus(keep_gu, got_gu), plus(keep_do, got_do)
    grad_tokens = move(d_x)
    if fast:
        keep_gu, send_gu = high_send(gu)
        keep_do, send_do = high_send(do)
        got_gu, got_do = swap(send_gu, "ctx", 3), swap(send_do, "ctx", 3)
        t = plus(keep_t, swap(send_t, "ctx", 0))
        keep_t, got_t = pick(t, rank), swap(pick(t, 1 - rank), "fsdp", 0)
        got_t, got_gu, got_do = pin(got_t, got_gu, got_do)
        gu, do = plus(keep_gu, got_gu)[None], plus(keep_do, got_do)[None]
        gu_h, do_h = swap(gu, "ctx", 3), swap(do, "ctx", 3)
        t = plus(keep_t, got_t)
        t = t.reshape((2, 4) + t.shape[1:])
        keep_t, got_t = pick(t, x_bit), swap(pick(t, 1 - x_bit), "ctx", 1)
        got_t, gu_h, do_h = pin(got_t, gu_h, do_h)
        gu, do = jnp.concatenate([gu, gu_h], axis=0), jnp.concatenate([do, do_h], axis=0)
        gu_l, do_l = swap(gu, "ctx", 2), swap(do, "ctx", 2)
        keep_t, send_t = z_low_send(plus(keep_t, got_t))
        t = plus(keep_t, swap(send_t, "ctx", 2))
        keep_t, send_t = high_send(t)
        got_t = swap(send_t, "ctx", 3)
        got_t, gu_l, do_l, grad_tokens = pin(got_t, gu_l, do_l, grad_tokens)
        gu_four, do_four = jnp.concatenate([gu, gu_l], axis=0), jnp.concatenate([do, do_l], axis=0)
        do_x, gu_x = swap(do_four, "ctx", 1), swap(gu_four, "ctx", 1)
        t_four = double(double(plus(keep_t, got_t)[None], 3), 2)
        t_x = swap(t_four, "ctx", 1)
        t_x, do_x, gu_x = pin(t_x, do_x, gu_x)
        gu_c = swap(jnp.concatenate([gu_four, gu_x], axis=0), "ctx", 0)
        do_c = swap(jnp.concatenate([do_four, do_x], axis=0), "ctx", 0)
        t_c = swap(jnp.concatenate([t_four, t_x], axis=0), "ctx", 0)
        at = jnp.stack([core, x_bit, lax.axis_index("ctx") >> 2])
        own_query, own_key, own_value, own_gains = final_t(at, t_four, t_x, t_c, width // 2, width, kv_width)
        own_gate, own_up, own_down, own_out = final_ffn(
            at, gu_four, gu_x, gu_c, do_four, do_x, do_c, width // 2, ff, width
        )
    else:
        pair = jnp.stack([keep_gu, send_gu])
        gate, up = (jnp.concatenate([natural_gu(pair[c, y]) for y in range(2)], axis=0) for c in range(2))
        do = jnp.stack([keep_do, send_do], axis=1).reshape((32,) + keep_do.shape[2:])
        deep = ff // 32
        own_gate, own_up = other_sum(gate), other_sum(up)
        own_down = other_sum(do[:, :deep].reshape(ff, width))
        out = do[:, deep:].reshape((2, -1, width))[:, : width // 2]
        own_out = other_sum(out.reshape(width, width))
        pair = jnp.stack([keep_t, send_t])
        t = [jnp.concatenate([natural_gu(pair[c, y]) for c in range(2)], axis=1) for y in range(2)]
        own_t = other_sum(jnp.concatenate(t, axis=0))
        own_query, own_key = own_t[:, :width], own_t[:, width : width + kv_width]
        own_value, own_gains = own_t[:, width + kv_width : qkv_cols], own_t[:, qkv_cols:].T
    return (
        mixed_out.reshape(tokens.shape),
        grad_tokens.reshape(tokens.shape),
        own_gains[0],
        own_query,
        own_key,
        own_value,
        own_out,
        own_gains[1],
        own_gate,
        own_up,
        own_down,
    )


def solution(mesh):
    rows, flat, seq = P("fsdp", None), P("fsdp"), P("fsdp", "ctx", None)
    return jax.shard_map(
        local,
        mesh=mesh,
        in_specs=(seq, flat, rows, rows, rows, rows, flat, rows, rows, rows, seq),
        out_specs=(seq, seq, flat, rows, rows, rows, rows, flat, rows, rows, rows),
        check_vma=False,
    )
```

```python
import functools

import jax
import jax.numpy as jnp
from jax import lax
from jax.experimental import pallas as pl
from jax.experimental.pallas import tpu as pltpu
from jax.sharding import PartitionSpec as P

HEADS = 9
KV_HEADS = 3
HEAD_DIM = 64
EPSILON = 1e-05
THETA = 100000.0
NEGATIVE = -1e30
LOG2E = 1.4426950408889634
LN2 = 0.6931471805599453
F32=jnp.float32; BF=jnp.bfloat16
NT=(((1,),(1,)),((),()))
NN=(((1,),(0,)),((),()))
def mm(a,b,dims=NN):
    return lax.dot_general(a,b,dims,preferred_element_type=F32)

def heads_of(ref, kv, group):
    return jnp.concatenate([ref[(kv*group+h)*64:(kv*group+h+1)*64,:] for h in range(group)],axis=1)

def fwd_kernel(bias_ref, q_ref, *refs, kvs, group, slots, rows, qb):
    kv_ref, (o_ref, lse_ref, k_scr, m_scr, acc_scr)=refs[:slots], refs[slots:]
    i=pl.program_id(0)
    kw=kvs*64
    @pl.when(i==0)
    def _():
        for s in range(slots):
            for h in range(kvs):
                k_scr[h,s]=kv_ref[s][h*64:(h+1)*64,:].T
    qs=[heads_of(q_ref,h,group) for h in range(kvs)]
    width=group*qb
    m_scr[...]=jnp.full(m_scr.shape,-1e30,F32)
    acc_scr[...]=jnp.zeros(acc_scr.shape,F32)
    ones=jnp.ones((8,slots*qb),BF)
    def chunk(c, masked):
        off=pl.multiple_of(c*qb,qb)
        for h in range(kvs):
            k=jnp.concatenate([k_scr[h,s,pl.ds(off,qb),:] for s in range(slots)],axis=0)
            v=jnp.concatenate([kv_ref[s][kw+h*64:kw+(h+1)*64,pl.ds(off,qb)] for s in range(slots)],axis=1)
            v=jnp.concatenate([v,ones],axis=0)
            st=mm(k,qs[h])
            if masked:
                b=bias_ref[...].reshape(slots*qb,qb)
                st=st+jnp.concatenate([b]*group,axis=1)
            m_old=m_scr[h:h+1,:]
            m_new=jnp.maximum(m_old,jnp.max(st,axis=0,keepdims=True))
            p=jnp.exp2(st-m_new).astype(BF)
            acc_scr[h]=acc_scr[h]*jnp.exp2(m_old-m_new)+mm(v,p)
            m_scr[h:h+1,:]=m_new
    def body(c,_):
        chunk(c,False); return 0
    lax.fori_loop(0,i,body,0)
    chunk(i,True)
    for h in range(kvs):
        acc=acc_scr[h]
        tot=acc[64:65,:]
        o=acc[:64,:]*(1.0/tot)
        lse=m_scr[h:h+1,:]+jnp.log2(tot)
        for g in range(group):
            r=h*group+g
            o_ref[r*64:(r+1)*64,:]=o[:,g*qb:(g+1)*qb]
            lse_ref[r:r+1,:]=lse[:,g*qb:(g+1)*qb]

def attn_fwd(bias, qT, kvT, kvs=3, group=3, qb=256):
    slots,rows=len(kvT),kvT[0].shape[1]
    n=rows//qb
    heads=kvs*group
    return pl.pallas_call(
        functools.partial(fwd_kernel,kvs=kvs,group=group,slots=slots,rows=rows,qb=qb),
        grid=(n,),
        in_specs=[pl.BlockSpec((slots,qb,qb),lambda i:(0,0,0)),
                  pl.BlockSpec((heads*64,qb),lambda i:(0,i)),
                  *[pl.BlockSpec((2*kvs*64,rows),lambda i:(0,0))]*slots],
        out_specs=[pl.BlockSpec((heads*64,qb),lambda i:(0,i)),
                   pl.BlockSpec((16,qb),lambda i:(0,i))],
        out_shape=[jax.ShapeDtypeStruct((heads*64,rows),F32),jax.ShapeDtypeStruct((16,rows),F32)],
        scratch_shapes=[pltpu.VMEM((kvs,slots,rows,64),BF),pltpu.VMEM((8,group*qb),F32),
                        pltpu.VMEM((kvs,72,group*qb),F32)],
        compiler_params=pltpu.CompilerParams(vmem_limit_bytes=56*2**20),
        cost_estimate=pl.CostEstimate(flops=int(25e9),bytes_accessed=int(8e6),transcendentals=int(1e7)),
    )(bias,qT,*kvT)

def bwd_kernel(*refs, kvs, group, slots, qb, lo, first, last):
    bias_ref, q_ref, do_ref, lse_ref, rd_ref = refs[:5]
    kv_ref, refs = refs[5 : 5 + slots], refs[5 + slots :]
    if not first:
        before_ref, refs = refs[0], refs[1:]
    if last:
        dq_ref, dkv_ref, low_ref, kv_scr = refs
    else:
        dq_ref, dkv_ref, kv_scr = refs
    step = pl.program_id(0)
    kw = kvs * 64

    @pl.when(step == 0)
    def _():
        for s in range(slots):
            for h in range(2 * kvs):
                kv_scr[h, s] = kv_ref[s][h * 64 : (h + 1) * 64, :].T
        dkv_ref[...] = jnp.zeros(dkv_ref.shape, F32) if first else before_ref[...]

    dq_ref[...] = jnp.zeros(dq_ref.shape, F32)
    qs = [heads_of(q_ref, h, group) for h in range(kvs)]
    dos = [heads_of(do_ref, h, group) for h in range(kvs)]

    def along(ref, h):
        return jnp.concatenate([ref[h * group + g : h * group + g + 1, :] for g in range(group)], axis=1)

    lses = [along(lse_ref, h) for h in range(kvs)]
    rds = [along(rd_ref, h) for h in range(kvs)]

    def chunk(c, masked):
        off = pl.multiple_of(c * qb, qb)
        for h in range(kvs):
            k = jnp.concatenate([kv_scr[h, s, pl.ds(off, qb), :] for s in range(slots)], axis=0)
            v = jnp.concatenate([kv_scr[kvs + h, s, pl.ds(off, qb), :] for s in range(slots)], axis=0)
            k_t = jnp.concatenate([kv_ref[s][h * 64 : (h + 1) * 64, pl.ds(off, qb)] for s in range(slots)], axis=1)
            st = mm(k, qs[h])
            if masked:
                st = st + jnp.concatenate([bias_ref[...].reshape(slots * qb, qb)] * group, axis=1)
            p = jnp.exp2(st - lses[h])
            dp = mm(v, dos[h])
            ds = (p * (dp - rds[h])).astype(BF)
            dk = mm(qs[h], ds, NT)
            dv = mm(dos[h], p.astype(BF), NT)
            dq = mm(k_t, ds)
            for s in range(slots):
                dkv_ref[s, h * 64 : (h + 1) * 64, pl.ds(off, qb)] += dk[:, s * qb : (s + 1) * qb]
                dkv_ref[s, kw + h * 64 : kw + (h + 1) * 64, pl.ds(off, qb)] += dv[:, s * qb : (s + 1) * qb]
            for g in range(group):
                r = h * group + g
                dq_ref[r * 64 : (r + 1) * 64, :] += dq[:, g * qb : (g + 1) * qb]

    def body(c, carry):
        chunk(c, False)
        return carry

    lax.fori_loop(0, step + lo, body, 0)
    chunk(step + lo, True)
    if last:

        @pl.when(step == pl.num_programs(0) - 1)
        def _():
            low_ref[...] = dkv_ref[slots - low_ref.shape[0] :].astype(BF)


def attn_bwd(bias, q_t, kv_t, do_t, lse, rd, lo, hi, before=None, last=False, kvs=3, group=3, qb=256):
    slots, rows = len(kv_t), kv_t[0].shape[1]
    width = kvs * group * 64
    whole = pl.BlockSpec((slots, 2 * kvs * 64, rows), lambda i: (0, 0, 0))
    tall = pl.BlockSpec((width, qb), lambda i: (0, i + lo))
    stat = pl.BlockSpec((16, qb), lambda i: (0, i + lo))
    out_specs = [pl.BlockSpec((width, qb), lambda i: (0, i)), whole]
    out_shape = [
        jax.ShapeDtypeStruct((width, (hi - lo) * qb), F32),
        jax.ShapeDtypeStruct((slots, 2 * kvs * 64, rows), F32),
    ]
    if last:
        sent = (1 if slots == 2 else slots, 2 * kvs * 64, rows)
        out_specs.append(pl.BlockSpec(sent, lambda i: (0, 0, 0)))
        out_shape.append(jax.ShapeDtypeStruct(sent, BF))
    args = (bias, q_t, do_t, lse, rd, *kv_t) + (() if before is None else (before,))
    units = sum(range(lo + 1, hi + 1))
    return pl.pallas_call(
        functools.partial(
            bwd_kernel, kvs=kvs, group=group, slots=slots, qb=qb, lo=lo, first=before is None, last=last
        ),
        grid=(hi - lo,),
        in_specs=[pl.BlockSpec((slots, qb, qb), lambda i: (0, 0, 0)), tall, tall, stat, stat]
        + [pl.BlockSpec((2 * kvs * 64, rows), lambda i: (0, 0))] * slots
        + ([] if before is None else [whole]),
        out_specs=out_specs,
        out_shape=out_shape,
        scratch_shapes=[pltpu.VMEM((2 * kvs, slots, rows, 64), BF)],
        compiler_params=pltpu.CompilerParams(vmem_limit_bytes=60 * 2**20),
        cost_estimate=pl.CostEstimate(flops=int(4e9) * units, bytes_accessed=int(16e6), transcendentals=0),
    )(*args)


TN = (((0,), (0,)), ((), ()))
TT = (((0,), (1,)), ((), ()))
BLOCK = 256
FF_BLOCK = 512
PIECES = 8
LIMIT = 60 * 2**20


def rotated(values, cosine, sine):
    a, b = values[:32], values[32:]
    return jnp.concatenate([a * cosine - b * sine, b * cosine + a * sine], axis=0)


def flat_rows(ref):
    count, sub, width = ref.shape
    return ref[...].reshape(count * sub, width)


def rms(values):
    return lax.rsqrt(jnp.mean(values * values, axis=-1, keepdims=True) + EPSILON)


def qkv_kernel(x_ref, w_ref, gain_ref, cos_ref, sin_ref, q_ref, kv_ref, wt_scr):
    @pl.when(pl.program_id(0) == 0)
    def _():
        wt_scr[...] = w_ref[:, : wt_scr.shape[0]].T

    source = flat_rows(x_ref).astype(F32)
    hidden = (source * rms(source) * gain_ref[0:1, :]).astype(BF)
    out = mm(wt_scr[...], hidden, NT)
    cosine, sine = cos_ref[...], sin_ref[...]
    for h in range(HEADS):
        part = rotated(out[h * 64 : (h + 1) * 64], cosine, sine)
        q_ref[h * 64 : (h + 1) * 64, :] = (part * (HEAD_DIM**-0.5 * LOG2E)).astype(BF)
    top = HEADS * 64
    for h in range(KV_HEADS):
        part = rotated(out[top + h * 64 : top + (h + 1) * 64], cosine, sine)
        kv_ref[h * 64 : (h + 1) * 64, :] = part.astype(BF)
    kv_ref[KV_HEADS * 64 :, :] = out[top + KV_HEADS * 64 :].astype(BF)


def project_qkv(x, first, gains, cosine, sine):
    count, sub, width = x.shape
    rows = count * sub
    per = BLOCK // sub
    kv2 = 2 * KV_HEADS * HEAD_DIM
    return pl.pallas_call(
        qkv_kernel,
        grid=(rows // BLOCK,),
        in_specs=[
            pl.BlockSpec((per, sub, width), lambda i: (i, 0, 0)),
            pl.BlockSpec(first.shape, lambda i: (0, 0)),
            pl.BlockSpec(gains.shape, lambda i: (0, 0)),
            pl.BlockSpec((32, BLOCK), lambda i: (0, i)),
            pl.BlockSpec((32, BLOCK), lambda i: (0, i)),
        ],
        out_specs=[pl.BlockSpec((width, BLOCK), lambda i: (0, i)), pl.BlockSpec((kv2, BLOCK), lambda i: (0, i))],
        out_shape=[jax.ShapeDtypeStruct((width, rows), BF), jax.ShapeDtypeStruct((kv2, rows), BF)],
        scratch_shapes=[pltpu.VMEM((width + kv2, width), BF)],
        compiler_params=pltpu.CompilerParams(vmem_limit_bytes=LIMIT),
        cost_estimate=pl.CostEstimate(flops=int(6e9), bytes_accessed=int(5e6), transcendentals=0),
    )(x, first, gains, cosine, sine)


def ffn_kernel(
    place_ref, o_ref, x_ref, cot_ref, first_ref, gain_ref,
    gate_own, gate_got, gate_swap, up_own, up_got, up_swap, down_own, down_got, down_swap,
    mixed_ref, dres_ref, datt_ref, rd_ref, keep_gu, send_gu, keep_do, send_do, gg_ref,
    acc_gu, acc_down, acc_out, gate_ref, up_ref, down_ref,
):
    step = pl.program_id(0)
    width = x_ref.shape[2]

    @pl.when(step == 0)
    def _():
        acc_gu[...] = jnp.zeros(acc_gu.shape, F32)
        acc_down[...] = jnp.zeros(acc_down.shape, F32)
        acc_out[...] = jnp.zeros(acc_out.shape, F32)
        gg_ref[...] = jnp.zeros(gg_ref.shape, F32)
        for rank in range(2):

            @pl.when(place_ref[1] == rank)
            def _():
                for ref, own in ((gate_ref, gate_own), (up_ref, up_own), (down_ref, down_own)):
                    n = own.shape[0]
                    ref[rank * n : (rank + 1) * n] = own[...]
                for core in range(2):

                    @pl.when(place_ref[0] == core)
                    def _():
                        for ref, parts in ((gate_ref, (gate_got, gate_swap)), (up_ref, (up_got, up_swap))):
                            n, m = parts[0].shape
                            for k, part in ((core, parts[0]), (1 - core, parts[1])):
                                ref[(1 - rank) * n : (2 - rank) * n, k * m : (k + 1) * m] = part[...]
                        n = down_got.shape[0]
                        for k, part in ((core, down_got), (1 - core, down_swap)):
                            low = (2 * (1 - rank) + k) * n
                            down_ref[low : low + n] = part[...]

    cols = first_ref.shape[1]
    out_w = first_ref[:, cols - width :]
    attended = o_ref[...]
    mixed = attended.astype(BF)
    residual = flat_rows(x_ref).astype(F32) + mm(mixed, out_w, TN)
    scale = rms(residual)
    normed = residual * scale
    gain = gain_ref[1:2, :]
    hidden = (normed * gain).astype(BF)
    gate = mm(hidden, gate_ref[...])
    up = mm(hidden, up_ref[...])
    sig = 0.5 * jnp.tanh(0.5 * gate) + 0.5
    silu = gate * sig
    activated = (silu * up).astype(BF)
    mixed_out = (residual + mm(activated, down_ref[...])).astype(BF)
    mixed_ref[...] = mixed_out.reshape(mixed_ref.shape)
    cot = flat_rows(cot_ref)
    d_act = mm(cot, down_ref[...], NT)
    acc_down[...] += mm(activated, cot, TN)
    d_gate = (d_act * up * sig * (1.0 + gate * (1.0 - sig))).astype(BF)
    d_up = (d_act * silu).astype(BF)
    acc_gu[0] += mm(hidden, d_gate, TN)
    acc_gu[1] += mm(hidden, d_up, TN)
    d_hidden = mm(d_gate, gate_ref[...], NT) + mm(d_up, up_ref[...], NT)
    dn = d_hidden * normed
    gg_ref[...] += jnp.sum(dn.reshape(-1, 8, width), axis=0)
    inner = jnp.mean(dn * gain, axis=-1, keepdims=True)
    d_res = cot.astype(F32) + scale * (d_hidden * gain - normed * inner)
    dres_ref[...] = d_res
    d_low = d_res.astype(BF)
    acc_out[...] += mm(mixed, d_low)
    d_att = mm(out_w, d_low, NT).astype(BF)
    datt_ref[...] = d_att
    prod = d_att.astype(F32) * attended
    for h in range(HEADS):
        rd_ref[h : h + 1, :] = jnp.sum(prod[h * 64 : (h + 1) * 64], axis=0, keepdims=True)
    rd_ref[HEADS:, :] = jnp.zeros((16 - HEADS, rd_ref.shape[1]), F32)

    @pl.when(step == pl.num_programs(0) - 1)
    def _():
        core = place_ref[0]
        half = width // 2
        ff = acc_gu.shape[2]
        for y in range(2):
            for p in range(PIECES):
                rs = slice(y * half + (p // 4) * (half // 2), y * half + (p // 4 + 1) * (half // 2))
                cs = slice((p % 4) * (ff // 4), (p % 4 + 1) * (ff // 4))
                keep_gu[y, p] = acc_gu[core, rs, cs].astype(BF)
                send_gu[y, p] = acc_gu[1 - core, rs, cs].astype(BF)
        down_rows, out_rows = ff // 32, width // 24
        for y in range(2):
            for p in range(PIECES):
                for ref, c in ((keep_do, core), (send_do, 1 - core)):
                    start = pl.multiple_of(y * (ff // 2) + (PIECES * c + p) * down_rows, 16)
                    ref[y, p, :down_rows] = acc_down[pl.ds(start, down_rows), :].astype(BF)
                    start = y * half + jnp.minimum(PIECES * c + p, half // out_rows - 1) * out_rows
                    ref[y, p, down_rows:] = acc_out[pl.ds(pl.multiple_of(start, 8), out_rows), :].astype(BF)


def feed_forward(place, attended, x, cot, first, gains, weights):
    count, sub, width = x.shape
    rows, ff = count * sub, weights[0].shape[1]
    per = FF_BLOCK // sub
    gu = (2, PIECES, width // 4, ff // 4)
    do = (2, PIECES, ff // 32 + width // 24, width)

    def whole(shape):
        return pl.BlockSpec(shape, lambda i: (0,) * len(shape), pipeline_mode=pl.Buffered(1))

    seq = pl.BlockSpec((per, sub, width), lambda i: (i, 0, 0))
    tall = pl.BlockSpec((width, FF_BLOCK), lambda i: (0, i))
    return pl.pallas_call(
        ffn_kernel,
        grid=(rows // FF_BLOCK,),
        in_specs=[
            pl.BlockSpec(memory_space=pltpu.SMEM), tall, seq, seq,
            whole(first.shape), whole(gains.shape), *(whole(w.shape) for w in weights),
        ],
        out_specs=[
            seq, pl.BlockSpec((FF_BLOCK, width), lambda i: (i, 0)), tall, pl.BlockSpec((16, FF_BLOCK), lambda i: (0, i)),
            whole(gu), whole(gu), whole(do), whole(do), whole((8, width)),
        ],
        out_shape=[
            jax.ShapeDtypeStruct(x.shape, BF),
            jax.ShapeDtypeStruct((rows, width), F32),
            jax.ShapeDtypeStruct((width, rows), BF),
            jax.ShapeDtypeStruct((16, rows), F32),
            jax.ShapeDtypeStruct(gu, BF), jax.ShapeDtypeStruct(gu, BF),
            jax.ShapeDtypeStruct(do, BF), jax.ShapeDtypeStruct(do, BF),
            jax.ShapeDtypeStruct((8, width), F32),
        ],
        scratch_shapes=[
            pltpu.VMEM((2, width, ff), F32), pltpu.VMEM((ff, width), F32), pltpu.VMEM((width, width), F32),
            pltpu.VMEM((width, ff), BF), pltpu.VMEM((width, ff), BF), pltpu.VMEM((ff, width), BF),
        ],
        compiler_params=pltpu.CompilerParams(vmem_limit_bytes=LIMIT),
        cost_estimate=pl.CostEstimate(flops=int(32e9), bytes_accessed=int(20e6), transcendentals=0),
    )(place, attended, x, cot, first, gains, *weights)


def back_kernel(*refs, spans):
    place_ref, refs = refs[0], refs[1:]
    dq_refs, refs = refs[: len(spans)], refs[len(spans) :]
    own_ref, got_ref, x_ref, dres_ref, first_ref, gain_ref, cos_ref, sin_ref, gg_ref, dx_ref = refs[:10]
    keep_ref, send_ref, acc, dt_scr, ga_scr, w_scr = refs[10:]
    step = pl.program_id(0)
    width = x_ref.shape[2]
    kv = KV_HEADS * 64
    total = width + 2 * kv

    @pl.when(step == 0)
    def _():
        acc[...] = jnp.zeros(acc.shape, F32)
        ga_scr[...] = jnp.zeros(ga_scr.shape, F32)
        w_scr[...] = first_ref[:, :total].T

    cosine, sine = cos_ref[...], -sin_ref[...]
    for (lo, hi), dq_ref in zip(spans, dq_refs):

        @pl.when((step >= lo) & (step < hi))
        def _():
            for h in range(HEADS):
                part = dq_ref[h * 64 : (h + 1) * 64, :] * (HEAD_DIM**-0.5)
                dt_scr[h * 64 : (h + 1) * 64, :] = rotated(part, cosine, sine).astype(BF)

    d_kv = own_ref[0] + got_ref[...].astype(F32)
    for h in range(KV_HEADS):
        part = d_kv[h * 64 : (h + 1) * 64] * LN2
        dt_scr[width + h * 64 : width + (h + 1) * 64, :] = rotated(part, cosine, sine).astype(BF)
    dt_scr[width + kv :, :] = d_kv[kv:].astype(BF)
    d_t = dt_scr[...]
    source = flat_rows(x_ref).astype(F32)
    scale = rms(source)
    normed = source * scale
    gain = gain_ref[0:1, :]
    hidden = (normed * gain).astype(BF)
    acc[:total] += mm(d_t, hidden)
    d_hidden = mm(d_t, w_scr[...], TN)
    dn = d_hidden * normed
    ga_scr[...] += jnp.sum(dn.reshape(-1, 8, width), axis=0)
    inner = jnp.mean(dn * gain, axis=-1, keepdims=True)
    grad = dres_ref[...] + scale * (d_hidden * gain - normed * inner)
    dx_ref[...] = grad.astype(BF).reshape(dx_ref.shape)

    @pl.when(step == pl.num_programs(0) - 1)
    def _():
        core = place_ref[0]
        acc[total : total + 1, :] = jnp.sum(ga_scr[...], axis=0, keepdims=True)
        acc[total + 1 : total + 2, :] = jnp.sum(gg_ref[...], axis=0, keepdims=True)
        half, deep = width // 2, width // 4
        for ct in range(4):
            for ref, c in ((keep_ref, core), (send_ref, 1 - core)):
                start = pl.multiple_of(c * 512 + ct * 128, 128)
                block = acc[pl.ds(start, 128), :].T.astype(BF)
                for y in range(2):
                    for rh in range(2):
                        low = y * half + rh * deep
                        ref[y, rh * 4 + ct] = block[low : low + deep]


def back_qkv(place, spans, d_query, d_kv, got, x, d_res, first, gains, cosine, sine, gg):
    count, sub, width = x.shape
    rows = count * sub
    per = BLOCK // sub
    kv2 = 2 * KV_HEADS * HEAD_DIM
    piece = (2, PIECES, width // 4, 128)

    def whole(shape):
        return pl.BlockSpec(shape, lambda i: (0,) * len(shape))

    seq = pl.BlockSpec((per, sub, width), lambda i: (i, 0, 0))
    return pl.pallas_call(
        functools.partial(back_kernel, spans=spans),
        grid=(rows // BLOCK,),
        in_specs=[
            pl.BlockSpec(memory_space=pltpu.SMEM),
            *(
                pl.BlockSpec((width, BLOCK), lambda i, lo=lo, hi=hi: (0, jnp.clip(i - lo, 0, hi - lo - 1)))
                for lo, hi in spans
            ),
            pl.BlockSpec((1, kv2, BLOCK), lambda i: (0, 0, i)),
            pl.BlockSpec((kv2, BLOCK), lambda i: (0, i)),
            seq, pl.BlockSpec((BLOCK, width), lambda i: (i, 0)),
            whole(first.shape), whole(gains.shape),
            pl.BlockSpec((32, BLOCK), lambda i: (0, i)), pl.BlockSpec((32, BLOCK), lambda i: (0, i)),
            whole(gg.shape),
        ],
        out_specs=[seq, whole(piece), whole(piece)],
        out_shape=[jax.ShapeDtypeStruct(x.shape, BF), jax.ShapeDtypeStruct(piece, BF), jax.ShapeDtypeStruct(piece, BF)],
        scratch_shapes=[
            pltpu.VMEM((1024, width), F32), pltpu.VMEM((width + kv2, BLOCK), BF), pltpu.VMEM((8, width), F32),
            pltpu.VMEM((width + kv2, width), BF),
        ],
        compiler_params=pltpu.CompilerParams(vmem_limit_bytes=LIMIT),
        cost_estimate=pl.CostEstimate(flops=int(10e9), bytes_accessed=int(10e6), transcendentals=0),
    )(place, *d_query, d_kv, got, x, d_res, first, gains, cosine, sine, gg)


def final_kernel(
    at_ref, gu4, gu_x, gu_c, do4, do_x, do_c, gate_ref, up_ref, down_ref, out_ref
):
    core, xb, z = at_ref[0], at_ref[1], at_ref[2]
    deep, wide = gu4.shape[1:]
    for f in range(2):
        for e in range(2):
            for j, d in enumerate((0, 2, 1, 3)):
                gu = (gu4[j] if e == 0 else gu_x[j]) if f == 0 else gu_c[e * 4 + j]
                do = (do4[j] if e == 0 else do_x[j]) if f == 0 else do_c[e * 4 + j]
                rs = pl.ds(pl.multiple_of((xb ^ e) * deep, 16), deep)
                cs = pl.ds(pl.multiple_of((z ^ d) * wide, 128), wide)
                for c, ref in ((0, gate_ref), (1, up_ref)):

                    @pl.when((core ^ f) == c)
                    def _():
                        ref[rs, cs] = gu.astype(F32)

                m = (core ^ f) * 8 + (xb ^ e) * 4 + (z ^ d)
                rows = down_ref.shape[0] // 16
                down_ref[pl.ds(pl.multiple_of(m * rows, 8), rows), :] = do[:rows].astype(F32)
                few = do.shape[0] - rows

                @pl.when(m < out_ref.shape[0] // few)
                def _():
                    out_ref[pl.ds(pl.multiple_of(m * few, 8), few), :] = do[rows:].astype(F32)


def final_ffn(at, gu4, gu_x, gu_c, do4, do_x, do_c, half, ff, width):
    f32 = lambda *s: jax.ShapeDtypeStruct(s, F32)
    return pl.pallas_call(
        final_kernel,
        in_specs=[pl.BlockSpec(memory_space=pltpu.SMEM)] + [pl.BlockSpec(memory_space=pltpu.VMEM)] * 6,
        out_specs=[pl.BlockSpec(memory_space=pltpu.VMEM)] * 4,
        out_shape=[f32(half, ff), f32(half, ff), f32(ff // 2, width), f32(half, width)],
        compiler_params=pltpu.CompilerParams(vmem_limit_bytes=LIMIT),
        cost_estimate=pl.CostEstimate(flops=int(5e9), bytes_accessed=int(10e6), transcendentals=0),
    )(at, gu4, gu_x, gu_c, do4, do_x, do_c)


def final_t_kernel(at_ref, t4, t_x, t_c, q_ref, k_ref, v_ref, g_ref, whole):
    core, xb, z = at_ref[0], at_ref[1], at_ref[2]
    deep, wide = t4.shape[1:]
    for f in range(2):
        for e in range(2):
            for j, d in enumerate((0, 2, 1, 3)):
                t = (t4[j] if e == 0 else t_x[j]) if f == 0 else t_c[e * 4 + j]
                rs = pl.ds(pl.multiple_of((xb ^ e) * deep, 16), deep)
                cs = pl.ds(pl.multiple_of((core ^ f) * 512 + (z ^ d) * wide, 128), wide)
                whole[rs, cs] = t.astype(F32)
    a = q_ref.shape[1]
    b = a + k_ref.shape[1]
    c = b + v_ref.shape[1]
    q_ref[...] = whole[:, :a]
    k_ref[...] = whole[:, a:b]
    v_ref[...] = whole[:, b:c]
    g_ref[...] = whole[:, c:].T[:8]


def final_t(at, t4, t_x, t_c, half, width, kv_width):
    f32 = lambda *s: jax.ShapeDtypeStruct(s, F32)
    return pl.pallas_call(
        final_t_kernel,
        in_specs=[pl.BlockSpec(memory_space=pltpu.SMEM)] + [pl.BlockSpec(memory_space=pltpu.VMEM)] * 3,
        out_specs=[pl.BlockSpec(memory_space=pltpu.VMEM)] * 4,
        out_shape=[f32(half, width), f32(half, kv_width), f32(half, kv_width), f32(8, half)],
        scratch_shapes=[pltpu.VMEM((half, 1024), F32)],
        compiler_params=pltpu.CompilerParams(vmem_limit_bytes=LIMIT),
        cost_estimate=pl.CostEstimate(flops=int(1e9), bytes_accessed=int(2e6), transcendentals=0),
    )(at, t4, t_x, t_c)


def swap(x, axis, bit):
    n = lax.axis_size(axis)
    return lax.ppermute(x, axis, [(i, i ^ (1 << bit)) for i in range(n)])


def bit_of(axis, bit):
    return (lax.axis_index(axis) >> bit) & 1


def pin(*arrays):
    return lax.optimization_barrier(arrays)


def pick(x, at):
    return lax.dynamic_index_in_dim(x, at, 0, keepdims=False)


def in_order(flag, mine, other, axis):
    return jnp.where(
        flag == 0,
        jnp.concatenate([mine, other], axis=axis),
        jnp.concatenate([other, mine], axis=axis),
    )


def plus(a, b):
    return (a.astype(F32) + b.astype(F32)).astype(BF)


def two_level():
    return lax.axis_size("fsdp") == 2 and lax.axis_size("ctx") == 16


def z_low_send(x):
    low = bit_of("ctx", 2)
    x = x.reshape((2, 2) + x.shape[1:]).swapaxes(0, 1)
    return pick(x, low), pick(x, 1 - low)


def high_send(x):
    high = bit_of("ctx", 3)
    return pick(x, high), pick(x, 1 - high)


def double(x, bit):
    return jnp.concatenate([x, swap(x, "ctx", bit)], axis=0)


def natural_gu(pieces):
    _, a, b = pieces.shape
    return pieces.reshape(2, 4, a, b).transpose(0, 2, 1, 3).reshape(2 * a, 4 * b).astype(F32)


def other_sum(x):
    x = lax.psum_scatter(x.astype(BF), "fsdp", scatter_dimension=0, tiled=True)
    return lax.psum(x, "ctx").astype(F32)


def local(tokens, gain_attn, w_query, w_key, w_value, w_out, gain_ffn, w_gate, w_up, w_down, cotangent):
    seqs, length, width = tokens.shape
    count = lax.axis_size("ctx")
    team = count // seqs
    sub = length // team
    rows = count * sub
    ff = w_gate.shape[1]
    kv_width = KV_HEADS * HEAD_DIM
    qkv_cols = width + 2 * kv_width
    place = lax.axis_index("ctx") % team
    own = gain_attn.shape[0]
    fast = two_level()

    def move(x):
        return lax.all_to_all(x.reshape(count, sub, width), "ctx", 0, 0, tiled=True)

    x = move(tokens)
    gain_rows = jnp.zeros((8, ff), BF).at[0, :own].set(gain_attn).at[1, :own].set(gain_ffn)
    first = jnp.concatenate([jnp.concatenate([w_query, w_key, w_value, w_out], axis=1), gain_rows], axis=0)
    if fast:
        core, rank = bit_of("ctx", 0), bit_of("fsdp", 0)

        def halved(shard, axis):
            half = shard.shape[axis] // 2
            return lax.dynamic_slice_in_dim(shard, core * half, half, axis)

        def other_shard(got, axis):
            return in_order(core, got, swap(got, "ctx", 0), axis)

        got = swap(halved(first, 1), "fsdp", 0)
        other = other_shard(got, 1)
        gains = in_order(rank, first[own : own + 2, :own], other[own : own + 2, :own], 1).astype(F32)
        first = in_order(rank, first[:own], other[:own], 0)
        gate_half, up_half, down_half, got = pin(halved(w_gate, 1), halved(w_up, 1), halved(w_down, 0), got)
        gate_got, up_got, down_got = (swap(h, "fsdp", 0) for h in (gate_half, up_half, down_half))
    else:
        first = lax.all_gather(first, "fsdp", axis=0)
        gains = first[:, own : own + 2, :own].transpose(1, 0, 2).reshape(2, width).astype(F32)
        first = first[:, :own].reshape(width, first.shape[2])
        gate_w, up_w, down_w = (lax.all_gather(w, "fsdp", axis=0, tiled=True) for w in (w_gate, w_up, w_down))
    gains = jnp.pad(gains, ((0, 6), (0, 0)))

    row = jnp.arange(rows, dtype=jnp.int32)
    position = (row // sub) * length + place * sub + row % sub
    frequency = THETA ** (-jnp.arange(HEAD_DIM // 2, dtype=F32) * 2.0 / HEAD_DIM)
    angles = frequency[:, None] * position.astype(F32)[None, :]
    cosine, sine = jnp.cos(angles), jnp.sin(angles)
    groups = [[t * team + p for p in range(team)] for t in range(seqs)]
    slots = jnp.stack([place, 1 - place]) if team == 2 else jnp.arange(team)
    block_row = jnp.arange(BLOCK, dtype=jnp.int32)
    base = (block_row // sub) * length + block_row % sub
    key_pos = base[None, :] + slots[:, None] * sub
    query_pos = base + place * sub
    bias = jnp.where(key_pos[:, :, None] <= query_pos[None, None, :], 0.0, NEGATIVE).astype(F32)
    flags = jnp.stack([core, rank]) if fast else jnp.zeros((2,), jnp.int32)

    x, cot_send = pin(x, cotangent)
    cot = move(cot_send)
    query, kv_own = project_qkv(x, first, gains, cosine, sine)
    if fast:
        kv_own, gate_got = pin(kv_own, gate_got)
    if team == 2:
        kv_all = (kv_own, swap(kv_own, "ctx", 0))
    else:
        kv_all = lax.all_gather(kv_own, "ctx", axis=0, axis_index_groups=groups)
        kv_all = tuple(kv_all[s] for s in range(team))
    attended, log_total = attn_fwd(bias, query, kv_all)
    if fast:
        attended, cot, *gots = pin(attended, cot, gate_got, up_got, down_got)
        gots = [(got, swap(got, "ctx", 0)) for got in gots]
        weights = [a for own_w, two in zip((w_gate, w_up, w_down), gots) for a in (own_w, *two)]
    else:
        attended, cot = pin(attended, cot)
        low, side = width // 2, ff // 2
        weights = [a for w in (gate_w, up_w) for a in (w[:low], w[low:, :side], w[low:, side:])]
        weights += [down_w[:side], down_w[side : side + side // 2], down_w[side + side // 2 :]]
    mixed, d_res, d_att, row_dot, keep_gu, send_gu, keep_do, send_do, gain_sum = feed_forward(
        flags, attended, x, cot, first, gains, weights
    )
    mixed_out = move(mixed)

    n = rows // BLOCK
    spans = ((0, n - 1), (n - 1, n))
    part = functools.partial(attn_bwd, bias, query, kv_all, d_att, log_total, row_dot)
    if fast:
        x_bit = bit_of("ctx", 1)
        got_gu, got_do = swap(send_gu, "ctx", 0), swap(send_do, "ctx", 0)
        gu, do = plus(keep_gu, got_gu), plus(keep_do, got_do)
        gu = gu.reshape((2, 2, 4) + gu.shape[2:]).swapaxes(0, 1)
        keep_gu, send_gu = pick(gu, x_bit), pick(gu, 1 - x_bit)
        keep_do, send_do = pick(do, rank), pick(do, 1 - rank)
        send_gu, send_do, row_dot = pin(send_gu, send_do, row_dot)
        part = functools.partial(attn_bwd, bias, query, kv_all, d_att, log_total, row_dot)
        got_gu, got_do = swap(send_gu, "ctx", 1), swap(send_do, "fsdp", 0)
        dq_a, before = part(*spans[0])
        got_gu, got_do, mixed_out, before = pin(got_gu, got_do, mixed_out, before)
        gu, do = plus(keep_gu, got_gu), plus(keep_do, got_do)
        do = do.reshape((2, 4) + do.shape[1:])
        keep_gu, send_gu = pick(gu, rank), pick(gu, 1 - rank)
        keep_do, send_do = pick(do, x_bit), pick(do, 1 - x_bit)
        send_gu, send_do, before = pin(send_gu, send_do, before)
        got_gu, got_do = swap(send_gu, "fsdp", 0), swap(send_do, "ctx", 1)
        dq_b, d_kv, d_kv_low = part(*spans[1], before=before, last=True)
        got_gu, got_do, d_kv_low, dq_b = pin(got_gu, got_do, d_kv_low, dq_b)
        gu, do = plus(keep_gu, got_gu), plus(keep_do, got_do)
    else:
        dq_a, before = part(*spans[0])
        dq_b, d_kv, d_kv_low = part(*spans[1], before=before, last=True)
    if team == 2:
        own_kv, got_kv = d_kv, swap(d_kv_low.reshape(2 * kv_width, rows), "ctx", 0)
    else:
        own_kv = lax.psum_scatter(d_kv_low, "ctx", scatter_dimension=0, axis_index_groups=groups)
        own_kv, got_kv = own_kv.astype(F32)[None], jnp.zeros((2 * kv_width, rows), BF)
    if fast:
        keep_gu, send_gu = z_low_send(gu)
        keep_do, send_do = z_low_send(do)
        own_kv, got_kv, send_gu, send_do = pin(own_kv, got_kv, send_gu, send_do)
        got_gu, got_do = swap(send_gu, "ctx", 2), swap(send_do, "ctx", 2)
    d_x, keep_t, send_t = back_qkv(
        flags, spans, (dq_a, dq_b), own_kv, got_kv, x, d_res, first, gains, cosine, sine, gain_sum
    )
    if fast:
        d_x, keep_t, send_t, got_gu, got_do = pin(d_x, keep_t, send_t, got_gu, got_do)
        gu, do = plus(keep_gu, got_gu), plus(keep_do, got_do)
    if fast:
        keep_gu, send_gu = high_send(gu)
        keep_do, send_do = high_send(do)
        got_gu, got_do = swap(send_gu, "ctx", 3), swap(send_do, "ctx", 3)
        got_t, got_gu, got_do = pin(swap(send_t, "ctx", 0), got_gu, got_do)
        t = plus(keep_t, got_t)
        gu, do = plus(keep_gu, got_gu)[None], plus(keep_do, got_do)[None]
        keep_t, got_t = pick(t, rank), swap(pick(t, 1 - rank), "fsdp", 0)
        gu_h, do_h = swap(gu, "ctx", 3), swap(do, "ctx", 3)
        d_x, got_t, gu_h, do_h = pin(d_x, got_t, gu_h, do_h)
        grad_tokens = move(d_x)
        t = plus(keep_t, got_t)
        t = t.reshape((2, 4) + t.shape[1:])
        keep_t, got_t = pick(t, x_bit), swap(pick(t, 1 - x_bit), "ctx", 1)
        gu, do = jnp.concatenate([gu, gu_h], axis=0), jnp.concatenate([do, do_h], axis=0)
        gu_l, do_l = swap(gu, "ctx", 2), swap(do, "ctx", 2)
        got_t, gu_l, do_l = pin(got_t, gu_l, do_l)
        keep_t, send_t = z_low_send(plus(keep_t, got_t))
        got_t = swap(send_t, "ctx", 2)
        gu_four, do_four = jnp.concatenate([gu, gu_l], axis=0), jnp.concatenate([do, do_l], axis=0)
        do_x, gu_x = swap(do_four, "ctx", 1), swap(gu_four, "ctx", 1)
        do_x, gu_x, got_t = pin(do_x, gu_x, got_t)
        gu_c = swap(jnp.concatenate([gu_four, gu_x], axis=0), "ctx", 0)
        do_c = swap(jnp.concatenate([do_four, do_x], axis=0), "ctx", 0)
        keep_t, send_t = high_send(plus(keep_t, got_t))
        send_t, gu_c, do_c, grad_tokens = pin(send_t, gu_c, do_c, grad_tokens)
        t = plus(keep_t, swap(send_t, "ctx", 3))[None]
        t_four = double(double(t, 3), 2)
        t_x = swap(t_four, "ctx", 1)
        t_c = swap(jnp.concatenate([t_four, t_x], axis=0), "ctx", 0)
        at = jnp.stack([core, x_bit, lax.axis_index("ctx") >> 2])
        own_query, own_key, own_value, own_gains = final_t(at, t_four, t_x, t_c, width // 2, width, kv_width)
        own_gate, own_up, own_down, own_out = final_ffn(
            at, gu_four, gu_x, gu_c, do_four, do_x, do_c, width // 2, ff, width
        )
    else:
        grad_tokens = move(d_x)
        pair = jnp.stack([keep_gu, send_gu])
        gate, up = (jnp.concatenate([natural_gu(pair[c, y]) for y in range(2)], axis=0) for c in range(2))
        do = jnp.stack([keep_do, send_do], axis=1).reshape((32,) + keep_do.shape[2:])
        deep = ff // 32
        own_gate, own_up = other_sum(gate), other_sum(up)
        own_down = other_sum(do[:, :deep].reshape(ff, width))
        out = do[:, deep:].reshape((2, -1, width))[:, : width // 2]
        own_out = other_sum(out.reshape(width, width))
        pair = jnp.stack([keep_t, send_t])
        t = [jnp.concatenate([natural_gu(pair[c, y]) for c in range(2)], axis=1) for y in range(2)]
        own_t = other_sum(jnp.concatenate(t, axis=0))
        own_query, own_key = own_t[:, :width], own_t[:, width : width + kv_width]
        own_value, own_gains = own_t[:, width + kv_width : qkv_cols], own_t[:, qkv_cols:].T
    return (
        mixed_out.reshape(tokens.shape),
        grad_tokens.reshape(tokens.shape),
        own_gains[0],
        own_query,
        own_key,
        own_value,
        own_out,
        own_gains[1],
        own_gate,
        own_up,
        own_down,
    )


def solution(mesh):
    rows, flat, seq = P("fsdp", None), P("fsdp"), P("fsdp", "ctx", None)
    return jax.shard_map(
        local,
        mesh=mesh,
        in_specs=(seq, flat, rows, rows, rows, rows, flat, rows, rows, rows, seq),
        out_specs=(seq, seq, flat, rows, rows, rows, rows, flat, rows, rows, rows),
        check_vma=False,
    )
```

```python
import functools

import jax
import jax.numpy as jnp
from jax import lax
from jax.experimental import pallas as pl
from jax.experimental.pallas import tpu as pltpu
from jax.sharding import PartitionSpec as P

HEADS = 9
KV_HEADS = 3
HEAD_DIM = 64
EPSILON = 1e-05
THETA = 100000.0
NEGATIVE = -1e30
LOG2E = 1.4426950408889634
LN2 = 0.6931471805599453
F32=jnp.float32; BF=jnp.bfloat16
NT=(((1,),(1,)),((),()))
NN=(((1,),(0,)),((),()))
def mm(a,b,dims=NN):
    return lax.dot_general(a,b,dims,preferred_element_type=F32)

def heads_of(ref, kv, group):
    return jnp.concatenate([ref[(kv*group+h)*64:(kv*group+h+1)*64,:] for h in range(group)],axis=1)

def fwd_kernel(bias_ref, q_ref, *refs, kvs, group, slots, rows, qb):
    kv_ref, (o_ref, lse_ref, k_scr, m_scr, acc_scr)=refs[:slots], refs[slots:]
    i=pl.program_id(0)
    kw=kvs*64
    @pl.when(i==0)
    def _():
        for s in range(slots):
            for h in range(kvs):
                k_scr[h,s]=kv_ref[s][h*64:(h+1)*64,:].T
    qs=[heads_of(q_ref,h,group) for h in range(kvs)]
    width=group*qb
    m_scr[...]=jnp.full(m_scr.shape,-1e30,F32)
    acc_scr[...]=jnp.zeros(acc_scr.shape,F32)
    ones=jnp.ones((8,slots*qb),BF)
    def chunk(c, masked):
        off=pl.multiple_of(c*qb,qb)
        for h in range(kvs):
            k=jnp.concatenate([k_scr[h,s,pl.ds(off,qb),:] for s in range(slots)],axis=0)
            v=jnp.concatenate([kv_ref[s][kw+h*64:kw+(h+1)*64,pl.ds(off,qb)] for s in range(slots)],axis=1)
            v=jnp.concatenate([v,ones],axis=0)
            st=mm(k,qs[h])
            if masked:
                b=bias_ref[...].reshape(slots*qb,qb)
                st=st+jnp.concatenate([b]*group,axis=1)
            m_old=m_scr[h:h+1,:]
            m_new=jnp.maximum(m_old,jnp.max(st,axis=0,keepdims=True))
            p=jnp.exp2(st-m_new).astype(BF)
            acc_scr[h]=acc_scr[h]*jnp.exp2(m_old-m_new)+mm(v,p)
            m_scr[h:h+1,:]=m_new
    def body(c,_):
        chunk(c,False); return 0
    lax.fori_loop(0,i,body,0)
    chunk(i,True)
    for h in range(kvs):
        acc=acc_scr[h]
        tot=acc[64:65,:]
        o=acc[:64,:]*(1.0/tot)
        lse=m_scr[h:h+1,:]+jnp.log2(tot)
        for g in range(group):
            r=h*group+g
            o_ref[r*64:(r+1)*64,:]=o[:,g*qb:(g+1)*qb]
            lse_ref[r:r+1,:]=lse[:,g*qb:(g+1)*qb]

def attn_fwd(bias, qT, kvT, kvs=3, group=3, qb=256):
    slots,rows=len(kvT),kvT[0].shape[1]
    n=rows//qb
    heads=kvs*group
    return pl.pallas_call(
        functools.partial(fwd_kernel,kvs=kvs,group=group,slots=slots,rows=rows,qb=qb),
        grid=(n,),
        in_specs=[pl.BlockSpec((slots,qb,qb),lambda i:(0,0,0)),
                  pl.BlockSpec((heads*64,qb),lambda i:(0,i)),
                  *[pl.BlockSpec((2*kvs*64,rows),lambda i:(0,0))]*slots],
        out_specs=[pl.BlockSpec((heads*64,qb),lambda i:(0,i)),
                   pl.BlockSpec((16,qb),lambda i:(0,i))],
        out_shape=[jax.ShapeDtypeStruct((heads*64,rows),F32),jax.ShapeDtypeStruct((16,rows),F32)],
        scratch_shapes=[pltpu.VMEM((kvs,slots,rows,64),BF),pltpu.VMEM((8,group*qb),F32),
                        pltpu.VMEM((kvs,72,group*qb),F32)],
        compiler_params=pltpu.CompilerParams(vmem_limit_bytes=56*2**20),
        cost_estimate=pl.CostEstimate(flops=int(25e9),bytes_accessed=int(8e6),transcendentals=int(1e7)),
    )(bias,qT,*kvT)

def bwd_kernel(*refs, kvs, group, slots, qb, lo, first, last):
    bias_ref, q_ref, do_ref, lse_ref, rd_ref = refs[:5]
    kv_ref, refs = refs[5 : 5 + slots], refs[5 + slots :]
    if not first:
        before_ref, refs = refs[0], refs[1:]
    if last:
        dq_ref, dkv_ref, low_ref, kv_scr = refs
    else:
        dq_ref, dkv_ref, kv_scr = refs
    step = pl.program_id(0)
    kw = kvs * 64

    @pl.when(step == 0)
    def _():
        for s in range(slots):
            for h in range(2 * kvs):
                kv_scr[h, s] = kv_ref[s][h * 64 : (h + 1) * 64, :].T
        dkv_ref[...] = jnp.zeros(dkv_ref.shape, F32) if first else before_ref[...]

    dq_ref[...] = jnp.zeros(dq_ref.shape, F32)
    qs = [heads_of(q_ref, h, group) for h in range(kvs)]
    dos = [heads_of(do_ref, h, group) for h in range(kvs)]

    def along(ref, h):
        return jnp.concatenate([ref[h * group + g : h * group + g + 1, :] for g in range(group)], axis=1)

    lses = [along(lse_ref, h) for h in range(kvs)]
    rds = [along(rd_ref, h) for h in range(kvs)]

    def chunk(c, masked):
        off = pl.multiple_of(c * qb, qb)
        for h in range(kvs):
            k = jnp.concatenate([kv_scr[h, s, pl.ds(off, qb), :] for s in range(slots)], axis=0)
            v = jnp.concatenate([kv_scr[kvs + h, s, pl.ds(off, qb), :] for s in range(slots)], axis=0)
            k_t = jnp.concatenate([kv_ref[s][h * 64 : (h + 1) * 64, pl.ds(off, qb)] for s in range(slots)], axis=1)
            st = mm(k, qs[h])
            if masked:
                st = st + jnp.concatenate([bias_ref[...].reshape(slots * qb, qb)] * group, axis=1)
            p = jnp.exp2(st - lses[h])
            dp = mm(v, dos[h])
            ds = (p * (dp - rds[h])).astype(BF)
            dk = mm(qs[h], ds, NT)
            dv = mm(dos[h], p.astype(BF), NT)
            dq = mm(k_t, ds)
            for s in range(slots):
                dkv_ref[s, h * 64 : (h + 1) * 64, pl.ds(off, qb)] += dk[:, s * qb : (s + 1) * qb]
                dkv_ref[s, kw + h * 64 : kw + (h + 1) * 64, pl.ds(off, qb)] += dv[:, s * qb : (s + 1) * qb]
            for g in range(group):
                r = h * group + g
                dq_ref[r * 64 : (r + 1) * 64, :] += dq[:, g * qb : (g + 1) * qb]

    def body(c, carry):
        chunk(c, False)
        return carry

    lax.fori_loop(0, step + lo, body, 0)
    chunk(step + lo, True)
    if last:

        @pl.when(step == pl.num_programs(0) - 1)
        def _():
            low_ref[...] = dkv_ref[slots - low_ref.shape[0] :].astype(BF)


def attn_bwd(bias, q_t, kv_t, do_t, lse, rd, lo, hi, before=None, last=False, kvs=3, group=3, qb=256):
    slots, rows = len(kv_t), kv_t[0].shape[1]
    width = kvs * group * 64
    whole = pl.BlockSpec((slots, 2 * kvs * 64, rows), lambda i: (0, 0, 0))
    tall = pl.BlockSpec((width, qb), lambda i: (0, i + lo))
    stat = pl.BlockSpec((16, qb), lambda i: (0, i + lo))
    out_specs = [pl.BlockSpec((width, qb), lambda i: (0, i)), whole]
    out_shape = [
        jax.ShapeDtypeStruct((width, (hi - lo) * qb), F32),
        jax.ShapeDtypeStruct((slots, 2 * kvs * 64, rows), F32),
    ]
    if last:
        sent = (1 if slots == 2 else slots, 2 * kvs * 64, rows)
        out_specs.append(pl.BlockSpec(sent, lambda i: (0, 0, 0)))
        out_shape.append(jax.ShapeDtypeStruct(sent, BF))
    args = (bias, q_t, do_t, lse, rd, *kv_t) + (() if before is None else (before,))
    units = sum(range(lo + 1, hi + 1))
    return pl.pallas_call(
        functools.partial(
            bwd_kernel, kvs=kvs, group=group, slots=slots, qb=qb, lo=lo, first=before is None, last=last
        ),
        grid=(hi - lo,),
        in_specs=[pl.BlockSpec((slots, qb, qb), lambda i: (0, 0, 0)), tall, tall, stat, stat]
        + [pl.BlockSpec((2 * kvs * 64, rows), lambda i: (0, 0))] * slots
        + ([] if before is None else [whole]),
        out_specs=out_specs,
        out_shape=out_shape,
        scratch_shapes=[pltpu.VMEM((2 * kvs, slots, rows, 64), BF)],
        compiler_params=pltpu.CompilerParams(vmem_limit_bytes=60 * 2**20),
        cost_estimate=pl.CostEstimate(flops=int(4e9) * units, bytes_accessed=int(16e6), transcendentals=0),
    )(*args)


TN = (((0,), (0,)), ((), ()))
TT = (((0,), (1,)), ((), ()))
BLOCK = 256
FF_BLOCK = 512
PIECES = 8
LIMIT = 60 * 2**20


def rotated(values, cosine, sine):
    a, b = values[:32], values[32:]
    return jnp.concatenate([a * cosine - b * sine, b * cosine + a * sine], axis=0)


def flat_rows(ref):
    count, sub, width = ref.shape
    return ref[...].reshape(count * sub, width)


def rms(values):
    return lax.rsqrt(jnp.mean(values * values, axis=-1, keepdims=True) + EPSILON)


def qkv_kernel(x_ref, w_ref, gain_ref, cos_ref, sin_ref, q_ref, kv_ref, wt_scr):
    @pl.when(pl.program_id(0) == 0)
    def _():
        wt_scr[...] = w_ref[:, : wt_scr.shape[0]].T

    source = flat_rows(x_ref).astype(F32)
    hidden = (source * rms(source) * gain_ref[0:1, :]).astype(BF)
    out = mm(wt_scr[...], hidden, NT)
    cosine, sine = cos_ref[...], sin_ref[...]
    for h in range(HEADS):
        part = rotated(out[h * 64 : (h + 1) * 64], cosine, sine)
        q_ref[h * 64 : (h + 1) * 64, :] = (part * (HEAD_DIM**-0.5 * LOG2E)).astype(BF)
    top = HEADS * 64
    for h in range(KV_HEADS):
        part = rotated(out[top + h * 64 : top + (h + 1) * 64], cosine, sine)
        kv_ref[h * 64 : (h + 1) * 64, :] = part.astype(BF)
    kv_ref[KV_HEADS * 64 :, :] = out[top + KV_HEADS * 64 :].astype(BF)


def project_qkv(x, first, gains, cosine, sine):
    count, sub, width = x.shape
    rows = count * sub
    per = BLOCK // sub
    kv2 = 2 * KV_HEADS * HEAD_DIM
    return pl.pallas_call(
        qkv_kernel,
        grid=(rows // BLOCK,),
        in_specs=[
            pl.BlockSpec((per, sub, width), lambda i: (i, 0, 0)),
            pl.BlockSpec(first.shape, lambda i: (0, 0)),
            pl.BlockSpec(gains.shape, lambda i: (0, 0)),
            pl.BlockSpec((32, BLOCK), lambda i: (0, i)),
            pl.BlockSpec((32, BLOCK), lambda i: (0, i)),
        ],
        out_specs=[pl.BlockSpec((width, BLOCK), lambda i: (0, i)), pl.BlockSpec((kv2, BLOCK), lambda i: (0, i))],
        out_shape=[jax.ShapeDtypeStruct((width, rows), BF), jax.ShapeDtypeStruct((kv2, rows), BF)],
        scratch_shapes=[pltpu.VMEM((width + kv2, width), BF)],
        compiler_params=pltpu.CompilerParams(vmem_limit_bytes=LIMIT),
        cost_estimate=pl.CostEstimate(flops=int(6e9), bytes_accessed=int(5e6), transcendentals=0),
    )(x, first, gains, cosine, sine)


def ffn_kernel(
    place_ref, o_ref, x_ref, cot_ref, first_ref, gain_ref,
    gate_own, gate_got, gate_swap, up_own, up_got, up_swap, down_own, down_got, down_swap,
    mixed_ref, dres_ref, datt_ref, rd_ref, keep_gu, send_gu, keep_do, send_do, gg_ref,
    acc_gu, acc_down, acc_out, gate_ref, up_ref, down_ref,
):
    step = pl.program_id(0)
    width = x_ref.shape[2]

    @pl.when(step == 0)
    def _():
        acc_gu[...] = jnp.zeros(acc_gu.shape, F32)
        acc_down[...] = jnp.zeros(acc_down.shape, F32)
        acc_out[...] = jnp.zeros(acc_out.shape, F32)
        gg_ref[...] = jnp.zeros(gg_ref.shape, F32)
        for rank in range(2):

            @pl.when(place_ref[1] == rank)
            def _():
                for ref, own in ((gate_ref, gate_own), (up_ref, up_own), (down_ref, down_own)):
                    n = own.shape[0]
                    ref[rank * n : (rank + 1) * n] = own[...]
                for core in range(2):

                    @pl.when(place_ref[0] == core)
                    def _():
                        for ref, parts in ((gate_ref, (gate_got, gate_swap)), (up_ref, (up_got, up_swap))):
                            n, m = parts[0].shape
                            for k, part in ((core, parts[0]), (1 - core, parts[1])):
                                ref[(1 - rank) * n : (2 - rank) * n, k * m : (k + 1) * m] = part[...]
                        n = down_got.shape[0]
                        for k, part in ((core, down_got), (1 - core, down_swap)):
                            low = (2 * (1 - rank) + k) * n
                            down_ref[low : low + n] = part[...]

    cols = first_ref.shape[1]
    out_w = first_ref[:, cols - width :]
    attended = o_ref[...]
    mixed = attended.astype(BF)
    residual = flat_rows(x_ref).astype(F32) + mm(mixed, out_w, TN)
    scale = rms(residual)
    normed = residual * scale
    gain = gain_ref[1:2, :]
    hidden = (normed * gain).astype(BF)
    gate = mm(hidden, gate_ref[...])
    up = mm(hidden, up_ref[...])
    sig = 0.5 * jnp.tanh(0.5 * gate) + 0.5
    silu = gate * sig
    activated = (silu * up).astype(BF)
    mixed_out = (residual + mm(activated, down_ref[...])).astype(BF)
    mixed_ref[...] = mixed_out.reshape(mixed_ref.shape)
    cot = flat_rows(cot_ref)
    d_act = mm(cot, down_ref[...], NT)
    acc_down[...] += mm(activated, cot, TN)
    d_gate = (d_act * up * sig * (1.0 + gate * (1.0 - sig))).astype(BF)
    d_up = (d_act * silu).astype(BF)
    acc_gu[0] += mm(hidden, d_gate, TN)
    acc_gu[1] += mm(hidden, d_up, TN)
    d_hidden = mm(d_gate, gate_ref[...], NT) + mm(d_up, up_ref[...], NT)
    dn = d_hidden * normed
    gg_ref[...] += jnp.sum(dn.reshape(-1, 8, width), axis=0)
    inner = jnp.mean(dn * gain, axis=-1, keepdims=True)
    d_res = cot.astype(F32) + scale * (d_hidden * gain - normed * inner)
    dres_ref[...] = d_res
    d_low = d_res.astype(BF)
    acc_out[...] += mm(mixed, d_low)
    d_att = mm(out_w, d_low, NT).astype(BF)
    datt_ref[...] = d_att
    prod = d_att.astype(F32) * attended
    for h in range(HEADS):
        rd_ref[h : h + 1, :] = jnp.sum(prod[h * 64 : (h + 1) * 64], axis=0, keepdims=True)
    rd_ref[HEADS:, :] = jnp.zeros((16 - HEADS, rd_ref.shape[1]), F32)

    @pl.when(step == pl.num_programs(0) - 1)
    def _():
        core = place_ref[0]
        half = width // 2
        ff = acc_gu.shape[2]
        for y in range(2):
            for p in range(PIECES):
                rs = slice(y * half + (p // 4) * (half // 2), y * half + (p // 4 + 1) * (half // 2))
                cs = slice((p % 4) * (ff // 4), (p % 4 + 1) * (ff // 4))
                keep_gu[y, p] = acc_gu[core, rs, cs].astype(BF)
                send_gu[y, p] = acc_gu[1 - core, rs, cs].astype(BF)
        down_rows, out_rows = ff // 32, width // 24
        for y in range(2):
            for p in range(PIECES):
                for ref, c in ((keep_do, core), (send_do, 1 - core)):
                    start = pl.multiple_of(y * (ff // 2) + (PIECES * c + p) * down_rows, 16)
                    ref[y, p, :down_rows] = acc_down[pl.ds(start, down_rows), :].astype(BF)
                    start = y * half + jnp.minimum(PIECES * c + p, half // out_rows - 1) * out_rows
                    ref[y, p, down_rows:] = acc_out[pl.ds(pl.multiple_of(start, 8), out_rows), :].astype(BF)


def feed_forward(place, attended, x, cot, first, gains, weights):
    count, sub, width = x.shape
    rows, ff = count * sub, weights[0].shape[1]
    per = FF_BLOCK // sub
    gu = (2, PIECES, width // 4, ff // 4)
    do = (2, PIECES, ff // 32 + width // 24, width)

    def whole(shape):
        return pl.BlockSpec(shape, lambda i: (0,) * len(shape), pipeline_mode=pl.Buffered(1))

    seq = pl.BlockSpec((per, sub, width), lambda i: (i, 0, 0))
    tall = pl.BlockSpec((width, FF_BLOCK), lambda i: (0, i))
    return pl.pallas_call(
        ffn_kernel,
        grid=(rows // FF_BLOCK,),
        in_specs=[
            pl.BlockSpec(memory_space=pltpu.SMEM), tall, seq, seq,
            whole(first.shape), whole(gains.shape), *(whole(w.shape) for w in weights),
        ],
        out_specs=[
            seq, pl.BlockSpec((FF_BLOCK, width), lambda i: (i, 0)), tall, pl.BlockSpec((16, FF_BLOCK), lambda i: (0, i)),
            whole(gu), whole(gu), whole(do), whole(do), whole((8, width)),
        ],
        out_shape=[
            jax.ShapeDtypeStruct(x.shape, BF),
            jax.ShapeDtypeStruct((rows, width), F32),
            jax.ShapeDtypeStruct((width, rows), BF),
            jax.ShapeDtypeStruct((16, rows), F32),
            jax.ShapeDtypeStruct(gu, BF), jax.ShapeDtypeStruct(gu, BF),
            jax.ShapeDtypeStruct(do, BF), jax.ShapeDtypeStruct(do, BF),
            jax.ShapeDtypeStruct((8, width), F32),
        ],
        scratch_shapes=[
            pltpu.VMEM((2, width, ff), F32), pltpu.VMEM((ff, width), F32), pltpu.VMEM((width, width), F32),
            pltpu.VMEM((width, ff), BF), pltpu.VMEM((width, ff), BF), pltpu.VMEM((ff, width), BF),
        ],
        compiler_params=pltpu.CompilerParams(vmem_limit_bytes=LIMIT),
        cost_estimate=pl.CostEstimate(flops=int(32e9), bytes_accessed=int(20e6), transcendentals=0),
    )(place, attended, x, cot, first, gains, *weights)


def back_kernel(*refs, spans):
    place_ref, refs = refs[0], refs[1:]
    dq_refs, refs = refs[: len(spans)], refs[len(spans) :]
    own_ref, got_ref, x_ref, dres_ref, first_ref, gain_ref, cos_ref, sin_ref, gg_ref, dx_ref = refs[:10]
    keep_ref, send_ref, acc, dt_scr, ga_scr, w_scr = refs[10:]
    step = pl.program_id(0)
    width = x_ref.shape[2]
    kv = KV_HEADS * 64
    total = width + 2 * kv

    @pl.when(step == 0)
    def _():
        acc[...] = jnp.zeros(acc.shape, F32)
        ga_scr[...] = jnp.zeros(ga_scr.shape, F32)
        w_scr[...] = first_ref[:, :total].T

    cosine, sine = cos_ref[...], -sin_ref[...]
    for (lo, hi), dq_ref in zip(spans, dq_refs):

        @pl.when((step >= lo) & (step < hi))
        def _():
            for h in range(HEADS):
                part = dq_ref[h * 64 : (h + 1) * 64, :] * (HEAD_DIM**-0.5)
                dt_scr[h * 64 : (h + 1) * 64, :] = rotated(part, cosine, sine).astype(BF)

    d_kv = own_ref[0] + got_ref[...].astype(F32)
    for h in range(KV_HEADS):
        part = d_kv[h * 64 : (h + 1) * 64] * LN2
        dt_scr[width + h * 64 : width + (h + 1) * 64, :] = rotated(part, cosine, sine).astype(BF)
    dt_scr[width + kv :, :] = d_kv[kv:].astype(BF)
    d_t = dt_scr[...]
    source = flat_rows(x_ref).astype(F32)
    scale = rms(source)
    normed = source * scale
    gain = gain_ref[0:1, :]
    hidden = (normed * gain).astype(BF)
    acc[:total] += mm(d_t, hidden)
    d_hidden = mm(d_t, w_scr[...], TN)
    dn = d_hidden * normed
    ga_scr[...] += jnp.sum(dn.reshape(-1, 8, width), axis=0)
    inner = jnp.mean(dn * gain, axis=-1, keepdims=True)
    grad = dres_ref[...] + scale * (d_hidden * gain - normed * inner)
    dx_ref[...] = grad.astype(BF).reshape(dx_ref.shape)

    @pl.when(step == pl.num_programs(0) - 1)
    def _():
        core = place_ref[0]
        acc[total : total + 1, :] = jnp.sum(ga_scr[...], axis=0, keepdims=True)
        acc[total + 1 : total + 2, :] = jnp.sum(gg_ref[...], axis=0, keepdims=True)
        half, deep = width // 2, width // 4
        for ct in range(4):
            for ref, c in ((keep_ref, core), (send_ref, 1 - core)):
                start = pl.multiple_of(c * 512 + ct * 128, 128)
                block = acc[pl.ds(start, 128), :].T.astype(BF)
                for y in range(2):
                    for rh in range(2):
                        low = y * half + rh * deep
                        ref[y, rh * 4 + ct] = block[low : low + deep]


def back_qkv(place, spans, d_query, d_kv, got, x, d_res, first, gains, cosine, sine, gg):
    count, sub, width = x.shape
    rows = count * sub
    per = BLOCK // sub
    kv2 = 2 * KV_HEADS * HEAD_DIM
    piece = (2, PIECES, width // 4, 128)

    def whole(shape):
        return pl.BlockSpec(shape, lambda i: (0,) * len(shape))

    seq = pl.BlockSpec((per, sub, width), lambda i: (i, 0, 0))
    return pl.pallas_call(
        functools.partial(back_kernel, spans=spans),
        grid=(rows // BLOCK,),
        in_specs=[
            pl.BlockSpec(memory_space=pltpu.SMEM),
            *(
                pl.BlockSpec((width, BLOCK), lambda i, lo=lo, hi=hi: (0, jnp.clip(i - lo, 0, hi - lo - 1)))
                for lo, hi in spans
            ),
            pl.BlockSpec((1, kv2, BLOCK), lambda i: (0, 0, i)),
            pl.BlockSpec((kv2, BLOCK), lambda i: (0, i)),
            seq, pl.BlockSpec((BLOCK, width), lambda i: (i, 0)),
            whole(first.shape), whole(gains.shape),
            pl.BlockSpec((32, BLOCK), lambda i: (0, i)), pl.BlockSpec((32, BLOCK), lambda i: (0, i)),
            whole(gg.shape),
        ],
        out_specs=[seq, whole(piece), whole(piece)],
        out_shape=[jax.ShapeDtypeStruct(x.shape, BF), jax.ShapeDtypeStruct(piece, BF), jax.ShapeDtypeStruct(piece, BF)],
        scratch_shapes=[
            pltpu.VMEM((1024, width), F32), pltpu.VMEM((width + kv2, BLOCK), BF), pltpu.VMEM((8, width), F32),
            pltpu.VMEM((width + kv2, width), BF),
        ],
        compiler_params=pltpu.CompilerParams(vmem_limit_bytes=LIMIT),
        cost_estimate=pl.CostEstimate(flops=int(10e9), bytes_accessed=int(10e6), transcendentals=0),
    )(place, *d_query, d_kv, got, x, d_res, first, gains, cosine, sine, gg)


def final_kernel(
    at_ref, gu4, gu_x, gu_c, do4, do_x, do_c, gate_ref, up_ref, turned_ref, out_ref, down_ref
):
    core, xb, z = at_ref[0], at_ref[1], at_ref[2]
    deep, wide = gu4.shape[1:]
    for f in range(2):
        for e in range(2):
            for j, d in enumerate((0, 2, 1, 3)):
                gu = (gu4[j] if e == 0 else gu_x[j]) if f == 0 else gu_c[e * 4 + j]
                do = (do4[j] if e == 0 else do_x[j]) if f == 0 else do_c[e * 4 + j]
                rs = pl.ds(pl.multiple_of((xb ^ e) * deep, 16), deep)
                cs = pl.ds(pl.multiple_of((z ^ d) * wide, 128), wide)
                for c, ref in ((0, gate_ref), (1, up_ref)):

                    @pl.when((core ^ f) == c)
                    def _():
                        ref[rs, cs] = gu.astype(F32)

                m = (core ^ f) * 8 + (xb ^ e) * 4 + (z ^ d)
                rows = down_ref.shape[0] // 16
                down_ref[pl.ds(pl.multiple_of(m * rows, 8), rows), :] = do[:rows].astype(F32)
                few = do.shape[0] - rows

                @pl.when(m < out_ref.shape[0] // few)
                def _():
                    out_ref[pl.ds(pl.multiple_of(m * few, 8), few), :] = do[rows:].astype(F32)

    turned_ref[...] = down_ref[...].T


def final_ffn(at, gu4, gu_x, gu_c, do4, do_x, do_c, half, ff, width):
    f32 = lambda *s: jax.ShapeDtypeStruct(s, F32)
    return pl.pallas_call(
        final_kernel,
        in_specs=[pl.BlockSpec(memory_space=pltpu.SMEM)] + [pl.BlockSpec(memory_space=pltpu.VMEM)] * 6,
        out_specs=[pl.BlockSpec(memory_space=pltpu.VMEM)] * 4,
        out_shape=[f32(half, ff), f32(half, ff), f32(width, ff // 2), f32(half, width)],
        scratch_shapes=[pltpu.VMEM((ff // 2, width), F32)],
        compiler_params=pltpu.CompilerParams(vmem_limit_bytes=LIMIT),
        cost_estimate=pl.CostEstimate(flops=int(5e9), bytes_accessed=int(10e6), transcendentals=0),
    )(at, gu4, gu_x, gu_c, do4, do_x, do_c)


def final_t_kernel(at_ref, t4, t_x, t_c, q_ref, k_ref, v_ref, g_ref, whole):
    core, xb, z = at_ref[0], at_ref[1], at_ref[2]
    deep, wide = t4.shape[1:]
    for f in range(2):
        for e in range(2):
            for j, d in enumerate((0, 2, 1, 3)):
                t = (t4[j] if e == 0 else t_x[j]) if f == 0 else t_c[e * 4 + j]
                rs = pl.ds(pl.multiple_of((xb ^ e) * deep, 16), deep)
                cs = pl.ds(pl.multiple_of((core ^ f) * 512 + (z ^ d) * wide, 128), wide)
                whole[rs, cs] = t.astype(F32)
    a = q_ref.shape[1]
    b = a + k_ref.shape[1]
    c = b + v_ref.shape[1]
    q_ref[...] = whole[:, :a]
    k_ref[...] = whole[:, a:b]
    v_ref[...] = whole[:, b:c]
    g_ref[...] = whole[:, c:].T[:8]


def final_t(at, t4, t_x, t_c, half, width, kv_width):
    f32 = lambda *s: jax.ShapeDtypeStruct(s, F32)
    return pl.pallas_call(
        final_t_kernel,
        in_specs=[pl.BlockSpec(memory_space=pltpu.SMEM)] + [pl.BlockSpec(memory_space=pltpu.VMEM)] * 3,
        out_specs=[pl.BlockSpec(memory_space=pltpu.VMEM)] * 4,
        out_shape=[f32(half, width), f32(half, kv_width), f32(half, kv_width), f32(8, half)],
        scratch_shapes=[pltpu.VMEM((half, 1024), F32)],
        compiler_params=pltpu.CompilerParams(vmem_limit_bytes=LIMIT),
        cost_estimate=pl.CostEstimate(flops=int(1e9), bytes_accessed=int(2e6), transcendentals=0),
    )(at, t4, t_x, t_c)


def swap(x, axis, bit):
    n = lax.axis_size(axis)
    return lax.ppermute(x, axis, [(i, i ^ (1 << bit)) for i in range(n)])


def bit_of(axis, bit):
    return (lax.axis_index(axis) >> bit) & 1


def pin(*arrays):
    return lax.optimization_barrier(arrays)


def pick(x, at):
    return lax.dynamic_index_in_dim(x, at, 0, keepdims=False)


def in_order(flag, mine, other, axis):
    return jnp.where(
        flag == 0,
        jnp.concatenate([mine, other], axis=axis),
        jnp.concatenate([other, mine], axis=axis),
    )


def plus(a, b):
    return (a.astype(F32) + b.astype(F32)).astype(BF)


def two_level():
    return lax.axis_size("fsdp") == 2 and lax.axis_size("ctx") == 16


def z_low_send(x):
    low = bit_of("ctx", 2)
    x = x.reshape((2, 2) + x.shape[1:]).swapaxes(0, 1)
    return pick(x, low), pick(x, 1 - low)


def high_send(x):
    high = bit_of("ctx", 3)
    return pick(x, high), pick(x, 1 - high)


def double(x, bit):
    return jnp.concatenate([x, swap(x, "ctx", bit)], axis=0)


def natural_gu(pieces):
    _, a, b = pieces.shape
    return pieces.reshape(2, 4, a, b).transpose(0, 2, 1, 3).reshape(2 * a, 4 * b).astype(F32)


def other_sum(x):
    x = lax.psum_scatter(x.astype(BF), "fsdp", scatter_dimension=0, tiled=True)
    return lax.psum(x, "ctx").astype(F32)


def local(tokens, gain_attn, w_query, w_key, w_value, w_out, gain_ffn, w_gate, w_up, w_down, cotangent):
    seqs, length, width = tokens.shape
    count = lax.axis_size("ctx")
    team = count // seqs
    sub = length // team
    rows = count * sub
    ff = w_gate.shape[1]
    kv_width = KV_HEADS * HEAD_DIM
    qkv_cols = width + 2 * kv_width
    place = lax.axis_index("ctx") % team
    own = gain_attn.shape[0]
    fast = two_level()

    def move(x):
        return lax.all_to_all(x.reshape(count, sub, width), "ctx", 0, 0, tiled=True)

    x = move(tokens)
    gain_rows = jnp.zeros((8, ff), BF).at[0, :own].set(gain_attn).at[1, :own].set(gain_ffn)
    first = jnp.concatenate([jnp.concatenate([w_query, w_key, w_value, w_out], axis=1), gain_rows], axis=0)
    if fast:
        core, rank = bit_of("ctx", 0), bit_of("fsdp", 0)

        def halved(shard, axis):
            half = shard.shape[axis] // 2
            return lax.dynamic_slice_in_dim(shard, core * half, half, axis)

        def other_shard(got, axis):
            return in_order(core, got, swap(got, "ctx", 0), axis)

        got = swap(halved(first, 1), "fsdp", 0)
        other = other_shard(got, 1)
        gains = in_order(rank, first[own : own + 2, :own], other[own : own + 2, :own], 1).astype(F32)
        first = in_order(rank, first[:own], other[:own], 0)
        gate_half, up_half, down_half, got = pin(halved(w_gate, 1), halved(w_up, 1), halved(w_down, 0), got)
        gate_got, up_got, down_got = (swap(h, "fsdp", 0) for h in (gate_half, up_half, down_half))
    else:
        first = lax.all_gather(first, "fsdp", axis=0)
        gains = first[:, own : own + 2, :own].transpose(1, 0, 2).reshape(2, width).astype(F32)
        first = first[:, :own].reshape(width, first.shape[2])
        gate_w, up_w, down_w = (lax.all_gather(w, "fsdp", axis=0, tiled=True) for w in (w_gate, w_up, w_down))
    gains = jnp.pad(gains, ((0, 6), (0, 0)))

    row = jnp.arange(rows, dtype=jnp.int32)
    position = (row // sub) * length + place * sub + row % sub
    frequency = THETA ** (-jnp.arange(HEAD_DIM // 2, dtype=F32) * 2.0 / HEAD_DIM)
    angles = frequency[:, None] * position.astype(F32)[None, :]
    cosine, sine = jnp.cos(angles), jnp.sin(angles)
    groups = [[t * team + p for p in range(team)] for t in range(seqs)]
    slots = jnp.stack([place, 1 - place]) if team == 2 else jnp.arange(team)
    block_row = jnp.arange(BLOCK, dtype=jnp.int32)
    base = (block_row // sub) * length + block_row % sub
    key_pos = base[None, :] + slots[:, None] * sub
    query_pos = base + place * sub
    bias = jnp.where(key_pos[:, :, None] <= query_pos[None, None, :], 0.0, NEGATIVE).astype(F32)
    flags = jnp.stack([core, rank]) if fast else jnp.zeros((2,), jnp.int32)

    x, cot_send = pin(x, cotangent)
    cot = move(cot_send)
    query, kv_own = project_qkv(x, first, gains, cosine, sine)
    if fast:
        kv_own, gate_got = pin(kv_own, gate_got)
    if team == 2:
        kv_all = (kv_own, swap(kv_own, "ctx", 0))
    else:
        kv_all = lax.all_gather(kv_own, "ctx", axis=0, axis_index_groups=groups)
        kv_all = tuple(kv_all[s] for s in range(team))
    attended, log_total = attn_fwd(bias, query, kv_all)
    if fast:
        attended, cot, *gots = pin(attended, cot, gate_got, up_got, down_got)
        gots = [(got, swap(got, "ctx", 0)) for got in gots]
        weights = [a for own_w, two in zip((w_gate, w_up, w_down), gots) for a in (own_w, *two)]
    else:
        attended, cot = pin(attended, cot)
        low, side = width // 2, ff // 2
        weights = [a for w in (gate_w, up_w) for a in (w[:low], w[low:, :side], w[low:, side:])]
        weights += [down_w[:side], down_w[side : side + side // 2], down_w[side + side // 2 :]]
    mixed, d_res, d_att, row_dot, keep_gu, send_gu, keep_do, send_do, gain_sum = feed_forward(
        flags, attended, x, cot, first, gains, weights
    )
    mixed_out = move(mixed)

    n = rows // BLOCK
    spans = ((0, n - 1), (n - 1, n))
    part = functools.partial(attn_bwd, bias, query, kv_all, d_att, log_total, row_dot)
    if fast:
        x_bit = bit_of("ctx", 1)
        got_gu, got_do = swap(send_gu, "ctx", 0), swap(send_do, "ctx", 0)
        gu, do = plus(keep_gu, got_gu), plus(keep_do, got_do)
        gu = gu.reshape((2, 2, 4) + gu.shape[2:]).swapaxes(0, 1)
        keep_gu, send_gu = pick(gu, x_bit), pick(gu, 1 - x_bit)
        keep_do, send_do = pick(do, rank), pick(do, 1 - rank)
        send_gu, send_do, row_dot = pin(send_gu, send_do, row_dot)
        part = functools.partial(attn_bwd, bias, query, kv_all, d_att, log_total, row_dot)
        got_gu, got_do = swap(send_gu, "ctx", 1), swap(send_do, "fsdp", 0)
        dq_a, before = part(*spans[0])
        got_gu, got_do, mixed_out, before = pin(got_gu, got_do, mixed_out, before)
        gu, do = plus(keep_gu, got_gu), plus(keep_do, got_do)
        do = do.reshape((2, 4) + do.shape[1:])
        keep_gu, send_gu = pick(gu, rank), pick(gu, 1 - rank)
        keep_do, send_do = pick(do, x_bit), pick(do, 1 - x_bit)
        send_gu, send_do, before = pin(send_gu, send_do, before)
        got_gu, got_do = swap(send_gu, "fsdp", 0), swap(send_do, "ctx", 1)
        dq_b, d_kv, d_kv_low = part(*spans[1], before=before, last=True)
        got_gu, got_do, d_kv_low, dq_b = pin(got_gu, got_do, d_kv_low, dq_b)
        gu, do = plus(keep_gu, got_gu), plus(keep_do, got_do)
    else:
        dq_a, before = part(*spans[0])
        dq_b, d_kv, d_kv_low = part(*spans[1], before=before, last=True)
    if team == 2:
        own_kv, got_kv = d_kv, swap(d_kv_low.reshape(2 * kv_width, rows), "ctx", 0)
    else:
        own_kv = lax.psum_scatter(d_kv_low, "ctx", scatter_dimension=0, axis_index_groups=groups)
        own_kv, got_kv = own_kv.astype(F32)[None], jnp.zeros((2 * kv_width, rows), BF)
    if fast:
        keep_gu, send_gu = z_low_send(gu)
        keep_do, send_do = z_low_send(do)
        own_kv, got_kv, send_gu, send_do = pin(own_kv, got_kv, send_gu, send_do)
        got_gu, got_do = swap(send_gu, "ctx", 2), swap(send_do, "ctx", 2)
    d_x, keep_t, send_t = back_qkv(
        flags, spans, (dq_a, dq_b), own_kv, got_kv, x, d_res, first, gains, cosine, sine, gain_sum
    )
    if fast:
        d_x, keep_t, send_t, got_gu, got_do = pin(d_x, keep_t, send_t, got_gu, got_do)
        gu, do = plus(keep_gu, got_gu), plus(keep_do, got_do)
    if fast:
        keep_gu, send_gu = high_send(gu)
        keep_do, send_do = high_send(do)
        got_gu, got_do = swap(send_gu, "ctx", 3), swap(send_do, "ctx", 3)
        got_t, got_gu, got_do = pin(swap(send_t, "ctx", 0), got_gu, got_do)
        t = plus(keep_t, got_t)
        gu, do = plus(keep_gu, got_gu)[None], plus(keep_do, got_do)[None]
        keep_t, got_t = pick(t, rank), swap(pick(t, 1 - rank), "fsdp", 0)
        gu_h, do_h = swap(gu, "ctx", 3), swap(do, "ctx", 3)
        d_x, got_t, gu_h, do_h = pin(d_x, got_t, gu_h, do_h)
        grad_tokens = move(d_x)
        t = plus(keep_t, got_t)
        t = t.reshape((2, 4) + t.shape[1:])
        keep_t, got_t = pick(t, x_bit), swap(pick(t, 1 - x_bit), "ctx", 1)
        gu, do = jnp.concatenate([gu, gu_h], axis=0), jnp.concatenate([do, do_h], axis=0)
        gu_l, do_l = swap(gu, "ctx", 2), swap(do, "ctx", 2)
        keep_t, send_t = z_low_send(plus(keep_t, got_t))
        got_t = swap(send_t, "ctx", 2)
        got_t, gu_l, do_l = pin(got_t, gu_l, do_l)
        gu_four, do_four = jnp.concatenate([gu, gu_l], axis=0), jnp.concatenate([do, do_l], axis=0)
        do_x, gu_x = swap(do_four, "ctx", 1), swap(gu_four, "ctx", 1)
        keep_t, send_t = high_send(plus(keep_t, got_t))
        got_t = swap(send_t, "ctx", 3)
        do_x, gu_x, got_t, grad_tokens = pin(do_x, gu_x, got_t, grad_tokens)
        gu_c = swap(jnp.concatenate([gu_four, gu_x], axis=0), "ctx", 0)
        do_c = swap(jnp.concatenate([do_four, do_x], axis=0), "ctx", 0)
        t = plus(keep_t, got_t)[None]
        t_high = swap(t, "ctx", 3)
        t_high, gu_c, do_c = pin(t_high, gu_c, do_c)
        at = jnp.stack([core, x_bit, lax.axis_index("ctx") >> 2])
        own_gate, own_up, own_down, own_out = final_ffn(
            at, gu_four, gu_x, gu_c, do_four, do_x, do_c, width // 2, ff, width
        )
        t_four = double(jnp.concatenate([t, t_high], axis=0), 2)
        t_four, own_gate, own_up, own_down, own_out = pin(t_four, own_gate, own_up, own_down, own_out)
        own_down = own_down.T
        t_x = swap(t_four, "ctx", 1)
        t_c = swap(jnp.concatenate([t_four, t_x], axis=0), "ctx", 0)
        own_query, own_key, own_value, own_gains = final_t(at, t_four, t_x, t_c, width // 2, width, kv_width)
    else:
        grad_tokens = move(d_x)
        pair = jnp.stack([keep_gu, send_gu])
        gate, up = (jnp.concatenate([natural_gu(pair[c, y]) for y in range(2)], axis=0) for c in range(2))
        do = jnp.stack([keep_do, send_do], axis=1).reshape((32,) + keep_do.shape[2:])
        deep = ff // 32
        own_gate, own_up = other_sum(gate), other_sum(up)
        own_down = other_sum(do[:, :deep].reshape(ff, width))
        out = do[:, deep:].reshape((2, -1, width))[:, : width // 2]
        own_out = other_sum(out.reshape(width, width))
        pair = jnp.stack([keep_t, send_t])
        t = [jnp.concatenate([natural_gu(pair[c, y]) for c in range(2)], axis=1) for y in range(2)]
        own_t = other_sum(jnp.concatenate(t, axis=0))
        own_query, own_key = own_t[:, :width], own_t[:, width : width + kv_width]
        own_value, own_gains = own_t[:, width + kv_width : qkv_cols], own_t[:, qkv_cols:].T
    return (
        mixed_out.reshape(tokens.shape),
        grad_tokens.reshape(tokens.shape),
        own_gains[0],
        own_query,
        own_key,
        own_value,
        own_out,
        own_gains[1],
        own_gate,
        own_up,
        own_down,
    )


def solution(mesh):
    rows, flat, seq = P("fsdp", None), P("fsdp"), P("fsdp", "ctx", None)
    return jax.shard_map(
        local,
        mesh=mesh,
        in_specs=(seq, flat, rows, rows, rows, rows, flat, rows, rows, rows, seq),
        out_specs=(seq, seq, flat, rows, rows, rows, rows, flat, rows, rows, rows),
        check_vma=False,
    )
```

```python
import functools

import jax
import jax.numpy as jnp
from jax import lax
from jax.experimental import pallas as pl
from jax.experimental.pallas import tpu as pltpu
from jax.sharding import PartitionSpec as P

HEADS = 9
KV_HEADS = 3
HEAD_DIM = 64
EPSILON = 1e-05
THETA = 100000.0
NEGATIVE = -1e30
LOG2E = 1.4426950408889634
LN2 = 0.6931471805599453
F32=jnp.float32; BF=jnp.bfloat16
NT=(((1,),(1,)),((),()))
NN=(((1,),(0,)),((),()))
def mm(a,b,dims=NN):
    return lax.dot_general(a,b,dims,preferred_element_type=F32)

def heads_of(ref, kv, group):
    return jnp.concatenate([ref[(kv*group+h)*64:(kv*group+h+1)*64,:] for h in range(group)],axis=1)

def fwd_kernel(bias_ref, q_ref, *refs, kvs, group, slots, rows, qb):
    kv_ref, (o_ref, lse_ref, k_scr, m_scr, acc_scr)=refs[:slots], refs[slots:]
    i=pl.program_id(0)
    kw=kvs*64
    @pl.when(i==0)
    def _():
        for s in range(slots):
            for h in range(kvs):
                k_scr[h,s]=kv_ref[s][h*64:(h+1)*64,:].T
    qs=[heads_of(q_ref,h,group) for h in range(kvs)]
    width=group*qb
    m_scr[...]=jnp.full(m_scr.shape,-1e30,F32)
    acc_scr[...]=jnp.zeros(acc_scr.shape,F32)
    ones=jnp.ones((8,slots*qb),BF)
    def chunk(c, masked):
        off=pl.multiple_of(c*qb,qb)
        for h in range(kvs):
            k=jnp.concatenate([k_scr[h,s,pl.ds(off,qb),:] for s in range(slots)],axis=0)
            v=jnp.concatenate([kv_ref[s][kw+h*64:kw+(h+1)*64,pl.ds(off,qb)] for s in range(slots)],axis=1)
            v=jnp.concatenate([v,ones],axis=0)
            st=mm(k,qs[h])
            if masked:
                b=bias_ref[...].reshape(slots*qb,qb)
                st=st+jnp.concatenate([b]*group,axis=1)
            m_old=m_scr[h:h+1,:]
            m_new=jnp.maximum(m_old,jnp.max(st,axis=0,keepdims=True))
            p=jnp.exp2(st-m_new).astype(BF)
            acc_scr[h]=acc_scr[h]*jnp.exp2(m_old-m_new)+mm(v,p)
            m_scr[h:h+1,:]=m_new
    def body(c,_):
        chunk(c,False); return 0
    lax.fori_loop(0,i,body,0)
    chunk(i,True)
    for h in range(kvs):
        acc=acc_scr[h]
        tot=acc[64:65,:]
        o=acc[:64,:]*(1.0/tot)
        lse=m_scr[h:h+1,:]+jnp.log2(tot)
        for g in range(group):
            r=h*group+g
            o_ref[r*64:(r+1)*64,:]=o[:,g*qb:(g+1)*qb]
            lse_ref[r:r+1,:]=lse[:,g*qb:(g+1)*qb]

def attn_fwd(bias, qT, kvT, kvs=3, group=3, qb=256):
    slots,rows=len(kvT),kvT[0].shape[1]
    n=rows//qb
    heads=kvs*group
    return pl.pallas_call(
        functools.partial(fwd_kernel,kvs=kvs,group=group,slots=slots,rows=rows,qb=qb),
        grid=(n,),
        in_specs=[pl.BlockSpec((slots,qb,qb),lambda i:(0,0,0)),
                  pl.BlockSpec((heads*64,qb),lambda i:(0,i)),
                  *[pl.BlockSpec((2*kvs*64,rows),lambda i:(0,0))]*slots],
        out_specs=[pl.BlockSpec((heads*64,qb),lambda i:(0,i)),
                   pl.BlockSpec((16,qb),lambda i:(0,i))],
        out_shape=[jax.ShapeDtypeStruct((heads*64,rows),F32),jax.ShapeDtypeStruct((16,rows),F32)],
        scratch_shapes=[pltpu.VMEM((kvs,slots,rows,64),BF),pltpu.VMEM((8,group*qb),F32),
                        pltpu.VMEM((kvs,72,group*qb),F32)],
        compiler_params=pltpu.CompilerParams(vmem_limit_bytes=56*2**20),
        cost_estimate=pl.CostEstimate(flops=int(25e9),bytes_accessed=int(8e6),transcendentals=int(1e7)),
    )(bias,qT,*kvT)

def bwd_kernel(*refs, kvs, group, slots, qb, lo, first, last):
    bias_ref, q_ref, do_ref, lse_ref, rd_ref = refs[:5]
    kv_ref, refs = refs[5 : 5 + slots], refs[5 + slots :]
    if not first:
        before_ref, refs = refs[0], refs[1:]
    if last:
        dq_ref, dkv_ref, low_ref, kv_scr = refs
    else:
        dq_ref, dkv_ref, kv_scr = refs
    step = pl.program_id(0)
    kw = kvs * 64

    @pl.when(step == 0)
    def _():
        for s in range(slots):
            for h in range(2 * kvs):
                kv_scr[h, s] = kv_ref[s][h * 64 : (h + 1) * 64, :].T
        dkv_ref[...] = jnp.zeros(dkv_ref.shape, F32) if first else before_ref[...]

    dq_ref[...] = jnp.zeros(dq_ref.shape, F32)
    qs = [heads_of(q_ref, h, group) for h in range(kvs)]
    dos = [heads_of(do_ref, h, group) for h in range(kvs)]

    def along(ref, h):
        return jnp.concatenate([ref[h * group + g : h * group + g + 1, :] for g in range(group)], axis=1)

    lses = [along(lse_ref, h) for h in range(kvs)]
    rds = [along(rd_ref, h) for h in range(kvs)]

    def chunk(c, masked):
        off = pl.multiple_of(c * qb, qb)
        for h in range(kvs):
            k = jnp.concatenate([kv_scr[h, s, pl.ds(off, qb), :] for s in range(slots)], axis=0)
            v = jnp.concatenate([kv_scr[kvs + h, s, pl.ds(off, qb), :] for s in range(slots)], axis=0)
            k_t = jnp.concatenate([kv_ref[s][h * 64 : (h + 1) * 64, pl.ds(off, qb)] for s in range(slots)], axis=1)
            st = mm(k, qs[h])
            if masked:
                st = st + jnp.concatenate([bias_ref[...].reshape(slots * qb, qb)] * group, axis=1)
            p = jnp.exp2(st - lses[h])
            dp = mm(v, dos[h])
            ds = (p * (dp - rds[h])).astype(BF)
            dk = mm(qs[h], ds, NT)
            dv = mm(dos[h], p.astype(BF), NT)
            dq = mm(k_t, ds)
            for s in range(slots):
                dkv_ref[s, h * 64 : (h + 1) * 64, pl.ds(off, qb)] += dk[:, s * qb : (s + 1) * qb]
                dkv_ref[s, kw + h * 64 : kw + (h + 1) * 64, pl.ds(off, qb)] += dv[:, s * qb : (s + 1) * qb]
            for g in range(group):
                r = h * group + g
                dq_ref[r * 64 : (r + 1) * 64, :] += dq[:, g * qb : (g + 1) * qb]

    def body(c, carry):
        chunk(c, False)
        return carry

    lax.fori_loop(0, step + lo, body, 0)
    chunk(step + lo, True)
    if last:

        @pl.when(step == pl.num_programs(0) - 1)
        def _():
            low_ref[...] = dkv_ref[slots - low_ref.shape[0] :].astype(BF)


def attn_bwd(bias, q_t, kv_t, do_t, lse, rd, lo, hi, before=None, last=False, kvs=3, group=3, qb=256):
    slots, rows = len(kv_t), kv_t[0].shape[1]
    width = kvs * group * 64
    whole = pl.BlockSpec((slots, 2 * kvs * 64, rows), lambda i: (0, 0, 0))
    tall = pl.BlockSpec((width, qb), lambda i: (0, i + lo))
    stat = pl.BlockSpec((16, qb), lambda i: (0, i + lo))
    out_specs = [pl.BlockSpec((width, qb), lambda i: (0, i)), whole]
    out_shape = [
        jax.ShapeDtypeStruct((width, (hi - lo) * qb), F32),
        jax.ShapeDtypeStruct((slots, 2 * kvs * 64, rows), F32),
    ]
    if last:
        sent = (1 if slots == 2 else slots, 2 * kvs * 64, rows)
        out_specs.append(pl.BlockSpec(sent, lambda i: (0, 0, 0)))
        out_shape.append(jax.ShapeDtypeStruct(sent, BF))
    args = (bias, q_t, do_t, lse, rd, *kv_t) + (() if before is None else (before,))
    units = sum(range(lo + 1, hi + 1))
    return pl.pallas_call(
        functools.partial(
            bwd_kernel, kvs=kvs, group=group, slots=slots, qb=qb, lo=lo, first=before is None, last=last
        ),
        grid=(hi - lo,),
        in_specs=[pl.BlockSpec((slots, qb, qb), lambda i: (0, 0, 0)), tall, tall, stat, stat]
        + [pl.BlockSpec((2 * kvs * 64, rows), lambda i: (0, 0))] * slots
        + ([] if before is None else [whole]),
        out_specs=out_specs,
        out_shape=out_shape,
        scratch_shapes=[pltpu.VMEM((2 * kvs, slots, rows, 64), BF)],
        compiler_params=pltpu.CompilerParams(vmem_limit_bytes=60 * 2**20),
        cost_estimate=pl.CostEstimate(flops=int(4e9) * units, bytes_accessed=int(16e6), transcendentals=0),
    )(*args)


TN = (((0,), (0,)), ((), ()))
TT = (((0,), (1,)), ((), ()))
BLOCK = 256
FF_BLOCK = 512
PIECES = 8
LIMIT = 60 * 2**20


def rotated(values, cosine, sine):
    a, b = values[:32], values[32:]
    return jnp.concatenate([a * cosine - b * sine, b * cosine + a * sine], axis=0)


def flat_rows(ref):
    count, sub, width = ref.shape
    return ref[...].reshape(count * sub, width)


def rms(values):
    return lax.rsqrt(jnp.mean(values * values, axis=-1, keepdims=True) + EPSILON)


def qkv_kernel(x_ref, w_ref, gain_ref, cos_ref, sin_ref, q_ref, kv_ref, wt_scr):
    @pl.when(pl.program_id(0) == 0)
    def _():
        wt_scr[...] = w_ref[:, : wt_scr.shape[0]].T

    source = flat_rows(x_ref).astype(F32)
    hidden = (source * rms(source) * gain_ref[0:1, :]).astype(BF)
    out = mm(wt_scr[...], hidden, NT)
    cosine, sine = cos_ref[...], sin_ref[...]
    for h in range(HEADS):
        part = rotated(out[h * 64 : (h + 1) * 64], cosine, sine)
        q_ref[h * 64 : (h + 1) * 64, :] = (part * (HEAD_DIM**-0.5 * LOG2E)).astype(BF)
    top = HEADS * 64
    for h in range(KV_HEADS):
        part = rotated(out[top + h * 64 : top + (h + 1) * 64], cosine, sine)
        kv_ref[h * 64 : (h + 1) * 64, :] = part.astype(BF)
    kv_ref[KV_HEADS * 64 :, :] = out[top + KV_HEADS * 64 :].astype(BF)


def project_qkv(x, first, gains, cosine, sine):
    count, sub, width = x.shape
    rows = count * sub
    per = BLOCK // sub
    kv2 = 2 * KV_HEADS * HEAD_DIM
    return pl.pallas_call(
        qkv_kernel,
        grid=(rows // BLOCK,),
        in_specs=[
            pl.BlockSpec((per, sub, width), lambda i: (i, 0, 0)),
            pl.BlockSpec(first.shape, lambda i: (0, 0)),
            pl.BlockSpec(gains.shape, lambda i: (0, 0)),
            pl.BlockSpec((32, BLOCK), lambda i: (0, i)),
            pl.BlockSpec((32, BLOCK), lambda i: (0, i)),
        ],
        out_specs=[pl.BlockSpec((width, BLOCK), lambda i: (0, i)), pl.BlockSpec((kv2, BLOCK), lambda i: (0, i))],
        out_shape=[jax.ShapeDtypeStruct((width, rows), BF), jax.ShapeDtypeStruct((kv2, rows), BF)],
        scratch_shapes=[pltpu.VMEM((width + kv2, width), BF)],
        compiler_params=pltpu.CompilerParams(vmem_limit_bytes=LIMIT),
        cost_estimate=pl.CostEstimate(flops=int(6e9), bytes_accessed=int(5e6), transcendentals=0),
    )(x, first, gains, cosine, sine)


def ffn_kernel(
    place_ref, o_ref, x_ref, cot_ref, first_ref, gain_ref,
    gate_own, gate_got, gate_swap, up_own, up_got, up_swap, down_own, down_got, down_swap,
    mixed_ref, dres_ref, datt_ref, rd_ref, keep_gu, send_gu, keep_do, send_do, gg_ref,
    acc_gu, acc_down, acc_out, gate_ref, up_ref, down_ref,
):
    step = pl.program_id(0)
    width = x_ref.shape[2]

    @pl.when(step == 0)
    def _():
        acc_gu[...] = jnp.zeros(acc_gu.shape, F32)
        acc_down[...] = jnp.zeros(acc_down.shape, F32)
        acc_out[...] = jnp.zeros(acc_out.shape, F32)
        gg_ref[...] = jnp.zeros(gg_ref.shape, F32)
        for rank in range(2):

            @pl.when(place_ref[1] == rank)
            def _():
                for ref, own in ((gate_ref, gate_own), (up_ref, up_own), (down_ref, down_own)):
                    n = own.shape[0]
                    ref[rank * n : (rank + 1) * n] = own[...]
                for core in range(2):

                    @pl.when(place_ref[0] == core)
                    def _():
                        for ref, parts in ((gate_ref, (gate_got, gate_swap)), (up_ref, (up_got, up_swap))):
                            n, m = parts[0].shape
                            for k, part in ((core, parts[0]), (1 - core, parts[1])):
                                ref[(1 - rank) * n : (2 - rank) * n, k * m : (k + 1) * m] = part[...]
                        n = down_got.shape[0]
                        for k, part in ((core, down_got), (1 - core, down_swap)):
                            low = (2 * (1 - rank) + k) * n
                            down_ref[low : low + n] = part[...]

    cols = first_ref.shape[1]
    out_w = first_ref[:, cols - width :]
    attended = o_ref[...]
    mixed = attended.astype(BF)
    residual = flat_rows(x_ref).astype(F32) + mm(mixed, out_w, TN)
    scale = rms(residual)
    normed = residual * scale
    gain = gain_ref[1:2, :]
    hidden = (normed * gain).astype(BF)
    gate = mm(hidden, gate_ref[...])
    up = mm(hidden, up_ref[...])
    sig = 0.5 * jnp.tanh(0.5 * gate) + 0.5
    silu = gate * sig
    activated = (silu * up).astype(BF)
    mixed_out = (residual + mm(activated, down_ref[...])).astype(BF)
    mixed_ref[...] = mixed_out.reshape(mixed_ref.shape)
    cot = flat_rows(cot_ref)
    d_act = mm(cot, down_ref[...], NT)
    acc_down[...] += mm(activated, cot, TN)
    d_gate = (d_act * up * sig * (1.0 + gate * (1.0 - sig))).astype(BF)
    d_up = (d_act * silu).astype(BF)
    acc_gu[0] += mm(hidden, d_gate, TN)
    acc_gu[1] += mm(hidden, d_up, TN)
    d_hidden = mm(d_gate, gate_ref[...], NT) + mm(d_up, up_ref[...], NT)
    dn = d_hidden * normed
    gg_ref[...] += jnp.sum(dn.reshape(-1, 8, width), axis=0)
    inner = jnp.mean(dn * gain, axis=-1, keepdims=True)
    d_res = cot.astype(F32) + scale * (d_hidden * gain - normed * inner)
    dres_ref[...] = d_res
    d_low = d_res.astype(BF)
    acc_out[...] += mm(mixed, d_low)
    d_att = mm(out_w, d_low, NT).astype(BF)
    datt_ref[...] = d_att
    prod = d_att.astype(F32) * attended
    for h in range(HEADS):
        rd_ref[h : h + 1, :] = jnp.sum(prod[h * 64 : (h + 1) * 64], axis=0, keepdims=True)
    rd_ref[HEADS:, :] = jnp.zeros((16 - HEADS, rd_ref.shape[1]), F32)

    @pl.when(step == pl.num_programs(0) - 1)
    def _():
        core = place_ref[0]
        half = width // 2
        ff = acc_gu.shape[2]
        for y in range(2):
            for p in range(PIECES):
                rs = slice(y * half + (p // 4) * (half // 2), y * half + (p // 4 + 1) * (half // 2))
                cs = slice((p % 4) * (ff // 4), (p % 4 + 1) * (ff // 4))
                keep_gu[y, p] = acc_gu[core, rs, cs].astype(BF)
                send_gu[y, p] = acc_gu[1 - core, rs, cs].astype(BF)
        down_rows, out_rows = ff // 32, width // 24
        for y in range(2):
            for p in range(PIECES):
                for ref, c in ((keep_do, core), (send_do, 1 - core)):
                    start = pl.multiple_of(y * (ff // 2) + (PIECES * c + p) * down_rows, 16)
                    ref[y, p, :down_rows] = acc_down[pl.ds(start, down_rows), :].astype(BF)
                    start = y * half + jnp.minimum(PIECES * c + p, half // out_rows - 1) * out_rows
                    ref[y, p, down_rows:] = acc_out[pl.ds(pl.multiple_of(start, 8), out_rows), :].astype(BF)


def feed_forward(place, attended, x, cot, first, gains, weights):
    count, sub, width = x.shape
    rows, ff = count * sub, weights[0].shape[1]
    per = FF_BLOCK // sub
    gu = (2, PIECES, width // 4, ff // 4)
    do = (2, PIECES, ff // 32 + width // 24, width)

    def whole(shape):
        return pl.BlockSpec(shape, lambda i: (0,) * len(shape), pipeline_mode=pl.Buffered(1))

    seq = pl.BlockSpec((per, sub, width), lambda i: (i, 0, 0))
    tall = pl.BlockSpec((width, FF_BLOCK), lambda i: (0, i))
    return pl.pallas_call(
        ffn_kernel,
        grid=(rows // FF_BLOCK,),
        in_specs=[
            pl.BlockSpec(memory_space=pltpu.SMEM), tall, seq, seq,
            whole(first.shape), whole(gains.shape), *(whole(w.shape) for w in weights),
        ],
        out_specs=[
            seq, pl.BlockSpec((FF_BLOCK, width), lambda i: (i, 0)), tall, pl.BlockSpec((16, FF_BLOCK), lambda i: (0, i)),
            whole(gu), whole(gu), whole(do), whole(do), whole((8, width)),
        ],
        out_shape=[
            jax.ShapeDtypeStruct(x.shape, BF),
            jax.ShapeDtypeStruct((rows, width), F32),
            jax.ShapeDtypeStruct((width, rows), BF),
            jax.ShapeDtypeStruct((16, rows), F32),
            jax.ShapeDtypeStruct(gu, BF), jax.ShapeDtypeStruct(gu, BF),
            jax.ShapeDtypeStruct(do, BF), jax.ShapeDtypeStruct(do, BF),
            jax.ShapeDtypeStruct((8, width), F32),
        ],
        scratch_shapes=[
            pltpu.VMEM((2, width, ff), F32), pltpu.VMEM((ff, width), F32), pltpu.VMEM((width, width), F32),
            pltpu.VMEM((width, ff), BF), pltpu.VMEM((width, ff), BF), pltpu.VMEM((ff, width), BF),
        ],
        compiler_params=pltpu.CompilerParams(vmem_limit_bytes=LIMIT),
        cost_estimate=pl.CostEstimate(flops=int(32e9), bytes_accessed=int(20e6), transcendentals=0),
    )(place, attended, x, cot, first, gains, *weights)


def back_kernel(*refs, spans):
    place_ref, refs = refs[0], refs[1:]
    dq_refs, refs = refs[: len(spans)], refs[len(spans) :]
    own_ref, got_ref, x_ref, dres_ref, first_ref, gain_ref, cos_ref, sin_ref, gg_ref, dx_ref = refs[:10]
    keep_ref, send_ref, acc, dt_scr, ga_scr, w_scr = refs[10:]
    step = pl.program_id(0)
    width = x_ref.shape[2]
    kv = KV_HEADS * 64
    total = width + 2 * kv

    @pl.when(step == 0)
    def _():
        acc[...] = jnp.zeros(acc.shape, F32)
        ga_scr[...] = jnp.zeros(ga_scr.shape, F32)
        w_scr[...] = first_ref[:, :total].T

    cosine, sine = cos_ref[...], -sin_ref[...]
    for (lo, hi), dq_ref in zip(spans, dq_refs):

        @pl.when((step >= lo) & (step < hi))
        def _():
            for h in range(HEADS):
                part = dq_ref[h * 64 : (h + 1) * 64, :] * (HEAD_DIM**-0.5)
                dt_scr[h * 64 : (h + 1) * 64, :] = rotated(part, cosine, sine).astype(BF)

    d_kv = own_ref[0] + got_ref[...].astype(F32)
    for h in range(KV_HEADS):
        part = d_kv[h * 64 : (h + 1) * 64] * LN2
        dt_scr[width + h * 64 : width + (h + 1) * 64, :] = rotated(part, cosine, sine).astype(BF)
    dt_scr[width + kv :, :] = d_kv[kv:].astype(BF)
    d_t = dt_scr[...]
    source = flat_rows(x_ref).astype(F32)
    scale = rms(source)
    normed = source * scale
    gain = gain_ref[0:1, :]
    hidden = (normed * gain).astype(BF)
    acc[:total] += mm(d_t, hidden)
    d_hidden = mm(d_t, w_scr[...], TN)
    dn = d_hidden * normed
    ga_scr[...] += jnp.sum(dn.reshape(-1, 8, width), axis=0)
    inner = jnp.mean(dn * gain, axis=-1, keepdims=True)
    grad = dres_ref[...] + scale * (d_hidden * gain - normed * inner)
    dx_ref[...] = grad.astype(BF).reshape(dx_ref.shape)

    @pl.when(step == pl.num_programs(0) - 1)
    def _():
        core = place_ref[0]
        acc[total : total + 1, :] = jnp.sum(ga_scr[...], axis=0, keepdims=True)
        acc[total + 1 : total + 2, :] = jnp.sum(gg_ref[...], axis=0, keepdims=True)
        half, deep = width // 2, width // 4
        for ct in range(4):
            for ref, c in ((keep_ref, core), (send_ref, 1 - core)):
                start = pl.multiple_of(c * 512 + ct * 128, 128)
                block = acc[pl.ds(start, 128), :].T.astype(BF)
                for y in range(2):
                    for rh in range(2):
                        low = y * half + rh * deep
                        ref[y, rh * 4 + ct] = block[low : low + deep]


def back_qkv(place, spans, d_query, d_kv, got, x, d_res, first, gains, cosine, sine, gg):
    count, sub, width = x.shape
    rows = count * sub
    per = BLOCK // sub
    kv2 = 2 * KV_HEADS * HEAD_DIM
    piece = (2, PIECES, width // 4, 128)

    def whole(shape):
        return pl.BlockSpec(shape, lambda i: (0,) * len(shape))

    seq = pl.BlockSpec((per, sub, width), lambda i: (i, 0, 0))
    return pl.pallas_call(
        functools.partial(back_kernel, spans=spans),
        grid=(rows // BLOCK,),
        in_specs=[
            pl.BlockSpec(memory_space=pltpu.SMEM),
            *(
                pl.BlockSpec((width, BLOCK), lambda i, lo=lo, hi=hi: (0, jnp.clip(i - lo, 0, hi - lo - 1)))
                for lo, hi in spans
            ),
            pl.BlockSpec((1, kv2, BLOCK), lambda i: (0, 0, i)),
            pl.BlockSpec((kv2, BLOCK), lambda i: (0, i)),
            seq, pl.BlockSpec((BLOCK, width), lambda i: (i, 0)),
            whole(first.shape), whole(gains.shape),
            pl.BlockSpec((32, BLOCK), lambda i: (0, i)), pl.BlockSpec((32, BLOCK), lambda i: (0, i)),
            whole(gg.shape),
        ],
        out_specs=[seq, whole(piece), whole(piece)],
        out_shape=[jax.ShapeDtypeStruct(x.shape, BF), jax.ShapeDtypeStruct(piece, BF), jax.ShapeDtypeStruct(piece, BF)],
        scratch_shapes=[
            pltpu.VMEM((1024, width), F32), pltpu.VMEM((width + kv2, BLOCK), BF), pltpu.VMEM((8, width), F32),
            pltpu.VMEM((width + kv2, width), BF),
        ],
        compiler_params=pltpu.CompilerParams(vmem_limit_bytes=LIMIT),
        cost_estimate=pl.CostEstimate(flops=int(10e9), bytes_accessed=int(10e6), transcendentals=0),
    )(place, *d_query, d_kv, got, x, d_res, first, gains, cosine, sine, gg)


def final_kernel(
    at_ref, gu4, gu_x, gu_c, do4, do_x, do_c, gate_ref, up_ref, turned_ref, out_ref, down_ref
):
    core, xb, z = at_ref[0], at_ref[1], at_ref[2]
    deep, wide = gu4.shape[1:]
    for f in range(2):
        for e in range(2):
            for d in range(4):
                gu = (gu4[d] if e == 0 else gu_x[d]) if f == 0 else gu_c[e * 4 + d]
                do = (do4[d] if e == 0 else do_x[d]) if f == 0 else do_c[e * 4 + d]
                rs = pl.ds(pl.multiple_of((xb ^ e) * deep, 16), deep)
                cs = pl.ds(pl.multiple_of((z ^ d) * wide, 128), wide)
                for c, ref in ((0, gate_ref), (1, up_ref)):

                    @pl.when((core ^ f) == c)
                    def _():
                        ref[rs, cs] = gu.astype(F32)

                m = (core ^ f) * 8 + (xb ^ e) * 4 + (z ^ d)
                rows = down_ref.shape[0] // 16
                down_ref[pl.ds(pl.multiple_of(m * rows, 8), rows), :] = do[:rows].astype(F32)
                few = do.shape[0] - rows

                @pl.when(m < out_ref.shape[0] // few)
                def _():
                    out_ref[pl.ds(pl.multiple_of(m * few, 8), few), :] = do[rows:].astype(F32)

    turned_ref[...] = down_ref[...].T


def final_ffn(at, gu4, gu_x, gu_c, do4, do_x, do_c, half, ff, width):
    f32 = lambda *s: jax.ShapeDtypeStruct(s, F32)
    return pl.pallas_call(
        final_kernel,
        in_specs=[pl.BlockSpec(memory_space=pltpu.SMEM)] + [pl.BlockSpec(memory_space=pltpu.VMEM)] * 6,
        out_specs=[pl.BlockSpec(memory_space=pltpu.VMEM)] * 4,
        out_shape=[f32(half, ff), f32(half, ff), f32(width, ff // 2), f32(half, width)],
        scratch_shapes=[pltpu.VMEM((ff // 2, width), F32)],
        compiler_params=pltpu.CompilerParams(vmem_limit_bytes=LIMIT),
        cost_estimate=pl.CostEstimate(flops=int(5e9), bytes_accessed=int(10e6), transcendentals=0),
    )(at, gu4, gu_x, gu_c, do4, do_x, do_c)


def final_t_kernel(at_ref, t4, t_x, t_c, q_ref, k_ref, v_ref, g_ref, whole):
    core, xb, z = at_ref[0], at_ref[1], at_ref[2]
    deep, wide = t4.shape[1:]
    for f in range(2):
        for e in range(2):
            for d in range(4):
                t = (t4[d] if e == 0 else t_x[d]) if f == 0 else t_c[e * 4 + d]
                rs = pl.ds(pl.multiple_of((xb ^ e) * deep, 16), deep)
                cs = pl.ds(pl.multiple_of((core ^ f) * 512 + (z ^ d) * wide, 128), wide)
                whole[rs, cs] = t.astype(F32)
    a = q_ref.shape[1]
    b = a + k_ref.shape[1]
    c = b + v_ref.shape[1]
    q_ref[...] = whole[:, :a]
    k_ref[...] = whole[:, a:b]
    v_ref[...] = whole[:, b:c]
    g_ref[...] = whole[:, c:].T[:8]


def final_t(at, t4, t_x, t_c, half, width, kv_width):
    f32 = lambda *s: jax.ShapeDtypeStruct(s, F32)
    return pl.pallas_call(
        final_t_kernel,
        in_specs=[pl.BlockSpec(memory_space=pltpu.SMEM)] + [pl.BlockSpec(memory_space=pltpu.VMEM)] * 3,
        out_specs=[pl.BlockSpec(memory_space=pltpu.VMEM)] * 4,
        out_shape=[f32(half, width), f32(half, kv_width), f32(half, kv_width), f32(8, half)],
        scratch_shapes=[pltpu.VMEM((half, 1024), F32)],
        compiler_params=pltpu.CompilerParams(vmem_limit_bytes=LIMIT),
        cost_estimate=pl.CostEstimate(flops=int(1e9), bytes_accessed=int(2e6), transcendentals=0),
    )(at, t4, t_x, t_c)


def swap(x, axis, bit):
    n = lax.axis_size(axis)
    return lax.ppermute(x, axis, [(i, i ^ (1 << bit)) for i in range(n)])


def bit_of(axis, bit):
    return (lax.axis_index(axis) >> bit) & 1


def pin(*arrays):
    return lax.optimization_barrier(arrays)


def pick(x, at):
    return lax.dynamic_index_in_dim(x, at, 0, keepdims=False)


def in_order(flag, mine, other, axis):
    return jnp.where(
        flag == 0,
        jnp.concatenate([mine, other], axis=axis),
        jnp.concatenate([other, mine], axis=axis),
    )


def plus(a, b):
    return (a.astype(F32) + b.astype(F32)).astype(BF)


def two_level():
    return lax.axis_size("fsdp") == 2 and lax.axis_size("ctx") == 16


def z_swap(x, by):
    return lax.ppermute(x, "ctx", [(i, i ^ (4 * by)) for i in range(16)])


def z_send(x):
    z = lax.axis_index("ctx") >> 2
    return pick(x, z), [pick(x, z ^ by) for by in range(1, 4)]


def z_pass(pieces):
    return [z_swap(p, by) for by, p in zip(range(1, 4), pieces)]


def z_total(mine, got):
    return sum((g.astype(F32) for g in got), mine.astype(F32)).astype(BF)


def z_join(piece):
    return [piece] + [z_swap(piece, by) for by in range(1, 4)]


def natural_gu(pieces):
    _, a, b = pieces.shape
    return pieces.reshape(2, 4, a, b).transpose(0, 2, 1, 3).reshape(2 * a, 4 * b).astype(F32)


def other_sum(x):
    x = lax.psum_scatter(x.astype(BF), "fsdp", scatter_dimension=0, tiled=True)
    return lax.psum(x, "ctx").astype(F32)


def local(tokens, gain_attn, w_query, w_key, w_value, w_out, gain_ffn, w_gate, w_up, w_down, cotangent):
    seqs, length, width = tokens.shape
    count = lax.axis_size("ctx")
    team = count // seqs
    sub = length // team
    rows = count * sub
    ff = w_gate.shape[1]
    kv_width = KV_HEADS * HEAD_DIM
    qkv_cols = width + 2 * kv_width
    place = lax.axis_index("ctx") % team
    own = gain_attn.shape[0]
    fast = two_level()

    def move(x):
        return lax.all_to_all(x.reshape(count, sub, width), "ctx", 0, 0, tiled=True)

    x = move(tokens)
    gain_rows = jnp.zeros((8, ff), BF).at[0, :own].set(gain_attn).at[1, :own].set(gain_ffn)
    first = jnp.concatenate([jnp.concatenate([w_query, w_key, w_value, w_out], axis=1), gain_rows], axis=0)
    if fast:
        core, rank = bit_of("ctx", 0), bit_of("fsdp", 0)

        def halved(shard, axis):
            half = shard.shape[axis] // 2
            return lax.dynamic_slice_in_dim(shard, core * half, half, axis)

        def other_shard(got, axis):
            return in_order(core, got, swap(got, "ctx", 0), axis)

        got = swap(halved(first, 1), "fsdp", 0)
        other = other_shard(got, 1)
        gains = in_order(rank, first[own : own + 2, :own], other[own : own + 2, :own], 1).astype(F32)
        first = in_order(rank, first[:own], other[:own], 0)
        gate_half, up_half, down_half, got = pin(halved(w_gate, 1), halved(w_up, 1), halved(w_down, 0), got)
        gate_got, up_got, down_got = (swap(h, "fsdp", 0) for h in (gate_half, up_half, down_half))
    else:
        first = lax.all_gather(first, "fsdp", axis=0)
        gains = first[:, own : own + 2, :own].transpose(1, 0, 2).reshape(2, width).astype(F32)
        first = first[:, :own].reshape(width, first.shape[2])
        gate_w, up_w, down_w = (lax.all_gather(w, "fsdp", axis=0, tiled=True) for w in (w_gate, w_up, w_down))
    gains = jnp.pad(gains, ((0, 6), (0, 0)))

    row = jnp.arange(rows, dtype=jnp.int32)
    position = (row // sub) * length + place * sub + row % sub
    frequency = THETA ** (-jnp.arange(HEAD_DIM // 2, dtype=F32) * 2.0 / HEAD_DIM)
    angles = frequency[:, None] * position.astype(F32)[None, :]
    cosine, sine = jnp.cos(angles), jnp.sin(angles)
    groups = [[t * team + p for p in range(team)] for t in range(seqs)]
    slots = jnp.stack([place, 1 - place]) if team == 2 else jnp.arange(team)
    block_row = jnp.arange(BLOCK, dtype=jnp.int32)
    base = (block_row // sub) * length + block_row % sub
    key_pos = base[None, :] + slots[:, None] * sub
    query_pos = base + place * sub
    bias = jnp.where(key_pos[:, :, None] <= query_pos[None, None, :], 0.0, NEGATIVE).astype(F32)
    flags = jnp.stack([core, rank]) if fast else jnp.zeros((2,), jnp.int32)

    x, cot_send = pin(x, cotangent)
    cot = move(cot_send)
    query, kv_own = project_qkv(x, first, gains, cosine, sine)
    if fast:
        kv_own, gate_got = pin(kv_own, gate_got)
    if team == 2:
        kv_all = (kv_own, swap(kv_own, "ctx", 0))
    else:
        kv_all = lax.all_gather(kv_own, "ctx", axis=0, axis_index_groups=groups)
        kv_all = tuple(kv_all[s] for s in range(team))
    attended, log_total = attn_fwd(bias, query, kv_all)
    if fast:
        attended, cot, *gots = pin(attended, cot, gate_got, up_got, down_got)
        gots = [(got, swap(got, "ctx", 0)) for got in gots]
        weights = [a for own_w, two in zip((w_gate, w_up, w_down), gots) for a in (own_w, *two)]
    else:
        attended, cot = pin(attended, cot)
        low, side = width // 2, ff // 2
        weights = [a for w in (gate_w, up_w) for a in (w[:low], w[low:, :side], w[low:, side:])]
        weights += [down_w[:side], down_w[side : side + side // 2], down_w[side + side // 2 :]]
    mixed, d_res, d_att, row_dot, keep_gu, send_gu, keep_do, send_do, gain_sum = feed_forward(
        flags, attended, x, cot, first, gains, weights
    )
    mixed_out = move(mixed)

    n = rows // BLOCK
    spans = ((0, n - 1), (n - 1, n))
    part = functools.partial(attn_bwd, bias, query, kv_all, d_att, log_total, row_dot)
    if fast:
        x_bit = bit_of("ctx", 1)
        got_gu, got_do = swap(send_gu, "ctx", 0), swap(send_do, "ctx", 0)
        gu, do = plus(keep_gu, got_gu), plus(keep_do, got_do)
        gu = gu.reshape((2, 2, 4) + gu.shape[2:]).swapaxes(0, 1)
        keep_gu, send_gu = pick(gu, x_bit), pick(gu, 1 - x_bit)
        keep_do, send_do = pick(do, rank), pick(do, 1 - rank)
        send_gu, send_do, row_dot = pin(send_gu, send_do, row_dot)
        part = functools.partial(attn_bwd, bias, query, kv_all, d_att, log_total, row_dot)
        got_gu, got_do = swap(send_gu, "ctx", 1), swap(send_do, "fsdp", 0)
        dq_a, before = part(*spans[0])
        got_gu, got_do, mixed_out, before = pin(got_gu, got_do, mixed_out, before)
        gu, do = plus(keep_gu, got_gu), plus(keep_do, got_do)
        do = do.reshape((2, 4) + do.shape[1:])
        keep_gu, send_gu = pick(gu, rank), pick(gu, 1 - rank)
        keep_do, send_do = pick(do, x_bit), pick(do, 1 - x_bit)
        send_gu, send_do, before = pin(send_gu, send_do, before)
        got_gu, got_do = swap(send_gu, "fsdp", 0), swap(send_do, "ctx", 1)
        dq_b, d_kv, d_kv_low = part(*spans[1], before=before, last=True)
        got_gu, got_do, d_kv_low, dq_b = pin(got_gu, got_do, d_kv_low, dq_b)
        gu, do = plus(keep_gu, got_gu), plus(keep_do, got_do)
    else:
        dq_a, before = part(*spans[0])
        dq_b, d_kv, d_kv_low = part(*spans[1], before=before, last=True)
    if team == 2:
        own_kv, got_kv = d_kv, swap(d_kv_low.reshape(2 * kv_width, rows), "ctx", 0)
    else:
        own_kv = lax.psum_scatter(d_kv_low, "ctx", scatter_dimension=0, axis_index_groups=groups)
        own_kv, got_kv = own_kv.astype(F32)[None], jnp.zeros((2 * kv_width, rows), BF)
    if fast:
        z_gu, z_do = z_send(gu), z_send(do)
        send_pin = pin(own_kv, got_kv, *z_gu[1], *z_do[1])
        own_kv, got_kv = send_pin[:2]
        z_gu, z_do = (z_gu[0], send_pin[2:5]), (z_do[0], send_pin[5:])
        z_got = [z_pass(z_gu[1]), z_pass(z_do[1])]
    d_x, keep_t, send_t = back_qkv(
        flags, spans, (dq_a, dq_b), own_kv, got_kv, x, d_res, first, gains, cosine, sine, gain_sum
    )
    if fast:
        d_x, keep_t, send_t, *got = pin(d_x, keep_t, send_t, *z_got[0], *z_got[1])
        gu, do = z_total(z_gu[0], got[:3]), z_total(z_do[0], got[3:])
    grad_tokens = move(d_x)
    if fast:
        gu_four, do_four = z_join(gu), z_join(do)
        t = plus(keep_t, swap(send_t, "ctx", 0))
        t = plus(pick(t, rank), swap(pick(t, 1 - rank), "fsdp", 0))
        t = t.reshape((2, 4) + t.shape[1:])
        t = plus(pick(t, x_bit), swap(pick(t, 1 - x_bit), "ctx", 1))
        keep_t, send_t = z_send(t)
        t_got = z_pass(send_t)
        *t_got, grad_tokens, d0, d1, d2 = pin(*t_got, grad_tokens, *do_four[1:])
        t_four = z_join(z_total(keep_t, t_got))
        do_four = jnp.stack([do_four[0], d0, d1, d2])
        do_x = swap(do_four, "ctx", 1)
        t0, t1, t2, g0, g1, g2 = pin(*t_four[1:], *gu_four[1:])
        gu_four = jnp.stack([gu_four[0], g0, g1, g2])
        gu_x = swap(gu_four, "ctx", 1)
        t_four = jnp.stack([t_four[0], t0, t1, t2])
        t_x = swap(t_four, "ctx", 1)
        t_x, do_x = pin(t_x, do_x)
        do_c = swap(jnp.concatenate([do_four, do_x], axis=0), "ctx", 0)
        t_c = swap(jnp.concatenate([t_four, t_x], axis=0), "ctx", 0)
        gu_x, t_c = pin(gu_x, t_c)
        gu_c = swap(jnp.concatenate([gu_four, gu_x], axis=0), "ctx", 0)
        at = jnp.stack([core, x_bit, lax.axis_index("ctx") >> 2])
        own_query, own_key, own_value, own_gains = final_t(at, t_four, t_x, t_c, width // 2, width, kv_width)
        own_gate, own_up, own_down, own_out = final_ffn(
            at, gu_four, gu_x, gu_c, do_four, do_x, do_c, width // 2, ff, width
        )
        own_down = own_down.T
    else:
        pair = jnp.stack([keep_gu, send_gu])
        gate, up = (jnp.concatenate([natural_gu(pair[c, y]) for y in range(2)], axis=0) for c in range(2))
        do = jnp.stack([keep_do, send_do], axis=1).reshape((32,) + keep_do.shape[2:])
        deep = ff // 32
        own_gate, own_up = other_sum(gate), other_sum(up)
        own_down = other_sum(do[:, :deep].reshape(ff, width))
        out = do[:, deep:].reshape((2, -1, width))[:, : width // 2]
        own_out = other_sum(out.reshape(width, width))
        pair = jnp.stack([keep_t, send_t])
        t = [jnp.concatenate([natural_gu(pair[c, y]) for c in range(2)], axis=1) for y in range(2)]
        own_t = other_sum(jnp.concatenate(t, axis=0))
        own_query, own_key = own_t[:, :width], own_t[:, width : width + kv_width]
        own_value, own_gains = own_t[:, width + kv_width : qkv_cols], own_t[:, qkv_cols:].T
    return (
        mixed_out.reshape(tokens.shape),
        grad_tokens.reshape(tokens.shape),
        own_gains[0],
        own_query,
        own_key,
        own_value,
        own_out,
        own_gains[1],
        own_gate,
        own_up,
        own_down,
    )


def solution(mesh):
    rows, flat, seq = P("fsdp", None), P("fsdp"), P("fsdp", "ctx", None)
    return jax.shard_map(
        local,
        mesh=mesh,
        in_specs=(seq, flat, rows, rows, rows, rows, flat, rows, rows, rows, seq),
        out_specs=(seq, seq, flat, rows, rows, rows, rows, flat, rows, rows, rows),
        check_vma=False,
    )
```
